32 devices in a mesh: exc: 8 (over z, y), space: 4 (over x, core).
Axes of the slice: x: 2, y: 2, z: 4, core: 2. Of those that a mesh axis runs over, the one named last changes fastest.
Arguments:
- adj_e: float32 [8, 192, 1024], P('exc', None, 'space'), may hold values from -6 to 6
- adj_h: float32 [8, 192, 1024], P('exc', None, 'space'), may hold values from -6 to 6
- adj_j: float32 [8, 192, 1024], P('exc', None, 'space'), may hold values from -6 to 6
- fwd_e: bfloat16 [8, 5, 192, 1024], P('exc', None, None, 'space'), may hold values from -6 to 6
- inv_eps: float32 [64, 1024], P(None, 'space'), may hold values from 0.08 to 1
- drude_weight: float32 [64, 1024], P(None, 'space'), may hold values from 0.5 to 20
- neighbor: int32 [6, 1024], P(None, 'space'), may hold values from -1 to 1023, as said below
- design_map: int32 [1024], P('space'), may hold values from 0 to 511, as said below
- port_elems: int32 [8, 512], P('exc', 'space'), may hold values from 0 to 1023, as said below
- port_profile: float32 [8, 192, 512], P('exc', None, 'space'), may hold values from -48 to 48
Outputs:
- adj_e_out: float32 [8, 192, 1024], P('exc', None, 'space')
- adj_h_out: float32 [8, 192, 1024], P('exc', None, 'space')
- grad_eps: float32 [64, 512], P(None, ('space', 'exc'))
- grad_drude: float32 [64, 512], P(None, ('space', 'exc'))
The draws below stay inside these ranges and needn't reach their ends.
Inputs may be any that keep to these rules, and one draw needn't show every extreme that they name: neighbor[f, e] is the element across face f (x-, x+, y-, y+, z-, z+) of element e, which touches it with its opposite face; it is -1 across the x- face of the first and the x+ face of the last element layer. Elements are stored layer by layer in layers of 128 elements along x, so each block of 256 elements is 2 whole layers; a y or z neighbour lies in the same layer (periodic in y and z), an x neighbour in the adjacent layer. `design_map`: an element of the b-th block of 256 elements maps to a pixel of the b-th block of 128 pixels, and every pixel holds exactly two elements. `port_elems`: columns b * 128 to (b + 1) * 128 - 1 of each row hold 128 distinct elements of the b-th block of 256 elements.
All inputs are finite; a program needn't handle non-finite values.
Results may differ from the reference program's by a relative error of at most 0.00035.
Values sent between devices are 32-bit elements; how exact they have to be, the bound alone decides.
No kernel may reach another device: no remote copies, remote signals or barrier semaphores. Data moves between devices by JAX's collectives and lax.ppermute only.
A program may use at most 64 MiB of HBM per device.

```python
import math
import jax
import jax.numpy as jnp
import numpy as np
from jax import lax

NODES = 64
GY = 16
GZ = 8
LX_DEV = 2
STEPS = 4
NSRC_DEV = 128
ELEM_DEV = 256
ELEMS = 1024
PIX_DEV = 128
PIX = 512
NSRC = 512
EXC = 8
N_SPACE = 4


def draw_neighbor(key, part):
    total_layers = LX_DEV * N_SPACE
    cells = GY * GZ

    def one_layer(number):
        return jax.random.permutation(jax.random.fold_in(key, number), cells).astype(jnp.int32)
    orders = jax.vmap(one_layer)(jnp.arange(total_layers, dtype=jnp.int32))
    places = jnp.argsort(orders, axis=1).astype(jnp.int32)
    layer_ids = jnp.arange(total_layers, dtype=jnp.int32)[:, None]
    cell_y = orders // GZ
    cell_z = orders % GZ

    def in_layer(target_cells):
        return layer_ids * cells + jnp.take_along_axis(places, target_cells, axis=1)
    below = (layer_ids - 1) * cells + jnp.take_along_axis(jnp.roll(places, 1, axis=0), orders, axis=1)
    below = jnp.where(layer_ids == 0, -1, below)
    above = (layer_ids + 1) * cells + jnp.take_along_axis(jnp.roll(places, -1, axis=0), orders, axis=1)
    above = jnp.where(layer_ids == total_layers - 1, -1, above)
    y_minus = in_layer((cell_y - 1) % GY * GZ + cell_z)
    y_plus = in_layer((cell_y + 1) % GY * GZ + cell_z)
    z_minus = in_layer(cell_y * GZ + (cell_z - 1) % GZ)
    z_plus = in_layer(cell_y * GZ + (cell_z + 1) % GZ)
    return jnp.stack([below, above, y_minus, y_plus, z_minus, z_plus]).reshape(6, total_layers * cells).astype(jnp.int32)


def draw_design_map(key, part):

    def one_block(number):
        order = jax.random.permutation(jax.random.fold_in(key, number), ELEM_DEV).astype(jnp.int32)
        return order // 2 + number * PIX_DEV
    return jax.vmap(one_block)(jnp.arange(N_SPACE, dtype=jnp.int32)).reshape(N_SPACE * ELEM_DEV).astype(jnp.int32)


def draw_port_elems(key, part):

    def one_block(number):
        inner_key = jax.random.fold_in(key, number)
        middle = 1 + jax.random.permutation(inner_key, ELEM_DEV - 2).astype(jnp.int32)[:NSRC_DEV - 2]
        chosen = jnp.concatenate([jnp.array([0, ELEM_DEV - 1], jnp.int32), middle])
        order = jax.random.permutation(jax.random.fold_in(inner_key, 7), NSRC_DEV)
        return chosen[order] + number % N_SPACE * ELEM_DEV
    numbers = jnp.arange(EXC * N_SPACE, dtype=jnp.int32)
    return jax.vmap(one_block)(numbers).reshape(EXC, N_SPACE * NSRC_DEV).astype(jnp.int32)


def levels(own_key, dims, cuts, low, largest):
    gain = 1.0
    for axis_at, shards_of in cuts:
        heights = jax.random.uniform(jax.random.fold_in(jax.random.fold_in(own_key, 6), axis_at), (shards_of,), jnp.float32, low / len(cuts), largest / len(cuts))
        gain = gain * jnp.repeat(jnp.exp(heights), dims[axis_at] // shards_of).reshape((-1,) + (1,) * (len(dims) - 1 - axis_at))
    return gain


def scatter_about(rng, extent, deviation, bound, shards=(), kind=jnp.bfloat16):
    values = deviation * jax.random.normal(rng, extent, jnp.float32)
    if shards:
        values = values * levels(rng, extent, shards, -0.22, 0.18)
    return jnp.clip(values, -bound, bound).astype(kind)


def setup_inputs(seed: int = 0) -> dict:
    keys = jax.random.split(jax.random.key(seed), 11)
    return {
        "adj_e": scatter_about(keys[0], (EXC, 3 * NODES, ELEMS), 1.0, 6.0, ((0, 8), (2, 4)), jnp.float32),
        "adj_h": scatter_about(keys[1], (EXC, 3 * NODES, ELEMS), 1.0, 6.0, ((0, 8), (2, 4)), jnp.float32),
        "adj_j": scatter_about(keys[2], (EXC, 3 * NODES, ELEMS), 1.0, 6.0, ((0, 8), (2, 4)), jnp.float32),
        "fwd_e": scatter_about(keys[3], (EXC, STEPS + 1, 3 * NODES, ELEMS), 1.0, 6.0, ((0, 8), (3, 4))),
        "inv_eps": jnp.clip(0.08 + 0.92 * jax.random.uniform(keys[4], (NODES, ELEMS), jnp.float32) ** levels(keys[4], (NODES, ELEMS), ((1, 4),), -0.2, 0.2), 0.08, 1.0),
        "drude_weight": jnp.clip(jnp.exp(math.log(20.0) - 3.6888795 * jax.random.uniform(keys[5], (NODES, ELEMS), jnp.float32) ** levels(keys[5], (NODES, ELEMS), ((1, 4),), -0.2, 0.2)), 0.5, 20.0),
        "neighbor": draw_neighbor(jax.random.fold_in(keys[10], 71), 0),
        "design_map": draw_design_map(jax.random.fold_in(keys[10], 71), 0),
        "port_elems": draw_port_elems(jax.random.fold_in(keys[10], 71), 0),
        "port_profile": scatter_about(keys[9], (EXC, 3 * NODES, NSRC), 8.0, 48.0, ((0, 8), (2, 4)), jnp.float32),
    }


TIME_STEP = 0.025
DAMPING = 0.5

def node_tables():
    points = np.array([-1.0, -1.0 / np.sqrt(5.0), 1.0 / np.sqrt(5.0), 1.0])
    barycentric = np.array([1.0 / np.prod([points[j] - points[k] for k in range(4) if k != j]) for j in range(4)])
    deriv = np.zeros((4, 4))
    for row in range(4):
        for column in range(4):
            if row != column:
                deriv[row, column] = barycentric[column] / barycentric[row] / (points[row] - points[column])
        deriv[row, row] = -np.sum(deriv[row])
    identity = np.eye(4)
    along_x = 2.0 * np.kron(np.kron(deriv, identity), identity)
    along_y = 2.0 * np.kron(np.kron(identity, deriv), identity)
    along_z = 2.0 * np.kron(np.kron(identity, identity), deriv)
    curl_table = np.zeros((192, 192))
    curl_table[0:64, 64:128] = -along_z
    curl_table[0:64, 128:192] = along_y
    curl_table[64:128, 0:64] = along_z
    curl_table[64:128, 128:192] = -along_x
    curl_table[128:192, 0:64] = -along_y
    curl_table[128:192, 64:128] = along_x
    numbers = np.arange(64).reshape(4, 4, 4)
    faces = np.stack([numbers[0].ravel(), numbers[3].ravel(), numbers[:, 0].ravel(), numbers[:, 3].ravel(), numbers[:, :, 0].ravel(), numbers[:, :, 3].ravel()])
    lift_table = np.zeros((192, 288))
    for face in range(6):
        direction = face // 2
        sign = 1.0 if face % 2 else -1.0
        for component in range(3):
            for other in range(3):
                parity = (component - direction) * (direction - other) * (other - component) / 2.0
                if parity != 0:
                    for node in range(16):
                        lift_table[component * 64 + faces[face, node], other * 96 + face * 16 + node] += 6.0 * sign * parity
    return (curl_table, faces, lift_table)

def flux_term(field, neighbor, faces, lift_table):
    count = field.shape[1]
    cube = field.reshape(3, 64, count)
    inner = cube[:, faces.reshape(-1), :].reshape(288, count)
    pieces = []
    for face in range(6):
        rows = cube[:, faces[face ^ 1], :]
        target = neighbor[face]
        picked = jnp.take(rows, jnp.clip(target, 0, count - 1), axis=2)
        pieces.append(picked * (target >= 0).astype(jnp.float32))
    outer = jnp.stack(pieces, axis=1).reshape(288, count)
    return jnp.dot(lift_table, inner - outer, preferred_element_type=jnp.float32, precision=lax.Precision.HIGHEST)

def reference(adj_e, adj_h, adj_j, fwd_e, inv_eps, drude_weight, neighbor, design_map, port_elems, port_profile):
    curl_np, faces, lift_np = node_tables()
    curl_table = jnp.asarray(curl_np, jnp.float32)
    lift_table = jnp.asarray(lift_np, jnp.float32)
    inverse = jnp.tile(inv_eps, (3, 1))
    plasma = jnp.tile(drude_weight, (3, 1))
    count = adj_e.shape[2]

    def one_excitation(carry, inputs):
        electric, magnetic, current, history, ports, profile = inputs
        source = jnp.zeros((3 * NODES, count), jnp.float32).at[:, ports].add(profile)
        sens_eps = jnp.zeros((NODES, count), jnp.float32)
        sens_drude = jnp.zeros((NODES, count), jnp.float32)
        for step in range(STEPS):
            magnetic = magnetic + TIME_STEP * (flux_term(electric, neighbor, faces, lift_table) - jnp.dot(curl_table, electric, preferred_element_type=jnp.float32, precision=lax.Precision.HIGHEST))
            current = (1.0 - TIME_STEP * DAMPING) * current + TIME_STEP * plasma * electric
            electric = electric + TIME_STEP * inverse * (jnp.dot(curl_table, magnetic, preferred_element_type=jnp.float32, precision=lax.Precision.HIGHEST) - flux_term(magnetic, neighbor, faces, lift_table) - current - source)
            before = history[step].astype(jnp.float32)
            change = history[step + 1].astype(jnp.float32) - before
            sens_eps = sens_eps + lax.optimization_barrier(jnp.sum((electric * change).reshape(3, NODES, count), axis=0))
            sens_drude = sens_drude + lax.optimization_barrier(jnp.sum((current * before).reshape(3, NODES, count), axis=0))
        return ((carry[0] + sens_eps, carry[1] + sens_drude), (electric, magnetic))
    start = (jnp.zeros((NODES, count), jnp.float32), jnp.zeros((NODES, count), jnp.float32))
    (total_eps, total_drude), (out_e, out_h) = lax.scan(one_excitation, start, (adj_e, adj_h, adj_j, fwd_e, port_elems, port_profile))
    excitations = adj_e.shape[0]
    grad_eps = jax.ops.segment_sum(total_eps.T, design_map, num_segments=PIX).T / excitations
    grad_drude = jax.ops.segment_sum(total_drude.T, design_map, num_segments=PIX).T / excitations
    return (out_e, out_h, grad_eps, grad_drude)
```

```python
import functools

import jax
import jax.numpy as jnp
import ml_dtypes
import numpy as np
from jax import lax
from jax.experimental import pallas as pl
from jax.experimental.pallas import tpu as pltpu
from jax.sharding import PartitionSpec as P

NODES = 64
ROWS = 3 * NODES
LAYER = 128
PIX_DEV = 128

TIME_STEP = 0.025
DAMPING = 0.5
KEEP = 1.0 - TIME_STEP * DAMPING

TANGENT = 32
PART = ROWS - 48
E_NEAR = 0
E_FAR = E_NEAR + ROWS
H_NEAR = E_FAR + PART
H_FAR = H_NEAR + ROWS
Q_NEAR = H_FAR + TANGENT
V_NEAR = Q_NEAR + PART
N_NEAR = V_NEAR + NODES
N_FAR = N_NEAR + 8
FIRST = N_FAR + 8
SECOND = V_NEAR

A2, A1, L0, L1, B1, B2 = range(6)
WIDE = 6 * LAYER

BF16 = jnp.bfloat16
F32 = jnp.float32


def tangential(face):
    return [c for c in range(3) if c != face // 2]


def node_tables():
    points = np.array([-1.0, -1.0 / np.sqrt(5.0), 1.0 / np.sqrt(5.0), 1.0])
    barycentric = np.array(
        [1.0 / np.prod([points[j] - points[k] for k in range(4) if k != j]) for j in range(4)]
    )
    deriv = np.zeros((4, 4))
    for row in range(4):
        for column in range(4):
            if row != column:
                deriv[row, column] = (
                    barycentric[column] / barycentric[row] / (points[row] - points[column])
                )
        deriv[row, row] = -np.sum(deriv[row])
    identity = np.eye(4)
    along_x = 2.0 * np.kron(np.kron(deriv, identity), identity)
    along_y = 2.0 * np.kron(np.kron(identity, deriv), identity)
    along_z = 2.0 * np.kron(np.kron(identity, identity), deriv)
    curl = np.zeros((192, 192))
    curl[0:64, 64:128] = -along_z
    curl[0:64, 128:192] = along_y
    curl[64:128, 0:64] = along_z
    curl[64:128, 128:192] = -along_x
    curl[128:192, 0:64] = -along_y
    curl[128:192, 64:128] = along_x
    numbers = np.arange(64).reshape(4, 4, 4)
    faces = np.stack(
        [
            numbers[0].ravel(),
            numbers[3].ravel(),
            numbers[:, 0].ravel(),
            numbers[:, 3].ravel(),
            numbers[:, :, 0].ravel(),
            numbers[:, :, 3].ravel(),
        ]
    )
    inner = np.zeros((192, 192))
    outer = np.zeros((192, 192))
    for face in range(6):
        direction = face // 2
        sign = 1.0 if face % 2 else -1.0
        for component in range(3):
            for place, other in enumerate(tangential(face)):
                parity = (component - direction) * (direction - other) * (other - component) / 2.0
                if parity != 0:
                    for node in range(16):
                        value = 6.0 * sign * parity
                        row = component * 64 + faces[face, node]
                        outer[row, face * 32 + place * 16 + node] += value
                        inner[row, other * 64 + faces[face, node]] += value
    return inner - curl, outer


def step_table():
    own, outer = node_tables()
    high = own.astype(ml_dtypes.bfloat16)
    low = (own - high.astype(np.float64)).astype(ml_dtypes.bfloat16)
    lift = (-outer).astype(ml_dtypes.bfloat16)
    return np.concatenate([high, high, low, lift, lift], axis=1)


def halves(x):
    high = x.astype(BF16)
    return high, (x - high.astype(F32)).astype(BF16)


def dot(a, b):
    return jnp.dot(a, b, preferred_element_type=F32)


def dot_t(a, b):
    return lax.dot_general(a, b, (((1,), (1,)), ((), ())), preferred_element_type=F32)


def thrice(x):
    return jnp.concatenate([x, x, x], axis=0)


def folded(x):
    return x[0:NODES] + x[NODES : 2 * NODES] + x[2 * NODES : ROWS]


def local_index(neighbor):
    return jnp.where(neighbor < 0, -1, jnp.bitwise_and(neighbor, LAYER - 1))


def first_columns(ref):
    return ref[:, 0:LAYER]


def last_columns(ref):
    return ref[:, LAYER : 2 * LAYER]


def send_fields(up, down, electric, magnetic, drive):
    left, right = slice(0, LAYER), slice(LAYER, 2 * LAYER)
    up[E_NEAR : E_NEAR + ROWS, :] = electric[:, right]
    up[E_FAR : E_FAR + PART, :] = electric[48:ROWS, left]
    up[H_NEAR : H_NEAR + ROWS, :] = magnetic[:, right]
    up[H_FAR : H_FAR + 16, :] = magnetic[112:128, left]
    up[H_FAR + 16 : H_FAR + 32, :] = magnetic[176:192, left]
    up[Q_NEAR : Q_NEAR + PART, :] = drive[48:ROWS, right]
    down[E_NEAR : E_NEAR + ROWS, :] = electric[:, left]
    down[E_FAR : E_FAR + 16, :] = electric[0:16, right]
    down[E_FAR + 16 : E_FAR + PART, :] = electric[64:ROWS, right]
    down[H_NEAR : H_NEAR + ROWS, :] = magnetic[:, left]
    down[H_FAR : H_FAR + 16, :] = magnetic[64:80, right]
    down[H_FAR + 16 : H_FAR + 32, :] = magnetic[128:144, right]
    down[Q_NEAR : Q_NEAR + 16, :] = drive[0:16, left]
    down[Q_NEAR + 16 : Q_NEAR + PART, :] = drive[64:ROWS, left]


def pack_kernel(e, h, j, v, w, neighbor, ports, profile, up, down, source):
    count = e.shape[1]
    place = jnp.bitwise_and(ports[...], count - 1)
    hot = lax.broadcasted_iota(jnp.int32, (count, place.shape[1]), 0) == place
    hot = hot.astype(F32).astype(BF16)
    high, low = halves(profile[...])
    spread = dot_t(high, hot) + dot_t(low, hot)
    source[...] = spread
    electric = e[...]
    drive = KEEP * j[...] + TIME_STEP * thrice(w[...]) * electric + spread
    send_fields(up, down, electric, h[...], drive)
    up[V_NEAR : V_NEAR + NODES, :] = last_columns(v)
    down[V_NEAR : V_NEAR + NODES, :] = first_columns(v)
    index = local_index(neighbor[...]).astype(F32)
    blank = jnp.zeros((2, LAYER), F32)
    head = jnp.concatenate([index[:, 0:LAYER], blank], axis=0)
    tail = jnp.concatenate([index[:, LAYER : 2 * LAYER], blank], axis=0)
    up[N_NEAR : N_NEAR + 8, :] = tail
    up[N_FAR : N_FAR + 8, :] = head
    down[N_NEAR : N_NEAR + 8, :] = head
    down[N_FAR : N_FAR + 8, :] = tail


class Block:
    def __init__(self, table, fe, fh, q, v, x, t, p):
        self.table, self.fe, self.fh, self.q, self.v = table, fe, fh, q, v
        self.x, self.t, self.p = x, t, p

    def load(self, e, h, first_a, first_b, now_a, now_b, neighbor, v):
        fe, fh, q = self.fe, self.fh, self.q
        for side, layer in enumerate((L0, L1)):
            columns = slice(side * LAYER, (side + 1) * LAYER)
            fe[layer] = e[:, columns]
            fh[layer] = h[:, columns]
            self.v[layer - A1] = v[:, columns]
        blank = jnp.zeros((48, LAYER), F32)
        fe[A1] = now_a[E_NEAR : E_NEAR + ROWS, :]
        fe[A2, 0:48, :] = blank
        fe[A2, 48:ROWS, :] = now_a[E_FAR : E_FAR + PART, :]
        fh[A1] = now_a[H_NEAR : H_NEAR + ROWS, :]
        fh[A2] = jnp.zeros((ROWS, LAYER), F32)
        fh[A2, 112:128, :] = now_a[H_FAR : H_FAR + 16, :]
        fh[A2, 176:192, :] = now_a[H_FAR + 16 : H_FAR + 32, :]
        q[0, 0:48, :] = blank
        q[0, 48:ROWS, :] = now_a[Q_NEAR : Q_NEAR + PART, :]
        fe[B1] = now_b[E_NEAR : E_NEAR + ROWS, :]
        fe[B2, 0:16, :] = now_b[E_FAR : E_FAR + 16, :]
        fe[B2, 16:64, :] = blank
        fe[B2, 64:ROWS, :] = now_b[E_FAR + 16 : E_FAR + PART, :]
        fh[B1] = now_b[H_NEAR : H_NEAR + ROWS, :]
        fh[B2] = jnp.zeros((ROWS, LAYER), F32)
        fh[B2, 64:80, :] = now_b[H_FAR : H_FAR + 16, :]
        fh[B2, 128:144, :] = now_b[H_FAR + 16 : H_FAR + 32, :]
        q[1, 0:16, :] = now_b[Q_NEAR : Q_NEAR + 16, :]
        q[1, 16:64, :] = blank
        q[1, 64:ROWS, :] = now_b[Q_NEAR + 16 : Q_NEAR + PART, :]
        self.v[0] = first_a[V_NEAR : V_NEAR + NODES, :]
        self.v[3] = first_b[V_NEAR : V_NEAR + NODES, :]
        index = local_index(neighbor[...])
        tables = [
            first_a[N_FAR : N_FAR + 8, :].astype(jnp.int32),
            first_a[N_NEAR : N_NEAR + 8, :].astype(jnp.int32),
            index[:, 0:LAYER],
            index[:, LAYER : 2 * LAYER],
            first_b[N_NEAR : N_NEAR + 8, :].astype(jnp.int32),
            first_b[N_FAR : N_FAR + 8, :].astype(jnp.int32),
        ]
        rows = lax.broadcasted_iota(jnp.int32, (LAYER, LAYER), 0)
        for layer in range(6):
            for face in range(6):
                if self.present(layer, face):
                    hot = rows == tables[layer][face : face + 1, :]
                    self.p[6 * layer + face] = hot.astype(F32).astype(BF16)
        nothing = jnp.zeros((32, LAYER), BF16)
        for layer, face in ((A2, 0), (B2, 1)):
            columns = slice(layer * LAYER, (layer + 1) * LAYER)
            for start in (3 * ROWS, 4 * ROWS):
                self.x[start + 32 * face : start + 32 * face + 32, columns] = nothing

    @staticmethod
    def present(layer, face):
        return not (layer == A2 and face == 0 or layer == B2 and face == 1)

    def face_rows(self, field, layer, face):
        offset = face % 2
        pieces = []
        for c in tangential(face):
            base = c * NODES
            if face < 2:
                pieces.append(field[layer, base + 48 * offset : base + 48 * offset + 16, :])
            elif face < 4:
                for i in range(4):
                    at = base + 16 * i + 12 * offset
                    pieces.append(field[layer, at : at + 4, :])
            else:
                pieces.append(field[layer, pl.ds(base + 3 * offset, 16, stride=4), :])
        return jnp.concatenate(pieces, axis=0)

    def rate(self, field, first, last, skip=()):
        wanted = [
            (layer, face)
            for layer in range(first, last + 1)
            for face in range(6)
            if self.present(layer, face) and (layer, face) not in skip
        ]
        for layer, face in wanted:
            there = layer + (-1, 1, 0, 0, 0, 0)[face]
            top, rest = halves(self.face_rows(field, there, face ^ 1))
            self.t[layer, face, 0:32, :] = top
            self.t[layer, face, 32:64, :] = rest
        for layer in range(first, last + 1):
            here = slice(layer * LAYER, (layer + 1) * LAYER)
            top, rest = halves(field[layer])
            self.x[0:ROWS, here] = top
            self.x[ROWS : 2 * ROWS, here] = rest
            self.x[2 * ROWS : 3 * ROWS, here] = top
        for layer, face in wanted:
            here = slice(layer * LAYER, (layer + 1) * LAYER)
            got = dot(self.t[layer, face], self.p[6 * layer + face]).astype(BF16)
            at = 3 * ROWS + 32 * face
            self.x[at : at + 32, here] = got[0:32]
            self.x[at + ROWS : at + ROWS + 32, here] = got[32:64]
        rates = []
        for layer in range(first, last + 1, 2):
            pair = dot(self.table[...], self.x[:, layer * LAYER : (layer + 2) * LAYER])
            rates += [pair[:, 0:LAYER], pair[:, LAYER : 2 * LAYER]]
        return rates

    def steps(self, current, source, w):
        weight = [TIME_STEP * thrice(w[:, 0:LAYER]), TIME_STEP * thrice(w[:, LAYER : 2 * LAYER])]
        driven = [source[:, 0:LAYER], source[:, LAYER : 2 * LAYER]]
        before_j = [current[:, 0:LAYER], current[:, LAYER : 2 * LAYER]]
        for layer, rate in enumerate(self.rate(self.fe, A2, B2)):
            self.fh[layer] += TIME_STEP * rate
        first_j = [KEEP * before_j[i] + weight[i] * self.fe[L0 + i] for i in range(2)]
        drive = [self.q[0], first_j[0] + driven[0], first_j[1] + driven[1], self.q[1]]
        for i, rate in enumerate(self.rate(self.fh, A1, B1)):
            self.fe[A1 + i] -= TIME_STEP * thrice(self.v[i]) * (rate + drive[i])
        first_e = [self.fe[L0], self.fe[L1]]
        for i, rate in enumerate(self.rate(self.fe, A1, B1, ((A1, 0), (B1, 1)))):
            self.fh[A1 + i] += TIME_STEP * rate
        second_j = [KEEP * first_j[i] + weight[i] * first_e[i] for i in range(2)]
        second_e = []
        for i, rate in enumerate(self.rate(self.fh, L0, L1)):
            scale = TIME_STEP * thrice(self.v[1 + i])
            second_e.append(first_e[i] - scale * (rate + second_j[i] + driven[i]))
        magnetic = [self.fh[L0], self.fh[L1]]
        return [
            jnp.concatenate(pair, axis=1)
            for pair in (first_e, first_j, second_e, second_j, magnetic)
        ]


def scratch():
    return [
        pltpu.VMEM((6, ROWS, LAYER), F32),
        pltpu.VMEM((6, ROWS, LAYER), F32),
        pltpu.VMEM((2, ROWS, LAYER), F32),
        pltpu.VMEM((4, NODES, LAYER), F32),
        pltpu.VMEM((5 * ROWS, WIDE), BF16),
        pltpu.VMEM((6, 6, 64, LAYER), BF16),
        pltpu.VMEM((36, LAYER, LAYER), BF16),
    ]


def middle_kernel(table, e, h, j, v, w, neighbor, source, from_a, from_b, *rest):
    out_e, out_h, out_j, mid_e, mid_j, up, down = rest[:7]
    block = Block(table, *rest[7:])
    block.load(e, h, from_a, from_b, from_a, from_b, neighbor, v)
    first_e, first_j, second_e, second_j, magnetic = block.steps(j, source, w)
    mid_e[...] = first_e
    mid_j[...] = first_j
    out_e[...] = second_e
    out_j[...] = second_j
    out_h[...] = magnetic
    drive = KEEP * second_j + TIME_STEP * thrice(w[...]) * second_e + source[...]
    send_fields(up, down, second_e, magnetic, drive)


def early_kernel(mid_e, mid_j, end_e, end_j, levels, out):
    start = levels[0].astype(F32)
    middle = levels[1].astype(F32)
    end = levels[2].astype(F32)
    out[0:NODES] = folded(mid_e[...] * (middle - start) + end_e[...] * (end - middle))
    out[NODES : 2 * NODES] = folded(mid_j[...] * start + end_j[...] * middle)


def last_kernel(
    table, e, h, j, v, w, neighbor, source, first_a, first_b, now_a, now_b, *rest
):
    levels, early, design, out_e, out_h, sums = rest[:6]
    block = Block(table, *rest[6:])
    block.load(e, h, first_a, first_b, now_a, now_b, neighbor, v)
    first_e, first_j, second_e, second_j, magnetic = block.steps(j, source, w)
    out_e[...] = second_e
    out_h[...] = magnetic
    start = levels[2].astype(F32)
    middle = levels[3].astype(F32)
    end = levels[4].astype(F32)
    eps = folded(first_e * (middle - start) + second_e * (end - middle))
    drude = folded(first_j * start + second_j * middle)
    both = jnp.concatenate([eps, drude], axis=0) + early[...]
    pixel = jnp.bitwise_and(design[...], PIX_DEV - 1)
    hot = lax.broadcasted_iota(jnp.int32, (PIX_DEV, both.shape[1]), 0) == pixel
    hot = hot.astype(F32).astype(BF16)
    high, low = halves(both)
    sums[...] = dot_t(hot, high) + dot_t(hot, low)


def total_kernel(owners, parts, eps, drude):
    share = parts.shape[0] // owners
    total = parts[0:share]
    for owner in range(1, owners):
        total = total + parts[owner * share : (owner + 1) * share]
    turned = (total * (1.0 / owners)).T
    eps[...] = turned[0:NODES]
    drude[...] = turned[NODES : 2 * NODES]


def call(kernel, outs, args, scratch_shapes=(), flops=0):
    whole = pl.BlockSpec(memory_space=pltpu.VMEM)
    moved = sum(4 * int(np.prod(o.shape)) for o in outs) + sum(
        a.dtype.itemsize * int(np.prod(a.shape)) for a in args
    )
    return pl.pallas_call(
        kernel,
        out_shape=outs,
        in_specs=[whole] * len(args),
        out_specs=[whole] * len(outs),
        scratch_shapes=list(scratch_shapes),
        compiler_params=pltpu.CompilerParams(vmem_limit_bytes=24 * 1024 * 1024),
        cost_estimate=pl.CostEstimate(flops=flops, bytes_accessed=moved, transcendentals=0),
    )(*args)


def f32(*shape):
    return jax.ShapeDtypeStruct(shape, F32)


def exchange(up, down):
    size = lax.axis_size("space")
    above = [(i, i + 1) for i in range(size - 1)]
    below = [(i + 1, i) for i in range(size - 1)]
    return lax.ppermute(up, "space", above), lax.ppermute(down, "space", below)


def local(
    adj_e,
    adj_h,
    adj_j,
    fwd_e,
    inv_eps,
    drude_weight,
    neighbor,
    design_map,
    port_elems,
    port_profile,
):
    count = adj_e.shape[2]
    owners = lax.axis_size("exc")
    table = jnp.asarray(step_table())
    e, h, j, levels = adj_e[0], adj_h[0], adj_j[0], fwd_e[0]
    field = f32(ROWS, count)
    flops = 2 * ROWS * 5 * ROWS * LAYER * 16

    up, down, source = call(
        pack_kernel,
        [f32(FIRST, LAYER), f32(FIRST, LAYER), field],
        [e, h, j, inv_eps, drude_weight, neighbor, port_elems, port_profile[0]],
    )
    first_a, first_b = exchange(up, down)
    e2, h2, j2, e1, j1, up, down = call(
        middle_kernel,
        [field] * 5 + [f32(SECOND, LAYER)] * 2,
        [table, e, h, j, inv_eps, drude_weight, neighbor, source, first_a, first_b],
        scratch_shapes=scratch(),
        flops=flops,
    )
    now_a, now_b = exchange(up, down)
    (early,) = call(
        early_kernel,
        [f32(2 * NODES, count)],
        [e1, j1, e2, j2, levels],
    )
    out_e, out_h, sums = call(
        last_kernel,
        [field, field, f32(PIX_DEV, 2 * NODES)],
        [table, e2, h2, j2, inv_eps, drude_weight, neighbor, source]
        + [first_a, first_b, now_a, now_b]
        + [levels, early, design_map.reshape(1, count)],
        scratch(),
        flops,
    )
    parts = lax.all_to_all(sums, "exc", split_axis=0, concat_axis=0, tiled=True)
    grad_eps, grad_drude = call(
        functools.partial(total_kernel, owners),
        [f32(NODES, PIX_DEV // owners)] * 2,
        [parts],
    )
    return out_e[None], out_h[None], grad_eps, grad_drude


def solution(mesh):
    return jax.shard_map(
        local,
        mesh=mesh,
        in_specs=(
            P("exc", None, "space"),
            P("exc", None, "space"),
            P("exc", None, "space"),
            P("exc", None, None, "space"),
            P(None, "space"),
            P(None, "space"),
            P(None, "space"),
            P("space"),
            P("exc", "space"),
            P("exc", None, "space"),
        ),
        out_specs=(
            P("exc", None, "space"),
            P("exc", None, "space"),
            P(None, ("space", "exc")),
            P(None, ("space", "exc")),
        ),
        check_vma=False,
    )
```

```python
import functools

import jax
import jax.numpy as jnp
import ml_dtypes
import numpy as np
from jax import lax
from jax.experimental import pallas as pl
from jax.experimental.pallas import tpu as pltpu
from jax.sharding import PartitionSpec as P

NODES = 64
ROWS = 3 * NODES
LAYER = 128
PIX_DEV = 128

TIME_STEP = 0.025
DAMPING = 0.5
KEEP = 1.0 - TIME_STEP * DAMPING

TANGENT = 32
E_START = 0
H_FIRST = 32
E_FIRST = 64
H_SECOND = 96
SECOND = 128
V_NEAR = 128
N_NEAR = V_NEAR + NODES
FIRST = N_NEAR + 8

A1, L0, L1, B1 = range(4)

BF16 = jnp.bfloat16
F32 = jnp.float32


def tangential(face):
    return [c for c in range(3) if c != face // 2]


def node_tables():
    points = np.array([-1.0, -1.0 / np.sqrt(5.0), 1.0 / np.sqrt(5.0), 1.0])
    barycentric = np.array(
        [1.0 / np.prod([points[j] - points[k] for k in range(4) if k != j]) for j in range(4)]
    )
    deriv = np.zeros((4, 4))
    for row in range(4):
        for column in range(4):
            if row != column:
                deriv[row, column] = (
                    barycentric[column] / barycentric[row] / (points[row] - points[column])
                )
        deriv[row, row] = -np.sum(deriv[row])
    identity = np.eye(4)
    along_x = 2.0 * np.kron(np.kron(deriv, identity), identity)
    along_y = 2.0 * np.kron(np.kron(identity, deriv), identity)
    along_z = 2.0 * np.kron(np.kron(identity, identity), deriv)
    curl = np.zeros((192, 192))
    curl[0:64, 64:128] = -along_z
    curl[0:64, 128:192] = along_y
    curl[64:128, 0:64] = along_z
    curl[64:128, 128:192] = -along_x
    curl[128:192, 0:64] = -along_y
    curl[128:192, 64:128] = along_x
    numbers = np.arange(64).reshape(4, 4, 4)
    faces = np.stack(
        [
            numbers[0].ravel(),
            numbers[3].ravel(),
            numbers[:, 0].ravel(),
            numbers[:, 3].ravel(),
            numbers[:, :, 0].ravel(),
            numbers[:, :, 3].ravel(),
        ]
    )
    inner = np.zeros((192, 192))
    outer = np.zeros((192, 192))
    for face in range(6):
        direction = face // 2
        sign = 1.0 if face % 2 else -1.0
        for component in range(3):
            for place, other in enumerate(tangential(face)):
                parity = (component - direction) * (direction - other) * (other - component) / 2.0
                if parity != 0:
                    for node in range(16):
                        value = 6.0 * sign * parity
                        row = component * 64 + faces[face, node]
                        outer[row, face * 32 + place * 16 + node] += value
                        inner[row, other * 64 + faces[face, node]] += value
    return inner - curl, outer


def step_table():
    own, outer = node_tables()
    high = own.astype(ml_dtypes.bfloat16)
    low = (own - high.astype(np.float64)).astype(ml_dtypes.bfloat16)
    lift = (-outer).astype(ml_dtypes.bfloat16)
    return np.concatenate([high, high, low, lift, lift], axis=1)


def halves(x):
    high = x.astype(BF16)
    return high, (x - high.astype(F32)).astype(BF16)


def dot(a, b):
    return jnp.dot(a, b, preferred_element_type=F32)


def dot_t(a, b):
    return lax.dot_general(a, b, (((1,), (1,)), ((), ())), preferred_element_type=F32)


def thrice(x):
    return jnp.concatenate([x, x, x], axis=0)


def folded(x):
    return x[0:NODES] + x[NODES : 2 * NODES] + x[2 * NODES : ROWS]


def local_index(neighbor):
    return jnp.where(neighbor < 0, -1, jnp.bitwise_and(neighbor, LAYER - 1))


def hot_at(layer, face):
    if layer in (L0, L1):
        return 6 * (layer - L0) + face
    return 12 + (face - 1 if layer == A1 else 5 + (face - 1 if face else 0))


def one_hot(rows, targets):
    return (rows == targets).astype(F32).astype(BF16)


def layer_rows():
    return lax.broadcasted_iota(jnp.int32, (LAYER, LAYER), 0)


def face_rows(field, layer, face):
    offset = face % 2
    pieces = []
    for c in tangential(face):
        base = c * NODES
        if face < 2:
            pieces.append(field[layer, base + 48 * offset : base + 48 * offset + 16, :])
        elif face < 4:
            for i in range(4):
                at = base + 16 * i + 12 * offset
                pieces.append(field[layer, at : at + 4, :])
        else:
            pieces.append(field[layer, pl.ds(base + 3 * offset, 16, stride=4), :])
    return jnp.concatenate(pieces, axis=0)


def gathered(traces, hot):
    high, low = halves(traces)
    return dot(jnp.concatenate([high, low], axis=0), hot)


def rate(table, x, hots, field, layers, outer):
    first, last = layers[0], layers[-1]
    for layer in layers:
        here = slice(layer * LAYER, (layer + 1) * LAYER)
        high, low = halves(field[layer])
        x[0:ROWS, here] = high
        x[ROWS : 2 * ROWS, here] = low
        x[2 * ROWS : 3 * ROWS, here] = high
        for face in range(6):
            at = 3 * ROWS + TANGENT * face
            traces = outer(layer, face)
            if traces is None:
                nothing = jnp.zeros((TANGENT, LAYER), BF16)
                x[at : at + TANGENT, here] = nothing
                x[at + ROWS : at + ROWS + TANGENT, here] = nothing
            else:
                got = gathered(traces, hots(layer, face)).astype(BF16)
                x[at : at + TANGENT, here] = got[0:TANGENT]
                x[at + ROWS : at + ROWS + TANGENT, here] = got[TANGENT : 2 * TANGENT]
    found = dot(table[...], x[:, first * LAYER : (last + 1) * LAYER])
    return [found[:, i * LAYER : (i + 1) * LAYER] for i in range(len(layers))]


def neighbour(layer, face):
    return layer + (-1, 1, 0, 0, 0, 0)[face]


def lonely(table, x, hots, fe, fh, drive, v):
    own = (L0, L1)

    def outer_of(field):
        def outer(layer, face):
            there = neighbour(layer, face)
            return face_rows(field, there, face ^ 1) if there in own else None

        return outer

    def ends(field):
        return face_rows(field, L1, 1), face_rows(field, L0, 0)

    found = [ends(fe)]
    for i, change in enumerate(rate(table, x, hots, fe, own, outer_of(fe))):
        fh[L0 + i] += TIME_STEP * change
    found.append(ends(fh))
    for i, change in enumerate(rate(table, x, hots, fh, own, outer_of(fh))):
        fe[L0 + i] -= TIME_STEP * thrice(v[i]) * (change + drive[i])
    found.append(ends(fe))
    for i, change in enumerate(rate(table, x, hots, fe, own, outer_of(fe))):
        fh[L0 + i] += TIME_STEP * change
    found.append(ends(fh))
    return [jnp.concatenate(traces, axis=0) for traces in zip(*found)]


def response(traces, hot, face):
    parts = gathered(traces, hot)
    both = (6.0 * TIME_STEP) * (parts[0:TANGENT] + parts[TANGENT : 2 * TANGENT])
    sign = 1.0 if face else -1.0
    return sign * both[16:32], -sign * both[0:16]


def two_steps(table, x, hots, fe, fh, e, h, j, source, v, w, v_near, sent_a, sent_b):
    own, wide = (L0, L1), (A1, L0, L1, B1)
    for i in range(2):
        fe[L0 + i] = e[i]
        fh[L0 + i] = h[i]
    blank = jnp.zeros((ROWS, LAYER), F32)
    fh[A1] = blank
    fh[B1] = blank

    def outer_of(field, start, answered=True):
        def outer(layer, face):
            if (layer, face) in ((A1, 0), (B1, 1)):
                return None
            there = neighbour(layer, face)
            if layer in own and there not in own:
                sent = sent_a if there == A1 else sent_b
                traces = sent[start : start + TANGENT, :]
                return traces + face_rows(field, there, face ^ 1) if answered else traces
            return face_rows(field, there, face ^ 1)

        return outer

    weight = [TIME_STEP * thrice(w[i]) for i in range(2)]
    changes = rate(table, x, hots, fe, own, outer_of(fe, E_START, False))
    for i in range(2):
        fh[L0 + i] += TIME_STEP * changes[i]
    at_y, at_z = response(face_rows(fe, L0, 0), hots(A1, 1), 1)
    fh[A1, 112:128, :] = at_y
    fh[A1, 176:192, :] = at_z
    at_y, at_z = response(face_rows(fe, L1, 1), hots(B1, 0), 0)
    fh[B1, 64:80, :] = at_y
    fh[B1, 128:144, :] = at_z

    first_j = [KEEP * j[i] + weight[i] * e[i] for i in range(2)]
    changes = rate(table, x, hots, fh, wide, outer_of(fh, H_FIRST))
    for i in range(2):
        fe[L0 + i] -= TIME_STEP * thrice(v[i]) * (changes[1 + i] + first_j[i] + source[i])
    fe[A1] = -TIME_STEP * thrice(v_near[0]) * changes[0]
    fe[B1] = -TIME_STEP * thrice(v_near[1]) * changes[3]
    first_e = [fe[L0], fe[L1]]

    for layer, change in zip(wide, rate(table, x, hots, fe, wide, outer_of(fe, E_FIRST))):
        fh[layer] += TIME_STEP * change
    second_j = [KEEP * first_j[i] + weight[i] * first_e[i] for i in range(2)]
    changes = rate(table, x, hots, fh, own, outer_of(fh, H_SECOND))
    for i in range(2):
        fe[L0 + i] -= TIME_STEP * thrice(v[i]) * (changes[i] + second_j[i] + source[i])
    return first_e, first_j, [fe[L0], fe[L1]], second_j, [fh[L0], fh[L1]]


def odd_rank():
    return lax.rem(lax.axis_index("space"), 2) == 1


def send(across, inside, at, up, down):
    odd = odd_rank()
    rows = slice(at, at + up.shape[0])
    across[rows, :] = jnp.where(odd, up, down)
    inside[rows, :] = jnp.where(odd, down, up)


def sides(across, inside, a, b, rows):
    odd = odd_rank()
    from_across, from_inside = across[0:rows, :], inside[0:rows, :]
    a[...] = jnp.where(odd, from_inside, from_across)
    b[...] = jnp.where(odd, from_across, from_inside)


def first_kernel(
    table_in, e_in, h_in, j_in, v_in, w_in, near_in, ports_in, profile_in, *rest
):
    table, e, h, j, v, w, near, source, hot, across, inside = rest[:11]
    fe, fh, x, ports, profile, sems = rest[11:]
    copies = []

    def fetch(origin, target):
        copies.append(pltpu.make_async_copy(origin, target, sems.at[len(copies)]))
        copies[-1].start()
        return copies[-1]

    early = [fetch(near_in, near), fetch(ports_in, ports), fetch(profile_in, profile)]
    fields = []
    for origin, target in ((e_in, e), (h_in, h), (j_in, j), (w_in, w), (v_in, v)):
        for i in range(2):
            fields.append(fetch(origin.at[:, pl.ds(i * LAYER, LAYER)], target.at[i]))
    last = fetch(table_in, table)

    for copy in early:
        copy.wait()
    rows = layer_rows()
    index = local_index(near[...])
    for i in range(2):
        for face in range(6):
            hot[6 * i + face] = one_hot(rows, index[face : face + 1, i * LAYER : (i + 1) * LAYER])
    count = 2 * LAYER
    place = jnp.bitwise_and(ports[...], count - 1)
    targets = lax.broadcasted_iota(jnp.int32, (count, place.shape[1]), 0)
    spread_hot = one_hot(targets, place)
    high, low = halves(profile[...])
    spread = dot_t(high, spread_hot) + dot_t(low, spread_hot)
    for i in range(2):
        source[i] = spread[:, i * LAYER : (i + 1) * LAYER]
    for copy in fields:
        copy.wait()
    drive = []
    for i in range(2):
        fe[L0 + i] = e[i]
        fh[L0 + i] = h[i]
        drive.append(KEEP * j[i] + TIME_STEP * thrice(w[i]) * e[i] + source[i])
    last.wait()
    up, down = lonely(table, x, lambda l, f: hot[hot_at(l, f)], fe, fh, drive, v)
    send(across, inside, 0, up, down)
    send(across, inside, V_NEAR, v[1], v[0])
    blank = jnp.zeros((2, LAYER), F32)
    index = index.astype(F32)
    send(
        across,
        inside,
        N_NEAR,
        jnp.concatenate([index[:, LAYER : 2 * LAYER], blank], axis=0),
        jnp.concatenate([index[:, 0:LAYER], blank], axis=0),
    )


def middle_kernel(table, e, h, j, v, w, source, hot, across_in, inside_in, *rest):
    out_e, out_h, out_j, mid_e, mid_j, v_near, hot_near, across, inside = rest[:9]
    fe, fh, x, sent_a, sent_b = rest[9:]
    sides(across_in, inside_in, sent_a, sent_b, FIRST)
    v_near[0] = sent_a[V_NEAR : V_NEAR + NODES, :]
    v_near[1] = sent_b[V_NEAR : V_NEAR + NODES, :]
    rows = layer_rows()
    for layer, sent in ((A1, sent_a), (B1, sent_b)):
        index = sent[N_NEAR : N_NEAR + 8, :].astype(jnp.int32)
        for face in range(6):
            if (layer, face) not in ((A1, 0), (B1, 1)):
                hot_near[hot_at(layer, face) - 12] = one_hot(rows, index[face : face + 1, :])

    def hots(layer, face):
        at = hot_at(layer, face)
        return hot[at] if at < 12 else hot_near[at - 12]

    first_e, first_j, second_e, second_j, magnetic = two_steps(
        table, x, hots, fe, fh, e, h, j, source, v, w, v_near, sent_a, sent_b
    )
    drive = []
    for i in range(2):
        mid_e[i] = first_e[i]
        mid_j[i] = first_j[i]
        out_e[i] = second_e[i]
        out_j[i] = second_j[i]
        out_h[i] = magnetic[i]
        drive.append(
            KEEP * second_j[i] + TIME_STEP * thrice(w[i]) * second_e[i] + source[i]
        )
    up, down = lonely(table, x, hots, fe, fh, drive, v)
    send(across, inside, 0, up, down)


def early_kernel(mid_e, mid_j, end_e, end_j, levels, out):
    for i in range(2):
        columns = slice(i * LAYER, (i + 1) * LAYER)
        start, middle, end = (levels[k, :, columns].astype(F32) for k in range(3))
        out[0:NODES, columns] = folded(
            mid_e[i] * (middle - start) + end_e[i] * (end - middle)
        )
        out[NODES : 2 * NODES, columns] = folded(mid_j[i] * start + end_j[i] * middle)


def split(total, keep, give, bit):
    half = total.shape[0] // 2
    side = lax.rem(lax.axis_index("exc") // bit, 2)
    keep[...] = total[pl.ds(pl.multiple_of(side * half, half), half), :]
    give[...] = total[pl.ds(pl.multiple_of((1 - side) * half, half), half), :]


def last_kernel(
    bit, table, e, h, j, v, w, source, hot, v_near, hot_near, across_in, inside_in, *rest
):
    levels, early, design, out_e, out_h, keep, give = rest[:7]
    fe, fh, x, sent_a, sent_b, sums = rest[7:]
    sides(across_in, inside_in, sent_a, sent_b, SECOND)

    def hots(layer, face):
        at = hot_at(layer, face)
        return hot[at] if at < 12 else hot_near[at - 12]

    first_e, first_j, second_e, second_j, magnetic = two_steps(
        table, x, hots, fe, fh, e, h, j, source, v, w, v_near, sent_a, sent_b
    )
    parts = []
    for i in range(2):
        out_e[i] = second_e[i]
        out_h[i] = magnetic[i]
        columns = slice(i * LAYER, (i + 1) * LAYER)
        start, middle, end = (levels[k, :, columns].astype(F32) for k in range(2, 5))
        eps = folded(first_e[i] * (middle - start) + second_e[i] * (end - middle))
        drude = folded(first_j[i] * start + second_j[i] * middle)
        parts.append(jnp.concatenate([eps, drude], axis=0) + early[:, columns])
    both = jnp.concatenate(parts, axis=1)
    pixel = jnp.bitwise_and(design[...], PIX_DEV - 1)
    pixels = one_hot(lax.broadcasted_iota(jnp.int32, (PIX_DEV, both.shape[1]), 0), pixel)
    high, low = halves(both)
    sums[...] = dot_t(pixels, high) + dot_t(pixels, low)
    split(sums, keep, give, bit)


def write_kernel(e, h, out_e, out_h):
    for i in range(2):
        columns = slice(i * LAYER, (i + 1) * LAYER)
        out_e[:, columns] = e[i]
        out_h[:, columns] = h[i]


def halve_kernel(bit, kept, came, keep, give, sums):
    sums[...] = kept[...] + came[...]
    split(sums, keep, give, bit)


def total_kernel(owners, kept, came, eps, drude):
    total = (kept[...] + came[...]) * (1.0 / owners)
    eps[...] = total[:, 0:NODES]
    drude[...] = total[:, NODES : 2 * NODES]


def call(kernel, outs, args, scratch=(), flops=0, space=pltpu.VMEM):
    moved = sum(4 * int(np.prod(o.shape)) for o in outs) + sum(
        a.dtype.itemsize * int(np.prod(a.shape)) for a in args
    )
    return pl.pallas_call(
        kernel,
        out_shape=outs,
        in_specs=[pl.BlockSpec(memory_space=space)] * len(args),
        out_specs=[pl.BlockSpec(memory_space=pltpu.VMEM)] * len(outs),
        scratch_shapes=list(scratch),
        compiler_params=pltpu.CompilerParams(vmem_limit_bytes=24 * 1024 * 1024),
        cost_estimate=pl.CostEstimate(flops=flops, bytes_accessed=moved, transcendentals=0),
    )(*args)


def f32(*shape):
    return jax.ShapeDtypeStruct(shape, F32)


def bf16(*shape):
    return jax.ShapeDtypeStruct(shape, BF16)


def exchange(across, inside):
    size = lax.axis_size("space")

    def pairs(start):
        found = [(i, i + 1) for i in range(start, size - 1, 2)]
        return found + [(j, i) for i, j in found]

    return lax.ppermute(across, "space", pairs(1)), lax.ppermute(inside, "space", pairs(0))


def local(
    adj_e,
    adj_h,
    adj_j,
    fwd_e,
    inv_eps,
    drude_weight,
    neighbor,
    design_map,
    port_elems,
    port_profile,
):
    count = adj_e.shape[2]
    owners = lax.axis_size("exc")
    table = jnp.asarray(step_table())
    levels = fwd_e[0]
    field, nodal = f32(2, ROWS, LAYER), f32(2, NODES, LAYER)
    work = [
        pltpu.VMEM((4, ROWS, LAYER), F32),
        pltpu.VMEM((4, ROWS, LAYER), F32),
        pltpu.VMEM((5 * ROWS, 4 * LAYER), BF16),
    ]
    once = 2 * ROWS * 5 * ROWS * LAYER

    table, e, h, j, v, w, _, source, hot, across, inside = call(
        first_kernel,
        [bf16(*table.shape), field, field, field, nodal, nodal]
        + [jax.ShapeDtypeStruct(neighbor.shape, jnp.int32), field, bf16(12, LAYER, LAYER)]
        + [f32(FIRST, LAYER)] * 2,
        [table, adj_e[0], adj_h[0], adj_j[0], inv_eps, drude_weight]
        + [neighbor, port_elems, port_profile[0]],
        work
        + [
            pltpu.VMEM(port_elems.shape, jnp.int32),
            pltpu.VMEM(port_profile.shape[1:], F32),
            pltpu.SemaphoreType.DMA((14,)),
        ],
        6 * once,
        pltpu.HBM,
    )
    across, inside = exchange(across, inside)
    e2, h2, j2, e1, j1, v_near, hot_near, across, inside = call(
        middle_kernel,
        [field] * 5 + [nodal, bf16(10, LAYER, LAYER)] + [f32(SECOND, LAYER)] * 2,
        [table, e, h, j, v, w, source, hot, across, inside],
        work + [pltpu.VMEM((FIRST, LAYER), F32)] * 2,
        18 * once,
    )
    across, inside = exchange(across, inside)
    (early,) = call(early_kernel, [f32(2 * NODES, count)], [e1, j1, e2, j2, levels])
    bit = owners // 2
    size = PIX_DEV // 2
    e4, h4, keep, give = call(
        functools.partial(last_kernel, bit),
        [field, field] + [f32(size, 2 * NODES)] * 2,
        [table, e2, h2, j2, v, w, source, hot, v_near, hot_near, across, inside]
        + [levels, early, design_map.reshape(1, count)],
        work
        + [pltpu.VMEM((SECOND, LAYER), F32)] * 2
        + [pltpu.VMEM((PIX_DEV, 2 * NODES), F32)],
        12 * once,
    )

    def swap(give, bit):
        return lax.ppermute(give, "exc", [(i, i ^ bit) for i in range(owners)])

    came = swap(give, bit)
    out_e, out_h = call(write_kernel, [f32(ROWS, count)] * 2, [e4, h4])
    while bit > 1:
        bit, size = bit // 2, size // 2
        keep, give = call(
            functools.partial(halve_kernel, bit),
            [f32(size, 2 * NODES)] * 2,
            [keep, came],
            [pltpu.VMEM((2 * size, 2 * NODES), F32)],
        )
        came = swap(give, bit)
    eps, drude = call(
        functools.partial(total_kernel, owners),
        [f32(size, NODES)] * 2,
        [keep, came],
    )
    return out_e[None], out_h[None], eps.T, drude.T


def solution(mesh):
    return jax.shard_map(
        local,
        mesh=mesh,
        in_specs=(
            P("exc", None, "space"),
            P("exc", None, "space"),
            P("exc", None, "space"),
            P("exc", None, None, "space"),
            P(None, "space"),
            P(None, "space"),
            P(None, "space"),
            P("space"),
            P("exc", "space"),
            P("exc", None, "space"),
        ),
        out_specs=(
            P("exc", None, "space"),
            P("exc", None, "space"),
            P(None, ("space", "exc")),
            P(None, ("space", "exc")),
        ),
        check_vma=False,
    )
```

```python
import functools

import jax
import jax.numpy as jnp
import ml_dtypes
import numpy as np
from jax import lax
from jax.experimental import pallas as pl
from jax.experimental.pallas import tpu as pltpu
from jax.sharding import PartitionSpec as P

NODES = 64
ROWS = 3 * NODES
LAYER = 128
PIX_DEV = 128

TIME_STEP = 0.025
DAMPING = 0.5
KEEP = 1.0 - TIME_STEP * DAMPING

TANGENT = 32
E_START = 0
H_FIRST = 32
E_FIRST = 64
H_SECOND = 96
SECOND = 128
V_NEAR = 128
N_NEAR = V_NEAR + NODES
FIRST = N_NEAR + 8

A1, L0, L1, B1 = range(4)

BF16 = jnp.bfloat16
F32 = jnp.float32


def tangential(face):
    return [c for c in range(3) if c != face // 2]


def node_tables():
    points = np.array([-1.0, -1.0 / np.sqrt(5.0), 1.0 / np.sqrt(5.0), 1.0])
    barycentric = np.array(
        [1.0 / np.prod([points[j] - points[k] for k in range(4) if k != j]) for j in range(4)]
    )
    deriv = np.zeros((4, 4))
    for row in range(4):
        for column in range(4):
            if row != column:
                deriv[row, column] = (
                    barycentric[column] / barycentric[row] / (points[row] - points[column])
                )
        deriv[row, row] = -np.sum(deriv[row])
    identity = np.eye(4)
    along_x = 2.0 * np.kron(np.kron(deriv, identity), identity)
    along_y = 2.0 * np.kron(np.kron(identity, deriv), identity)
    along_z = 2.0 * np.kron(np.kron(identity, identity), deriv)
    curl = np.zeros((192, 192))
    curl[0:64, 64:128] = -along_z
    curl[0:64, 128:192] = along_y
    curl[64:128, 0:64] = along_z
    curl[64:128, 128:192] = -along_x
    curl[128:192, 0:64] = -along_y
    curl[128:192, 64:128] = along_x
    numbers = np.arange(64).reshape(4, 4, 4)
    faces = np.stack(
        [
            numbers[0].ravel(),
            numbers[3].ravel(),
            numbers[:, 0].ravel(),
            numbers[:, 3].ravel(),
            numbers[:, :, 0].ravel(),
            numbers[:, :, 3].ravel(),
        ]
    )
    inner = np.zeros((192, 192))
    outer = np.zeros((192, 192))
    for face in range(6):
        direction = face // 2
        sign = 1.0 if face % 2 else -1.0
        for component in range(3):
            for place, other in enumerate(tangential(face)):
                parity = (component - direction) * (direction - other) * (other - component) / 2.0
                if parity != 0:
                    for node in range(16):
                        value = 6.0 * sign * parity
                        row = component * 64 + faces[face, node]
                        outer[row, face * 32 + place * 16 + node] += value
                        inner[row, other * 64 + faces[face, node]] += value
    return inner - curl, outer


def step_table():
    own, outer = node_tables()
    high = own.astype(ml_dtypes.bfloat16)
    low = (own - high.astype(np.float64)).astype(ml_dtypes.bfloat16)
    lift = (-outer).astype(ml_dtypes.bfloat16)
    return np.concatenate([high, high, low, lift, lift], axis=1)


def halves(x):
    high = x.astype(BF16)
    return high, (x - high.astype(F32)).astype(BF16)


def dot(a, b):
    return jnp.dot(a, b, preferred_element_type=F32)


def dot_t(a, b):
    return lax.dot_general(a, b, (((1,), (1,)), ((), ())), preferred_element_type=F32)


def thrice(x):
    return jnp.concatenate([x, x, x], axis=0)


def folded(x):
    return x[0:NODES] + x[NODES : 2 * NODES] + x[2 * NODES : ROWS]


def local_index(neighbor):
    return jnp.where(neighbor < 0, -1, jnp.bitwise_and(neighbor, LAYER - 1))


def hot_at(layer, face):
    if layer in (L0, L1):
        return 6 * (layer - L0) + face
    return 12 + (face - 1 if layer == A1 else 5 + (face - 1 if face else 0))


def one_hot(rows, targets):
    return (rows == targets).astype(F32).astype(BF16)


def layer_rows():
    return lax.broadcasted_iota(jnp.int32, (LAYER, LAYER), 0)


def face_rows(field, layer, face):
    offset = face % 2
    pieces = []
    for c in tangential(face):
        base = c * NODES
        if face < 2:
            pieces.append(field[layer, base + 48 * offset : base + 48 * offset + 16, :])
        elif face < 4:
            for i in range(4):
                at = base + 16 * i + 12 * offset
                pieces.append(field[layer, at : at + 4, :])
        else:
            pieces.append(field[layer, pl.ds(base + 3 * offset, 16, stride=4), :])
    return jnp.concatenate(pieces, axis=0)


def gathered(traces, hot):
    high, low = halves(traces)
    return dot(jnp.concatenate([high, low], axis=0), hot)


def rate(table, x, hots, field, layers, outer):
    first, last = layers[0], layers[-1]
    for layer in layers:
        here = slice(layer * LAYER, (layer + 1) * LAYER)
        high, low = halves(field[layer])
        x[0:ROWS, here] = high
        x[ROWS : 2 * ROWS, here] = low
        x[2 * ROWS : 3 * ROWS, here] = high
        for face in range(6):
            at = 3 * ROWS + TANGENT * face
            traces = outer(layer, face)
            if traces is None:
                nothing = jnp.zeros((TANGENT, LAYER), BF16)
                x[at : at + TANGENT, here] = nothing
                x[at + ROWS : at + ROWS + TANGENT, here] = nothing
            else:
                got = gathered(traces, hots(layer, face)).astype(BF16)
                x[at : at + TANGENT, here] = got[0:TANGENT]
                x[at + ROWS : at + ROWS + TANGENT, here] = got[TANGENT : 2 * TANGENT]
    found = dot(table[...], x[:, first * LAYER : (last + 1) * LAYER])
    return [found[:, i * LAYER : (i + 1) * LAYER] for i in range(len(layers))]


def neighbour(layer, face):
    return layer + (-1, 1, 0, 0, 0, 0)[face]


def lonely(table, x, hots, fe, fh, drive, v):
    own = (L0, L1)

    def outer_of(field):
        def outer(layer, face):
            there = neighbour(layer, face)
            return face_rows(field, there, face ^ 1) if there in own else None

        return outer

    def ends(field):
        return face_rows(field, L1, 1), face_rows(field, L0, 0)

    found = [ends(fe)]
    for i, change in enumerate(rate(table, x, hots, fe, own, outer_of(fe))):
        fh[L0 + i] += TIME_STEP * change
    found.append(ends(fh))
    for i, change in enumerate(rate(table, x, hots, fh, own, outer_of(fh))):
        fe[L0 + i] -= TIME_STEP * thrice(v[i]) * (change + drive[i])
    found.append(ends(fe))
    for i, change in enumerate(rate(table, x, hots, fe, own, outer_of(fe))):
        fh[L0 + i] += TIME_STEP * change
    found.append(ends(fh))
    return [jnp.concatenate(traces, axis=0) for traces in zip(*found)]


def response(traces, hot, face):
    parts = gathered(traces, hot)
    both = (6.0 * TIME_STEP) * (parts[0:TANGENT] + parts[TANGENT : 2 * TANGENT])
    sign = 1.0 if face else -1.0
    return sign * both[16:32], -sign * both[0:16]


def two_steps(
    table, x, hots, fe, fh, e, h, j, source, v, w, v_near, sent_a, sent_b, when_h=lambda: None
):
    own, wide = (L0, L1), (A1, L0, L1, B1)
    for i in range(2):
        fe[L0 + i] = e[i]
        fh[L0 + i] = h[i]
    blank = jnp.zeros((ROWS, LAYER), F32)
    fh[A1] = blank
    fh[B1] = blank

    def outer_of(field, start, answered=True):
        def outer(layer, face):
            if (layer, face) in ((A1, 0), (B1, 1)):
                return None
            there = neighbour(layer, face)
            if layer in own and there not in own:
                sent = sent_a if there == A1 else sent_b
                traces = sent[start : start + TANGENT, :]
                return traces + face_rows(field, there, face ^ 1) if answered else traces
            return face_rows(field, there, face ^ 1)

        return outer

    weight = [TIME_STEP * thrice(w[i]) for i in range(2)]
    changes = rate(table, x, hots, fe, own, outer_of(fe, E_START, False))
    for i in range(2):
        fh[L0 + i] += TIME_STEP * changes[i]
    at_y, at_z = response(face_rows(fe, L0, 0), hots(A1, 1), 1)
    fh[A1, 112:128, :] = at_y
    fh[A1, 176:192, :] = at_z
    at_y, at_z = response(face_rows(fe, L1, 1), hots(B1, 0), 0)
    fh[B1, 64:80, :] = at_y
    fh[B1, 128:144, :] = at_z

    first_j = [KEEP * j[i] + weight[i] * e[i] for i in range(2)]
    changes = rate(table, x, hots, fh, wide, outer_of(fh, H_FIRST))
    for i in range(2):
        fe[L0 + i] -= TIME_STEP * thrice(v[i]) * (changes[1 + i] + first_j[i] + source[i])
    fe[A1] = -TIME_STEP * thrice(v_near[0]) * changes[0]
    fe[B1] = -TIME_STEP * thrice(v_near[1]) * changes[3]
    first_e = [fe[L0], fe[L1]]

    for layer, change in zip(wide, rate(table, x, hots, fe, wide, outer_of(fe, E_FIRST))):
        fh[layer] += TIME_STEP * change
    when_h()
    second_j = [KEEP * first_j[i] + weight[i] * first_e[i] for i in range(2)]
    changes = rate(table, x, hots, fh, own, outer_of(fh, H_SECOND))
    for i in range(2):
        fe[L0 + i] -= TIME_STEP * thrice(v[i]) * (changes[i] + second_j[i] + source[i])
    return first_e, first_j, [fe[L0], fe[L1]], second_j, [fh[L0], fh[L1]]


def odd_rank():
    return lax.rem(lax.axis_index("space"), 2) == 1


def send(across, inside, at, up, down):
    odd = odd_rank()
    rows = slice(at, at + up.shape[0])
    across[rows, :] = jnp.where(odd, up, down)
    inside[rows, :] = jnp.where(odd, down, up)


def sides(across, inside, a, b, rows):
    odd = odd_rank()
    from_across, from_inside = across[0:rows, :], inside[0:rows, :]
    a[...] = jnp.where(odd, from_inside, from_across)
    b[...] = jnp.where(odd, from_across, from_inside)


def first_kernel(
    table_in, e_in, h_in, j_in, v_in, w_in, near_in, ports_in, profile_in, *rest
):
    table, e, h, j, v, w, near, source, hot, across, inside = rest[:11]
    fe, fh, x, ports, profile, sems = rest[11:]
    copies = []

    def fetch(origin, target):
        copies.append(pltpu.make_async_copy(origin, target, sems.at[len(copies)]))
        copies[-1].start()
        return copies[-1]

    early = [fetch(near_in, near), fetch(ports_in, ports), fetch(profile_in, profile)]
    fields = []
    for origin, target in ((e_in, e), (h_in, h), (j_in, j), (w_in, w), (v_in, v)):
        for i in range(2):
            fields.append(fetch(origin.at[:, pl.ds(i * LAYER, LAYER)], target.at[i]))
    last = fetch(table_in, table)

    for copy in early:
        copy.wait()
    rows = layer_rows()
    index = local_index(near[...])
    for i in range(2):
        for face in range(6):
            hot[6 * i + face] = one_hot(rows, index[face : face + 1, i * LAYER : (i + 1) * LAYER])
    count = 2 * LAYER
    place = jnp.bitwise_and(ports[...], count - 1)
    targets = lax.broadcasted_iota(jnp.int32, (count, place.shape[1]), 0)
    spread_hot = one_hot(targets, place)
    high, low = halves(profile[...])
    spread = dot_t(high, spread_hot) + dot_t(low, spread_hot)
    for i in range(2):
        source[i] = spread[:, i * LAYER : (i + 1) * LAYER]
    for copy in fields:
        copy.wait()
    drive = []
    for i in range(2):
        fe[L0 + i] = e[i]
        fh[L0 + i] = h[i]
        drive.append(KEEP * j[i] + TIME_STEP * thrice(w[i]) * e[i] + source[i])
    last.wait()
    up, down = lonely(table, x, lambda l, f: hot[hot_at(l, f)], fe, fh, drive, v)
    send(across, inside, 0, up, down)
    send(across, inside, V_NEAR, v[1], v[0])
    blank = jnp.zeros((2, LAYER), F32)
    index = index.astype(F32)
    send(
        across,
        inside,
        N_NEAR,
        jnp.concatenate([index[:, LAYER : 2 * LAYER], blank], axis=0),
        jnp.concatenate([index[:, 0:LAYER], blank], axis=0),
    )


def middle_kernel(table, e, h, j, v, w, source, hot, across_in, inside_in, *rest):
    out_e, out_h, out_j, mid_e, mid_j, v_near, hot_near, across, inside = rest[:9]
    fe, fh, x, sent_a, sent_b = rest[9:]
    sides(across_in, inside_in, sent_a, sent_b, FIRST)
    v_near[0] = sent_a[V_NEAR : V_NEAR + NODES, :]
    v_near[1] = sent_b[V_NEAR : V_NEAR + NODES, :]
    rows = layer_rows()
    for layer, sent in ((A1, sent_a), (B1, sent_b)):
        index = sent[N_NEAR : N_NEAR + 8, :].astype(jnp.int32)
        for face in range(6):
            if (layer, face) not in ((A1, 0), (B1, 1)):
                hot_near[hot_at(layer, face) - 12] = one_hot(rows, index[face : face + 1, :])

    def hots(layer, face):
        at = hot_at(layer, face)
        return hot[at] if at < 12 else hot_near[at - 12]

    first_e, first_j, second_e, second_j, magnetic = two_steps(
        table, x, hots, fe, fh, e, h, j, source, v, w, v_near, sent_a, sent_b
    )
    drive = []
    for i in range(2):
        mid_e[i] = first_e[i]
        mid_j[i] = first_j[i]
        out_e[i] = second_e[i]
        out_j[i] = second_j[i]
        out_h[i] = magnetic[i]
        drive.append(
            KEEP * second_j[i] + TIME_STEP * thrice(w[i]) * second_e[i] + source[i]
        )
    up, down = lonely(table, x, hots, fe, fh, drive, v)
    send(across, inside, 0, up, down)


def early_kernel(mid_e, mid_j, end_e, end_j, levels, design, out, pixels):
    pixel = jnp.bitwise_and(design[...], PIX_DEV - 1)
    pixels[...] = one_hot(lax.broadcasted_iota(jnp.int32, pixels.shape, 0), pixel)
    for i in range(2):
        columns = slice(i * LAYER, (i + 1) * LAYER)
        start, middle, end = (levels[k, :, columns].astype(F32) for k in range(3))
        out[0:NODES, columns] = folded(
            mid_e[i] * (middle - start) + end_e[i] * (end - middle)
        )
        out[NODES : 2 * NODES, columns] = folded(mid_j[i] * start + end_j[i] * middle)


def last_kernel(
    table, e, h, j, v, w, source, hot, v_near, hot_near, across_in, inside_in, *rest
):
    levels, early, pixels, out_e, out_h, sums = rest[:6]
    fe, fh, x, sent_a, sent_b, sems = rest[6:]
    sides(across_in, inside_in, sent_a, sent_b, SECOND)

    def hots(layer, face):
        at = hot_at(layer, face)
        return hot[at] if at < 12 else hot_near[at - 12]

    copies = []

    def write(field, target):
        for i in range(2):
            columns = pl.ds(i * LAYER, LAYER)
            sem = sems.at[len(copies)]
            copies.append(pltpu.make_async_copy(field.at[L0 + i], target.at[:, columns], sem))
            copies[-1].start()

    first_e, first_j, second_e, second_j, _ = two_steps(
        table, x, hots, fe, fh, e, h, j, source, v, w, v_near, sent_a, sent_b,
        lambda: write(fh, out_h),
    )
    write(fe, out_e)
    parts = []
    for i in range(2):
        columns = slice(i * LAYER, (i + 1) * LAYER)
        start, middle, end = (levels[k, :, columns].astype(F32) for k in range(2, 5))
        eps = folded(first_e[i] * (middle - start) + second_e[i] * (end - middle))
        drude = folded(first_j[i] * start + second_j[i] * middle)
        parts.append(jnp.concatenate([eps, drude], axis=0) + early[:, columns])
    both = jnp.concatenate(parts, axis=1)
    high, low = halves(both)
    sums[...] = dot_t(pixels[...], high) + dot_t(pixels[...], low)
    for copy in copies:
        copy.wait()


def total_kernel(owners, parts, eps, drude):
    share = parts.shape[0] // owners
    total = parts[0:share]
    for owner in range(1, owners):
        total = total + parts[owner * share : (owner + 1) * share]
    total = total * (1.0 / owners)
    eps[...] = total[:, 0:NODES]
    drude[...] = total[:, NODES : 2 * NODES]


def call(kernel, outs, args, scratch=(), flops=0, spaces=None, out_spaces=None):
    moved = sum(4 * int(np.prod(o.shape)) for o in outs) + sum(
        a.dtype.itemsize * int(np.prod(a.shape)) for a in args
    )
    return pl.pallas_call(
        kernel,
        out_shape=outs,
        in_specs=[pl.BlockSpec(memory_space=s) for s in spaces or [pltpu.VMEM] * len(args)],
        out_specs=[pl.BlockSpec(memory_space=s) for s in out_spaces or [pltpu.VMEM] * len(outs)],
        scratch_shapes=list(scratch),
        compiler_params=pltpu.CompilerParams(vmem_limit_bytes=24 * 1024 * 1024),
        cost_estimate=pl.CostEstimate(flops=flops, bytes_accessed=moved, transcendentals=0),
    )(*args)


def f32(*shape):
    return jax.ShapeDtypeStruct(shape, F32)


def bf16(*shape):
    return jax.ShapeDtypeStruct(shape, BF16)


def exchange(across, inside):
    size = lax.axis_size("space")

    def pairs(start):
        found = [(i, i + 1) for i in range(start, size - 1, 2)]
        return found + [(j, i) for i, j in found]

    return lax.ppermute(across, "space", pairs(1)), lax.ppermute(inside, "space", pairs(0))


def local(
    adj_e,
    adj_h,
    adj_j,
    fwd_e,
    inv_eps,
    drude_weight,
    neighbor,
    design_map,
    port_elems,
    port_profile,
):
    count = adj_e.shape[2]
    owners = lax.axis_size("exc")
    table = jnp.asarray(step_table())
    levels = fwd_e[0]
    field, nodal = f32(2, ROWS, LAYER), f32(2, NODES, LAYER)
    work = [
        pltpu.VMEM((4, ROWS, LAYER), F32),
        pltpu.VMEM((4, ROWS, LAYER), F32),
        pltpu.VMEM((5 * ROWS, 4 * LAYER), BF16),
    ]
    given = [table, adj_e[0], adj_h[0], adj_j[0], inv_eps, drude_weight]
    given += [neighbor, port_elems, port_profile[0]]
    once = 2 * ROWS * 5 * ROWS * LAYER

    table, e, h, j, v, w, _, source, hot, across, inside = call(
        first_kernel,
        [bf16(*table.shape), field, field, field, nodal, nodal]
        + [jax.ShapeDtypeStruct(neighbor.shape, jnp.int32), field, bf16(12, LAYER, LAYER)]
        + [f32(FIRST, LAYER)] * 2,
        [pltpu.with_memory_space_constraint(a, pltpu.HBM) for a in given],
        work
        + [
            pltpu.VMEM(port_elems.shape, jnp.int32),
            pltpu.VMEM(port_profile.shape[1:], F32),
            pltpu.SemaphoreType.DMA((14,)),
        ],
        6 * once,
        [pltpu.HBM] * len(given),
    )
    across, inside = exchange(across, inside)
    e2, h2, j2, e1, j1, v_near, hot_near, across, inside = call(
        middle_kernel,
        [field] * 5 + [nodal, bf16(10, LAYER, LAYER)] + [f32(SECOND, LAYER)] * 2,
        [table, e, h, j, v, w, source, hot, across, inside],
        work + [pltpu.VMEM((FIRST, LAYER), F32)] * 2,
        18 * once,
    )
    across, inside = exchange(across, inside)
    early, pixels = call(
        early_kernel,
        [f32(2 * NODES, count), bf16(PIX_DEV, count)],
        [e1, j1, e2, j2, levels, design_map.reshape(1, count)],
    )
    out_e, out_h, sums = call(
        last_kernel,
        [f32(ROWS, count)] * 2 + [f32(PIX_DEV, 2 * NODES)],
        [table, e2, h2, j2, v, w, source, hot, v_near, hot_near, across, inside]
        + [levels, early, pixels],
        work + [pltpu.VMEM((SECOND, LAYER), F32)] * 2 + [pltpu.SemaphoreType.DMA((4,))],
        12 * once,
        None,
        [pltpu.HBM, pltpu.HBM, pltpu.VMEM],
    )
    parts = lax.all_to_all(sums, "exc", split_axis=0, concat_axis=0, tiled=True)
    eps, drude = call(
        functools.partial(total_kernel, owners),
        [f32(PIX_DEV // owners, NODES)] * 2,
        [parts],
    )
    return out_e[None], out_h[None], eps.T, drude.T


def solution(mesh):
    return jax.shard_map(
        local,
        mesh=mesh,
        in_specs=(
            P("exc", None, "space"),
            P("exc", None, "space"),
            P("exc", None, "space"),
            P("exc", None, None, "space"),
            P(None, "space"),
            P(None, "space"),
            P(None, "space"),
            P("space"),
            P("exc", "space"),
            P("exc", None, "space"),
        ),
        out_specs=(
            P("exc", None, "space"),
            P("exc", None, "space"),
            P(None, ("space", "exc")),
            P(None, ("space", "exc")),
        ),
        check_vma=False,
    )
```

```python
import functools

import jax
import jax.numpy as jnp
import ml_dtypes
import numpy as np
from jax import lax
from jax.experimental import pallas as pl
from jax.experimental.pallas import tpu as pltpu
from jax.sharding import PartitionSpec as P

NODES = 64
ROWS = 3 * NODES
LAYER = 128
PIX_DEV = 128

TIME_STEP = 0.025
DAMPING = 0.5
KEEP = 1.0 - TIME_STEP * DAMPING

TANGENT = 32
E_START = 0
H_FIRST = 32
E_FIRST = 64
H_SECOND = 96
SECOND = 128
V_NEAR = 128
N_NEAR = V_NEAR + NODES
FIRST = N_NEAR + 8

A1, L0, L1, B1 = range(4)

BASE = (NODES, 0, 2 * NODES)

BF16 = jnp.bfloat16
F32 = jnp.float32


def parity(c, face, other):
    d = face // 2
    sign = 1.0 if face % 2 else -1.0
    return 6.0 * sign * (c - d) * (d - other) * (other - c) / 2.0


def own_rate():
    points = np.array([-1.0, -1.0 / np.sqrt(5.0), 1.0 / np.sqrt(5.0), 1.0])
    barycentric = np.array(
        [1.0 / np.prod([points[j] - points[k] for k in range(4) if k != j]) for j in range(4)]
    )
    deriv = np.zeros((4, 4))
    for row in range(4):
        for column in range(4):
            if row != column:
                deriv[row, column] = (
                    barycentric[column] / barycentric[row] / (points[row] - points[column])
                )
        deriv[row, row] = -np.sum(deriv[row])
    identity = np.eye(4)
    along_x = 2.0 * np.kron(np.kron(deriv, identity), identity)
    along_y = 2.0 * np.kron(np.kron(identity, deriv), identity)
    along_z = 2.0 * np.kron(np.kron(identity, identity), deriv)
    curl = np.zeros((192, 192))
    curl[0:64, 64:128] = -along_z
    curl[0:64, 128:192] = along_y
    curl[64:128, 0:64] = along_z
    curl[64:128, 128:192] = -along_x
    curl[128:192, 0:64] = -along_y
    curl[128:192, 64:128] = along_x
    numbers = np.arange(64).reshape(4, 4, 4)
    faces = np.stack(
        [
            numbers[0].ravel(),
            numbers[3].ravel(),
            numbers[:, 0].ravel(),
            numbers[:, 3].ravel(),
            numbers[:, :, 0].ravel(),
            numbers[:, :, 3].ravel(),
        ]
    )
    inner = np.zeros((192, 192))
    for face in range(6):
        for c in range(3):
            for other in range(3):
                value = parity(c, face, other)
                if value != 0:
                    for node in faces[face]:
                        inner[c * 64 + node, other * 64 + node] += value
    return inner - curl


def step_tables():
    order = np.concatenate([np.arange(64) + 64 * c for c in (1, 0, 2)])
    own = own_rate()[order][:, order]
    high = own.astype(ml_dtypes.bfloat16)
    low = (own - high.astype(np.float64)).astype(ml_dtypes.bfloat16)
    table = np.concatenate([high, high, low], axis=1)
    ends = [table[BASE[c] + 16 * i : BASE[c] + 16 * i + 16] for i in (0, 3) for c in (1, 2)]
    return table, np.concatenate(ends, axis=0)


def halves(x):
    high = x.astype(BF16)
    return high, (x - high.astype(F32)).astype(BF16)


def dot(a, b):
    return jnp.dot(a, b, preferred_element_type=F32)


def dot_t(a, b):
    return lax.dot_general(a, b, (((1,), (1,)), ((), ())), preferred_element_type=F32)


def thrice(x):
    return jnp.concatenate([x, x, x], axis=0)


def folded(x):
    return x[0:NODES] + x[NODES : 2 * NODES] + x[2 * NODES : ROWS]


def stored(x):
    return jnp.concatenate([x[NODES : 2 * NODES], x[0:NODES], x[2 * NODES : ROWS]], axis=0)


def one_hot(rows, targets):
    return (rows == targets).astype(F32).astype(BF16)


def picked(x, index):
    rows = x.shape[0]
    if rows < 8:
        index = index[0:rows]
    elif rows > 8:
        index = jnp.concatenate([index] * (rows // 8), axis=0)
    along = lax.GatherDimensionNumbers(
        offset_dims=(),
        collapsed_slice_dims=(1,),
        start_index_map=(1,),
        operand_batching_dims=(0,),
        start_indices_batching_dims=(0,),
    )
    mode = lax.GatherScatterMode.PROMISE_IN_BOUNDS
    return lax.gather(x, index[..., None], along, (1, 1), mode=mode)


def at_end(face):
    return 3 if face % 2 else 0


def x_traces(field, layer, face):
    at = 16 * at_end(face)
    return [field[layer, BASE[c] + at : BASE[c] + at + 16, :] for c in (1, 2)]


def lift_x(target, layer, face, scale, y, z):
    at = 16 * at_end(face)
    rows = slice(BASE[1] + at, BASE[1] + at + 16)
    target[layer, rows, :] += (-scale * parity(1, face, 2)) * z
    rows = slice(BASE[2] + at, BASE[2] + at + 16)
    target[layer, rows, :] += (-scale * parity(2, face, 1)) * y


def lift_inside(target, field, layer, index, scale):
    first = lax.broadcasted_iota(jnp.int32, (8, LAYER), 0) < 4
    for face in (2, 3):
        factor = jnp.where(first, -scale * parity(0, face, 2), -scale * parity(2, face, 0))
        for k in range(4):
            at = BASE[0] + 4 * at_end(face ^ 1) + k
            got = picked(field[layer, pl.ds(at, 8, stride=16), :], index(layer, face))
            at = BASE[0] + 4 * at_end(face) + k
            turned = pltpu.roll(got, 4, 0)
            target[layer, pl.ds(at, 8, stride=16), :] += factor * turned
    for face in (4, 5):
        here, there = at_end(face), at_end(face ^ 1)
        x, y = (
            picked(field[layer, pl.ds(BASE[c] + there, 16, stride=4), :], index(layer, face))
            for c in (0, 1)
        )
        target[layer, pl.ds(BASE[0] + here, 16, stride=4), :] += (-scale * parity(0, face, 1)) * y
        target[layer, pl.ds(BASE[1] + here, 16, stride=4), :] += (-scale * parity(1, face, 0)) * x


def lift_end(target, field, layer, i, index, scale, to_x):
    for face in (2, 3):
        source, sink = (2, 0) if to_x else (0, 2)
        at = BASE[source] + 16 * i + 4 * at_end(face ^ 1)
        got = picked(field[layer, at : at + 4, :], index(layer, face))
        at = BASE[sink] + 16 * i + 4 * at_end(face)
        target[layer, at : at + 4, :] += (-scale * parity(sink, face, source)) * got
    for face in (4, 5):
        source, sink = (1, 0) if to_x else (0, 1)
        at = BASE[source] + 16 * i + at_end(face ^ 1)
        got = picked(field[layer, pl.ds(at, 4, stride=4), :], index(layer, face))
        at = BASE[sink] + 16 * i + at_end(face)
        target[layer, pl.ds(at, 4, stride=4), :] += (-scale * parity(sink, face, source)) * got


def own_parts(table, x, values):
    for i, value in enumerate(values):
        here = slice(i * LAYER, (i + 1) * LAYER)
        high, low = halves(value)
        x[0:ROWS, here] = high
        x[ROWS : 2 * ROWS, here] = low
        x[2 * ROWS : 3 * ROWS, here] = high
    found = dot(table[...], x[...])
    return [found[:, i * LAYER : (i + 1) * LAYER] for i in range(2)]


def near_parts(table, a, b):
    both = jnp.concatenate([a.astype(BF16), b.astype(BF16)], axis=1)
    found = dot(table[:, 0:ROWS], both)
    return found[:, 0:LAYER], found[:, LAYER : 2 * LAYER]


def lonely(table, ends, x, index, fe, fh, acc, electric, drive, v):
    own = (L0, L1)

    def between(target, field, scale):
        for layer, face in ((L0, 1), (L1, 0)):
            y, z = x_traces(field, L0 + L1 - layer, face ^ 1)
            got = [picked(t, index(layer, face)) for t in (y, z)]
            lift_x(target, layer, face, scale, *got)

    def ends_of(field):
        return x_traces(field, L1, 1), x_traces(field, L0, 0)

    found = [ends_of(fe)]
    parts = own_parts(table, x, electric)
    between(fh, fe, TIME_STEP)
    magnetic = []
    for i, layer in enumerate(own):
        lift_inside(fh, fe, layer, index, TIME_STEP)
        magnetic.append(fh[layer] + TIME_STEP * parts[i])
        fh[layer] = magnetic[i]
    found.append(ends_of(fh))
    parts = own_parts(table, x, magnetic)
    for i, layer in enumerate(own):
        acc[layer] = drive[i]
    between(acc, fh, 1.0)
    for i, layer in enumerate(own):
        lift_inside(acc, fh, layer, index, 1.0)
        electric[i] = electric[i] - TIME_STEP * thrice(v[i]) * (parts[i] + acc[layer])
        fe[layer] = electric[i]
    found.append(ends_of(fe))
    parts = own_parts(ends, x, electric)
    for i, layer in enumerate(own):
        face = i
        lift_end(fh, fe, layer, at_end(face), index, TIME_STEP, False)
        for place, c in enumerate((1, 2)):
            at = BASE[c] + 16 * at_end(face)
            part = parts[i][32 * i + 16 * place : 32 * i + 16 * place + 16]
            fh[layer, at : at + 16, :] += TIME_STEP * part
    found.append(ends_of(fh))
    return [jnp.concatenate(sum(traces, []), axis=0) for traces in zip(*found)]


def two_steps(
    tables, x, index, valid, fe, fh, acc, e, h, j, source, v, w, v_near, sent_a, sent_b, when_h
):
    table, ends = tables
    own = (L0, L1)
    sides = ((A1, 1, L0, sent_a), (B1, 0, L1, sent_b))
    electric = [e[0], e[1]]
    magnetic = [h[0], h[1]]
    for i, layer in enumerate(own):
        fe[layer] = electric[i]
        fh[layer] = magnetic[i]

    def between(target, field, scale, start, answered=True):
        for layer, face in ((L0, 1), (L1, 0)):
            y, z = x_traces(field, L0 + L1 - layer, face ^ 1)
            got = [picked(t, index(layer, face)) for t in (y, z)]
            lift_x(target, layer, face, scale, *got)
        for side, (near, face, layer, sent) in enumerate(sides):
            traces = [sent[start + 16 * t : start + 16 * t + 16, :] for t in range(2)]
            if answered:
                traces = [a + b for a, b in zip(traces, x_traces(field, near, face))]
            mask = jnp.concatenate([valid[side]] * 2, axis=0)
            got = [picked(t, index(layer, face ^ 1)) * mask for t in traces]
            lift_x(target, layer, face ^ 1, scale, *got)

    def outward(target, field, scale):
        for near, face, layer, _ in sides:
            y, z = x_traces(field, layer, face ^ 1)
            got = [picked(t, index(near, face)) for t in (y, z)]
            lift_x(target, near, face, scale, *got)

    weight = [TIME_STEP * thrice(w[i]) for i in range(2)]
    blank = jnp.zeros((ROWS, LAYER), F32)

    parts = own_parts(table, x, electric)
    for near, _, _, _ in sides:
        fh[near] = blank
        acc[near] = blank
    outward(fh, fe, TIME_STEP)
    between(fh, fe, TIME_STEP, E_START, False)
    for i, layer in enumerate(own):
        lift_inside(fh, fe, layer, index, TIME_STEP)
        magnetic[i] = fh[layer] + TIME_STEP * parts[i]
        fh[layer] = magnetic[i]

    first_j = [KEEP * j[i] + weight[i] * electric[i] for i in range(2)]
    parts = own_parts(table, x, magnetic)
    near_found = near_parts(table, fh[A1], fh[B1])
    for i, layer in enumerate(own):
        acc[layer] = first_j[i] + source[i]
    between(acc, fh, 1.0, H_FIRST)
    outward(acc, fh, 1.0)
    for i, layer in enumerate(own):
        lift_inside(acc, fh, layer, index, 1.0)
        electric[i] = electric[i] - TIME_STEP * thrice(v[i]) * (parts[i] + acc[layer])
        fe[layer] = electric[i]
    first_e = list(electric)
    near_e = []
    for side, (near, face, _, _) in enumerate(sides):
        lift_end(acc, fh, near, at_end(face), index, 1.0, True)
        near_e.append(-TIME_STEP * thrice(v_near[side]) * (near_found[side] + acc[near]))
        fe[near] = near_e[side]

    parts = own_parts(table, x, electric)
    near_found = near_parts(ends, *near_e)
    between(fh, fe, TIME_STEP, E_FIRST)
    outward(fh, fe, TIME_STEP)
    for i, layer in enumerate(own):
        lift_inside(fh, fe, layer, index, TIME_STEP)
        magnetic[i] = fh[layer] + TIME_STEP * parts[i]
        fh[layer] = magnetic[i]
    when_h()
    for side, (near, face, _, _) in enumerate(sides):
        lift_end(fh, fe, near, at_end(face), index, TIME_STEP, False)
        for place, c in enumerate((1, 2)):
            at = BASE[c] + 16 * at_end(face)
            start = 32 * face + 16 * place
            fh[near, at : at + 16, :] += TIME_STEP * near_found[side][start : start + 16]

    second_j = [KEEP * first_j[i] + weight[i] * electric[i] for i in range(2)]
    parts = own_parts(table, x, magnetic)
    for i, layer in enumerate(own):
        acc[layer] = second_j[i] + source[i]
    between(acc, fh, 1.0, H_SECOND)
    for i, layer in enumerate(own):
        lift_inside(acc, fh, layer, index, 1.0)
        electric[i] = electric[i] - TIME_STEP * thrice(v[i]) * (parts[i] + acc[layer])
        fe[layer] = electric[i]
    return first_e, first_j, electric, second_j, magnetic


def odd_rank():
    return lax.rem(lax.axis_index("space"), 2) == 1


def send(across, inside, at, up, down):
    odd = odd_rank()
    rows = slice(at, at + up.shape[0])
    across[rows, :] = jnp.where(odd, up, down)
    inside[rows, :] = jnp.where(odd, down, up)


def sides_of(across, inside, a, b, rows):
    odd = odd_rank()
    from_across, from_inside = across[0:rows, :], inside[0:rows, :]
    a[...] = jnp.where(odd, from_inside, from_across)
    b[...] = jnp.where(odd, from_across, from_inside)


def first_kernel(
    table_in, ends_in, e_in, h_in, j_in, v_in, w_in, near_in, ports_in, profile_in, *rest
):
    table, ends, e, h, j, v, w, source, places, valid, across, inside = rest[:12]
    fe, fh, acc, x, neighbor, ports, profile, sems = rest[12:]
    copies = []

    def fetch(origin, target):
        copies.append(pltpu.make_async_copy(origin, target, sems.at[len(copies)]))
        copies[-1].start()
        return copies[-1]

    early = [fetch(near_in, neighbor), fetch(ports_in, ports), fetch(profile_in, profile)]
    fields = []
    for origin, target in ((e_in, e), (h_in, h), (j_in, j), (w_in, w), (v_in, v)):
        for i in range(2):
            fields.append(fetch(origin.at[:, pl.ds(i * LAYER, LAYER)], target.at[i]))
    last = [fetch(table_in, table), fetch(ends_in, ends)]

    for copy in early:
        copy.wait()
    found = neighbor[...]
    place = jnp.where(found < 0, 0, jnp.bitwise_and(found, LAYER - 1))
    for i in range(2):
        columns = slice(i * LAYER, (i + 1) * LAYER)
        for face in range(6):
            places[6 * i + face] = jnp.broadcast_to(place[face : face + 1, columns], (8, LAYER))
        there = (found[i : i + 1, columns] >= 0).astype(F32)
        valid[i] = jnp.broadcast_to(there, (8, LAYER))
    count = 2 * LAYER
    targets = lax.broadcasted_iota(jnp.int32, (count, ports.shape[1]), 0)
    spread_hot = one_hot(targets, jnp.bitwise_and(ports[...], count - 1))
    high, low = halves(profile[...])
    spread = dot_t(high, spread_hot) + dot_t(low, spread_hot)
    for i in range(2):
        source[i] = stored(spread[:, i * LAYER : (i + 1) * LAYER])
    for copy in fields:
        copy.wait()
    electric, drive = [], []
    for i in range(2):
        electric.append(stored(e[i]))
        fe[L0 + i] = electric[i]
        fh[L0 + i] = stored(h[i])
        weight = TIME_STEP * thrice(w[i])
        drive.append(KEEP * stored(j[i]) + weight * electric[i] + source[i])
    for copy in last:
        copy.wait()

    def index(layer, face):
        return places[6 * (layer - L0) + face]

    up, down = lonely(table, ends, x, index, fe, fh, acc, electric, drive, v)
    send(across, inside, 0, up, down)
    send(across, inside, V_NEAR, v[1], v[0])
    blank = jnp.zeros((2, LAYER), F32)
    place = place.astype(F32)
    send(
        across,
        inside,
        N_NEAR,
        jnp.concatenate([place[:, LAYER : 2 * LAYER], blank], axis=0),
        jnp.concatenate([place[:, 0:LAYER], blank], axis=0),
    )


def index_of(places, near_places):
    def index(layer, face):
        if layer in (L0, L1):
            return places[6 * (layer - L0) + face]
        return near_places[6 * (layer == B1) + face]

    return index


def middle_kernel(
    table, ends, e, h, j, v, w, source, places, valid, across_in, inside_in, *rest
):
    out_e, out_h, out_j, mid_e, mid_j, v_near, near_places, across, inside = rest[:9]
    fe, fh, acc, x, sent_a, sent_b = rest[9:]
    sides_of(across_in, inside_in, sent_a, sent_b, FIRST)
    for side, sent in enumerate((sent_a, sent_b)):
        v_near[side] = sent[V_NEAR : V_NEAR + NODES, :]
        place = sent[N_NEAR : N_NEAR + 8, :].astype(jnp.int32)
        for face in range(6):
            near_places[6 * side + face] = jnp.broadcast_to(place[face : face + 1], (8, LAYER))
    index = index_of(places, near_places)
    start = [[stored(field[i]) for i in range(2)] for field in (e, h, j)]
    first_e, first_j, second_e, second_j, magnetic = two_steps(
        (table, ends), x, index, valid, fe, fh, acc, *start, source, v, w, v_near,
        sent_a, sent_b, lambda: None,
    )
    drive = []
    for i in range(2):
        mid_e[i] = first_e[i]
        mid_j[i] = first_j[i]
        out_e[i] = second_e[i]
        out_j[i] = second_j[i]
        out_h[i] = magnetic[i]
        weight = TIME_STEP * thrice(w[i])
        drive.append(KEEP * second_j[i] + weight * second_e[i] + source[i])
    up, down = lonely(table, ends, x, index, fe, fh, acc, list(second_e), drive, v)
    send(across, inside, 0, up, down)


def early_kernel(mid_e, mid_j, end_e, end_j, levels, design, out, pixels):
    pixel = jnp.bitwise_and(design[...], PIX_DEV - 1)
    pixels[...] = one_hot(lax.broadcasted_iota(jnp.int32, pixels.shape, 0), pixel)
    for i in range(2):
        columns = slice(i * LAYER, (i + 1) * LAYER)
        start, middle, end = (stored(levels[k, :, columns].astype(F32)) for k in range(3))
        out[0:NODES, columns] = folded(
            mid_e[i] * (middle - start) + end_e[i] * (end - middle)
        )
        out[NODES : 2 * NODES, columns] = folded(mid_j[i] * start + end_j[i] * middle)


def last_kernel(
    table, ends, e, h, j, v, w, source, places, valid, v_near, near_places,
    across_in, inside_in, levels, early, pixels, *rest
):
    out_e, out_h, sums = rest[:3]
    fe, fh, acc, x, sent_a, sent_b, sems = rest[3:]
    sides_of(across_in, inside_in, sent_a, sent_b, SECOND)
    copies = []

    def write(field, target):
        for i in range(2):
            for c in range(3):
                origin = field.at[L0 + i, pl.ds(BASE[c], NODES), :]
                there = target.at[pl.ds(c * NODES, NODES), pl.ds(i * LAYER, LAYER)]
                copies.append(pltpu.make_async_copy(origin, there, sems.at[len(copies)]))
                copies[-1].start()

    first_e, first_j, second_e, second_j, _ = two_steps(
        (table, ends), x, index_of(places, near_places), valid, fe, fh, acc,
        e, h, j, source, v, w, v_near, sent_a, sent_b, lambda: write(fh, out_h),
    )
    write(fe, out_e)
    parts = []
    for i in range(2):
        columns = slice(i * LAYER, (i + 1) * LAYER)
        start, middle, end = (stored(levels[k, :, columns].astype(F32)) for k in range(2, 5))
        eps = folded(first_e[i] * (middle - start) + second_e[i] * (end - middle))
        drude = folded(first_j[i] * start + second_j[i] * middle)
        parts.append(jnp.concatenate([eps, drude], axis=0) + early[:, columns])
    both = jnp.concatenate(parts, axis=1)
    high, low = halves(both)
    sums[...] = dot_t(pixels[...], high) + dot_t(pixels[...], low)
    for copy in copies:
        copy.wait()


def total_kernel(owners, parts, eps, drude):
    share = parts.shape[0] // owners
    total = parts[0:share]
    for owner in range(1, owners):
        total = total + parts[owner * share : (owner + 1) * share]
    total = total * (1.0 / owners)
    eps[...] = total[:, 0:NODES]
    drude[...] = total[:, NODES : 2 * NODES]


def call(kernel, outs, args, scratch=(), flops=0, spaces=None, out_spaces=None):
    moved = sum(4 * int(np.prod(o.shape)) for o in outs) + sum(
        a.dtype.itemsize * int(np.prod(a.shape)) for a in args
    )
    return pl.pallas_call(
        kernel,
        out_shape=outs,
        in_specs=[pl.BlockSpec(memory_space=s) for s in spaces or [pltpu.VMEM] * len(args)],
        out_specs=[pl.BlockSpec(memory_space=s) for s in out_spaces or [pltpu.VMEM] * len(outs)],
        scratch_shapes=list(scratch),
        compiler_params=pltpu.CompilerParams(vmem_limit_bytes=24 * 1024 * 1024),
        cost_estimate=pl.CostEstimate(flops=flops, bytes_accessed=moved, transcendentals=0),
    )(*args)


def f32(*shape):
    return jax.ShapeDtypeStruct(shape, F32)


def bf16(*shape):
    return jax.ShapeDtypeStruct(shape, BF16)


def exchange(across, inside):
    size = lax.axis_size("space")

    def pairs(start):
        found = [(i, i + 1) for i in range(start, size - 1, 2)]
        return found + [(j, i) for i, j in found]

    return lax.ppermute(across, "space", pairs(1)), lax.ppermute(inside, "space", pairs(0))


def local(
    adj_e,
    adj_h,
    adj_j,
    fwd_e,
    inv_eps,
    drude_weight,
    neighbor,
    design_map,
    port_elems,
    port_profile,
):
    count = adj_e.shape[2]
    owners = lax.axis_size("exc")
    table, ends = (jnp.asarray(t) for t in step_tables())
    levels = fwd_e[0]
    field, nodal = f32(2, ROWS, LAYER), f32(2, NODES, LAYER)
    indices = jax.ShapeDtypeStruct((12, 8, LAYER), jnp.int32)
    work = [pltpu.VMEM((4, ROWS, LAYER), F32)] * 3
    work += [pltpu.VMEM((3 * ROWS, 2 * LAYER), BF16)]
    given = [table, ends, adj_e[0], adj_h[0], adj_j[0], inv_eps, drude_weight]
    given += [neighbor, port_elems, port_profile[0]]
    once = 2 * ROWS * 3 * ROWS * LAYER

    table, ends, e, h, j, v, w, source, places, valid, across, inside = call(
        first_kernel,
        [bf16(*table.shape), bf16(*ends.shape), field, field, field, nodal, nodal]
        + [field, indices, f32(2, 8, LAYER)]
        + [f32(FIRST, LAYER)] * 2,
        [pltpu.with_memory_space_constraint(a, pltpu.HBM) for a in given],
        work
        + [
            pltpu.VMEM(neighbor.shape, jnp.int32),
            pltpu.VMEM(port_elems.shape, jnp.int32),
            pltpu.VMEM(port_profile.shape[1:], F32),
            pltpu.SemaphoreType.DMA((15,)),
        ],
        6 * once,
        [pltpu.HBM] * len(given),
    )
    across, inside = exchange(across, inside)
    e2, h2, j2, e1, j1, v_near, near_places, across, inside = call(
        middle_kernel,
        [field] * 5 + [nodal, indices] + [f32(SECOND, LAYER)] * 2,
        [table, ends, e, h, j, v, w, source, places, valid, across, inside],
        work + [pltpu.VMEM((FIRST, LAYER), F32)] * 2,
        18 * once,
    )
    across, inside = exchange(across, inside)
    early, pixels = call(
        early_kernel,
        [f32(2 * NODES, count), bf16(PIX_DEV, count)],
        [e1, j1, e2, j2, levels, design_map.reshape(1, count)],
    )
    out_e, out_h, sums = call(
        last_kernel,
        [f32(ROWS, count)] * 2 + [f32(PIX_DEV, 2 * NODES)],
        [table, ends, e2, h2, j2, v, w, source, places, valid, v_near, near_places]
        + [across, inside, levels, early, pixels],
        work + [pltpu.VMEM((SECOND, LAYER), F32)] * 2 + [pltpu.SemaphoreType.DMA((12,))],
        12 * once,
        None,
        [pltpu.HBM, pltpu.HBM, pltpu.VMEM],
    )
    parts = lax.all_to_all(sums, "exc", split_axis=0, concat_axis=0, tiled=True)
    eps, drude = call(
        functools.partial(total_kernel, owners),
        [f32(PIX_DEV // owners, NODES)] * 2,
        [parts],
    )
    return out_e[None], out_h[None], eps.T, drude.T


def solution(mesh):
    return jax.shard_map(
        local,
        mesh=mesh,
        in_specs=(
            P("exc", None, "space"),
            P("exc", None, "space"),
            P("exc", None, "space"),
            P("exc", None, None, "space"),
            P(None, "space"),
            P(None, "space"),
            P(None, "space"),
            P("space"),
            P("exc", "space"),
            P("exc", None, "space"),
        ),
        out_specs=(
            P("exc", None, "space"),
            P("exc", None, "space"),
            P(None, ("space", "exc")),
            P(None, ("space", "exc")),
        ),
        check_vma=False,
    )
```

```python
import functools

import jax
import jax.numpy as jnp
import ml_dtypes
import numpy as np
from jax import lax
from jax.experimental import pallas as pl
from jax.experimental.pallas import tpu as pltpu
from jax.sharding import PartitionSpec as P

NODES = 64
ROWS = 3 * NODES
LAYER = 128
PIX_DEV = 128

TIME_STEP = 0.025
DAMPING = 0.5
KEEP = 1.0 - TIME_STEP * DAMPING

TANGENT = 32
E_START = 0
H_FIRST = 32
E_FIRST = 64
H_SECOND = 96
SECOND = 128
V_NEAR = 128
N_NEAR = V_NEAR + NODES
FIRST = N_NEAR + 8

A1, L0, L1, B1 = range(4)

BASE = (NODES, 0, 2 * NODES)

BF16 = jnp.bfloat16
F32 = jnp.float32


def parity(c, face, other):
    d = face // 2
    sign = 1.0 if face % 2 else -1.0
    return 6.0 * sign * (c - d) * (d - other) * (other - c) / 2.0


def own_rate():
    points = np.array([-1.0, -1.0 / np.sqrt(5.0), 1.0 / np.sqrt(5.0), 1.0])
    barycentric = np.array(
        [1.0 / np.prod([points[j] - points[k] for k in range(4) if k != j]) for j in range(4)]
    )
    deriv = np.zeros((4, 4))
    for row in range(4):
        for column in range(4):
            if row != column:
                deriv[row, column] = (
                    barycentric[column] / barycentric[row] / (points[row] - points[column])
                )
        deriv[row, row] = -np.sum(deriv[row])
    identity = np.eye(4)
    along_x = 2.0 * np.kron(np.kron(deriv, identity), identity)
    along_y = 2.0 * np.kron(np.kron(identity, deriv), identity)
    along_z = 2.0 * np.kron(np.kron(identity, identity), deriv)
    curl = np.zeros((192, 192))
    curl[0:64, 64:128] = -along_z
    curl[0:64, 128:192] = along_y
    curl[64:128, 0:64] = along_z
    curl[64:128, 128:192] = -along_x
    curl[128:192, 0:64] = -along_y
    curl[128:192, 64:128] = along_x
    numbers = np.arange(64).reshape(4, 4, 4)
    faces = np.stack(
        [
            numbers[0].ravel(),
            numbers[3].ravel(),
            numbers[:, 0].ravel(),
            numbers[:, 3].ravel(),
            numbers[:, :, 0].ravel(),
            numbers[:, :, 3].ravel(),
        ]
    )
    inner = np.zeros((192, 192))
    for face in range(6):
        for c in range(3):
            for other in range(3):
                value = parity(c, face, other)
                if value != 0:
                    for node in faces[face]:
                        inner[c * 64 + node, other * 64 + node] += value
    return inner - curl


def step_tables():
    order = np.concatenate([np.arange(64) + 64 * c for c in (1, 0, 2)])
    own = own_rate()[order][:, order]
    high = own.astype(ml_dtypes.bfloat16)
    low = (own - high.astype(np.float64)).astype(ml_dtypes.bfloat16)
    table = np.concatenate([high, high, low], axis=1)
    ends = [table[BASE[c] + 16 * i : BASE[c] + 16 * i + 16] for i in (0, 3) for c in (1, 2)]
    return table, np.concatenate(ends, axis=0)


def halves(x):
    high = x.astype(BF16)
    return high, (x - high.astype(F32)).astype(BF16)


def dot(a, b):
    return jnp.dot(a, b, preferred_element_type=F32)


def dot_t(a, b):
    return lax.dot_general(a, b, (((1,), (1,)), ((), ())), preferred_element_type=F32)


def thrice(x):
    return jnp.concatenate([x, x, x], axis=0)


def folded(x):
    return x[0:NODES] + x[NODES : 2 * NODES] + x[2 * NODES : ROWS]


def stored(x):
    return jnp.concatenate([x[NODES : 2 * NODES], x[0:NODES], x[2 * NODES : ROWS]], axis=0)


def one_hot(rows, targets):
    return (rows == targets).astype(F32).astype(BF16)


def picked(x, index):
    rows = x.shape[0]
    if rows < 8:
        index = index[0:rows]
    elif rows > 8:
        index = jnp.concatenate([index] * (rows // 8), axis=0)
    along = lax.GatherDimensionNumbers(
        offset_dims=(),
        collapsed_slice_dims=(1,),
        start_index_map=(1,),
        operand_batching_dims=(0,),
        start_indices_batching_dims=(0,),
    )
    mode = lax.GatherScatterMode.PROMISE_IN_BOUNDS
    return lax.gather(x, index[..., None], along, (1, 1), mode=mode)


def at_end(face):
    return 3 if face % 2 else 0


def x_traces(field, layer, face):
    at = 16 * at_end(face)
    return [field[layer, BASE[c] + at : BASE[c] + at + 16, :] for c in (1, 2)]


def lift_x(target, layer, face, scale, y, z):
    at = 16 * at_end(face)
    rows = slice(BASE[1] + at, BASE[1] + at + 16)
    target[layer, rows, :] += (-scale * parity(1, face, 2)) * z
    rows = slice(BASE[2] + at, BASE[2] + at + 16)
    target[layer, rows, :] += (-scale * parity(2, face, 1)) * y


def lift_inside(target, field, layer, index, scale):
    first = lax.broadcasted_iota(jnp.int32, (8, LAYER), 0) < 4
    for face in (2, 3):
        factor = jnp.where(first, -scale * parity(0, face, 2), -scale * parity(2, face, 0))
        for k in range(4):
            at = BASE[0] + 4 * at_end(face ^ 1) + k
            got = picked(field[layer, pl.ds(at, 8, stride=16), :], index(layer, face))
            at = BASE[0] + 4 * at_end(face) + k
            turned = pltpu.roll(got, 4, 0)
            target[layer, pl.ds(at, 8, stride=16), :] += factor * turned
    for face in (4, 5):
        here, there = at_end(face), at_end(face ^ 1)
        x, y = (
            picked(field[layer, pl.ds(BASE[c] + there, 16, stride=4), :], index(layer, face))
            for c in (0, 1)
        )
        target[layer, pl.ds(BASE[0] + here, 16, stride=4), :] += (-scale * parity(0, face, 1)) * y
        target[layer, pl.ds(BASE[1] + here, 16, stride=4), :] += (-scale * parity(1, face, 0)) * x


def lift_end(target, field, layer, i, index, scale, to_x):
    for face in (2, 3):
        source, sink = (2, 0) if to_x else (0, 2)
        at = BASE[source] + 16 * i + 4 * at_end(face ^ 1)
        got = picked(field[layer, at : at + 4, :], index(layer, face))
        at = BASE[sink] + 16 * i + 4 * at_end(face)
        target[layer, at : at + 4, :] += (-scale * parity(sink, face, source)) * got
    for face in (4, 5):
        source, sink = (1, 0) if to_x else (0, 1)
        at = BASE[source] + 16 * i + at_end(face ^ 1)
        got = picked(field[layer, pl.ds(at, 4, stride=4), :], index(layer, face))
        at = BASE[sink] + 16 * i + at_end(face)
        target[layer, pl.ds(at, 4, stride=4), :] += (-scale * parity(sink, face, source)) * got


def own_parts(table, x, values):
    for i, value in enumerate(values):
        here = slice(i * LAYER, (i + 1) * LAYER)
        high, low = halves(value)
        x[0:ROWS, here] = high
        x[ROWS : 2 * ROWS, here] = low
        x[2 * ROWS : 3 * ROWS, here] = high
    found = dot(table[...], x[...])
    return [found[:, i * LAYER : (i + 1) * LAYER] for i in range(2)]


def near_parts(table, a, b):
    both = jnp.concatenate([a.astype(BF16), b.astype(BF16)], axis=1)
    found = dot(table[:, 0:ROWS], both)
    return found[:, 0:LAYER], found[:, LAYER : 2 * LAYER]


def lonely(table, ends, x, index, fe, fh, acc, electric, drive_of, v, before_h=lambda: None):
    own = (L0, L1)

    def between(target, field, scale):
        for layer, face in ((L0, 1), (L1, 0)):
            y, z = x_traces(field, L0 + L1 - layer, face ^ 1)
            got = [picked(t, index(layer, face)) for t in (y, z)]
            lift_x(target, layer, face, scale, *got)

    def ends_of(field):
        return x_traces(field, L1, 1), x_traces(field, L0, 0)

    found = [ends_of(fe)]
    parts = own_parts(table, x, electric)
    before_h()
    between(fh, fe, TIME_STEP)
    magnetic = []
    for i, layer in enumerate(own):
        lift_inside(fh, fe, layer, index, TIME_STEP)
        magnetic.append(fh[layer] + TIME_STEP * parts[i])
        fh[layer] = magnetic[i]
    found.append(ends_of(fh))
    parts = own_parts(table, x, magnetic)
    drive = drive_of()
    for i, layer in enumerate(own):
        acc[layer] = drive[i]
    between(acc, fh, 1.0)
    for i, layer in enumerate(own):
        lift_inside(acc, fh, layer, index, 1.0)
        electric[i] = electric[i] - TIME_STEP * thrice(v[i]) * (parts[i] + acc[layer])
        fe[layer] = electric[i]
    found.append(ends_of(fe))
    parts = own_parts(ends, x, electric)
    for i, layer in enumerate(own):
        face = i
        lift_end(fh, fe, layer, at_end(face), index, TIME_STEP, False)
        for place, c in enumerate((1, 2)):
            at = BASE[c] + 16 * at_end(face)
            part = parts[i][32 * i + 16 * place : 32 * i + 16 * place + 16]
            fh[layer, at : at + 16, :] += TIME_STEP * part
    found.append(ends_of(fh))
    return [jnp.concatenate(sum(traces, []), axis=0) for traces in zip(*found)]


def two_steps(
    tables, x, index, valid, fe, fh, acc, e, h, j, source, v, w, v_near, sent_a, sent_b
):
    table, ends = tables
    own = (L0, L1)
    sides = ((A1, 1, L0, sent_a), (B1, 0, L1, sent_b))
    electric = [e[0], e[1]]
    magnetic = [h[0], h[1]]
    for i, layer in enumerate(own):
        fe[layer] = electric[i]
        fh[layer] = magnetic[i]

    def between(target, field, scale, start, answered=True):
        for layer, face in ((L0, 1), (L1, 0)):
            y, z = x_traces(field, L0 + L1 - layer, face ^ 1)
            got = [picked(t, index(layer, face)) for t in (y, z)]
            lift_x(target, layer, face, scale, *got)
        for side, (near, face, layer, sent) in enumerate(sides):
            traces = [sent[start + 16 * t : start + 16 * t + 16, :] for t in range(2)]
            if answered:
                traces = [a + b for a, b in zip(traces, x_traces(field, near, face))]
            mask = jnp.concatenate([valid[side]] * 2, axis=0)
            got = [picked(t, index(layer, face ^ 1)) * mask for t in traces]
            lift_x(target, layer, face ^ 1, scale, *got)

    def outward(target, field, scale):
        for near, face, layer, _ in sides:
            y, z = x_traces(field, layer, face ^ 1)
            got = [picked(t, index(near, face)) for t in (y, z)]
            lift_x(target, near, face, scale, *got)

    weight = [TIME_STEP * thrice(w[i]) for i in range(2)]
    blank = jnp.zeros((ROWS, LAYER), F32)

    parts = own_parts(table, x, electric)
    for near, _, _, _ in sides:
        fh[near] = blank
        acc[near] = blank
    outward(fh, fe, TIME_STEP)
    between(fh, fe, TIME_STEP, E_START, False)
    for i, layer in enumerate(own):
        lift_inside(fh, fe, layer, index, TIME_STEP)
        magnetic[i] = fh[layer] + TIME_STEP * parts[i]
        fh[layer] = magnetic[i]

    first_j = [KEEP * j[i] + weight[i] * electric[i] for i in range(2)]
    parts = own_parts(table, x, magnetic)
    near_found = near_parts(table, fh[A1], fh[B1])
    for i, layer in enumerate(own):
        acc[layer] = first_j[i] + source[i]
    between(acc, fh, 1.0, H_FIRST)
    outward(acc, fh, 1.0)
    for i, layer in enumerate(own):
        lift_inside(acc, fh, layer, index, 1.0)
        electric[i] = electric[i] - TIME_STEP * thrice(v[i]) * (parts[i] + acc[layer])
        fe[layer] = electric[i]
    first_e = list(electric)
    near_e = []
    for side, (near, face, _, _) in enumerate(sides):
        lift_end(acc, fh, near, at_end(face), index, 1.0, True)
        near_e.append(-TIME_STEP * thrice(v_near[side]) * (near_found[side] + acc[near]))
        fe[near] = near_e[side]

    parts = own_parts(table, x, electric)
    near_found = near_parts(ends, *near_e)
    between(fh, fe, TIME_STEP, E_FIRST)
    outward(fh, fe, TIME_STEP)
    for i, layer in enumerate(own):
        lift_inside(fh, fe, layer, index, TIME_STEP)
        magnetic[i] = fh[layer] + TIME_STEP * parts[i]
        fh[layer] = magnetic[i]
    for side, (near, face, _, _) in enumerate(sides):
        lift_end(fh, fe, near, at_end(face), index, TIME_STEP, False)
        for place, c in enumerate((1, 2)):
            at = BASE[c] + 16 * at_end(face)
            start = 32 * face + 16 * place
            fh[near, at : at + 16, :] += TIME_STEP * near_found[side][start : start + 16]

    second_j = [KEEP * first_j[i] + weight[i] * electric[i] for i in range(2)]
    parts = own_parts(table, x, magnetic)
    for i, layer in enumerate(own):
        acc[layer] = second_j[i] + source[i]
    between(acc, fh, 1.0, H_SECOND)
    for i, layer in enumerate(own):
        lift_inside(acc, fh, layer, index, 1.0)
        electric[i] = electric[i] - TIME_STEP * thrice(v[i]) * (parts[i] + acc[layer])
        fe[layer] = electric[i]
    return first_e, first_j, electric, second_j, magnetic


def odd_rank():
    return lax.rem(lax.axis_index("space"), 2) == 1


def send(across, inside, at, up, down):
    odd = odd_rank()
    rows = slice(at, at + up.shape[0])
    across[rows, :] = jnp.where(odd, up, down)
    inside[rows, :] = jnp.where(odd, down, up)


def sides_of(across, inside, a, b, rows):
    odd = odd_rank()
    from_across, from_inside = across[0:rows, :], inside[0:rows, :]
    a[...] = jnp.where(odd, from_inside, from_across)
    b[...] = jnp.where(odd, from_across, from_inside)


def first_kernel(
    table_in, ends_in, e_in, h_in, j_in, v_in, w_in, near_in, ports_in, profile_in, *rest
):
    table, ends, e, h, j, v, w, source, places, valid, across, inside = rest[:12]
    fe, fh, acc, x, neighbor, ports, profile, sems = rest[12:]
    started = []

    def fetch(origin, target):
        started.append(pltpu.make_async_copy(origin, target, sems.at[len(started)]))
        started[-1].start()
        return [started[-1]]

    def fetch_layers(origin, target):
        return [
            fetch(origin.at[:, pl.ds(i * LAYER, LAYER)], target.at[i])[0] for i in range(2)
        ]

    def wait(copies):
        for copy in copies:
            copy.wait()

    start = fetch_layers(e_in, e) + fetch(table_in, table) + fetch(near_in, neighbor)
    second = fetch_layers(h_in, h) + fetch(ports_in, ports) + fetch(profile_in, profile)
    third = fetch_layers(w_in, w) + fetch_layers(j_in, j) + fetch_layers(v_in, v)
    third += fetch(ends_in, ends)

    wait(start)
    found = neighbor[...]
    place = jnp.where(found < 0, 0, jnp.bitwise_and(found, LAYER - 1))
    for i in range(2):
        columns = slice(i * LAYER, (i + 1) * LAYER)
        for face in range(6):
            places[6 * i + face] = jnp.broadcast_to(place[face : face + 1, columns], (8, LAYER))
        there = (found[i : i + 1, columns] >= 0).astype(F32)
        valid[i] = jnp.broadcast_to(there, (8, LAYER))
    electric = [stored(e[i]) for i in range(2)]
    for i in range(2):
        fe[L0 + i] = electric[i]

    def before_h():
        wait(second)
        for i in range(2):
            fh[L0 + i] = stored(h[i])
        count = 2 * LAYER
        targets = lax.broadcasted_iota(jnp.int32, (count, ports.shape[1]), 0)
        spread_hot = one_hot(targets, jnp.bitwise_and(ports[...], count - 1))
        high, low = halves(profile[...])
        spread = dot_t(high, spread_hot) + dot_t(low, spread_hot)
        for i in range(2):
            source[i] = stored(spread[:, i * LAYER : (i + 1) * LAYER])

    first_e = list(electric)

    def drive_of():
        wait(third)
        drive = []
        for i in range(2):
            weight = TIME_STEP * thrice(w[i])
            drive.append(KEEP * stored(j[i]) + weight * first_e[i] + source[i])
        return drive

    def index(layer, face):
        return places[6 * (layer - L0) + face]

    up, down = lonely(
        table, ends, x, index, fe, fh, acc, electric, drive_of, v, before_h
    )
    send(across, inside, 0, up, down)
    send(across, inside, V_NEAR, v[1], v[0])
    blank = jnp.zeros((2, LAYER), F32)
    place = place.astype(F32)
    send(
        across,
        inside,
        N_NEAR,
        jnp.concatenate([place[:, LAYER : 2 * LAYER], blank], axis=0),
        jnp.concatenate([place[:, 0:LAYER], blank], axis=0),
    )


def index_of(places, near_places):
    def index(layer, face):
        if layer in (L0, L1):
            return places[6 * (layer - L0) + face]
        return near_places[6 * (layer == B1) + face]

    return index


def middle_kernel(
    table, ends, e, h, j, v, w, source, places, valid, across_in, inside_in, *rest
):
    out_e, out_h, out_j, mid_e, mid_j, v_near, near_places, across, inside = rest[:9]
    fe, fh, acc, x, sent_a, sent_b = rest[9:]
    sides_of(across_in, inside_in, sent_a, sent_b, FIRST)
    for side, sent in enumerate((sent_a, sent_b)):
        v_near[side] = sent[V_NEAR : V_NEAR + NODES, :]
        place = sent[N_NEAR : N_NEAR + 8, :].astype(jnp.int32)
        for face in range(6):
            near_places[6 * side + face] = jnp.broadcast_to(place[face : face + 1], (8, LAYER))
    index = index_of(places, near_places)
    start = [[stored(field[i]) for i in range(2)] for field in (e, h, j)]
    first_e, first_j, second_e, second_j, magnetic = two_steps(
        (table, ends), x, index, valid, fe, fh, acc, *start, source, v, w, v_near,
        sent_a, sent_b,
    )
    drive = []
    for i in range(2):
        mid_e[i] = first_e[i]
        mid_j[i] = first_j[i]
        out_e[i] = second_e[i]
        out_j[i] = second_j[i]
        out_h[i] = magnetic[i]
        weight = TIME_STEP * thrice(w[i])
        drive.append(KEEP * second_j[i] + weight * second_e[i] + source[i])
    up, down = lonely(table, ends, x, index, fe, fh, acc, list(second_e), lambda: drive, v)
    send(across, inside, 0, up, down)


def early_kernel(mid_e, mid_j, end_e, end_j, levels, design, out, pixels):
    pixel = jnp.bitwise_and(design[...], PIX_DEV - 1)
    pixels[...] = one_hot(lax.broadcasted_iota(jnp.int32, pixels.shape, 0), pixel)
    for i in range(2):
        columns = slice(i * LAYER, (i + 1) * LAYER)
        start, middle, end = (stored(levels[k, :, columns].astype(F32)) for k in range(3))
        out[0:NODES, columns] = folded(
            mid_e[i] * (middle - start) + end_e[i] * (end - middle)
        )
        out[NODES : 2 * NODES, columns] = folded(mid_j[i] * start + end_j[i] * middle)


def last_kernel(
    table, ends, e, h, j, v, w, source, places, valid, v_near, near_places,
    across_in, inside_in, levels, early, pixels, *rest
):
    out_e, out_h, sums = rest[:3]
    fe, fh, acc, x, sent_a, sent_b = rest[3:]
    sides_of(across_in, inside_in, sent_a, sent_b, SECOND)
    first_e, first_j, second_e, second_j, magnetic = two_steps(
        (table, ends), x, index_of(places, near_places), valid, fe, fh, acc,
        e, h, j, source, v, w, v_near, sent_a, sent_b,
    )
    for i in range(2):
        out_e[i] = second_e[i]
        out_h[i] = magnetic[i]
    parts = []
    for i in range(2):
        columns = slice(i * LAYER, (i + 1) * LAYER)
        start, middle, end = (stored(levels[k, :, columns].astype(F32)) for k in range(2, 5))
        eps = folded(first_e[i] * (middle - start) + second_e[i] * (end - middle))
        drude = folded(first_j[i] * start + second_j[i] * middle)
        parts.append(jnp.concatenate([eps, drude], axis=0) + early[:, columns])
    both = jnp.concatenate(parts, axis=1)
    high, low = halves(both)
    sums[...] = dot_t(pixels[...], high) + dot_t(pixels[...], low)


def total_kernel(owners, parts, e, h, out_e, out_h, eps, drude, sums, sems):
    copies = []

    def write(origin, target):
        copies.append(pltpu.make_async_copy(origin, target, sems.at[len(copies)]))
        copies[-1].start()

    for field, target in ((e, out_e), (h, out_h)):
        for i in range(2):
            for c in range(3):
                there = target.at[pl.ds(c * NODES, NODES), pl.ds(i * LAYER, LAYER)]
                write(field.at[i, pl.ds(BASE[c], NODES), :], there)
    share = parts.shape[0] // owners
    total = parts[0:share]
    for owner in range(1, owners):
        total = total + parts[owner * share : (owner + 1) * share]
    total = total * (1.0 / owners)
    sums[0] = total[:, 0:NODES]
    sums[1] = total[:, NODES : 2 * NODES]
    write(sums.at[0], eps)
    write(sums.at[1], drude)
    for copy in copies:
        copy.wait()


def call(kernel, outs, args, scratch=(), flops=0, spaces=None, out_spaces=None):
    moved = sum(4 * int(np.prod(o.shape)) for o in outs) + sum(
        a.dtype.itemsize * int(np.prod(a.shape)) for a in args
    )
    return pl.pallas_call(
        kernel,
        out_shape=outs,
        in_specs=[pl.BlockSpec(memory_space=s) for s in spaces or [pltpu.VMEM] * len(args)],
        out_specs=[pl.BlockSpec(memory_space=s) for s in out_spaces or [pltpu.VMEM] * len(outs)],
        scratch_shapes=list(scratch),
        compiler_params=pltpu.CompilerParams(vmem_limit_bytes=24 * 1024 * 1024),
        cost_estimate=pl.CostEstimate(flops=flops, bytes_accessed=moved, transcendentals=0),
    )(*args)


def f32(*shape):
    return jax.ShapeDtypeStruct(shape, F32)


def bf16(*shape):
    return jax.ShapeDtypeStruct(shape, BF16)


def exchange(across, inside):
    size = lax.axis_size("space")

    def pairs(start):
        found = [(i, i + 1) for i in range(start, size - 1, 2)]
        return found + [(j, i) for i, j in found]

    return lax.ppermute(across, "space", pairs(1)), lax.ppermute(inside, "space", pairs(0))


def local(
    adj_e,
    adj_h,
    adj_j,
    fwd_e,
    inv_eps,
    drude_weight,
    neighbor,
    design_map,
    port_elems,
    port_profile,
):
    count = adj_e.shape[2]
    owners = lax.axis_size("exc")
    table, ends = (jnp.asarray(t) for t in step_tables())
    levels = fwd_e[0]
    field, nodal = f32(2, ROWS, LAYER), f32(2, NODES, LAYER)
    indices = jax.ShapeDtypeStruct((12, 8, LAYER), jnp.int32)
    work = [pltpu.VMEM((4, ROWS, LAYER), F32)] * 3
    work += [pltpu.VMEM((3 * ROWS, 2 * LAYER), BF16)]
    given = [table, ends, adj_e[0], adj_h[0], adj_j[0], inv_eps, drude_weight]
    given += [neighbor, port_elems, port_profile[0]]
    once = 2 * ROWS * 3 * ROWS * LAYER

    table, ends, e, h, j, v, w, source, places, valid, across, inside = call(
        first_kernel,
        [bf16(*table.shape), bf16(*ends.shape), field, field, field, nodal, nodal]
        + [field, indices, f32(2, 8, LAYER)]
        + [f32(FIRST, LAYER)] * 2,
        [pltpu.with_memory_space_constraint(a, pltpu.HBM) for a in given],
        work
        + [
            pltpu.VMEM(neighbor.shape, jnp.int32),
            pltpu.VMEM(port_elems.shape, jnp.int32),
            pltpu.VMEM(port_profile.shape[1:], F32),
            pltpu.SemaphoreType.DMA((15,)),
        ],
        6 * once,
        [pltpu.HBM] * len(given),
    )
    across, inside = exchange(across, inside)
    e2, h2, j2, e1, j1, v_near, near_places, across, inside = call(
        middle_kernel,
        [field] * 5 + [nodal, indices] + [f32(SECOND, LAYER)] * 2,
        [table, ends, e, h, j, v, w, source, places, valid, across, inside],
        work + [pltpu.VMEM((FIRST, LAYER), F32)] * 2,
        18 * once,
    )
    across, inside = exchange(across, inside)
    early, pixels = call(
        early_kernel,
        [f32(2 * NODES, count), bf16(PIX_DEV, count)],
        [e1, j1, e2, j2, levels, design_map.reshape(1, count)],
    )
    e4, h4, sums = call(
        last_kernel,
        [field, field, f32(PIX_DEV, 2 * NODES)],
        [table, ends, e2, h2, j2, v, w, source, places, valid, v_near, near_places]
        + [across, inside, levels, early, pixels],
        work + [pltpu.VMEM((SECOND, LAYER), F32)] * 2,
        12 * once,
    )
    parts = lax.all_to_all(sums, "exc", split_axis=0, concat_axis=0, tiled=True)
    share = PIX_DEV // owners
    out_e, out_h, eps, drude = call(
        functools.partial(total_kernel, owners),
        [f32(ROWS, count)] * 2 + [f32(share, NODES)] * 2,
        [parts, e4, h4],
        [pltpu.VMEM((2, share, NODES), F32), pltpu.SemaphoreType.DMA((14,))],
        out_spaces=[pltpu.HBM] * 4,
    )
    return out_e[None], out_h[None], eps.T, drude.T


def solution(mesh):
    return jax.shard_map(
        local,
        mesh=mesh,
        in_specs=(
            P("exc", None, "space"),
            P("exc", None, "space"),
            P("exc", None, "space"),
            P("exc", None, None, "space"),
            P(None, "space"),
            P(None, "space"),
            P(None, "space"),
            P("space"),
            P("exc", "space"),
            P("exc", None, "space"),
        ),
        out_specs=(
            P("exc", None, "space"),
            P("exc", None, "space"),
            P(None, ("space", "exc")),
            P(None, ("space", "exc")),
        ),
        check_vma=False,
    )
```

```python
import functools

import jax
import jax.numpy as jnp
import ml_dtypes
import numpy as np
from jax import lax
from jax.experimental import pallas as pl
from jax.experimental.pallas import tpu as pltpu
from jax.sharding import PartitionSpec as P

NODES = 64
ROWS = 3 * NODES
LAYER = 128
PIX_DEV = 128

TIME_STEP = 0.025
DAMPING = 0.5
KEEP = 1.0 - TIME_STEP * DAMPING

TANGENT = 32
E_START = 0
H_FIRST = 32
E_FIRST = 64
H_SECOND = 96
SECOND = 128
V_NEAR = 128
N_NEAR = V_NEAR + NODES
FIRST = N_NEAR + 8

A1, L0, L1, B1 = range(4)

BASE = (NODES, 0, 2 * NODES)

BF16 = jnp.bfloat16
F32 = jnp.float32


def parity(c, face, other):
    d = face // 2
    sign = 1.0 if face % 2 else -1.0
    return 6.0 * sign * (c - d) * (d - other) * (other - c) / 2.0


def own_rate():
    points = np.array([-1.0, -1.0 / np.sqrt(5.0), 1.0 / np.sqrt(5.0), 1.0])
    barycentric = np.array(
        [1.0 / np.prod([points[j] - points[k] for k in range(4) if k != j]) for j in range(4)]
    )
    deriv = np.zeros((4, 4))
    for row in range(4):
        for column in range(4):
            if row != column:
                deriv[row, column] = (
                    barycentric[column] / barycentric[row] / (points[row] - points[column])
                )
        deriv[row, row] = -np.sum(deriv[row])
    identity = np.eye(4)
    along_x = 2.0 * np.kron(np.kron(deriv, identity), identity)
    along_y = 2.0 * np.kron(np.kron(identity, deriv), identity)
    along_z = 2.0 * np.kron(np.kron(identity, identity), deriv)
    curl = np.zeros((192, 192))
    curl[0:64, 64:128] = -along_z
    curl[0:64, 128:192] = along_y
    curl[64:128, 0:64] = along_z
    curl[64:128, 128:192] = -along_x
    curl[128:192, 0:64] = -along_y
    curl[128:192, 64:128] = along_x
    numbers = np.arange(64).reshape(4, 4, 4)
    faces = np.stack(
        [
            numbers[0].ravel(),
            numbers[3].ravel(),
            numbers[:, 0].ravel(),
            numbers[:, 3].ravel(),
            numbers[:, :, 0].ravel(),
            numbers[:, :, 3].ravel(),
        ]
    )
    inner = np.zeros((192, 192))
    for face in range(6):
        for c in range(3):
            for other in range(3):
                value = parity(c, face, other)
                if value != 0:
                    for node in faces[face]:
                        inner[c * 64 + node, other * 64 + node] += value
    return inner - curl


def step_tables():
    order = np.concatenate([np.arange(64) + 64 * c for c in (1, 0, 2)])
    own = own_rate()[order][:, order]
    high = own.astype(ml_dtypes.bfloat16)
    low = (own - high.astype(np.float64)).astype(ml_dtypes.bfloat16)
    table = np.concatenate([high, high, low], axis=1)
    ends = [table[BASE[c] + 16 * i : BASE[c] + 16 * i + 16] for i in (0, 3) for c in (1, 2)]
    return table, np.concatenate(ends, axis=0)


def halves(x):
    high = x.astype(BF16)
    return high, (x - high.astype(F32)).astype(BF16)


def dot(a, b):
    return jnp.dot(a, b, preferred_element_type=F32)


def dot_t(a, b):
    return lax.dot_general(a, b, (((1,), (1,)), ((), ())), preferred_element_type=F32)


def thrice(x):
    return jnp.concatenate([x, x, x], axis=0)


def folded(x):
    return x[0:NODES] + x[NODES : 2 * NODES] + x[2 * NODES : ROWS]


def stored(x):
    return jnp.concatenate([x[NODES : 2 * NODES], x[0:NODES], x[2 * NODES : ROWS]], axis=0)


def one_hot(rows, targets):
    return (rows == targets).astype(F32).astype(BF16)


def picked(x, index):
    rows = x.shape[0]
    if rows < 8:
        index = index[0:rows]
    elif rows > 8:
        index = jnp.concatenate([index] * (rows // 8), axis=0)
    along = lax.GatherDimensionNumbers(
        offset_dims=(),
        collapsed_slice_dims=(1,),
        start_index_map=(1,),
        operand_batching_dims=(0,),
        start_indices_batching_dims=(0,),
    )
    mode = lax.GatherScatterMode.PROMISE_IN_BOUNDS
    return lax.gather(x, index[..., None], along, (1, 1), mode=mode)


def at_end(face):
    return 3 if face % 2 else 0


def x_traces(field, layer, face):
    at = 16 * at_end(face)
    return [field[layer, BASE[c] + at : BASE[c] + at + 16, :] for c in (1, 2)]


def lift_x(target, layer, face, scale, y, z):
    at = 16 * at_end(face)
    rows = slice(BASE[1] + at, BASE[1] + at + 16)
    target[layer, rows, :] += (-scale * parity(1, face, 2)) * z
    rows = slice(BASE[2] + at, BASE[2] + at + 16)
    target[layer, rows, :] += (-scale * parity(2, face, 1)) * y


def lift_inside(target, field, layer, index, scale):
    first = lax.broadcasted_iota(jnp.int32, (8, LAYER), 0) < 4
    for face in (2, 3):
        factor = jnp.where(first, -scale * parity(0, face, 2), -scale * parity(2, face, 0))
        for k in range(4):
            at = BASE[0] + 4 * at_end(face ^ 1) + k
            got = picked(field[layer, pl.ds(at, 8, stride=16), :], index(layer, face))
            at = BASE[0] + 4 * at_end(face) + k
            turned = pltpu.roll(got, 4, 0)
            target[layer, pl.ds(at, 8, stride=16), :] += factor * turned
    for face in (4, 5):
        here, there = at_end(face), at_end(face ^ 1)
        x, y = (
            picked(field[layer, pl.ds(BASE[c] + there, 16, stride=4), :], index(layer, face))
            for c in (0, 1)
        )
        target[layer, pl.ds(BASE[0] + here, 16, stride=4), :] += (-scale * parity(0, face, 1)) * y
        target[layer, pl.ds(BASE[1] + here, 16, stride=4), :] += (-scale * parity(1, face, 0)) * x


def lift_end(target, field, layer, i, index, scale, to_x):
    for face in (2, 3):
        source, sink = (2, 0) if to_x else (0, 2)
        at = BASE[source] + 16 * i + 4 * at_end(face ^ 1)
        got = picked(field[layer, at : at + 4, :], index(layer, face))
        at = BASE[sink] + 16 * i + 4 * at_end(face)
        target[layer, at : at + 4, :] += (-scale * parity(sink, face, source)) * got
    for face in (4, 5):
        source, sink = (1, 0) if to_x else (0, 1)
        at = BASE[source] + 16 * i + at_end(face ^ 1)
        got = picked(field[layer, pl.ds(at, 4, stride=4), :], index(layer, face))
        at = BASE[sink] + 16 * i + at_end(face)
        target[layer, pl.ds(at, 4, stride=4), :] += (-scale * parity(sink, face, source)) * got


def own_parts(table, x, values):
    for i, value in enumerate(values):
        here = slice(i * LAYER, (i + 1) * LAYER)
        high, low = halves(value)
        x[0:ROWS, here] = high
        x[ROWS : 2 * ROWS, here] = low
        x[2 * ROWS : 3 * ROWS, here] = high
    return layers_of(dot(table[...], x[...]))


def rough_parts(table, values):
    both = jnp.concatenate([value.astype(BF16) for value in values], axis=1)
    return layers_of(dot(table[:, 0:ROWS], both))


def layers_of(x):
    return [x[:, at : at + LAYER] for at in range(0, x.shape[1], LAYER)]


def lift_between(target, field, index, scale):
    for layer, face in ((L0, 1), (L1, 0)):
        got = [picked(t, index(layer, face)) for t in x_traces(field, L0 + L1 - layer, face ^ 1)]
        lift_x(target, layer, face, scale, *got)


def lone_h(table, x, index, fe, fh, electric, before=lambda: None):
    parts = own_parts(table, x, electric)
    before()
    lift_between(fh, fe, index, TIME_STEP)
    magnetic = []
    for i, layer in enumerate((L0, L1)):
        lift_inside(fh, fe, layer, index, TIME_STEP)
        magnetic.append(fh[layer] + TIME_STEP * parts[i])
        fh[layer] = magnetic[i]
    return magnetic


def lone_e(table, x, index, fe, fh, acc, electric, magnetic, drive_of, v):
    parts = own_parts(table, x, magnetic)
    drive = drive_of()
    for i, layer in enumerate((L0, L1)):
        acc[layer] = drive[i]
    lift_between(acc, fh, index, 1.0)
    found = []
    for i, layer in enumerate((L0, L1)):
        lift_inside(acc, fh, layer, index, 1.0)
        found.append(electric[i] - TIME_STEP * thrice(v[i]) * (parts[i] + acc[layer]))
        fe[layer] = found[i]
    return found


def lonely(table, ends, x, index, fe, fh, acc, electric, drive_of, v, before_h=lambda: None):
    def ends_of(field):
        return x_traces(field, L1, 1), x_traces(field, L0, 0)

    found = [ends_of(fe)]
    magnetic = lone_h(table, x, index, fe, fh, electric, before_h)
    found.append(ends_of(fh))
    electric = lone_e(table, x, index, fe, fh, acc, electric, magnetic, drive_of, v)
    found.append(ends_of(fe))
    parts = own_parts(ends, x, electric)
    for i, layer in enumerate((L0, L1)):
        face = i
        lift_end(fh, fe, layer, at_end(face), index, TIME_STEP, False)
        for place, c in enumerate((1, 2)):
            at = BASE[c] + 16 * at_end(face)
            part = parts[i][32 * i + 16 * place : 32 * i + 16 * place + 16]
            fh[layer, at : at + 16, :] += TIME_STEP * part
    found.append(ends_of(fh))
    traces = [jnp.concatenate(sum(pairs, []), axis=0) for pairs in zip(*found)]
    return electric, magnetic, *traces


def respond(tables, index, valid, fe, fh, acc, lone, v, w, v_near, sent_a, sent_b):
    table, ends = tables
    start_e, lone_h1, lone_e1 = lone
    own, wide = (L0, L1), (A1, L0, L1, B1)
    sides = ((A1, 1, L0, sent_a), (B1, 0, L1, sent_b))
    blank = jnp.zeros((ROWS, LAYER), F32)

    def inward(target, field, scale, start, answered=True):
        for side, (near, face, layer, sent) in enumerate(sides):
            traces = [sent[start + 16 * t : start + 16 * t + 16, :] for t in range(2)]
            if answered:
                traces = [a + b for a, b in zip(traces, x_traces(field, near, face))]
            mask = jnp.concatenate([valid[side]] * 2, axis=0)
            got = [picked(t, index(layer, face ^ 1)) * mask for t in traces]
            lift_x(target, layer, face ^ 1, scale, *got)

    def outward(target, field, alone, scale, answered=True):
        for near, face, layer, _ in sides:
            traces = x_traces(alone, layer - L0, face ^ 1)
            if answered:
                traces = [a + b for a, b in zip(traces, x_traces(field, layer, face ^ 1))]
            got = [picked(t, index(near, face)) for t in traces]
            lift_x(target, near, face, scale, *got)

    for layer in wide:
        fh[layer] = blank
        acc[layer] = blank
    inward(fh, fe, TIME_STEP, E_START, False)
    outward(fh, fe, start_e, TIME_STEP, False)

    parts = rough_parts(table, [fh[layer] for layer in wide])
    inward(acc, fh, 1.0, H_FIRST)
    outward(acc, fh, lone_h1, 1.0)
    scales = [v_near[0], v[0], v[1], v_near[1]]
    first_e = []
    for i, layer in enumerate(wide):
        lift_end(acc, fh, layer, 3 if layer in (A1, L1) else 0, index, 1.0, True)
        first_e.append(-TIME_STEP * thrice(scales[i]) * (parts[i] + acc[layer]))
        fe[layer] = first_e[i]

    parts = rough_parts(table, first_e[1:3])
    near_found = rough_parts(ends, [first_e[0], first_e[3]])
    inward(fh, fe, TIME_STEP, E_FIRST)
    outward(fh, fe, lone_e1, TIME_STEP)
    lift_between(fh, fe, index, TIME_STEP)
    magnetic = []
    for i, layer in enumerate(own):
        lift_inside(fh, fe, layer, index, TIME_STEP)
        magnetic.append(fh[layer] + TIME_STEP * parts[i])
        fh[layer] = magnetic[i]
    for side, (near, face, _, _) in enumerate(sides):
        lift_end(fh, fe, near, at_end(face), index, TIME_STEP, False)
        for place, c in enumerate((1, 2)):
            at = BASE[c] + 16 * at_end(face)
            start = 32 * face + 16 * place
            fh[near, at : at + 16, :] += TIME_STEP * near_found[side][start : start + 16]

    parts = rough_parts(table, magnetic)
    current = [TIME_STEP * thrice(w[i]) * first_e[1 + i] for i in range(2)]
    for i, layer in enumerate(own):
        acc[layer] = current[i]
    inward(acc, fh, 1.0, H_SECOND)
    lift_between(acc, fh, index, 1.0)
    second_e = []
    for i, layer in enumerate(own):
        lift_inside(acc, fh, layer, index, 1.0)
        change = TIME_STEP * thrice(v[i]) * (parts[i] + acc[layer])
        second_e.append(first_e[1 + i] - change)
    return first_e[1:3], magnetic, second_e, current


def odd_rank():
    return lax.rem(lax.axis_index("space"), 2) == 1


def send(across, inside, at, up, down):
    odd = odd_rank()
    rows = slice(at, at + up.shape[0])
    across[rows, :] = jnp.where(odd, up, down)
    inside[rows, :] = jnp.where(odd, down, up)


def sides_of(across, inside, a, b, rows):
    odd = odd_rank()
    from_across, from_inside = across[0:rows, :], inside[0:rows, :]
    a[...] = jnp.where(odd, from_inside, from_across)
    b[...] = jnp.where(odd, from_across, from_inside)


def first_kernel(
    table_in, ends_in, e_in, h_in, j_in, v_in, w_in, near_in, ports_in, profile_in, *rest
):
    table, ends, start_e, lone_h1, lone_e1, first_j, v, w = rest[:8]
    source, places, valid, across, inside = rest[8:13]
    fe, fh, acc, x, neighbor, ports, profile, e, h, j, v_all, w_all, sems = rest[13:]
    started = []

    def fetch(origin, target):
        started.append(pltpu.make_async_copy(origin, target, sems.at[len(started)]))
        started[-1].start()
        return started[-1]

    scatter = [fetch(near_in, neighbor), fetch(ports_in, ports), fetch(profile_in, profile)]
    fields = [fetch(e_in, e), fetch(table_in, table), fetch(h_in, h)]
    rest = [fetch(j_in, j), fetch(w_in, w_all), fetch(v_in, v_all), fetch(ends_in, ends)]

    for copy in scatter:
        copy.wait()
    found = neighbor[...]
    place = jnp.where(found < 0, 0, jnp.bitwise_and(found, LAYER - 1))
    for i in range(2):
        columns = slice(i * LAYER, (i + 1) * LAYER)
        for face in range(6):
            places[6 * i + face] = jnp.broadcast_to(place[face : face + 1, columns], (8, LAYER))
        there = (found[i : i + 1, columns] >= 0).astype(F32)
        valid[i] = jnp.broadcast_to(there, (8, LAYER))
    targets = lax.broadcasted_iota(jnp.int32, (2 * LAYER, ports.shape[1]), 0)
    spread_hot = one_hot(targets, jnp.bitwise_and(ports[...], 2 * LAYER - 1))
    high, low = halves(profile[...])
    spread = layers_of(dot_t(high, spread_hot) + dot_t(low, spread_hot))
    for copy in fields + rest:
        copy.wait()
    electric = [stored(part) for part in layers_of(e[...])]
    magnetic = [stored(part) for part in layers_of(h[...])]
    current = [stored(part) for part in layers_of(j[...])]
    weight = layers_of(w_all[...])
    scale = layers_of(v_all[...])
    drive = []
    for i in range(2):
        source[i] = stored(spread[i])
        w[i] = weight[i]
        v[i] = scale[i]
        start_e[i] = electric[i]
        fe[L0 + i] = electric[i]
        fh[L0 + i] = magnetic[i]
        now = KEEP * current[i] + TIME_STEP * thrice(weight[i]) * electric[i]
        first_j[i] = now
        drive.append(now + source[i])

    def index(layer, face):
        return places[6 * (layer - L0) + face]

    electric, magnetic, up, down = lonely(
        table, ends, x, index, fe, fh, acc, electric, lambda: drive, v
    )
    for i in range(2):
        lone_e1[i] = electric[i]
        lone_h1[i] = magnetic[i]
    send(across, inside, 0, up, down)
    send(across, inside, V_NEAR, v[1], v[0])
    blank = jnp.zeros((2, LAYER), F32)
    place = place.astype(F32)
    send(
        across,
        inside,
        N_NEAR,
        jnp.concatenate([place[:, LAYER : 2 * LAYER], blank], axis=0),
        jnp.concatenate([place[:, 0:LAYER], blank], axis=0),
    )


def own_index(places):
    def index(layer, face):
        return places[6 * (layer - L0) + face]

    return index


def second_lone_step(table, lone_h1, lone_e1, first_j, v, w, source, places, work):
    fe, fh, acc, x = work
    index = own_index(places)
    electric = [lone_e1[i] for i in range(2)]
    for i in range(2):
        fe[L0 + i] = electric[i]
        fh[L0 + i] = lone_h1[i]
    current = [
        KEEP * first_j[i] + TIME_STEP * thrice(w[i]) * electric[i] for i in range(2)
    ]
    magnetic = lone_h(table, x, index, fe, fh, electric)
    electric = lone_e(
        table, x, index, fe, fh, acc, electric, magnetic,
        lambda: [current[i] + source[i] for i in range(2)], v,
    )
    return magnetic, electric, current


def lone_kernel(table, lone_h1, lone_e1, first_j, v, w, source, places, *rest):
    lone_h2, lone_e2, lone_j2 = rest[:3]
    found = second_lone_step(table, lone_h1, lone_e1, first_j, v, w, source, places, rest[3:])
    for out, values in zip((lone_h2, lone_e2, lone_j2), found):
        for i in range(2):
            out[i] = values[i]


def index_of(places, near_places):
    def index(layer, face):
        if layer in (L0, L1):
            return places[6 * (layer - L0) + face]
        return near_places[6 * (layer == B1) + face]

    return index


def middle_kernel(
    table, ends, start_e, lone_h1, lone_e1, lone_h2, lone_e2, lone_j2, v, w, source,
    places, valid, across_in, inside_in, *rest
):
    end_e, next_h, next_e, next_j, answer_e, answer_j, v_near, near_places = rest[:8]
    across, inside = rest[8:10]
    fe, fh, acc, x, sent_a, sent_b = rest[10:]
    sides_of(across_in, inside_in, sent_a, sent_b, FIRST)
    for side, sent in enumerate((sent_a, sent_b)):
        v_near[side] = sent[V_NEAR : V_NEAR + NODES, :]
        place = sent[N_NEAR : N_NEAR + 8, :].astype(jnp.int32)
        for face in range(6):
            near_places[6 * side + face] = jnp.broadcast_to(place[face : face + 1], (8, LAYER))
    index = index_of(places, near_places)
    first_e, magnetic, second_e, current = respond(
        (table, ends), index, valid, fe, fh, acc, (start_e, lone_h1, lone_e1),
        v, w, v_near, sent_a, sent_b,
    )
    electric, drive = [], []
    for i in range(2):
        answer_e[i] = first_e[i]
        answer_j[i] = current[i]
        electric.append(lone_e2[i] + second_e[i])
        end_e[i] = electric[i]
        fe[L0 + i] = electric[i]
        fh[L0 + i] = lone_h2[i] + magnetic[i]
        before = lone_j2[i] + current[i]
        now = KEEP * before + TIME_STEP * thrice(w[i]) * electric[i]
        next_j[i] = now
        drive.append(now + source[i])
    electric, magnetic, up, down = lonely(
        table, ends, x, index, fe, fh, acc, electric, lambda: drive, v
    )
    for i in range(2):
        next_e[i] = electric[i]
        next_h[i] = magnetic[i]
    send(across, inside, 0, up, down)


def early_kernel(
    table, lone_e1, answer_e, lone_j1, lone_j2, answer_j, end_e, next_h, next_e, next_j,
    v, w, source, places, levels, design, *rest
):
    last_h, last_e, last_j, out, pixels = rest[:5]
    pixel = jnp.bitwise_and(design[...], PIX_DEV - 1)
    pixels[...] = one_hot(lax.broadcasted_iota(jnp.int32, pixels.shape, 0), pixel)
    magnetic, electric, current = second_lone_step(
        table, next_h, next_e, next_j, v, w, source, places, rest[5:]
    )
    for i in range(2):
        last_h[i] = magnetic[i]
        last_e[i] = electric[i]
        last_j[i] = current[i]
        columns = slice(i * LAYER, (i + 1) * LAYER)
        level = [stored(levels[k, :, columns].astype(F32)) for k in range(5)]
        eps = (lone_e1[i] + answer_e[i]) * (level[1] - level[0])
        eps += end_e[i] * (level[2] - level[1]) + next_e[i] * (level[3] - level[2])
        eps += electric[i] * (level[4] - level[3])
        drude = lone_j1[i] * level[0] + (lone_j2[i] + answer_j[i]) * level[1]
        drude += next_j[i] * level[2] + current[i] * level[3]
        out[0:NODES, columns] = folded(eps)
        out[NODES : 2 * NODES, columns] = folded(drude)


def last_kernel(
    table, ends, start_e, lone_h1, lone_e1, lone_h2, lone_e2, v, w, places, valid,
    v_near, near_places, across_in, inside_in, levels, early, pixels, *rest
):
    out_e, out_h, sums = rest[:3]
    fe, fh, acc, sent_a, sent_b = rest[3:]
    sides_of(across_in, inside_in, sent_a, sent_b, SECOND)
    first_e, magnetic, second_e, current = respond(
        (table, ends), index_of(places, near_places), valid, fe, fh, acc,
        (start_e, lone_h1, lone_e1), v, w, v_near, sent_a, sent_b,
    )
    parts = []
    for i in range(2):
        out_e[i] = lone_e2[i] + second_e[i]
        out_h[i] = lone_h2[i] + magnetic[i]
        columns = slice(i * LAYER, (i + 1) * LAYER)
        start, middle, end = (stored(levels[k, :, columns].astype(F32)) for k in range(2, 5))
        eps = folded(first_e[i] * (middle - start) + second_e[i] * (end - middle))
        drude = folded(current[i] * middle)
        parts.append(jnp.concatenate([eps, drude], axis=0) + early[:, columns])
    both = jnp.concatenate(parts, axis=1)
    high, low = halves(both)
    sums[...] = dot_t(pixels[...], high) + dot_t(pixels[...], low)


def total_kernel(owners, parts, e, h, out_e, out_h, eps, drude, sums, sems):
    copies = []

    def write(origin, target):
        copies.append(pltpu.make_async_copy(origin, target, sems.at[len(copies)]))
        copies[-1].start()

    for field, target in ((e, out_e), (h, out_h)):
        for i in range(2):
            for c in range(3):
                there = target.at[pl.ds(c * NODES, NODES), pl.ds(i * LAYER, LAYER)]
                write(field.at[i, pl.ds(BASE[c], NODES), :], there)
    share = parts.shape[0] // owners
    total = parts[0:share]
    for owner in range(1, owners):
        total = total + parts[owner * share : (owner + 1) * share]
    total = total * (1.0 / owners)
    sums[0] = total[:, 0:NODES]
    sums[1] = total[:, NODES : 2 * NODES]
    write(sums.at[0], eps)
    write(sums.at[1], drude)
    for copy in copies:
        copy.wait()


def call(kernel, outs, args, scratch=(), flops=0, spaces=None, out_spaces=None):
    moved = sum(4 * int(np.prod(o.shape)) for o in outs) + sum(
        a.dtype.itemsize * int(np.prod(a.shape)) for a in args
    )
    return pl.pallas_call(
        kernel,
        out_shape=outs,
        in_specs=[pl.BlockSpec(memory_space=s) for s in spaces or [pltpu.VMEM] * len(args)],
        out_specs=[pl.BlockSpec(memory_space=s) for s in out_spaces or [pltpu.VMEM] * len(outs)],
        scratch_shapes=list(scratch),
        compiler_params=pltpu.CompilerParams(vmem_limit_bytes=24 * 1024 * 1024),
        cost_estimate=pl.CostEstimate(flops=flops, bytes_accessed=moved, transcendentals=0),
    )(*args)


def f32(*shape):
    return jax.ShapeDtypeStruct(shape, F32)


def bf16(*shape):
    return jax.ShapeDtypeStruct(shape, BF16)


def exchange(across, inside):
    size = lax.axis_size("space")

    def pairs(start):
        found = [(i, i + 1) for i in range(start, size - 1, 2)]
        return found + [(j, i) for i, j in found]

    return lax.ppermute(across, "space", pairs(1)), lax.ppermute(inside, "space", pairs(0))


def local(
    adj_e,
    adj_h,
    adj_j,
    fwd_e,
    inv_eps,
    drude_weight,
    neighbor,
    design_map,
    port_elems,
    port_profile,
):
    count = adj_e.shape[2]
    owners = lax.axis_size("exc")
    table, ends = (jnp.asarray(t) for t in step_tables())
    levels = fwd_e[0]
    field, nodal = f32(2, ROWS, LAYER), f32(2, NODES, LAYER)
    indices = jax.ShapeDtypeStruct((12, 8, LAYER), jnp.int32)
    work = [pltpu.VMEM((4, ROWS, LAYER), F32)] * 3
    work += [pltpu.VMEM((3 * ROWS, 2 * LAYER), BF16)]
    given = [table, ends, adj_e[0], adj_h[0], adj_j[0], inv_eps, drude_weight]
    given += [neighbor, port_elems, port_profile[0]]
    once = 2 * ROWS * 3 * ROWS * LAYER

    received = [pltpu.VMEM((FIRST, LAYER), F32)] * 2
    table, ends, start_e, h1, e1, j1, v, w, source, places, valid, across, inside = call(
        first_kernel,
        [bf16(*table.shape), bf16(*ends.shape)]
        + [field] * 4
        + [nodal, nodal, field, indices, f32(2, 8, LAYER)]
        + [f32(FIRST, LAYER)] * 2,
        [pltpu.with_memory_space_constraint(a, pltpu.HBM) for a in given],
        work
        + [pltpu.VMEM(a.shape, a.dtype) for a in [neighbor, port_elems, port_profile[0]]]
        + [pltpu.VMEM((ROWS, count), F32)] * 3
        + [pltpu.VMEM((NODES, count), F32)] * 2
        + [pltpu.SemaphoreType.DMA((10,))],
        6 * once,
        [pltpu.HBM] * len(given),
    )
    across, inside = exchange(across, inside)
    h2, e2, j2 = call(
        lone_kernel, [field] * 3, [table, h1, e1, j1, v, w, source, places], work, 4 * once
    )
    end_e, h3, e3, j3, answer_e, answer_j, v_near, near_places, across, inside = call(
        middle_kernel,
        [field] * 6 + [nodal, indices] + [f32(SECOND, LAYER)] * 2,
        [table, ends, start_e, h1, e1, h2, e2, j2, v, w, source]
        + [places, valid, across, inside],
        work + received,
        10 * once,
    )
    across, inside = exchange(across, inside)
    h4, e4, _, early, pixels = call(
        early_kernel,
        [field] * 3 + [f32(2 * NODES, count), bf16(PIX_DEV, count)],
        [table, e1, answer_e, j1, j2, answer_j, end_e, h3, e3, j3, v, w, source, places]
        + [levels, design_map.reshape(1, count)],
        work,
        4 * once,
    )
    e4, h4, sums = call(
        last_kernel,
        [field, field, f32(PIX_DEV, 2 * NODES)],
        [table, ends, end_e, h3, e3, h4, e4, v, w, places, valid, v_near, near_places]
        + [across, inside, levels, early, pixels],
        work[:3] + [pltpu.VMEM((SECOND, LAYER), F32)] * 2,
        4 * once,
    )
    parts = lax.all_to_all(sums, "exc", split_axis=0, concat_axis=0, tiled=True)
    share = PIX_DEV // owners
    out_e, out_h, eps, drude = call(
        functools.partial(total_kernel, owners),
        [f32(ROWS, count)] * 2 + [f32(share, NODES)] * 2,
        [parts, e4, h4],
        [pltpu.VMEM((2, share, NODES), F32), pltpu.SemaphoreType.DMA((14,))],
        out_spaces=[pltpu.HBM] * 4,
    )
    return out_e[None], out_h[None], eps.T, drude.T


def solution(mesh):
    return jax.shard_map(
        local,
        mesh=mesh,
        in_specs=(
            P("exc", None, "space"),
            P("exc", None, "space"),
            P("exc", None, "space"),
            P("exc", None, None, "space"),
            P(None, "space"),
            P(None, "space"),
            P(None, "space"),
            P("space"),
            P("exc", "space"),
            P("exc", None, "space"),
        ),
        out_specs=(
            P("exc", None, "space"),
            P("exc", None, "space"),
            P(None, ("space", "exc")),
            P(None, ("space", "exc")),
        ),
        check_vma=False,
    )
```

```python
import functools

import jax
import jax.numpy as jnp
import ml_dtypes
import numpy as np
from jax import lax
from jax.experimental import pallas as pl
from jax.experimental.pallas import tpu as pltpu
from jax.sharding import PartitionSpec as P

NODES = 64
ROWS = 3 * NODES
LAYER = 128
PIX_DEV = 128

TIME_STEP = 0.025
DAMPING = 0.5
KEEP = 1.0 - TIME_STEP * DAMPING

TANGENT = 32
E_START = 0
H_FIRST = 32
E_FIRST = 64
H_SECOND = 96
SECOND = 128
V_NEAR = 128
N_NEAR = V_NEAR + NODES
FIRST = N_NEAR + 8

A1, L0, L1, B1 = range(4)

BASE = (NODES, 0, 2 * NODES)

BF16 = jnp.bfloat16
F32 = jnp.float32


def parity(c, face, other):
    d = face // 2
    sign = 1.0 if face % 2 else -1.0
    return 6.0 * sign * (c - d) * (d - other) * (other - c) / 2.0


def own_rate():
    points = np.array([-1.0, -1.0 / np.sqrt(5.0), 1.0 / np.sqrt(5.0), 1.0])
    barycentric = np.array(
        [1.0 / np.prod([points[j] - points[k] for k in range(4) if k != j]) for j in range(4)]
    )
    deriv = np.zeros((4, 4))
    for row in range(4):
        for column in range(4):
            if row != column:
                deriv[row, column] = (
                    barycentric[column] / barycentric[row] / (points[row] - points[column])
                )
        deriv[row, row] = -np.sum(deriv[row])
    identity = np.eye(4)
    along_x = 2.0 * np.kron(np.kron(deriv, identity), identity)
    along_y = 2.0 * np.kron(np.kron(identity, deriv), identity)
    along_z = 2.0 * np.kron(np.kron(identity, identity), deriv)
    curl = np.zeros((192, 192))
    curl[0:64, 64:128] = -along_z
    curl[0:64, 128:192] = along_y
    curl[64:128, 0:64] = along_z
    curl[64:128, 128:192] = -along_x
    curl[128:192, 0:64] = -along_y
    curl[128:192, 64:128] = along_x
    numbers = np.arange(64).reshape(4, 4, 4)
    faces = np.stack(
        [
            numbers[0].ravel(),
            numbers[3].ravel(),
            numbers[:, 0].ravel(),
            numbers[:, 3].ravel(),
            numbers[:, :, 0].ravel(),
            numbers[:, :, 3].ravel(),
        ]
    )
    inner = np.zeros((192, 192))
    for face in range(6):
        for c in range(3):
            for other in range(3):
                value = parity(c, face, other)
                if value != 0:
                    for node in faces[face]:
                        inner[c * 64 + node, other * 64 + node] += value
    return inner - curl


def step_tables():
    order = np.concatenate([np.arange(64) + 64 * c for c in (1, 0, 2)])
    own = own_rate()[order][:, order]
    high = own.astype(ml_dtypes.bfloat16)
    low = (own - high.astype(np.float64)).astype(ml_dtypes.bfloat16)
    table = np.concatenate([high, high, low], axis=1)
    rows = [
        np.concatenate([BASE[c] + 16 * i + np.arange(16) for c in (1, 2)]) for i in (0, 3)
    ]
    edges = [part[:, r] for r in rows for part in (high, high, low)]
    return table, table[np.concatenate(rows)], np.concatenate(edges, axis=1)


def halves(x):
    high = x.astype(BF16)
    return high, (x - high.astype(F32)).astype(BF16)


def dot(a, b):
    return jnp.dot(a, b, preferred_element_type=F32)


def dot_t(a, b):
    return lax.dot_general(a, b, (((1,), (1,)), ((), ())), preferred_element_type=F32)


def thrice(x):
    return jnp.concatenate([x, x, x], axis=0)


def folded(x):
    return x[0:NODES] + x[NODES : 2 * NODES] + x[2 * NODES : ROWS]


def stored(x):
    return jnp.concatenate([x[NODES : 2 * NODES], x[0:NODES], x[2 * NODES : ROWS]], axis=0)


def one_hot(rows, targets):
    return (rows == targets).astype(F32).astype(BF16)


def picked(x, index):
    rows = x.shape[0]
    if rows < 8:
        index = index[0:rows]
    elif rows > 8:
        index = jnp.concatenate([index] * (rows // 8), axis=0)
    along = lax.GatherDimensionNumbers(
        offset_dims=(),
        collapsed_slice_dims=(1,),
        start_index_map=(1,),
        operand_batching_dims=(0,),
        start_indices_batching_dims=(0,),
    )
    mode = lax.GatherScatterMode.PROMISE_IN_BOUNDS
    return lax.gather(x, index[..., None], along, (1, 1), mode=mode)


def at_end(face):
    return 3 if face % 2 else 0


def x_traces(field, layer, face):
    at = 16 * at_end(face)
    return [field[layer, BASE[c] + at : BASE[c] + at + 16, :] for c in (1, 2)]


def lift_x(target, layer, face, scale, y, z):
    at = 16 * at_end(face)
    rows = slice(BASE[1] + at, BASE[1] + at + 16)
    target[layer, rows, :] += (-scale * parity(1, face, 2)) * z
    rows = slice(BASE[2] + at, BASE[2] + at + 16)
    target[layer, rows, :] += (-scale * parity(2, face, 1)) * y


def lift_inside(target, field, layer, index, scale):
    first = lax.broadcasted_iota(jnp.int32, (8, LAYER), 0) < 4
    for face in (2, 3):
        factor = jnp.where(first, -scale * parity(0, face, 2), -scale * parity(2, face, 0))
        for k in range(4):
            at = BASE[0] + 4 * at_end(face ^ 1) + k
            got = picked(field[layer, pl.ds(at, 8, stride=16), :], index(layer, face))
            at = BASE[0] + 4 * at_end(face) + k
            turned = pltpu.roll(got, 4, 0)
            target[layer, pl.ds(at, 8, stride=16), :] += factor * turned
    for face in (4, 5):
        here, there = at_end(face), at_end(face ^ 1)
        x, y = (
            picked(field[layer, pl.ds(BASE[c] + there, 16, stride=4), :], index(layer, face))
            for c in (0, 1)
        )
        target[layer, pl.ds(BASE[0] + here, 16, stride=4), :] += (-scale * parity(0, face, 1)) * y
        target[layer, pl.ds(BASE[1] + here, 16, stride=4), :] += (-scale * parity(1, face, 0)) * x


def lift_end(target, field, layer, i, index, scale, to_x):
    for face in (2, 3):
        source, sink = (2, 0) if to_x else (0, 2)
        at = BASE[source] + 16 * i + 4 * at_end(face ^ 1)
        got = picked(field[layer, at : at + 4, :], index(layer, face))
        at = BASE[sink] + 16 * i + 4 * at_end(face)
        target[layer, at : at + 4, :] += (-scale * parity(sink, face, source)) * got
    for face in (4, 5):
        source, sink = (1, 0) if to_x else (0, 1)
        at = BASE[source] + 16 * i + at_end(face ^ 1)
        got = picked(field[layer, pl.ds(at, 4, stride=4), :], index(layer, face))
        at = BASE[sink] + 16 * i + at_end(face)
        target[layer, pl.ds(at, 4, stride=4), :] += (-scale * parity(sink, face, source)) * got


def own_parts(table, x, values):
    for i, value in enumerate(values):
        here = slice(i * LAYER, (i + 1) * LAYER)
        high, low = halves(value)
        x[0:ROWS, here] = high
        x[ROWS : 2 * ROWS, here] = low
        x[2 * ROWS : 3 * ROWS, here] = high
    return layers_of(dot(table[...], x[...]))


def rough_parts(table, values):
    both = jnp.concatenate([value.astype(BF16) for value in values], axis=1)
    return layers_of(dot(table[:, 0:ROWS], both))


def edge_parts(edges, x, values):
    nothing = jnp.zeros((96, LAYER), BF16)
    for at, (side, value) in enumerate(values):
        here = slice(at * LAYER, (at + 1) * LAYER)
        high, low = halves(value)
        both = jnp.concatenate([high, low, high], axis=0)
        x[96 * side : 96 * side + 96, here] = both
        x[96 - 96 * side : 192 - 96 * side, here] = nothing
    return layers_of(dot(edges[...], x[...]))


def layers_of(x):
    return [x[:, at : at + LAYER] for at in range(0, x.shape[1], LAYER)]


def lift_between(target, field, index, scale):
    for layer, face in ((L0, 1), (L1, 0)):
        got = [picked(t, index(layer, face)) for t in x_traces(field, L0 + L1 - layer, face ^ 1)]
        lift_x(target, layer, face, scale, *got)


def lone_h(table, x, index, fe, fh, electric, before=lambda: None):
    parts = own_parts(table, x, electric)
    before()
    lift_between(fh, fe, index, TIME_STEP)
    magnetic = []
    for i, layer in enumerate((L0, L1)):
        lift_inside(fh, fe, layer, index, TIME_STEP)
        magnetic.append(fh[layer] + TIME_STEP * parts[i])
        fh[layer] = magnetic[i]
    return magnetic


def lone_e(table, x, index, fe, fh, acc, electric, magnetic, drive_of, v):
    parts = own_parts(table, x, magnetic)
    drive = drive_of()
    for i, layer in enumerate((L0, L1)):
        acc[layer] = drive[i]
    lift_between(acc, fh, index, 1.0)
    found = []
    for i, layer in enumerate((L0, L1)):
        lift_inside(acc, fh, layer, index, 1.0)
        found.append(electric[i] - TIME_STEP * thrice(v[i]) * (parts[i] + acc[layer]))
        fe[layer] = found[i]
    return found


def lonely(table, ends, x, index, fe, fh, acc, electric, drive_of, v, before_h=lambda: None):
    def ends_of(field):
        return x_traces(field, L1, 1), x_traces(field, L0, 0)

    found = [ends_of(fe)]
    magnetic = lone_h(table, x, index, fe, fh, electric, before_h)
    found.append(ends_of(fh))
    electric = lone_e(table, x, index, fe, fh, acc, electric, magnetic, drive_of, v)
    found.append(ends_of(fe))
    parts = own_parts(ends, x, electric)
    for i, layer in enumerate((L0, L1)):
        face = i
        lift_end(fh, fe, layer, at_end(face), index, TIME_STEP, False)
        for place, c in enumerate((1, 2)):
            at = BASE[c] + 16 * at_end(face)
            part = parts[i][32 * i + 16 * place : 32 * i + 16 * place + 16]
            fh[layer, at : at + 16, :] += TIME_STEP * part
    found.append(ends_of(fh))
    traces = [jnp.concatenate(sum(pairs, []), axis=0) for pairs in zip(*found)]
    return electric, magnetic, *traces


def respond(tables, x, index, valid, fe, fh, acc, lone, v, w, v_near, sent_a, sent_b):
    table, ends, edges = tables
    start_e, lone_h1, lone_e1 = lone
    own, wide = (L0, L1), (A1, L0, L1, B1)
    sides = ((A1, 1, L0, sent_a), (B1, 0, L1, sent_b))
    blank = jnp.zeros((ROWS, LAYER), F32)

    def inward(target, field, scale, start, answered=True):
        for side, (near, face, layer, sent) in enumerate(sides):
            traces = [sent[start + 16 * t : start + 16 * t + 16, :] for t in range(2)]
            if answered:
                traces = [a + b for a, b in zip(traces, x_traces(field, near, face))]
            mask = jnp.concatenate([valid[side]] * 2, axis=0)
            got = [picked(t, index(layer, face ^ 1)) * mask for t in traces]
            lift_x(target, layer, face ^ 1, scale, *got)

    def outward(target, field, alone, scale, answered=True):
        for near, face, layer, _ in sides:
            traces = x_traces(alone, layer - L0, face ^ 1)
            if answered:
                traces = [a + b for a, b in zip(traces, x_traces(field, layer, face ^ 1))]
            got = [picked(t, index(near, face)) for t in traces]
            lift_x(target, near, face, scale, *got)

    for layer in wide:
        fh[layer] = blank
        acc[layer] = blank
    inward(fh, fe, TIME_STEP, E_START, False)
    outward(fh, fe, start_e, TIME_STEP, False)

    edge = []
    for layer in wide:
        side = 1 if layer in (A1, L1) else 0
        edge.append((side, jnp.concatenate(x_traces(fh, layer, side), axis=0)))
    parts = edge_parts(edges, x, edge)
    inward(acc, fh, 1.0, H_FIRST)
    outward(acc, fh, lone_h1, 1.0)
    scales = [v_near[0], v[0], v[1], v_near[1]]
    first_e = []
    for i, layer in enumerate(wide):
        lift_end(acc, fh, layer, 3 if layer in (A1, L1) else 0, index, 1.0, True)
        first_e.append(-TIME_STEP * thrice(scales[i]) * (parts[i] + acc[layer]))
        fe[layer] = first_e[i]

    parts = rough_parts(table, first_e[1:3])
    near_found = rough_parts(ends, [first_e[0], first_e[3]])
    inward(fh, fe, TIME_STEP, E_FIRST)
    outward(fh, fe, lone_e1, TIME_STEP)
    lift_between(fh, fe, index, TIME_STEP)
    magnetic = []
    for i, layer in enumerate(own):
        lift_inside(fh, fe, layer, index, TIME_STEP)
        magnetic.append(fh[layer] + TIME_STEP * parts[i])
        fh[layer] = magnetic[i]
    for side, (near, face, _, _) in enumerate(sides):
        lift_end(fh, fe, near, at_end(face), index, TIME_STEP, False)
        for place, c in enumerate((1, 2)):
            at = BASE[c] + 16 * at_end(face)
            start = 32 * face + 16 * place
            fh[near, at : at + 16, :] += TIME_STEP * near_found[side][start : start + 16]

    parts = rough_parts(table, magnetic)
    current = [TIME_STEP * thrice(w[i]) * first_e[1 + i] for i in range(2)]
    for i, layer in enumerate(own):
        acc[layer] = current[i]
    inward(acc, fh, 1.0, H_SECOND)
    lift_between(acc, fh, index, 1.0)
    second_e = []
    for i, layer in enumerate(own):
        lift_inside(acc, fh, layer, index, 1.0)
        change = TIME_STEP * thrice(v[i]) * (parts[i] + acc[layer])
        second_e.append(first_e[1 + i] - change)
    return first_e[1:3], magnetic, second_e, current


def odd_rank():
    return lax.rem(lax.axis_index("space"), 2) == 1


def send(across, inside, at, up, down):
    odd = odd_rank()
    rows = slice(at, at + up.shape[0])
    across[rows, :] = jnp.where(odd, up, down)
    inside[rows, :] = jnp.where(odd, down, up)


def sides_of(across, inside, a, b, rows):
    odd = odd_rank()
    from_across, from_inside = across[0:rows, :], inside[0:rows, :]
    a[...] = jnp.where(odd, from_inside, from_across)
    b[...] = jnp.where(odd, from_across, from_inside)


def first_kernel(
    table_in, ends_in, edges_in, e_in, h_in, j_in, v_in, w_in, near_in, ports_in, profile_in,
    design_in, *rest
):
    table, ends, edges, design, start_e, lone_h1, lone_e1, first_j, v, w = rest[:10]
    source, places, valid, across, inside = rest[10:15]
    fe, fh, acc, x, neighbor, ports, profile, e, h, j, v_all, w_all, sems = rest[15:]
    started = []

    def fetch(origin, target):
        started.append(pltpu.make_async_copy(origin, target, sems.at[len(started)]))
        started[-1].start()
        return started[-1]

    scatter = [fetch(near_in, neighbor), fetch(ports_in, ports), fetch(profile_in, profile)]
    fields = [fetch(e_in, e), fetch(table_in, table), fetch(h_in, h)]
    rest = [fetch(j_in, j), fetch(w_in, w_all), fetch(v_in, v_all), fetch(ends_in, ends)]
    later = [fetch(edges_in, edges), fetch(design_in, design)]

    for copy in scatter:
        copy.wait()
    found = neighbor[...]
    place = jnp.where(found < 0, 0, jnp.bitwise_and(found, LAYER - 1))
    for i in range(2):
        columns = slice(i * LAYER, (i + 1) * LAYER)
        for face in range(6):
            places[6 * i + face] = jnp.broadcast_to(place[face : face + 1, columns], (8, LAYER))
        there = (found[i : i + 1, columns] >= 0).astype(F32)
        valid[i] = jnp.broadcast_to(there, (8, LAYER))
    targets = lax.broadcasted_iota(jnp.int32, (2 * LAYER, ports.shape[1]), 0)
    spread_hot = one_hot(targets, jnp.bitwise_and(ports[...], 2 * LAYER - 1))
    high, low = halves(profile[...])
    spread = layers_of(dot_t(high, spread_hot) + dot_t(low, spread_hot))
    for copy in fields + rest:
        copy.wait()
    electric = [stored(part) for part in layers_of(e[...])]
    magnetic = [stored(part) for part in layers_of(h[...])]
    current = [stored(part) for part in layers_of(j[...])]
    weight = layers_of(w_all[...])
    scale = layers_of(v_all[...])
    drive = []
    for i in range(2):
        source[i] = stored(spread[i])
        w[i] = weight[i]
        v[i] = scale[i]
        start_e[i] = electric[i]
        fe[L0 + i] = electric[i]
        fh[L0 + i] = magnetic[i]
        now = KEEP * current[i] + TIME_STEP * thrice(weight[i]) * electric[i]
        first_j[i] = now
        drive.append(now + source[i])

    def index(layer, face):
        return places[6 * (layer - L0) + face]

    electric, magnetic, up, down = lonely(
        table, ends, x, index, fe, fh, acc, electric, lambda: drive, v
    )
    for i in range(2):
        lone_e1[i] = electric[i]
        lone_h1[i] = magnetic[i]
    for copy in later:
        copy.wait()
    send(across, inside, 0, up, down)
    send(across, inside, V_NEAR, v[1], v[0])
    blank = jnp.zeros((2, LAYER), F32)
    place = place.astype(F32)
    send(
        across,
        inside,
        N_NEAR,
        jnp.concatenate([place[:, LAYER : 2 * LAYER], blank], axis=0),
        jnp.concatenate([place[:, 0:LAYER], blank], axis=0),
    )


def own_index(places):
    def index(layer, face):
        return places[6 * (layer - L0) + face]

    return index


def second_lone_step(table, lone_h1, lone_e1, first_j, v, w, source, places, work):
    fe, fh, acc, x = work
    index = own_index(places)
    electric = [lone_e1[i] for i in range(2)]
    for i in range(2):
        fe[L0 + i] = electric[i]
        fh[L0 + i] = lone_h1[i]
    current = [
        KEEP * first_j[i] + TIME_STEP * thrice(w[i]) * electric[i] for i in range(2)
    ]
    magnetic = lone_h(table, x, index, fe, fh, electric)
    electric = lone_e(
        table, x, index, fe, fh, acc, electric, magnetic,
        lambda: [current[i] + source[i] for i in range(2)], v,
    )
    return magnetic, electric, current


def lone_kernel(table, lone_h1, lone_e1, first_j, v, w, source, places, design, *rest):
    lone_h2, lone_e2, lone_j2, pixels = rest[:4]
    pixel = jnp.bitwise_and(design[...], PIX_DEV - 1)
    pixels[...] = one_hot(lax.broadcasted_iota(jnp.int32, pixels.shape, 0), pixel)
    found = second_lone_step(table, lone_h1, lone_e1, first_j, v, w, source, places, rest[4:])
    for out, values in zip((lone_h2, lone_e2, lone_j2), found):
        for i in range(2):
            out[i] = values[i]


def index_of(places, near_places):
    def index(layer, face):
        if layer in (L0, L1):
            return places[6 * (layer - L0) + face]
        return near_places[6 * (layer == B1) + face]

    return index


def middle_kernel(
    table, ends, edges, start_e, lone_h1, lone_e1, lone_h2, lone_e2, lone_j2, v, w, source,
    places, valid, across_in, inside_in, *rest
):
    end_e, next_h, next_e, next_j, answer_e, answer_j, v_near, near_places = rest[:8]
    across, inside = rest[8:10]
    fe, fh, acc, x, y, sent_a, sent_b = rest[10:]
    sides_of(across_in, inside_in, sent_a, sent_b, FIRST)
    for side, sent in enumerate((sent_a, sent_b)):
        v_near[side] = sent[V_NEAR : V_NEAR + NODES, :]
        place = sent[N_NEAR : N_NEAR + 8, :].astype(jnp.int32)
        for face in range(6):
            near_places[6 * side + face] = jnp.broadcast_to(place[face : face + 1], (8, LAYER))
    index = index_of(places, near_places)
    first_e, magnetic, second_e, current = respond(
        (table, ends, edges), y, index, valid, fe, fh, acc, (start_e, lone_h1, lone_e1),
        v, w, v_near, sent_a, sent_b,
    )
    electric, drive = [], []
    for i in range(2):
        answer_e[i] = first_e[i]
        answer_j[i] = current[i]
        electric.append(lone_e2[i] + second_e[i])
        end_e[i] = electric[i]
        fe[L0 + i] = electric[i]
        fh[L0 + i] = lone_h2[i] + magnetic[i]
        before = lone_j2[i] + current[i]
        now = KEEP * before + TIME_STEP * thrice(w[i]) * electric[i]
        next_j[i] = now
        drive.append(now + source[i])
    electric, magnetic, up, down = lonely(
        table, ends, x, index, fe, fh, acc, electric, lambda: drive, v
    )
    for i in range(2):
        next_e[i] = electric[i]
        next_h[i] = magnetic[i]
    send(across, inside, 0, up, down)


def early_kernel(
    table, lone_e1, answer_e, lone_j1, lone_j2, answer_j, end_e, next_h, next_e, next_j,
    v, w, source, places, levels, *rest
):
    last_h, last_e, out = rest[:3]
    magnetic, electric, current = second_lone_step(
        table, next_h, next_e, next_j, v, w, source, places, rest[3:]
    )
    for i in range(2):
        last_h[i] = magnetic[i]
        last_e[i] = electric[i]
        columns = slice(i * LAYER, (i + 1) * LAYER)
        level = [stored(levels[k, :, columns].astype(F32)) for k in range(5)]
        eps = (lone_e1[i] + answer_e[i]) * (level[1] - level[0])
        eps += end_e[i] * (level[2] - level[1]) + next_e[i] * (level[3] - level[2])
        eps += electric[i] * (level[4] - level[3])
        drude = lone_j1[i] * level[0] + (lone_j2[i] + answer_j[i]) * level[1]
        drude += next_j[i] * level[2] + current[i] * level[3]
        out[0:NODES, columns] = folded(eps)
        out[NODES : 2 * NODES, columns] = folded(drude)


def last_kernel(
    table, ends, edges, start_e, lone_h1, lone_e1, lone_h2, lone_e2, v, w, places, valid,
    v_near, near_places, across_in, inside_in, levels, early, pixels, *rest
):
    out_e, out_h, sums = rest[:3]
    fe, fh, acc, y, sent_a, sent_b = rest[3:]
    sides_of(across_in, inside_in, sent_a, sent_b, SECOND)
    first_e, magnetic, second_e, current = respond(
        (table, ends, edges), y, index_of(places, near_places), valid, fe, fh, acc,
        (start_e, lone_h1, lone_e1), v, w, v_near, sent_a, sent_b,
    )
    parts = []
    for i in range(2):
        out_e[i] = lone_e2[i] + second_e[i]
        out_h[i] = lone_h2[i] + magnetic[i]
        columns = slice(i * LAYER, (i + 1) * LAYER)
        start, middle, end = (stored(levels[k, :, columns].astype(F32)) for k in range(2, 5))
        eps = folded(first_e[i] * (middle - start) + second_e[i] * (end - middle))
        drude = folded(current[i] * middle)
        parts.append(jnp.concatenate([eps, drude], axis=0) + early[:, columns])
    both = jnp.concatenate(parts, axis=1)
    high, low = halves(both)
    sums[...] = dot_t(pixels[...], high) + dot_t(pixels[...], low)


def total_kernel(owners, parts, e, h, out_e, out_h, eps, drude, sums, sems):
    copies = []

    def write(origin, target):
        copies.append(pltpu.make_async_copy(origin, target, sems.at[len(copies)]))
        copies[-1].start()

    for field, target in ((e, out_e), (h, out_h)):
        for i in range(2):
            for c in range(3):
                there = target.at[pl.ds(c * NODES, NODES), pl.ds(i * LAYER, LAYER)]
                write(field.at[i, pl.ds(BASE[c], NODES), :], there)
    share = parts.shape[0] // owners
    total = parts[0:share]
    for owner in range(1, owners):
        total = total + parts[owner * share : (owner + 1) * share]
    total = total * (1.0 / owners)
    sums[0] = total[:, 0:NODES]
    sums[1] = total[:, NODES : 2 * NODES]
    write(sums.at[0], eps)
    write(sums.at[1], drude)
    for copy in copies:
        copy.wait()


def call(kernel, outs, args, scratch=(), flops=0, spaces=None, out_spaces=None):
    moved = sum(4 * int(np.prod(o.shape)) for o in outs) + sum(
        a.dtype.itemsize * int(np.prod(a.shape)) for a in args
    )
    return pl.pallas_call(
        kernel,
        out_shape=outs,
        in_specs=[pl.BlockSpec(memory_space=s) for s in spaces or [pltpu.VMEM] * len(args)],
        out_specs=[pl.BlockSpec(memory_space=s) for s in out_spaces or [pltpu.VMEM] * len(outs)],
        scratch_shapes=list(scratch),
        compiler_params=pltpu.CompilerParams(vmem_limit_bytes=24 * 1024 * 1024),
        cost_estimate=pl.CostEstimate(flops=flops, bytes_accessed=moved, transcendentals=0),
    )(*args)


def f32(*shape):
    return jax.ShapeDtypeStruct(shape, F32)


def bf16(*shape):
    return jax.ShapeDtypeStruct(shape, BF16)


def exchange(across, inside):
    size = lax.axis_size("space")

    def pairs(start):
        found = [(i, i + 1) for i in range(start, size - 1, 2)]
        return found + [(j, i) for i, j in found]

    return lax.ppermute(across, "space", pairs(1)), lax.ppermute(inside, "space", pairs(0))


def local(
    adj_e,
    adj_h,
    adj_j,
    fwd_e,
    inv_eps,
    drude_weight,
    neighbor,
    design_map,
    port_elems,
    port_profile,
):
    count = adj_e.shape[2]
    owners = lax.axis_size("exc")
    table, ends, edges = (jnp.asarray(t) for t in step_tables())
    levels = fwd_e[0]
    field, nodal = f32(2, ROWS, LAYER), f32(2, NODES, LAYER)
    indices = jax.ShapeDtypeStruct((12, 8, LAYER), jnp.int32)
    work = [pltpu.VMEM((4, ROWS, LAYER), F32)] * 3
    work += [pltpu.VMEM((3 * ROWS, 2 * LAYER), BF16)]
    given = [table, ends, edges, adj_e[0], adj_h[0], adj_j[0], inv_eps, drude_weight]
    given += [neighbor, port_elems, port_profile[0], design_map.reshape(1, count)]
    edge_work = [pltpu.VMEM((ROWS, 4 * LAYER), BF16)]
    once = 2 * ROWS * 3 * ROWS * LAYER

    received = [pltpu.VMEM((FIRST, LAYER), F32)] * 2
    table, ends, edges, design, start_e, h1, e1, j1, v, w, source, places, valid, *sent = call(
        first_kernel,
        [bf16(*table.shape), bf16(*ends.shape), bf16(*edges.shape)]
        + [jax.ShapeDtypeStruct((1, count), jnp.int32)]
        + [field] * 4
        + [nodal, nodal, field, indices, f32(2, 8, LAYER)]
        + [f32(FIRST, LAYER)] * 2,
        [pltpu.with_memory_space_constraint(a, pltpu.HBM) for a in given],
        work
        + [pltpu.VMEM(a.shape, a.dtype) for a in [neighbor, port_elems, port_profile[0]]]
        + [pltpu.VMEM((ROWS, count), F32)] * 3
        + [pltpu.VMEM((NODES, count), F32)] * 2
        + [pltpu.SemaphoreType.DMA((12,))],
        6 * once,
        [pltpu.HBM] * len(given),
    )
    across, inside = exchange(*sent)
    h2, e2, j2, pixels = call(
        lone_kernel,
        [field] * 3 + [bf16(PIX_DEV, count)],
        [table, h1, e1, j1, v, w, source, places, design],
        work,
        4 * once,
    )
    end_e, h3, e3, j3, answer_e, answer_j, v_near, near_places, across, inside = call(
        middle_kernel,
        [field] * 6 + [nodal, indices] + [f32(SECOND, LAYER)] * 2,
        [table, ends, edges, start_e, h1, e1, h2, e2, j2, v, w, source]
        + [places, valid, across, inside],
        work + edge_work + received,
        10 * once,
    )
    across, inside = exchange(across, inside)
    h4, e4, early = call(
        early_kernel,
        [field] * 2 + [f32(2 * NODES, count)],
        [table, e1, answer_e, j1, j2, answer_j, end_e, h3, e3, j3, v, w, source, places]
        + [levels],
        work,
        4 * once,
    )
    e4, h4, sums = call(
        last_kernel,
        [field, field, f32(PIX_DEV, 2 * NODES)],
        [table, ends, edges, end_e, h3, e3, h4, e4, v, w, places, valid, v_near, near_places]
        + [across, inside, levels, early, pixels],
        work[:3] + edge_work + [pltpu.VMEM((SECOND, LAYER), F32)] * 2,
        4 * once,
    )
    parts = lax.all_to_all(sums, "exc", split_axis=0, concat_axis=0, tiled=True)
    share = PIX_DEV // owners
    out_e, out_h, eps, drude = call(
        functools.partial(total_kernel, owners),
        [f32(ROWS, count)] * 2 + [f32(share, NODES)] * 2,
        [parts, e4, h4],
        [pltpu.VMEM((2, share, NODES), F32), pltpu.SemaphoreType.DMA((14,))],
        out_spaces=[pltpu.HBM] * 4,
    )
    return out_e[None], out_h[None], eps.T, drude.T


def solution(mesh):
    return jax.shard_map(
        local,
        mesh=mesh,
        in_specs=(
            P("exc", None, "space"),
            P("exc", None, "space"),
            P("exc", None, "space"),
            P("exc", None, None, "space"),
            P(None, "space"),
            P(None, "space"),
            P(None, "space"),
            P("space"),
            P("exc", "space"),
            P("exc", None, "space"),
        ),
        out_specs=(
            P("exc", None, "space"),
            P("exc", None, "space"),
            P(None, ("space", "exc")),
            P(None, ("space", "exc")),
        ),
        check_vma=False,
    )
```

```python
import functools

import jax
import jax.numpy as jnp
import ml_dtypes
import numpy as np
from jax import lax
from jax.experimental import pallas as pl
from jax.experimental.pallas import tpu as pltpu
from jax.sharding import PartitionSpec as P

NODES = 64
ROWS = 3 * NODES
LAYER = 128
PIX_DEV = 128

TIME_STEP = 0.025
DAMPING = 0.5
KEEP = 1.0 - TIME_STEP * DAMPING

TANGENT = 32
E_START = 0
H_FIRST = 32
E_FIRST = 64
H_SECOND = 96
SECOND = 128
V_NEAR = 128
N_NEAR = V_NEAR + NODES
FIRST = N_NEAR + 8

A1, L0, L1, B1 = range(4)

BASE = (NODES, 0, 2 * NODES)

BF16 = jnp.bfloat16
F32 = jnp.float32


def parity(c, face, other):
    d = face // 2
    sign = 1.0 if face % 2 else -1.0
    return 6.0 * sign * (c - d) * (d - other) * (other - c) / 2.0


def own_rate():
    points = np.array([-1.0, -1.0 / np.sqrt(5.0), 1.0 / np.sqrt(5.0), 1.0])
    barycentric = np.array(
        [1.0 / np.prod([points[j] - points[k] for k in range(4) if k != j]) for j in range(4)]
    )
    deriv = np.zeros((4, 4))
    for row in range(4):
        for column in range(4):
            if row != column:
                deriv[row, column] = (
                    barycentric[column] / barycentric[row] / (points[row] - points[column])
                )
        deriv[row, row] = -np.sum(deriv[row])
    identity = np.eye(4)
    along_x = 2.0 * np.kron(np.kron(deriv, identity), identity)
    along_y = 2.0 * np.kron(np.kron(identity, deriv), identity)
    along_z = 2.0 * np.kron(np.kron(identity, identity), deriv)
    curl = np.zeros((192, 192))
    curl[0:64, 64:128] = -along_z
    curl[0:64, 128:192] = along_y
    curl[64:128, 0:64] = along_z
    curl[64:128, 128:192] = -along_x
    curl[128:192, 0:64] = -along_y
    curl[128:192, 64:128] = along_x
    numbers = np.arange(64).reshape(4, 4, 4)
    faces = np.stack(
        [
            numbers[0].ravel(),
            numbers[3].ravel(),
            numbers[:, 0].ravel(),
            numbers[:, 3].ravel(),
            numbers[:, :, 0].ravel(),
            numbers[:, :, 3].ravel(),
        ]
    )
    inner = np.zeros((192, 192))
    for face in range(6):
        for c in range(3):
            for other in range(3):
                value = parity(c, face, other)
                if value != 0:
                    for node in faces[face]:
                        inner[c * 64 + node, other * 64 + node] += value
    return inner - curl


def step_tables():
    order = np.concatenate([np.arange(64) + 64 * c for c in (1, 0, 2)])
    own = own_rate()[order][:, order]
    high = own.astype(ml_dtypes.bfloat16)
    low = (own - high.astype(np.float64)).astype(ml_dtypes.bfloat16)
    table = np.concatenate([high, high, low], axis=1)
    rows = [
        np.concatenate([BASE[c] + 16 * i + np.arange(16) for c in (1, 2)]) for i in (0, 3)
    ]
    edges = [part[:, r] for r in rows for part in (high, high, low)]
    return table, table[np.concatenate(rows)], np.concatenate(edges, axis=1)


def halves(x):
    high = x.astype(BF16)
    return high, (x - high.astype(F32)).astype(BF16)


def dot(a, b):
    return jnp.dot(a, b, preferred_element_type=F32)


def dot_t(a, b):
    return lax.dot_general(a, b, (((1,), (1,)), ((), ())), preferred_element_type=F32)


def thrice(x):
    return jnp.concatenate([x, x, x], axis=0)


def folded(x):
    return x[0:NODES] + x[NODES : 2 * NODES] + x[2 * NODES : ROWS]


def stored(x):
    return jnp.concatenate([x[NODES : 2 * NODES], x[0:NODES], x[2 * NODES : ROWS]], axis=0)


def one_hot(rows, targets):
    return (rows == targets).astype(F32).astype(BF16)


def picked(x, index):
    rows = x.shape[0]
    if rows < 8:
        index = index[0:rows]
    elif rows > 8:
        index = jnp.concatenate([index] * (rows // 8), axis=0)
    along = lax.GatherDimensionNumbers(
        offset_dims=(),
        collapsed_slice_dims=(1,),
        start_index_map=(1,),
        operand_batching_dims=(0,),
        start_indices_batching_dims=(0,),
    )
    mode = lax.GatherScatterMode.PROMISE_IN_BOUNDS
    return lax.gather(x, index[..., None], along, (1, 1), mode=mode)


def at_end(face):
    return 3 if face % 2 else 0


def x_traces(field, layer, face):
    at = 16 * at_end(face)
    return [field[layer, BASE[c] + at : BASE[c] + at + 16, :] for c in (1, 2)]


def lift_x(target, layer, face, scale, y, z):
    at = 16 * at_end(face)
    rows = slice(BASE[1] + at, BASE[1] + at + 16)
    target[layer, rows, :] += (-scale * parity(1, face, 2)) * z
    rows = slice(BASE[2] + at, BASE[2] + at + 16)
    target[layer, rows, :] += (-scale * parity(2, face, 1)) * y


def lift_inside(target, field, layer, index, scale):
    first = lax.broadcasted_iota(jnp.int32, (8, LAYER), 0) < 4
    for face in (2, 3):
        factor = jnp.where(first, -scale * parity(0, face, 2), -scale * parity(2, face, 0))
        for k in range(4):
            at = BASE[0] + 4 * at_end(face ^ 1) + k
            got = picked(field[layer, pl.ds(at, 8, stride=16), :], index(layer, face))
            at = BASE[0] + 4 * at_end(face) + k
            turned = pltpu.roll(got, 4, 0)
            target[layer, pl.ds(at, 8, stride=16), :] += factor * turned
    for face in (4, 5):
        here, there = at_end(face), at_end(face ^ 1)
        x, y = (
            picked(field[layer, pl.ds(BASE[c] + there, 16, stride=4), :], index(layer, face))
            for c in (0, 1)
        )
        target[layer, pl.ds(BASE[0] + here, 16, stride=4), :] += (-scale * parity(0, face, 1)) * y
        target[layer, pl.ds(BASE[1] + here, 16, stride=4), :] += (-scale * parity(1, face, 0)) * x


def lift_end(target, field, layer, i, index, scale, to_x):
    for face in (2, 3):
        source, sink = (2, 0) if to_x else (0, 2)
        at = BASE[source] + 16 * i + 4 * at_end(face ^ 1)
        got = picked(field[layer, at : at + 4, :], index(layer, face))
        at = BASE[sink] + 16 * i + 4 * at_end(face)
        target[layer, at : at + 4, :] += (-scale * parity(sink, face, source)) * got
    for face in (4, 5):
        source, sink = (1, 0) if to_x else (0, 1)
        at = BASE[source] + 16 * i + at_end(face ^ 1)
        got = picked(field[layer, pl.ds(at, 4, stride=4), :], index(layer, face))
        at = BASE[sink] + 16 * i + at_end(face)
        target[layer, pl.ds(at, 4, stride=4), :] += (-scale * parity(sink, face, source)) * got


def own_parts(table, x, values):
    for i, value in enumerate(values):
        here = slice(i * LAYER, (i + 1) * LAYER)
        high, low = halves(value)
        x[0:ROWS, here] = high
        x[ROWS : 2 * ROWS, here] = low
        x[2 * ROWS : 3 * ROWS, here] = high
    return layers_of(dot(table[...], x[...]))


def rough_parts(table, values):
    both = jnp.concatenate([value.astype(BF16) for value in values], axis=1)
    return layers_of(dot(table[:, 0:ROWS], both))


def edge_parts(edges, x, values):
    nothing = jnp.zeros((96, LAYER), BF16)
    for at, (side, value) in enumerate(values):
        here = slice(at * LAYER, (at + 1) * LAYER)
        high, low = halves(value)
        both = jnp.concatenate([high, low, high], axis=0)
        x[96 * side : 96 * side + 96, here] = both
        x[96 - 96 * side : 192 - 96 * side, here] = nothing
    return layers_of(dot(edges[...], x[...]))


def layers_of(x):
    return [x[:, at : at + LAYER] for at in range(0, x.shape[1], LAYER)]


def lift_between(target, field, index, scale):
    for layer, face in ((L0, 1), (L1, 0)):
        got = [picked(t, index(layer, face)) for t in x_traces(field, L0 + L1 - layer, face ^ 1)]
        lift_x(target, layer, face, scale, *got)


def lone_h(table, x, index, fe, fh, electric, before=lambda: None):
    parts = own_parts(table, x, electric)
    before()
    lift_between(fh, fe, index, TIME_STEP)
    magnetic = []
    for i, layer in enumerate((L0, L1)):
        lift_inside(fh, fe, layer, index, TIME_STEP)
        magnetic.append(fh[layer] + TIME_STEP * parts[i])
        fh[layer] = magnetic[i]
    return magnetic


def lone_e(table, x, index, fe, fh, acc, electric, magnetic, drive_of, v):
    parts = own_parts(table, x, magnetic)
    drive = drive_of()
    for i, layer in enumerate((L0, L1)):
        acc[layer] = drive[i]
    lift_between(acc, fh, index, 1.0)
    found = []
    for i, layer in enumerate((L0, L1)):
        lift_inside(acc, fh, layer, index, 1.0)
        found.append(electric[i] - TIME_STEP * thrice(v[i]) * (parts[i] + acc[layer]))
        fe[layer] = found[i]
    return found


def lonely(table, ends, x, index, fe, fh, acc, electric, drive_of, v, before_h=lambda: None):
    def ends_of(field):
        return x_traces(field, L1, 1), x_traces(field, L0, 0)

    found = [ends_of(fe)]
    magnetic = lone_h(table, x, index, fe, fh, electric, before_h)
    found.append(ends_of(fh))
    electric = lone_e(table, x, index, fe, fh, acc, electric, magnetic, drive_of, v)
    found.append(ends_of(fe))
    parts = own_parts(ends, x, electric)
    for i, layer in enumerate((L0, L1)):
        face = i
        lift_end(fh, fe, layer, at_end(face), index, TIME_STEP, False)
        for place, c in enumerate((1, 2)):
            at = BASE[c] + 16 * at_end(face)
            part = parts[i][32 * i + 16 * place : 32 * i + 16 * place + 16]
            fh[layer, at : at + 16, :] += TIME_STEP * part
    found.append(ends_of(fh))
    traces = [jnp.concatenate(sum(pairs, []), axis=0) for pairs in zip(*found)]
    return electric, magnetic, *traces


def respond(tables, x, index, valid, fe, fh, acc, lone, v, w, v_near, sent_a, sent_b):
    table, ends, edges = tables
    start_e, lone_h1, lone_e1 = lone
    own, wide = (L0, L1), (A1, L0, L1, B1)
    sides = ((A1, 1, L0, sent_a), (B1, 0, L1, sent_b))
    blank = jnp.zeros((ROWS, LAYER), F32)

    def inward(target, field, scale, start, answered=True):
        for side, (near, face, layer, sent) in enumerate(sides):
            traces = [sent[start + 16 * t : start + 16 * t + 16, :] for t in range(2)]
            if answered:
                traces = [a + b for a, b in zip(traces, x_traces(field, near, face))]
            mask = jnp.concatenate([valid[side]] * 2, axis=0)
            got = [picked(t, index(layer, face ^ 1)) * mask for t in traces]
            lift_x(target, layer, face ^ 1, scale, *got)

    def outward(target, field, alone, scale, answered=True):
        for near, face, layer, _ in sides:
            traces = x_traces(alone, layer - L0, face ^ 1)
            if answered:
                traces = [a + b for a, b in zip(traces, x_traces(field, layer, face ^ 1))]
            got = [picked(t, index(near, face)) for t in traces]
            lift_x(target, near, face, scale, *got)

    for layer in wide:
        fh[layer] = blank
        acc[layer] = blank
    inward(fh, fe, TIME_STEP, E_START, False)
    outward(fh, fe, start_e, TIME_STEP, False)

    edge = []
    for layer in wide:
        side = 1 if layer in (A1, L1) else 0
        edge.append((side, jnp.concatenate(x_traces(fh, layer, side), axis=0)))
    parts = edge_parts(edges, x, edge)
    inward(acc, fh, 1.0, H_FIRST)
    outward(acc, fh, lone_h1, 1.0)
    scales = [v_near[0], v[0], v[1], v_near[1]]
    first_e = []
    for i, layer in enumerate(wide):
        lift_end(acc, fh, layer, 3 if layer in (A1, L1) else 0, index, 1.0, True)
        first_e.append(-TIME_STEP * thrice(scales[i]) * (parts[i] + acc[layer]))
        fe[layer] = first_e[i]

    parts = rough_parts(table, first_e[1:3])
    near_found = rough_parts(ends, [first_e[0], first_e[3]])
    inward(fh, fe, TIME_STEP, E_FIRST)
    outward(fh, fe, lone_e1, TIME_STEP)
    lift_between(fh, fe, index, TIME_STEP)
    magnetic = []
    for i, layer in enumerate(own):
        lift_inside(fh, fe, layer, index, TIME_STEP)
        magnetic.append(fh[layer] + TIME_STEP * parts[i])
        fh[layer] = magnetic[i]
    for side, (near, face, _, _) in enumerate(sides):
        lift_end(fh, fe, near, at_end(face), index, TIME_STEP, False)
        for place, c in enumerate((1, 2)):
            at = BASE[c] + 16 * at_end(face)
            start = 32 * face + 16 * place
            fh[near, at : at + 16, :] += TIME_STEP * near_found[side][start : start + 16]

    parts = rough_parts(table, magnetic)
    current = [TIME_STEP * thrice(w[i]) * first_e[1 + i] for i in range(2)]
    for i, layer in enumerate(own):
        acc[layer] = current[i]
    inward(acc, fh, 1.0, H_SECOND)
    lift_between(acc, fh, index, 1.0)
    second_e = []
    for i, layer in enumerate(own):
        lift_inside(acc, fh, layer, index, 1.0)
        change = TIME_STEP * thrice(v[i]) * (parts[i] + acc[layer])
        second_e.append(first_e[1 + i] - change)
    return first_e[1:3], magnetic, second_e, current


def odd_rank():
    return lax.rem(lax.axis_index("space"), 2) == 1


def send(across, inside, at, up, down):
    odd = odd_rank()
    rows = slice(at, at + up.shape[0])
    across[rows, :] = jnp.where(odd, up, down)
    inside[rows, :] = jnp.where(odd, down, up)


def sides_of(across, inside, a, b, rows):
    odd = odd_rank()
    from_across, from_inside = across[0:rows, :], inside[0:rows, :]
    a[...] = jnp.where(odd, from_inside, from_across)
    b[...] = jnp.where(odd, from_across, from_inside)


def first_kernel(
    table_in, ends_in, edges_in, e_in, h_in, j_in, v_in, w_in, near_in, ports_in, profile_in,
    design_in, *rest
):
    table, ends, edges, design, start_e, lone_h1, lone_e1, first_j, v, w = rest[:10]
    source, places, valid, across, inside = rest[10:15]
    fe, fh, acc, x, neighbor, ports, profile, e, h, j, v_all, w_all, sems = rest[15:]
    started = []

    def fetch(origin, target):
        started.append(pltpu.make_async_copy(origin, target, sems.at[len(started)]))
        started[-1].start()
        return started[-1]

    scatter = [fetch(near_in, neighbor), fetch(ports_in, ports), fetch(profile_in, profile)]
    fields = [fetch(e_in, e), fetch(table_in, table), fetch(h_in, h)]
    rest = [fetch(j_in, j), fetch(w_in, w_all), fetch(v_in, v_all), fetch(ends_in, ends)]
    later = [fetch(edges_in, edges), fetch(design_in, design)]

    for copy in scatter + fields + rest:
        copy.wait()
    found = neighbor[...]
    place = jnp.where(found < 0, 0, jnp.bitwise_and(found, LAYER - 1))
    for i in range(2):
        columns = slice(i * LAYER, (i + 1) * LAYER)
        for face in range(6):
            places[6 * i + face] = jnp.broadcast_to(place[face : face + 1, columns], (8, LAYER))
        there = (found[i : i + 1, columns] >= 0).astype(F32)
        valid[i] = jnp.broadcast_to(there, (8, LAYER))
    electric = [stored(part) for part in layers_of(e[...])]
    magnetic = [stored(part) for part in layers_of(h[...])]
    current = [stored(part) for part in layers_of(j[...])]
    weight = layers_of(w_all[...])
    scale = layers_of(v_all[...])
    for i in range(2):
        w[i] = weight[i]
        v[i] = scale[i]
        start_e[i] = electric[i]
        fe[L0 + i] = electric[i]
        fh[L0 + i] = magnetic[i]
    drive = []

    def scatter_source():
        targets = lax.broadcasted_iota(jnp.int32, (2 * LAYER, ports.shape[1]), 0)
        spread_hot = one_hot(targets, jnp.bitwise_and(ports[...], 2 * LAYER - 1))
        high, low = halves(profile[...])
        spread = layers_of(dot_t(high, spread_hot) + dot_t(low, spread_hot))
        for i in range(2):
            source[i] = stored(spread[i])
            now = KEEP * current[i] + TIME_STEP * thrice(weight[i]) * start_e[i]
            first_j[i] = now
            drive.append(now + source[i])

    def index(layer, face):
        return places[6 * (layer - L0) + face]

    electric, magnetic, up, down = lonely(
        table, ends, x, index, fe, fh, acc, electric, lambda: drive, v, scatter_source
    )
    for i in range(2):
        lone_e1[i] = electric[i]
        lone_h1[i] = magnetic[i]
    for copy in later:
        copy.wait()
    send(across, inside, 0, up, down)
    send(across, inside, V_NEAR, v[1], v[0])
    blank = jnp.zeros((2, LAYER), F32)
    place = place.astype(F32)
    send(
        across,
        inside,
        N_NEAR,
        jnp.concatenate([place[:, LAYER : 2 * LAYER], blank], axis=0),
        jnp.concatenate([place[:, 0:LAYER], blank], axis=0),
    )


def own_index(places):
    def index(layer, face):
        return places[6 * (layer - L0) + face]

    return index


def second_lone_step(table, lone_h1, lone_e1, first_j, v, w, source, places, work):
    fe, fh, acc, x = work
    index = own_index(places)
    electric = [lone_e1[i] for i in range(2)]
    for i in range(2):
        fe[L0 + i] = electric[i]
        fh[L0 + i] = lone_h1[i]
    current = [
        KEEP * first_j[i] + TIME_STEP * thrice(w[i]) * electric[i] for i in range(2)
    ]
    magnetic = lone_h(table, x, index, fe, fh, electric)
    electric = lone_e(
        table, x, index, fe, fh, acc, electric, magnetic,
        lambda: [current[i] + source[i] for i in range(2)], v,
    )
    return magnetic, electric, current


def lone_kernel(table, lone_h1, lone_e1, first_j, v, w, source, places, design, *rest):
    lone_h2, lone_e2, lone_j2, pixels = rest[:4]
    pixel = jnp.bitwise_and(design[...], PIX_DEV - 1)
    pixels[...] = one_hot(lax.broadcasted_iota(jnp.int32, pixels.shape, 0), pixel)
    found = second_lone_step(table, lone_h1, lone_e1, first_j, v, w, source, places, rest[4:])
    for out, values in zip((lone_h2, lone_e2, lone_j2), found):
        for i in range(2):
            out[i] = values[i]


def index_of(places, near_places):
    def index(layer, face):
        if layer in (L0, L1):
            return places[6 * (layer - L0) + face]
        return near_places[6 * (layer == B1) + face]

    return index


def middle_kernel(
    table, ends, edges, start_e, lone_h1, lone_e1, lone_h2, lone_e2, lone_j2, v, w, source,
    places, valid, across_in, inside_in, *rest
):
    end_e, next_h, next_e, next_j, answer_e, answer_j, v_near, near_places = rest[:8]
    inside, across = rest[8:10]
    fe, fh, acc, x, y, sent_a, sent_b = rest[10:]
    sides_of(across_in, inside_in, sent_a, sent_b, FIRST)
    for side, sent in enumerate((sent_a, sent_b)):
        v_near[side] = sent[V_NEAR : V_NEAR + NODES, :]
        place = sent[N_NEAR : N_NEAR + 8, :].astype(jnp.int32)
        for face in range(6):
            near_places[6 * side + face] = jnp.broadcast_to(place[face : face + 1], (8, LAYER))
    index = index_of(places, near_places)
    first_e, magnetic, second_e, current = respond(
        (table, ends, edges), y, index, valid, fe, fh, acc, (start_e, lone_h1, lone_e1),
        v, w, v_near, sent_a, sent_b,
    )
    electric, drive = [], []
    for i in range(2):
        answer_e[i] = first_e[i]
        answer_j[i] = current[i]
        electric.append(lone_e2[i] + second_e[i])
        end_e[i] = electric[i]
        fe[L0 + i] = electric[i]
        fh[L0 + i] = lone_h2[i] + magnetic[i]
        before = lone_j2[i] + current[i]
        now = KEEP * before + TIME_STEP * thrice(w[i]) * electric[i]
        next_j[i] = now
        drive.append(now + source[i])
    electric, magnetic, up, down = lonely(
        table, ends, x, index, fe, fh, acc, electric, lambda: drive, v
    )
    for i in range(2):
        next_e[i] = electric[i]
        next_h[i] = magnetic[i]
    send(across, inside, 0, up, down)


def early_kernel(
    table, lone_e1, answer_e, lone_j1, lone_j2, answer_j, end_e, next_h, next_e, next_j,
    v, w, source, places, levels, *rest
):
    last_h, last_e, out = rest[:3]
    magnetic, electric, current = second_lone_step(
        table, next_h, next_e, next_j, v, w, source, places, rest[3:]
    )
    for i in range(2):
        last_h[i] = magnetic[i]
        last_e[i] = electric[i]
        columns = slice(i * LAYER, (i + 1) * LAYER)
        level = [stored(levels[k, :, columns].astype(F32)) for k in range(5)]
        eps = (lone_e1[i] + answer_e[i]) * (level[1] - level[0])
        eps += end_e[i] * (level[2] - level[1]) + next_e[i] * (level[3] - level[2])
        eps += electric[i] * (level[4] - level[3])
        drude = lone_j1[i] * level[0] + (lone_j2[i] + answer_j[i]) * level[1]
        drude += next_j[i] * level[2] + current[i] * level[3]
        out[0:NODES, columns] = folded(eps)
        out[NODES : 2 * NODES, columns] = folded(drude)


def last_kernel(
    table, ends, edges, start_e, lone_h1, lone_e1, lone_h2, lone_e2, v, w, places, valid,
    v_near, near_places, inside_in, across_in, levels, early, pixels, *rest
):
    out_e, out_h, sums = rest[:3]
    fe, fh, acc, y, sent_a, sent_b = rest[3:]
    sides_of(across_in, inside_in, sent_a, sent_b, SECOND)
    first_e, magnetic, second_e, current = respond(
        (table, ends, edges), y, index_of(places, near_places), valid, fe, fh, acc,
        (start_e, lone_h1, lone_e1), v, w, v_near, sent_a, sent_b,
    )
    parts = []
    for i in range(2):
        out_e[i] = lone_e2[i] + second_e[i]
        out_h[i] = lone_h2[i] + magnetic[i]
        columns = slice(i * LAYER, (i + 1) * LAYER)
        start, middle, end = (stored(levels[k, :, columns].astype(F32)) for k in range(2, 5))
        eps = folded(first_e[i] * (middle - start) + second_e[i] * (end - middle))
        drude = folded(current[i] * middle)
        parts.append(jnp.concatenate([eps, drude], axis=0) + early[:, columns])
    both = jnp.concatenate(parts, axis=1)
    high, low = halves(both)
    sums[...] = dot_t(pixels[...], high) + dot_t(pixels[...], low)


def total_kernel(owners, parts, e, h, out_e, out_h, eps, drude, sums, sems):
    copies = []

    def write(origin, target):
        copies.append(pltpu.make_async_copy(origin, target, sems.at[len(copies)]))
        copies[-1].start()

    for field, target in ((e, out_e), (h, out_h)):
        for i in range(2):
            for c in range(3):
                there = target.at[pl.ds(c * NODES, NODES), pl.ds(i * LAYER, LAYER)]
                write(field.at[i, pl.ds(BASE[c], NODES), :], there)
    share = parts.shape[0] // owners
    total = parts[0:share]
    for owner in range(1, owners):
        total = total + parts[owner * share : (owner + 1) * share]
    total = total * (1.0 / owners)
    sums[0] = total[:, 0:NODES]
    sums[1] = total[:, NODES : 2 * NODES]
    write(sums.at[0], eps)
    write(sums.at[1], drude)
    for copy in copies:
        copy.wait()


def call(kernel, outs, args, scratch=(), flops=0, spaces=None, out_spaces=None):
    moved = sum(4 * int(np.prod(o.shape)) for o in outs) + sum(
        a.dtype.itemsize * int(np.prod(a.shape)) for a in args
    )
    return pl.pallas_call(
        kernel,
        out_shape=outs,
        in_specs=[pl.BlockSpec(memory_space=s) for s in spaces or [pltpu.VMEM] * len(args)],
        out_specs=[pl.BlockSpec(memory_space=s) for s in out_spaces or [pltpu.VMEM] * len(outs)],
        scratch_shapes=list(scratch),
        compiler_params=pltpu.CompilerParams(vmem_limit_bytes=24 * 1024 * 1024),
        cost_estimate=pl.CostEstimate(flops=flops, bytes_accessed=moved, transcendentals=0),
    )(*args)


def f32(*shape):
    return jax.ShapeDtypeStruct(shape, F32)


def bf16(*shape):
    return jax.ShapeDtypeStruct(shape, BF16)


def exchange(across, inside, inside_first):
    size = lax.axis_size("space")

    def pairs(start):
        found = [(i, i + 1) for i in range(start, size - 1, 2)]
        return found + [(j, i) for i, j in found]

    if inside_first:
        inside = lax.ppermute(inside, "space", pairs(0))
    across = lax.ppermute(across, "space", pairs(1))
    if not inside_first:
        inside = lax.ppermute(inside, "space", pairs(0))
    return across, inside


def local(
    adj_e,
    adj_h,
    adj_j,
    fwd_e,
    inv_eps,
    drude_weight,
    neighbor,
    design_map,
    port_elems,
    port_profile,
):
    count = adj_e.shape[2]
    owners = lax.axis_size("exc")
    table, ends, edges = (jnp.asarray(t) for t in step_tables())
    levels = fwd_e[0]
    field, nodal = f32(2, ROWS, LAYER), f32(2, NODES, LAYER)
    indices = jax.ShapeDtypeStruct((12, 8, LAYER), jnp.int32)
    work = [pltpu.VMEM((4, ROWS, LAYER), F32)] * 3
    work += [pltpu.VMEM((3 * ROWS, 2 * LAYER), BF16)]
    given = [table, ends, edges, adj_e[0], adj_h[0], adj_j[0], inv_eps, drude_weight]
    given += [neighbor, port_elems, port_profile[0], design_map.reshape(1, count)]
    edge_work = [pltpu.VMEM((ROWS, 4 * LAYER), BF16)]
    once = 2 * ROWS * 3 * ROWS * LAYER

    received = [pltpu.VMEM((FIRST, LAYER), F32)] * 2
    table, ends, edges, design, start_e, h1, e1, j1, v, w, source, places, valid, *sent = call(
        first_kernel,
        [bf16(*table.shape), bf16(*ends.shape), bf16(*edges.shape)]
        + [jax.ShapeDtypeStruct((1, count), jnp.int32)]
        + [field] * 4
        + [nodal, nodal, field, indices, f32(2, 8, LAYER)]
        + [f32(FIRST, LAYER)] * 2,
        [pltpu.with_memory_space_constraint(a, pltpu.HBM) for a in given],
        work
        + [pltpu.VMEM(a.shape, a.dtype) for a in [neighbor, port_elems, port_profile[0]]]
        + [pltpu.VMEM((ROWS, count), F32)] * 3
        + [pltpu.VMEM((NODES, count), F32)] * 2
        + [pltpu.SemaphoreType.DMA((12,))],
        6 * once,
        [pltpu.HBM] * len(given),
    )
    across, inside = exchange(*sent, False)
    h2, e2, j2, pixels = call(
        lone_kernel,
        [field] * 3 + [bf16(PIX_DEV, count)],
        [table, h1, e1, j1, v, w, source, places, design],
        work,
        4 * once,
    )
    end_e, h3, e3, j3, answer_e, answer_j, v_near, near_places, inside, across = call(
        middle_kernel,
        [field] * 6 + [nodal, indices] + [f32(SECOND, LAYER)] * 2,
        [table, ends, edges, start_e, h1, e1, h2, e2, j2, v, w, source]
        + [places, valid, across, inside],
        work + edge_work + received,
        10 * once,
    )
    across, inside = exchange(across, inside, True)
    h4, e4, early = call(
        early_kernel,
        [field] * 2 + [f32(2 * NODES, count)],
        [table, e1, answer_e, j1, j2, answer_j, end_e, h3, e3, j3, v, w, source, places]
        + [levels],
        work,
        4 * once,
    )
    e4, h4, sums = call(
        last_kernel,
        [field, field, f32(PIX_DEV, 2 * NODES)],
        [table, ends, edges, end_e, h3, e3, h4, e4, v, w, places, valid, v_near, near_places]
        + [inside, across, levels, early, pixels],
        work[:3] + edge_work + [pltpu.VMEM((SECOND, LAYER), F32)] * 2,
        4 * once,
    )
    parts = lax.all_to_all(sums, "exc", split_axis=0, concat_axis=0, tiled=True)
    share = PIX_DEV // owners
    out_e, out_h, eps, drude = call(
        functools.partial(total_kernel, owners),
        [f32(ROWS, count)] * 2 + [f32(share, NODES)] * 2,
        [parts, e4, h4],
        [pltpu.VMEM((2, share, NODES), F32), pltpu.SemaphoreType.DMA((14,))],
        out_spaces=[pltpu.HBM] * 4,
    )
    return out_e[None], out_h[None], eps.T, drude.T


def solution(mesh):
    return jax.shard_map(
        local,
        mesh=mesh,
        in_specs=(
            P("exc", None, "space"),
            P("exc", None, "space"),
            P("exc", None, "space"),
            P("exc", None, None, "space"),
            P(None, "space"),
            P(None, "space"),
            P(None, "space"),
            P("space"),
            P("exc", "space"),
            P("exc", None, "space"),
        ),
        out_specs=(
            P("exc", None, "space"),
            P("exc", None, "space"),
            P(None, ("space", "exc")),
            P(None, ("space", "exc")),
        ),
        check_vma=False,
    )
```

```python
import functools

import jax
import jax.numpy as jnp
import numpy as np
from jax import lax
from jax.experimental import pallas as pl
from jax.experimental.pallas import tpu as pltpu
from jax.sharding import PartitionSpec as P

NODES = 64
ROWS = 3 * NODES
LAYER = 128
PIX_DEV = 128

TIME_STEP = 0.025
DAMPING = 0.5
KEEP = 1.0 - TIME_STEP * DAMPING

TANGENT = 32
E_START = 0
H_FIRST = 32
E_FIRST = 64
H_SECOND = 96
SECOND = 128
V_NEAR = 128
N_NEAR = V_NEAR + NODES
FIRST = N_NEAR + 8

A1, L0, L1, B1 = range(4)

BASE = (NODES, 0, 2 * NODES)

BF16 = jnp.bfloat16
F32 = jnp.float32


def parity(c, face, other):
    d = face // 2
    sign = 1.0 if face % 2 else -1.0
    return 6.0 * sign * (c - d) * (d - other) * (other - c) / 2.0


def off_diagonal():
    points = np.array([-1.0, -1.0 / np.sqrt(5.0), 1.0 / np.sqrt(5.0), 1.0])
    barycentric = np.array(
        [1.0 / np.prod([points[j] - points[k] for k in range(4) if k != j]) for j in range(4)]
    )
    deriv = np.zeros((4, 4))
    for row in range(4):
        for column in range(4):
            if row != column:
                deriv[row, column] = (
                    barycentric[column] / barycentric[row] / (points[row] - points[column])
                )
    return (2.0 * deriv).tolist()


SLOPES = off_diagonal()


def slope(parts, row, scale):
    terms = [(scale * SLOPES[row][i]) * parts[i] for i in range(4) if i != row]
    return terms[0] + terms[1] + terms[2]


def halves(x):
    high = x.astype(BF16)
    return high, (x - high.astype(F32)).astype(BF16)


def dot_t(a, b):
    return lax.dot_general(a, b, (((1,), (1,)), ((), ())), preferred_element_type=F32)


def thrice(x):
    return jnp.concatenate([x, x, x], axis=0)


def folded(x):
    return x[0:NODES] + x[NODES : 2 * NODES] + x[2 * NODES : ROWS]


def stored(x):
    return jnp.concatenate([x[NODES : 2 * NODES], x[0:NODES], x[2 * NODES : ROWS]], axis=0)


def one_hot(rows, targets):
    return (rows == targets).astype(F32).astype(BF16)


def picked(x, index):
    rows = x.shape[0]
    if rows < 8:
        index = index[0:rows]
    elif rows > 8:
        index = jnp.concatenate([index] * (rows // 8), axis=0)
    along = lax.GatherDimensionNumbers(
        offset_dims=(),
        collapsed_slice_dims=(1,),
        start_index_map=(1,),
        operand_batching_dims=(0,),
        start_indices_batching_dims=(0,),
    )
    mode = lax.GatherScatterMode.PROMISE_IN_BOUNDS
    return lax.gather(x, index[..., None], along, (1, 1), mode=mode)


def at_end(face):
    return 3 if face % 2 else 0


def x_traces(field, layer, face):
    at = 16 * at_end(face)
    return [field[layer, BASE[c] + at : BASE[c] + at + 16, :] for c in (1, 2)]


def lift_x(target, layer, face, scale, y, z):
    at = 16 * at_end(face)
    rows = slice(BASE[1] + at, BASE[1] + at + 16)
    target[layer, rows, :] += (-scale * parity(1, face, 2)) * z
    rows = slice(BASE[2] + at, BASE[2] + at + 16)
    target[layer, rows, :] += (-scale * parity(2, face, 1)) * y


def add_x(target, field, layer, scale, outer, base=None):
    for c, other, sign in ((1, 2, 1.0), (2, 1, -1.0)):
        parts = [field[layer, BASE[other] + 16 * i : BASE[other] + 16 * i + 16, :] for i in range(4)]
        for i in range(4):
            change = slope(parts, i, scale * sign)
            face = {0: 0, 3: 1}.get(i)
            traces = None if face is None else outer(face)
            if traces is not None:
                change += (-scale * parity(c, face, other)) * traces[other - 1]
            rows = slice(BASE[c] + 16 * i, BASE[c] + 16 * i + 16)
            before = target[layer, rows, :] if base is None else base[rows]
            target[layer, rows, :] = before + change
    if base is not None:
        rows = slice(BASE[0], BASE[0] + NODES)
        target[layer, rows, :] = base[rows]


def add_yz(target, field, layer, index, scale):
    for c, other, sign in ((0, 1, 1.0), (1, 0, -1.0)):
        parts = [field[layer, pl.ds(BASE[other] + k, 16, stride=4), :] for k in range(4)]
        for k in range(4):
            change = slope(parts, k, scale * sign)
            if k in (0, 3):
                face = 4 if k == 0 else 5
                got = picked(parts[3 - k], index(layer, face))
                change += (-scale * parity(c, face, other)) * got
            target[layer, pl.ds(BASE[c] + k, 16, stride=4), :] += change
    sign = jnp.where(lax.broadcasted_iota(jnp.int32, (8, LAYER), 0) < 4, -1.0, 1.0)
    for k in range(4):
        parts = [field[layer, pl.ds(BASE[0] + 4 * j + k, 8, stride=16), :] for j in range(4)]
        for j in range(4):
            change = slope(parts, j, scale)
            if j in (0, 3):
                face = 2 if j == 0 else 3
                got = picked(parts[3 - j], index(layer, face))
                change += (scale * parity(0, face, 2)) * got
            rows = pl.ds(BASE[0] + 4 * j + k, 8, stride=16)
            target[layer, rows, :] += sign * pltpu.roll(change, 4, 0)


def add_end(target, field, layer, i, index, scale, to_x):
    c, other, sign = (0, 1, 1.0) if to_x else (1, 0, -1.0)
    at = BASE[other] + 16 * i
    parts = [field[layer, pl.ds(at + k, 4, stride=4), :] for k in range(4)]
    for k in range(4):
        change = slope(parts, k, scale * sign)
        if k in (0, 3):
            face = 4 if k == 0 else 5
            got = picked(parts[3 - k], index(layer, face))
            change += (-scale * parity(c, face, other)) * got
        target[layer, pl.ds(BASE[c] + 16 * i + k, 4, stride=4), :] += change
    c, other, sign = (0, 2, -1.0) if to_x else (2, 0, 1.0)
    at = BASE[other] + 16 * i
    parts = [field[layer, at + 4 * j : at + 4 * j + 4, :] for j in range(4)]
    for j in range(4):
        change = slope(parts, j, scale * sign)
        if j in (0, 3):
            face = 2 if j == 0 else 3
            got = picked(parts[3 - j], index(layer, face))
            change += (-scale * parity(c, face, other)) * got
        at = BASE[c] + 16 * i + 4 * j
        target[layer, at : at + 4, :] += change


def add_into_end(target, field, layer, i, index, scale):
    for c, other, sign in ((1, 2, 1.0), (2, 1, -1.0)):
        parts = [field[layer, BASE[other] + 16 * n : BASE[other] + 16 * n + 16, :] for n in range(4)]
        rows = slice(BASE[c] + 16 * i, BASE[c] + 16 * i + 16)
        target[layer, rows, :] += slope(parts, i, scale * sign)
    add_end(target, field, layer, i, index, scale, False)


def add_from_end(target, field, layer, i, index, scale):
    for c, other, sign in ((1, 2, 1.0), (2, 1, -1.0)):
        part = field[layer, BASE[other] + 16 * i : BASE[other] + 16 * i + 16, :]
        for n in range(4):
            if n != i:
                rows = slice(BASE[c] + 16 * n, BASE[c] + 16 * n + 16)
                target[layer, rows, :] += (scale * sign * SLOPES[n][i]) * part
    add_end(target, field, layer, i, index, scale, True)


def layers_of(x):
    return [x[:, at : at + LAYER] for at in range(0, x.shape[1], LAYER)]


def between(field, index, layer):
    def outer(face):
        if (layer, face) not in ((L0, 1), (L1, 0)):
            return None
        traces = x_traces(field, L0 + L1 - layer, face ^ 1)
        return [picked(t, index(layer, face)) for t in traces]

    return outer


def lone_h(index, fe, fh):
    for layer in (L0, L1):
        add_x(fh, fe, layer, TIME_STEP, between(fe, index, layer))
        add_yz(fh, fe, layer, index, TIME_STEP)


def lone_e(index, fe, fh, acc, drive, v):
    for i, layer in enumerate((L0, L1)):
        add_x(acc, fh, layer, 1.0, between(fh, index, layer), drive[i])
        add_yz(acc, fh, layer, index, 1.0)
        fe[layer] -= TIME_STEP * thrice(v[i]) * acc[layer]


def lonely(index, fe, fh, acc, drive, v, out_h, out_e):
    def ends_of(field):
        return x_traces(field, L1, 1), x_traces(field, L0, 0)

    found = [ends_of(fe)]
    lone_h(index, fe, fh)
    found.append(ends_of(fh))
    for i in range(2):
        out_h[i] = fh[L0 + i]
    lone_e(index, fe, fh, acc, drive, v)
    found.append(ends_of(fe))
    for i in range(2):
        out_e[i] = fe[L0 + i]
    for face, layer in enumerate((L0, L1)):
        add_into_end(fh, fe, layer, at_end(face), index, TIME_STEP)
    found.append(ends_of(fh))
    return [jnp.concatenate(sum(traces, []), axis=0) for traces in zip(*found)]


def respond(index, valid, fe, fh, acc, lone, v, w, v_near, sent_a, sent_b):
    start_e, lone_h1, lone_e1 = lone
    own, wide = (L0, L1), (A1, L0, L1, B1)
    sides = ((A1, 1, L0, sent_a), (B1, 0, L1, sent_b))
    blank = jnp.zeros((ROWS, LAYER), F32)

    def inward(target, field, scale, start, answered=True):
        for side, (near, face, layer, sent) in enumerate(sides):
            traces = [sent[start + 16 * t : start + 16 * t + 16, :] for t in range(2)]
            if answered:
                traces = [a + b for a, b in zip(traces, x_traces(field, near, face))]
            mask = jnp.concatenate([valid[side]] * 2, axis=0)
            got = [picked(t, index(layer, face ^ 1)) * mask for t in traces]
            lift_x(target, layer, face ^ 1, scale, *got)

    def outward(target, field, alone, scale, answered=True):
        for near, face, layer, _ in sides:
            traces = x_traces(alone, layer - L0, face ^ 1)
            if answered:
                traces = [a + b for a, b in zip(traces, x_traces(field, layer, face ^ 1))]
            got = [picked(t, index(near, face)) for t in traces]
            lift_x(target, near, face, scale, *got)

    for layer in wide:
        fh[layer] = blank
        acc[layer] = blank
    inward(fh, fe, TIME_STEP, E_START, False)
    outward(fh, fe, start_e, TIME_STEP, False)

    inward(acc, fh, 1.0, H_FIRST)
    outward(acc, fh, lone_h1, 1.0)
    first_e = []
    for layer, scale in zip(wide, [v_near[0], v[0], v[1], v_near[1]]):
        add_from_end(acc, fh, layer, 3 if layer in (A1, L1) else 0, index, 1.0)
        first_e.append(-TIME_STEP * thrice(scale) * acc[layer])
        fe[layer] = first_e[-1]

    inward(fh, fe, TIME_STEP, E_FIRST)
    outward(fh, fe, lone_e1, TIME_STEP)
    for near, face, _, _ in sides:
        add_into_end(fh, fe, near, at_end(face), index, TIME_STEP)
    lone_h(index, fe, fh)

    current = [TIME_STEP * thrice(w[i]) * first_e[1 + i] for i in range(2)]
    second_e = []
    for i, layer in enumerate(own):
        add_x(acc, fh, layer, 1.0, between(fh, index, layer), current[i])
        add_yz(acc, fh, layer, index, 1.0)
    inward(acc, fh, 1.0, H_SECOND)
    for i, layer in enumerate(own):
        second_e.append(first_e[1 + i] - TIME_STEP * thrice(v[i]) * acc[layer])
    return first_e[1:3], [fh[layer] for layer in own], second_e, current


def odd_rank():
    return lax.rem(lax.axis_index("space"), 2) == 1


def send(across, inside, at, up, down):
    odd = odd_rank()
    rows = slice(at, at + up.shape[0])
    across[rows, :] = jnp.where(odd, up, down)
    inside[rows, :] = jnp.where(odd, down, up)


def sides_of(across, inside, a, b, rows):
    odd = odd_rank()
    from_across, from_inside = across[0:rows, :], inside[0:rows, :]
    a[...] = jnp.where(odd, from_inside, from_across)
    b[...] = jnp.where(odd, from_across, from_inside)


def first_kernel(
    e_in, h_in, j_in, v_in, w_in, near_in, ports_in, profile_in, design_in, *rest
):
    design, start_e, lone_h1, lone_e1, first_j, v, w, source, places, valid = rest[:10]
    across, inside, fe, fh, acc, neighbor, ports, profile, e, h, j, v_all, w_all, sems = rest[10:]
    started = []

    def fetch(origin, target):
        started.append(pltpu.make_async_copy(origin, target, sems.at[len(started)]))
        started[-1].start()

    fetch(near_in, neighbor)
    fetch(ports_in, ports)
    fetch(profile_in, profile)
    for origin, target in ((e_in, e), (h_in, h), (j_in, j), (w_in, w_all), (v_in, v_all)):
        fetch(origin, target)
    fetch(design_in, design)
    for copy in started:
        copy.wait()
    found = neighbor[...]
    place = jnp.where(found < 0, 0, jnp.bitwise_and(found, LAYER - 1))
    for i in range(2):
        columns = slice(i * LAYER, (i + 1) * LAYER)
        for face in range(6):
            places[6 * i + face] = jnp.broadcast_to(place[face : face + 1, columns], (8, LAYER))
        there = (found[i : i + 1, columns] >= 0).astype(F32)
        valid[i] = jnp.broadcast_to(there, (8, LAYER))
    electric = [stored(part) for part in layers_of(e[...])]
    magnetic = [stored(part) for part in layers_of(h[...])]
    current = [stored(part) for part in layers_of(j[...])]
    weight = layers_of(w_all[...])
    scale = layers_of(v_all[...])
    for i in range(2):
        w[i] = weight[i]
        v[i] = scale[i]
        start_e[i] = electric[i]
        fe[L0 + i] = electric[i]
        fh[L0 + i] = magnetic[i]
    targets = lax.broadcasted_iota(jnp.int32, (2 * LAYER, ports.shape[1]), 0)
    spread_hot = one_hot(targets, jnp.bitwise_and(ports[...], 2 * LAYER - 1))
    high, low = halves(profile[...])
    spread = layers_of(dot_t(high, spread_hot) + dot_t(low, spread_hot))
    drive = []
    for i in range(2):
        source[i] = stored(spread[i])
        now = KEEP * current[i] + TIME_STEP * thrice(weight[i]) * electric[i]
        first_j[i] = now
        drive.append(now + source[i])

    up, down = lonely(own_index(places), fe, fh, acc, drive, v, lone_h1, lone_e1)
    send(across, inside, 0, up, down)
    send(across, inside, V_NEAR, v[1], v[0])
    blank = jnp.zeros((2, LAYER), F32)
    place = place.astype(F32)
    send(
        across,
        inside,
        N_NEAR,
        jnp.concatenate([place[:, LAYER : 2 * LAYER], blank], axis=0),
        jnp.concatenate([place[:, 0:LAYER], blank], axis=0),
    )


def own_index(places):
    def index(layer, face):
        return places[6 * (layer - L0) + face]

    return index


def second_lone_step(lone_h1, lone_e1, first_j, v, w, source, places, work):
    fe, fh, acc = work
    index = own_index(places)
    for i in range(2):
        fe[L0 + i] = lone_e1[i]
        fh[L0 + i] = lone_h1[i]
    current = [KEEP * first_j[i] + TIME_STEP * thrice(w[i]) * lone_e1[i] for i in range(2)]
    lone_h(index, fe, fh)
    lone_e(index, fe, fh, acc, [current[i] + source[i] for i in range(2)], v)
    return current


def lone_kernel(lone_h1, lone_e1, first_j, v, w, source, places, design, *rest):
    lone_h2, lone_e2, lone_j2, pixels, fe, fh, acc = rest
    pixel = jnp.bitwise_and(design[...], PIX_DEV - 1)
    pixels[...] = one_hot(lax.broadcasted_iota(jnp.int32, pixels.shape, 0), pixel)
    current = second_lone_step(
        lone_h1, lone_e1, first_j, v, w, source, places, (fe, fh, acc)
    )
    for i in range(2):
        lone_h2[i] = fh[L0 + i]
        lone_e2[i] = fe[L0 + i]
        lone_j2[i] = current[i]


def index_of(places, near_places):
    def index(layer, face):
        if layer in (L0, L1):
            return places[6 * (layer - L0) + face]
        return near_places[6 * (layer == B1) + face]

    return index


def middle_kernel(
    start_e, lone_h1, lone_e1, lone_h2, lone_e2, lone_j2, v, w, source, places,
    valid, across_in, inside_in, *rest
):
    end_e, next_h, next_e, next_j, answer_e, answer_j, v_near, near_places = rest[:8]
    inside, across = rest[8:10]
    fe, fh, acc, sent_a, sent_b = rest[10:]
    sides_of(across_in, inside_in, sent_a, sent_b, FIRST)
    for side, sent in enumerate((sent_a, sent_b)):
        v_near[side] = sent[V_NEAR : V_NEAR + NODES, :]
        place = sent[N_NEAR : N_NEAR + 8, :].astype(jnp.int32)
        for face in range(6):
            near_places[6 * side + face] = jnp.broadcast_to(place[face : face + 1], (8, LAYER))
    index = index_of(places, near_places)
    first_e, magnetic, second_e, current = respond(
        index, valid, fe, fh, acc, (start_e, lone_h1, lone_e1), v, w, v_near, sent_a, sent_b
    )
    drive = []
    for i in range(2):
        answer_e[i] = first_e[i]
        answer_j[i] = current[i]
        electric = lone_e2[i] + second_e[i]
        end_e[i] = electric
        fe[L0 + i] = electric
        fh[L0 + i] = lone_h2[i] + magnetic[i]
        before = lone_j2[i] + current[i]
        now = KEEP * before + TIME_STEP * thrice(w[i]) * electric
        next_j[i] = now
        drive.append(now + source[i])
    up, down = lonely(index, fe, fh, acc, drive, v, next_h, next_e)
    send(across, inside, 0, up, down)


def early_kernel(
    lone_e1, answer_e, lone_j1, lone_j2, answer_j, end_e, next_h, next_e, next_j, v, w,
    source, places, levels, *rest
):
    last_h, last_e, out, fe, fh, acc = rest
    current = second_lone_step(next_h, next_e, next_j, v, w, source, places, (fe, fh, acc))
    for i in range(2):
        electric = fe[L0 + i]
        last_h[i] = fh[L0 + i]
        last_e[i] = electric
        columns = slice(i * LAYER, (i + 1) * LAYER)
        level = [stored(levels[k, :, columns].astype(F32)) for k in range(5)]
        eps = (lone_e1[i] + answer_e[i]) * (level[1] - level[0])
        eps += end_e[i] * (level[2] - level[1]) + next_e[i] * (level[3] - level[2])
        eps += electric * (level[4] - level[3])
        drude = lone_j1[i] * level[0] + (lone_j2[i] + answer_j[i]) * level[1]
        drude += next_j[i] * level[2] + current[i] * level[3]
        out[0:NODES, columns] = folded(eps)
        out[NODES : 2 * NODES, columns] = folded(drude)


def last_kernel(
    start_e, lone_h1, lone_e1, lone_h2, lone_e2, v, w, places, valid, v_near, near_places,
    inside_in, across_in, levels, early, pixels, *rest
):
    out_e, out_h, sums = rest[:3]
    fe, fh, acc, sent_a, sent_b = rest[3:]
    sides_of(across_in, inside_in, sent_a, sent_b, SECOND)
    first_e, magnetic, second_e, current = respond(
        index_of(places, near_places), valid, fe, fh, acc, (start_e, lone_h1, lone_e1),
        v, w, v_near, sent_a, sent_b,
    )
    parts = []
    for i in range(2):
        out_e[i] = lone_e2[i] + second_e[i]
        out_h[i] = lone_h2[i] + magnetic[i]
        columns = slice(i * LAYER, (i + 1) * LAYER)
        start, middle, end = (stored(levels[k, :, columns].astype(F32)) for k in range(2, 5))
        eps = folded(first_e[i] * (middle - start) + second_e[i] * (end - middle))
        drude = folded(current[i] * middle)
        parts.append(jnp.concatenate([eps, drude], axis=0) + early[:, columns])
    both = jnp.concatenate(parts, axis=1)
    high, low = halves(both)
    sums[...] = dot_t(pixels[...], high) + dot_t(pixels[...], low)


def total_kernel(owners, parts, e, h, out_e, out_h, eps, drude, sums, sems):
    copies = []

    def write(origin, target):
        copies.append(pltpu.make_async_copy(origin, target, sems.at[len(copies)]))
        copies[-1].start()

    for field, target in ((e, out_e), (h, out_h)):
        for i in range(2):
            for c in range(3):
                there = target.at[pl.ds(c * NODES, NODES), pl.ds(i * LAYER, LAYER)]
                write(field.at[i, pl.ds(BASE[c], NODES), :], there)
    share = parts.shape[0] // owners
    total = parts[0:share]
    for owner in range(1, owners):
        total = total + parts[owner * share : (owner + 1) * share]
    total = total * (1.0 / owners)
    sums[0] = total[:, 0:NODES]
    sums[1] = total[:, NODES : 2 * NODES]
    write(sums.at[0], eps)
    write(sums.at[1], drude)
    for copy in copies:
        copy.wait()


def call(kernel, outs, args, scratch=(), spaces=None, out_spaces=None):
    moved = sum(4 * int(np.prod(o.shape)) for o in outs) + sum(
        a.dtype.itemsize * int(np.prod(a.shape)) for a in args
    )
    return pl.pallas_call(
        kernel,
        out_shape=outs,
        in_specs=[pl.BlockSpec(memory_space=s) for s in spaces or [pltpu.VMEM] * len(args)],
        out_specs=[pl.BlockSpec(memory_space=s) for s in out_spaces or [pltpu.VMEM] * len(outs)],
        scratch_shapes=list(scratch),
        compiler_params=pltpu.CompilerParams(vmem_limit_bytes=24 * 1024 * 1024),
        cost_estimate=pl.CostEstimate(flops=moved, bytes_accessed=moved, transcendentals=0),
    )(*args)


def f32(*shape):
    return jax.ShapeDtypeStruct(shape, F32)


def bf16(*shape):
    return jax.ShapeDtypeStruct(shape, BF16)


def exchange(across, inside, inside_first):
    size = lax.axis_size("space")

    def pairs(start):
        found = [(i, i + 1) for i in range(start, size - 1, 2)]
        return found + [(j, i) for i, j in found]

    if inside_first:
        inside = lax.ppermute(inside, "space", pairs(0))
    across = lax.ppermute(across, "space", pairs(1))
    if not inside_first:
        inside = lax.ppermute(inside, "space", pairs(0))
    return across, inside


def local(
    adj_e,
    adj_h,
    adj_j,
    fwd_e,
    inv_eps,
    drude_weight,
    neighbor,
    design_map,
    port_elems,
    port_profile,
):
    count = adj_e.shape[2]
    owners = lax.axis_size("exc")
    levels = fwd_e[0]
    field, nodal = f32(2, ROWS, LAYER), f32(2, NODES, LAYER)
    indices = jax.ShapeDtypeStruct((12, 8, LAYER), jnp.int32)
    work = [pltpu.VMEM((4, ROWS, LAYER), F32)] * 3
    given = [adj_e[0], adj_h[0], adj_j[0], inv_eps, drude_weight]
    given += [neighbor, port_elems, port_profile[0], design_map.reshape(1, count)]
    received = [pltpu.VMEM((FIRST, LAYER), F32)] * 2
    design, start_e, h1, e1, j1, v, w, source, places, valid, *sent = call(
        first_kernel,
        [jax.ShapeDtypeStruct((1, count), jnp.int32)]
        + [field] * 4
        + [nodal, nodal, field, indices, f32(2, 8, LAYER)]
        + [f32(FIRST, LAYER)] * 2,
        [pltpu.with_memory_space_constraint(a, pltpu.HBM) for a in given],
        work
        + [pltpu.VMEM(a.shape, a.dtype) for a in [neighbor, port_elems, port_profile[0]]]
        + [pltpu.VMEM((ROWS, count), F32)] * 3
        + [pltpu.VMEM((NODES, count), F32)] * 2
        + [pltpu.SemaphoreType.DMA((9,))],
        spaces=[pltpu.HBM] * len(given),
    )
    across, inside = exchange(*sent, False)
    h2, e2, j2, pixels = call(
        lone_kernel,
        [field] * 3 + [bf16(PIX_DEV, count)],
        [h1, e1, j1, v, w, source, places, design],
        work,
    )
    end_e, h3, e3, j3, answer_e, answer_j, v_near, near_places, inside, across = call(
        middle_kernel,
        [field] * 6 + [nodal, indices] + [f32(SECOND, LAYER)] * 2,
        [start_e, h1, e1, h2, e2, j2, v, w, source, places, valid, across, inside],
        work + received,
    )
    across, inside = exchange(across, inside, True)
    h4, e4, early = call(
        early_kernel,
        [field] * 2 + [f32(2 * NODES, count)],
        [e1, answer_e, j1, j2, answer_j, end_e, h3, e3, j3, v, w, source, places, levels],
        work,
    )
    e4, h4, sums = call(
        last_kernel,
        [field, field, f32(PIX_DEV, 2 * NODES)],
        [end_e, h3, e3, h4, e4, v, w, places, valid, v_near, near_places]
        + [inside, across, levels, early, pixels],
        work + [pltpu.VMEM((SECOND, LAYER), F32)] * 2,
    )
    parts = lax.all_to_all(sums, "exc", split_axis=0, concat_axis=0, tiled=True)
    share = PIX_DEV // owners
    out_e, out_h, eps, drude = call(
        functools.partial(total_kernel, owners),
        [f32(ROWS, count)] * 2 + [f32(share, NODES)] * 2,
        [parts, e4, h4],
        [pltpu.VMEM((2, share, NODES), F32), pltpu.SemaphoreType.DMA((14,))],
        out_spaces=[pltpu.HBM] * 4,
    )
    return out_e[None], out_h[None], eps.T, drude.T


def solution(mesh):
    return jax.shard_map(
        local,
        mesh=mesh,
        in_specs=(
            P("exc", None, "space"),
            P("exc", None, "space"),
            P("exc", None, "space"),
            P("exc", None, None, "space"),
            P(None, "space"),
            P(None, "space"),
            P(None, "space"),
            P("space"),
            P("exc", "space"),
            P("exc", None, "space"),
        ),
        out_specs=(
            P("exc", None, "space"),
            P("exc", None, "space"),
            P(None, ("space", "exc")),
            P(None, ("space", "exc")),
        ),
        check_vma=False,
    )
```

```python
import functools

import jax
import jax.numpy as jnp
import numpy as np
from jax import lax
from jax.experimental import pallas as pl
from jax.experimental.pallas import tpu as pltpu
from jax.sharding import PartitionSpec as P

NODES = 64
ROWS = 3 * NODES
LAYER = 128
PIX_DEV = 128

TIME_STEP = 0.025
DAMPING = 0.5
KEEP = 1.0 - TIME_STEP * DAMPING

TANGENT = 32
E_START = 0
H_FIRST = 32
E_FIRST = 64
H_SECOND = 96
SECOND = 128
V_NEAR = 128
N_NEAR = V_NEAR + 32
FIRST = N_NEAR + 8

A1, L0, L1, B1 = range(4)

BASE = (NODES, 0, 2 * NODES)

BF16 = jnp.bfloat16
F32 = jnp.float32


def parity(c, face, other):
    d = face // 2
    sign = 1.0 if face % 2 else -1.0
    return 6.0 * sign * (c - d) * (d - other) * (other - c) / 2.0


def off_diagonal():
    points = np.array([-1.0, -1.0 / np.sqrt(5.0), 1.0 / np.sqrt(5.0), 1.0])
    barycentric = np.array(
        [1.0 / np.prod([points[j] - points[k] for k in range(4) if k != j]) for j in range(4)]
    )
    deriv = np.zeros((4, 4))
    for row in range(4):
        for column in range(4):
            if row != column:
                deriv[row, column] = (
                    barycentric[column] / barycentric[row] / (points[row] - points[column])
                )
    return (2.0 * deriv).tolist()


SLOPES = off_diagonal()


def slope(parts, row, scale):
    terms = [(scale * SLOPES[row][i]) * parts[i] for i in range(4) if i != row]
    return terms[0] + terms[1] + terms[2]


def halves(x):
    high = x.astype(BF16)
    return high, (x - high.astype(F32)).astype(BF16)


def dot_t(a, b):
    return lax.dot_general(a, b, (((1,), (1,)), ((), ())), preferred_element_type=F32)


def thrice(x):
    return jnp.concatenate([x, x, x], axis=0)


def folded(x):
    return x[0:NODES] + x[NODES : 2 * NODES] + x[2 * NODES : ROWS]


def stored(x):
    return jnp.concatenate([x[NODES : 2 * NODES], x[0:NODES], x[2 * NODES : ROWS]], axis=0)


def one_hot(rows, targets):
    return (rows == targets).astype(F32).astype(BF16)


def picked(x, index):
    rows = x.shape[0]
    if rows < 8:
        index = index[0:rows]
    elif rows > 8:
        index = jnp.concatenate([index] * (rows // 8), axis=0)
    along = lax.GatherDimensionNumbers(
        offset_dims=(),
        collapsed_slice_dims=(1,),
        start_index_map=(1,),
        operand_batching_dims=(0,),
        start_indices_batching_dims=(0,),
    )
    mode = lax.GatherScatterMode.PROMISE_IN_BOUNDS
    return lax.gather(x, index[..., None], along, (1, 1), mode=mode)


def at_end(face):
    return 3 if face % 2 else 0


def x_traces(field, layer, face):
    at = 16 * at_end(face)
    return [field[layer, BASE[c] + at : BASE[c] + at + 16, :] for c in (1, 2)]


def lift_x(target, layer, face, scale, y, z):
    at = 16 * at_end(face)
    rows = slice(BASE[1] + at, BASE[1] + at + 16)
    target[layer, rows, :] += (-scale * parity(1, face, 2)) * z
    rows = slice(BASE[2] + at, BASE[2] + at + 16)
    target[layer, rows, :] += (-scale * parity(2, face, 1)) * y


def add_x(target, field, layer, scale, outer, base=None, ends=None):
    for c, other, sign in ((1, 2, 1.0), (2, 1, -1.0)):
        parts = [field[layer, BASE[other] + 16 * i : BASE[other] + 16 * i + 16, :] for i in range(4)]
        for i in range(4):
            change = slope(parts, i, scale * sign)
            face = {0: 0, 3: 1}.get(i)
            traces = None if face is None else outer(face)
            if traces is not None:
                change += (-scale * parity(c, face, other)) * traces[other - 1]
            rows = slice(BASE[c] + 16 * i, BASE[c] + 16 * i + 16)
            if ends is None:
                change += target[layer, rows, :] if base is None else base[rows]
            elif ends[0] == i:
                change += ends[c]
            target[layer, rows, :] = change
    if base is not None:
        rows = slice(BASE[0], BASE[0] + NODES)
        target[layer, rows, :] = base[rows]


def add_yz(target, field, layer, index, scale, fresh=False):
    for c, other, sign in ((0, 1, 1.0), (1, 0, -1.0)):
        parts = [field[layer, pl.ds(BASE[other] + k, 16, stride=4), :] for k in range(4)]
        for k in range(4):
            change = slope(parts, k, scale * sign)
            if k in (0, 3):
                face = 4 if k == 0 else 5
                got = picked(parts[3 - k], index(layer, face))
                change += (-scale * parity(c, face, other)) * got
            rows = pl.ds(BASE[c] + k, 16, stride=4)
            if fresh and c == 0:
                target[layer, rows, :] = change
            else:
                target[layer, rows, :] += change
    sign = jnp.where(lax.broadcasted_iota(jnp.int32, (8, LAYER), 0) < 4, -1.0, 1.0)
    for k in range(4):
        parts = [field[layer, pl.ds(BASE[0] + 4 * j + k, 8, stride=16), :] for j in range(4)]
        for j in range(4):
            change = slope(parts, j, scale)
            if j in (0, 3):
                face = 2 if j == 0 else 3
                got = picked(parts[3 - j], index(layer, face))
                change += (scale * parity(0, face, 2)) * got
            rows = pl.ds(BASE[0] + 4 * j + k, 8, stride=16)
            target[layer, rows, :] += sign * pltpu.roll(change, 4, 0)


def add_end(target, field, layer, i, index, scale, to_x):
    c, other, sign = (0, 1, 1.0) if to_x else (1, 0, -1.0)
    at = BASE[other] + 16 * i
    parts = [field[layer, pl.ds(at + k, 4, stride=4), :] for k in range(4)]
    for k in range(4):
        change = slope(parts, k, scale * sign)
        if k in (0, 3):
            face = 4 if k == 0 else 5
            got = picked(parts[3 - k], index(layer, face))
            change += (-scale * parity(c, face, other)) * got
        target[layer, pl.ds(BASE[c] + 16 * i + k, 4, stride=4), :] += change
    c, other, sign = (0, 2, -1.0) if to_x else (2, 0, 1.0)
    at = BASE[other] + 16 * i
    parts = [field[layer, at + 4 * j : at + 4 * j + 4, :] for j in range(4)]
    for j in range(4):
        change = slope(parts, j, scale * sign)
        if j in (0, 3):
            face = 2 if j == 0 else 3
            got = picked(parts[3 - j], index(layer, face))
            change += (-scale * parity(c, face, other)) * got
        at = BASE[c] + 16 * i + 4 * j
        target[layer, at : at + 4, :] += change


def add_into_end(target, field, layer, i, index, scale):
    for c, other, sign in ((1, 2, 1.0), (2, 1, -1.0)):
        parts = [field[layer, BASE[other] + 16 * n : BASE[other] + 16 * n + 16, :] for n in range(4)]
        rows = slice(BASE[c] + 16 * i, BASE[c] + 16 * i + 16)
        target[layer, rows, :] += slope(parts, i, scale * sign)
    add_end(target, field, layer, i, index, scale, False)


def passed_back(v, i):
    terms = [
        (SLOPES[i][n] * SLOPES[n][i]) * v[16 * n : 16 * n + 16] for n in range(4) if n != i
    ]
    return terms[0] + terms[1] + terms[2]


def layers_of(x):
    return [x[:, at : at + LAYER] for at in range(0, x.shape[1], LAYER)]


def between(field, index, layer):
    def outer(face):
        if (layer, face) not in ((L0, 1), (L1, 0)):
            return None
        traces = x_traces(field, L0 + L1 - layer, face ^ 1)
        return [picked(t, index(layer, face)) for t in traces]

    return outer


def lone_h(index, fe, fh):
    for layer in (L0, L1):
        add_x(fh, fe, layer, TIME_STEP, between(fe, index, layer))
        add_yz(fh, fe, layer, index, TIME_STEP)


def lone_e(index, fe, fh, acc, drive, v):
    for i, layer in enumerate((L0, L1)):
        add_x(acc, fh, layer, 1.0, between(fh, index, layer), drive[i])
        add_yz(acc, fh, layer, index, 1.0)
        fe[layer] -= TIME_STEP * thrice(v[i]) * acc[layer]


def lonely(index, fe, fh, acc, drive, v, out_h, out_e):
    def ends_of(field):
        return x_traces(field, L1, 1), x_traces(field, L0, 0)

    found = [ends_of(fe)]
    lone_h(index, fe, fh)
    found.append(ends_of(fh))
    for i in range(2):
        out_h[i] = fh[L0 + i]
    lone_e(index, fe, fh, acc, drive, v)
    found.append(ends_of(fe))
    for i in range(2):
        out_e[i] = fe[L0 + i]
    for face, layer in enumerate((L0, L1)):
        add_into_end(fh, fe, layer, at_end(face), index, TIME_STEP)
    found.append(ends_of(fh))
    return [jnp.concatenate(sum(traces, []), axis=0) for traces in zip(*found)]


def respond(index, valid, fe, fh, acc, lone, v, w, near_v, sent_a, sent_b):
    start_e, lone_h1, lone_e1 = lone
    own = (L0, L1)
    sides = ((A1, 1, L0, 0), (B1, 0, L1, 1))
    sent = (sent_a, sent_b)
    empty = jnp.zeros((16, LAYER), F32)

    def rows_at(c, i):
        return slice(BASE[c] + 16 * i, BASE[c] + 16 * i + 16)

    def lifted(face, scale, y, z):
        return (-scale * parity(1, face, 2)) * z, (-scale * parity(2, face, 1)) * y

    def inward(side, start, scale, answers=None):
        near, _, layer, face = sides[side]
        traces = [sent[side][start + 16 * t : start + 16 * t + 16, :] for t in range(2)]
        if answers is not None:
            traces = [a + b for a, b in zip(traces, answers)]
        mask = jnp.concatenate([valid[side]] * 2, axis=0)
        return lifted(face, scale, *[picked(t, index(layer, face)) * mask for t in traces])

    def outward(side, alone, scale, answers=None):
        near, face, layer, own_face = sides[side]
        traces = x_traces(alone, layer - L0, own_face)
        if answers is not None:
            traces = [a + b for a, b in zip(traces, answers)]
        return lifted(face, scale, *[picked(t, index(near, face)) for t in traces])

    def put(target, layer, i, pair):
        target[layer, rows_at(1, i), :] = pair[0]
        target[layer, rows_at(2, i), :] = pair[1]

    def add(target, layer, i, pair):
        target[layer, rows_at(1, i), :] += pair[0]
        target[layer, rows_at(2, i), :] += pair[1]

    near_h, own_h = [], []
    for side, (near, face, layer, own_face) in enumerate(sides):
        near_h.append(outward(side, start_e, TIME_STEP))
        own_h.append(inward(side, E_START, TIME_STEP))
        put(fh, near, at_end(face), near_h[side])
        put(fh, layer, at_end(own_face), own_h[side])

    for side, (near, face, layer, own_face) in enumerate(sides):
        i = at_end(face)
        pair = outward(side, lone_h1, 1.0, own_h[side])
        acc[near, rows_at(0, i), :] = empty
        add_end(acc, fh, near, i, index, 1.0, True)
        scale = -TIME_STEP * near_v[side, 0:16, :]
        put(fe, near, i, [scale * part for part in pair])
        fe[near, rows_at(0, i), :] = scale * acc[near, rows_at(0, i), :]

        i = at_end(own_face)
        pair = inward(side, H_FIRST, 1.0, near_h[side])
        acc[layer, rows_at(0, i), :] = empty
        add_end(acc, fh, layer, i, index, 1.0, True)
        for n in range(4):
            scale = -TIME_STEP * v[side, 16 * n : 16 * n + 16, :]
            if n == i:
                put(fe, layer, n, [scale * part for part in pair])
                fe[layer, rows_at(0, n), :] = scale * acc[layer, rows_at(0, n), :]
            else:
                y, z = own_h[side]
                put(fe, layer, n, [scale * (SLOPES[n][i] * z), scale * (-SLOPES[n][i] * y)])
                fe[layer, rows_at(0, n), :] = empty

    for side, (near, face, layer, own_face) in enumerate(sides):
        i = at_end(face)
        pair = outward(side, lone_e1, TIME_STEP, x_traces(fe, layer, own_face))
        back = 1.0 + TIME_STEP * TIME_STEP * near_v[side, 16:32, :]
        put(fh, near, i, [a + back * b for a, b in zip(pair, near_h[side])])
        add_end(fh, fe, near, i, index, TIME_STEP, False)
        ends = (at_end(own_face), *own_h[side])
        add_x(fh, fe, layer, TIME_STEP, between(fe, index, layer), None, ends)
        add_yz(fh, fe, layer, index, TIME_STEP, True)
        i = at_end(own_face)
        add(fh, layer, i, inward(side, E_FIRST, TIME_STEP, x_traces(fe, near, face)))

    current, second_e = [], []
    for i, layer in enumerate(own):
        current.append(TIME_STEP * thrice(w[i]) * fe[layer])
        add_x(acc, fh, layer, 1.0, between(fh, index, layer), current[i])
        add_yz(acc, fh, layer, index, 1.0)
    for side, (near, face, layer, own_face) in enumerate(sides):
        i = at_end(own_face)
        add(acc, layer, i, inward(side, H_SECOND, 1.0, x_traces(fh, near, face)))
        second_e.append(fe[layer] - TIME_STEP * thrice(v[side]) * acc[layer])
    return second_e, current


def odd_rank():
    return lax.rem(lax.axis_index("space"), 2) == 1


def send(across, inside, at, up, down):
    odd = odd_rank()
    rows = slice(at, at + up.shape[0])
    across[rows, :] = jnp.where(odd, up, down)
    inside[rows, :] = jnp.where(odd, down, up)


def sides_of(across, inside, a, b, rows):
    odd = odd_rank()
    from_across, from_inside = across[0:rows, :], inside[0:rows, :]
    a[...] = jnp.where(odd, from_inside, from_across)
    b[...] = jnp.where(odd, from_across, from_inside)


def first_kernel(
    e_in, h_in, j_in, v_in, w_in, near_in, ports_in, profile_in, design_in, *rest
):
    design, start_e, lone_h1, lone_e1, first_j, v, w, source, places, valid = rest[:10]
    across, inside, fe, fh, acc, neighbor, ports, profile, e, h, j, v_all, w_all, sems = rest[10:]
    started = []

    def fetch(origin, target):
        started.append(pltpu.make_async_copy(origin, target, sems.at[len(started)]))
        started[-1].start()

    fetch(near_in, neighbor)
    fetch(ports_in, ports)
    fetch(profile_in, profile)
    for origin, target in ((e_in, e), (h_in, h), (j_in, j), (w_in, w_all), (v_in, v_all)):
        fetch(origin, target)
    fetch(design_in, design)
    for copy in started:
        copy.wait()
    found = neighbor[...]
    place = jnp.where(found < 0, 0, jnp.bitwise_and(found, LAYER - 1))
    for i in range(2):
        columns = slice(i * LAYER, (i + 1) * LAYER)
        for face in range(6):
            places[6 * i + face] = jnp.broadcast_to(place[face : face + 1, columns], (8, LAYER))
        there = (found[i : i + 1, columns] >= 0).astype(F32)
        valid[i] = jnp.broadcast_to(there, (8, LAYER))
    electric = [stored(part) for part in layers_of(e[...])]
    magnetic = [stored(part) for part in layers_of(h[...])]
    current = [stored(part) for part in layers_of(j[...])]
    weight = layers_of(w_all[...])
    scale = layers_of(v_all[...])
    for i in range(2):
        w[i] = weight[i]
        v[i] = scale[i]
        start_e[i] = electric[i]
        fe[L0 + i] = electric[i]
        fh[L0 + i] = magnetic[i]
    targets = lax.broadcasted_iota(jnp.int32, (2 * LAYER, ports.shape[1]), 0)
    spread_hot = one_hot(targets, jnp.bitwise_and(ports[...], 2 * LAYER - 1))
    high, low = halves(profile[...])
    spread = layers_of(dot_t(high, spread_hot) + dot_t(low, spread_hot))
    drive = []
    for i in range(2):
        source[i] = stored(spread[i])
        now = KEEP * current[i] + TIME_STEP * thrice(weight[i]) * electric[i]
        first_j[i] = now
        drive.append(now + source[i])

    up, down = lonely(own_index(places), fe, fh, acc, drive, v, lone_h1, lone_e1)
    send(across, inside, 0, up, down)
    send(across, inside, V_NEAR, scale[1][48:NODES], scale[0][0:16])
    send(across, inside, V_NEAR + 16, passed_back(scale[1], 3), passed_back(scale[0], 0))
    blank = jnp.zeros((2, LAYER), F32)
    place = place.astype(F32)
    send(
        across,
        inside,
        N_NEAR,
        jnp.concatenate([place[:, LAYER : 2 * LAYER], blank], axis=0),
        jnp.concatenate([place[:, 0:LAYER], blank], axis=0),
    )


def own_index(places):
    def index(layer, face):
        return places[6 * (layer - L0) + face]

    return index


def second_lone_step(lone_h1, lone_e1, first_j, v, w, source, places, work):
    fe, fh, acc = work
    index = own_index(places)
    for i in range(2):
        fe[L0 + i] = lone_e1[i]
        fh[L0 + i] = lone_h1[i]
    current = [KEEP * first_j[i] + TIME_STEP * thrice(w[i]) * lone_e1[i] for i in range(2)]
    lone_h(index, fe, fh)
    lone_e(index, fe, fh, acc, [current[i] + source[i] for i in range(2)], v)
    return current


def lone_kernel(lone_h1, lone_e1, first_j, v, w, source, places, design, *rest):
    lone_h2, lone_e2, lone_j2, pixels, fe, fh, acc = rest
    pixel = jnp.bitwise_and(design[...], PIX_DEV - 1)
    pixels[...] = one_hot(lax.broadcasted_iota(jnp.int32, pixels.shape, 0), pixel)
    current = second_lone_step(
        lone_h1, lone_e1, first_j, v, w, source, places, (fe, fh, acc)
    )
    for i in range(2):
        lone_h2[i] = fh[L0 + i]
        lone_e2[i] = fe[L0 + i]
        lone_j2[i] = current[i]


def index_of(places, near_places):
    def index(layer, face):
        if layer in (L0, L1):
            return places[6 * (layer - L0) + face]
        return near_places[6 * (layer == B1) + face]

    return index


def middle_kernel(
    start_e, lone_h1, lone_e1, lone_h2, lone_e2, lone_j2, v, w, source, places,
    valid, across_in, inside_in, *rest
):
    end_e, next_h, next_e, next_j, answer_e, answer_j, near_v, near_places = rest[:8]
    inside, across = rest[8:10]
    fe, fh, acc, sent_a, sent_b = rest[10:]
    sides_of(across_in, inside_in, sent_a, sent_b, FIRST)
    for side, sent in enumerate((sent_a, sent_b)):
        near_v[side] = sent[V_NEAR : V_NEAR + 32, :]
        place = sent[N_NEAR : N_NEAR + 8, :].astype(jnp.int32)
        for face in range(6):
            near_places[6 * side + face] = jnp.broadcast_to(place[face : face + 1], (8, LAYER))
    index = index_of(places, near_places)
    second_e, current = respond(
        index, valid, fe, fh, acc, (start_e, lone_h1, lone_e1), v, w, near_v, sent_a, sent_b
    )
    drive = []
    for i in range(2):
        answer_e[i] = fe[L0 + i]
        answer_j[i] = current[i]
        electric = lone_e2[i] + second_e[i]
        end_e[i] = electric
        fe[L0 + i] = electric
        fh[L0 + i] += lone_h2[i]
        before = lone_j2[i] + current[i]
        now = KEEP * before + TIME_STEP * thrice(w[i]) * electric
        next_j[i] = now
        drive.append(now + source[i])
    up, down = lonely(index, fe, fh, acc, drive, v, next_h, next_e)
    send(across, inside, 0, up, down)


def early_kernel(
    lone_e1, answer_e, lone_j1, lone_j2, answer_j, end_e, next_h, next_e, next_j, v, w,
    source, places, levels, *rest
):
    last_h, last_e, out, changes, fe, fh, acc = rest
    current = second_lone_step(next_h, next_e, next_j, v, w, source, places, (fe, fh, acc))
    for i in range(2):
        electric = fe[L0 + i]
        last_h[i] = fh[L0 + i]
        last_e[i] = electric
        columns = slice(i * LAYER, (i + 1) * LAYER)
        level = [stored(levels[k, :, columns].astype(F32)) for k in range(5)]
        eps = (lone_e1[i] + answer_e[i]) * (level[1] - level[0])
        eps += end_e[i] * (level[2] - level[1]) + next_e[i] * (level[3] - level[2])
        eps += electric * (level[4] - level[3])
        drude = lone_j1[i] * level[0] + (lone_j2[i] + answer_j[i]) * level[1]
        drude += next_j[i] * level[2] + current[i] * level[3]
        out[0:NODES, columns] = folded(eps)
        out[NODES : 2 * NODES, columns] = folded(drude)
        changes[0, i] = level[3] - level[2]
        changes[1, i] = level[4] - level[3]
        changes[2, i] = level[3]


def last_kernel(
    start_e, lone_h1, lone_e1, lone_h2, lone_e2, v, w, places, valid, near_v, near_places,
    inside_in, across_in, changes, early, pixels, *rest
):
    out_e, out_h, sums = rest[:3]
    fe, fh, acc, sent_a, sent_b = rest[3:]
    sides_of(across_in, inside_in, sent_a, sent_b, SECOND)
    second_e, current = respond(
        index_of(places, near_places), valid, fe, fh, acc, (start_e, lone_h1, lone_e1),
        v, w, near_v, sent_a, sent_b,
    )
    parts = []
    for i in range(2):
        out_e[i] = lone_e2[i] + second_e[i]
        out_h[i] = lone_h2[i] + fh[L0 + i]
        eps = folded(fe[L0 + i] * changes[0, i] + second_e[i] * changes[1, i])
        drude = folded(current[i] * changes[2, i])
        columns = slice(i * LAYER, (i + 1) * LAYER)
        parts.append(jnp.concatenate([eps, drude], axis=0) + early[:, columns])
    both = jnp.concatenate(parts, axis=1)
    high, low = halves(both)
    sums[...] = dot_t(pixels[...], high) + dot_t(pixels[...], low)


def total_kernel(owners, parts, e, h, out_e, out_h, eps, drude, sums, sems):
    copies = []

    def write(origin, target):
        copies.append(pltpu.make_async_copy(origin, target, sems.at[len(copies)]))
        copies[-1].start()

    for field, target in ((e, out_e), (h, out_h)):
        for i in range(2):
            for c in range(3):
                there = target.at[pl.ds(c * NODES, NODES), pl.ds(i * LAYER, LAYER)]
                write(field.at[i, pl.ds(BASE[c], NODES), :], there)
    share = parts.shape[0] // owners
    total = parts[0:share]
    for owner in range(1, owners):
        total = total + parts[owner * share : (owner + 1) * share]
    total = total * (1.0 / owners)
    sums[0] = total[:, 0:NODES]
    sums[1] = total[:, NODES : 2 * NODES]
    write(sums.at[0], eps)
    write(sums.at[1], drude)
    for copy in copies:
        copy.wait()


def call(kernel, outs, args, scratch=(), spaces=None, out_spaces=None):
    moved = sum(4 * int(np.prod(o.shape)) for o in outs) + sum(
        a.dtype.itemsize * int(np.prod(a.shape)) for a in args
    )
    return pl.pallas_call(
        kernel,
        out_shape=outs,
        in_specs=[pl.BlockSpec(memory_space=s) for s in spaces or [pltpu.VMEM] * len(args)],
        out_specs=[pl.BlockSpec(memory_space=s) for s in out_spaces or [pltpu.VMEM] * len(outs)],
        scratch_shapes=list(scratch),
        compiler_params=pltpu.CompilerParams(vmem_limit_bytes=24 * 1024 * 1024),
        cost_estimate=pl.CostEstimate(flops=moved, bytes_accessed=moved, transcendentals=0),
    )(*args)


def f32(*shape):
    return jax.ShapeDtypeStruct(shape, F32)


def bf16(*shape):
    return jax.ShapeDtypeStruct(shape, BF16)


def exchange(across, inside, inside_first):
    size = lax.axis_size("space")

    def pairs(start):
        found = [(i, i + 1) for i in range(start, size - 1, 2)]
        return found + [(j, i) for i, j in found]

    if inside_first:
        inside = lax.ppermute(inside, "space", pairs(0))
    across = lax.ppermute(across, "space", pairs(1))
    if not inside_first:
        inside = lax.ppermute(inside, "space", pairs(0))
    return across, inside


def local(
    adj_e,
    adj_h,
    adj_j,
    fwd_e,
    inv_eps,
    drude_weight,
    neighbor,
    design_map,
    port_elems,
    port_profile,
):
    count = adj_e.shape[2]
    owners = lax.axis_size("exc")
    levels = fwd_e[0]
    field, nodal = f32(2, ROWS, LAYER), f32(2, NODES, LAYER)
    indices = jax.ShapeDtypeStruct((12, 8, LAYER), jnp.int32)
    work = [pltpu.VMEM((4, ROWS, LAYER), F32)] * 3
    given = [adj_e[0], adj_h[0], adj_j[0], inv_eps, drude_weight]
    given += [neighbor, port_elems, port_profile[0], design_map.reshape(1, count)]
    received = [pltpu.VMEM((FIRST, LAYER), F32)] * 2
    design, start_e, h1, e1, j1, v, w, source, places, valid, *sent = call(
        first_kernel,
        [jax.ShapeDtypeStruct((1, count), jnp.int32)]
        + [field] * 4
        + [nodal, nodal, field, indices, f32(2, 8, LAYER)]
        + [f32(FIRST, LAYER)] * 2,
        [pltpu.with_memory_space_constraint(a, pltpu.HBM) for a in given],
        work
        + [pltpu.VMEM(a.shape, a.dtype) for a in [neighbor, port_elems, port_profile[0]]]
        + [pltpu.VMEM((ROWS, count), F32)] * 3
        + [pltpu.VMEM((NODES, count), F32)] * 2
        + [pltpu.SemaphoreType.DMA((9,))],
        spaces=[pltpu.HBM] * len(given),
    )
    across, inside = exchange(*sent, False)
    h2, e2, j2, pixels = call(
        lone_kernel,
        [field] * 3 + [bf16(PIX_DEV, count)],
        [h1, e1, j1, v, w, source, places, design],
        work,
    )
    end_e, h3, e3, j3, answer_e, answer_j, near_v, near_places, inside, across = call(
        middle_kernel,
        [field] * 6 + [f32(2, 32, LAYER), indices] + [f32(SECOND, LAYER)] * 2,
        [start_e, h1, e1, h2, e2, j2, v, w, source, places, valid, across, inside],
        work + received,
    )
    across, inside = exchange(across, inside, True)
    h4, e4, early, changes = call(
        early_kernel,
        [field] * 2 + [f32(2 * NODES, count), f32(3, 2, ROWS, LAYER)],
        [e1, answer_e, j1, j2, answer_j, end_e, h3, e3, j3, v, w, source, places, levels],
        work,
    )
    e4, h4, sums = call(
        last_kernel,
        [field, field, f32(PIX_DEV, 2 * NODES)],
        [end_e, h3, e3, h4, e4, v, w, places, valid, near_v, near_places]
        + [inside, across, changes, early, pixels],
        work + [pltpu.VMEM((SECOND, LAYER), F32)] * 2,
    )
    parts = lax.all_to_all(sums, "exc", split_axis=0, concat_axis=0, tiled=True)
    share = PIX_DEV // owners
    out_e, out_h, eps, drude = call(
        functools.partial(total_kernel, owners),
        [f32(ROWS, count)] * 2 + [f32(share, NODES)] * 2,
        [parts, e4, h4],
        [pltpu.VMEM((2, share, NODES), F32), pltpu.SemaphoreType.DMA((14,))],
        out_spaces=[pltpu.HBM] * 4,
    )
    return out_e[None], out_h[None], eps.T, drude.T


def solution(mesh):
    return jax.shard_map(
        local,
        mesh=mesh,
        in_specs=(
            P("exc", None, "space"),
            P("exc", None, "space"),
            P("exc", None, "space"),
            P("exc", None, None, "space"),
            P(None, "space"),
            P(None, "space"),
            P(None, "space"),
            P("space"),
            P("exc", "space"),
            P("exc", None, "space"),
        ),
        out_specs=(
            P("exc", None, "space"),
            P("exc", None, "space"),
            P(None, ("space", "exc")),
            P(None, ("space", "exc")),
        ),
        check_vma=False,
    )
```

```python
import functools

import jax
import jax.numpy as jnp
import numpy as np
from jax import lax
from jax.experimental import pallas as pl
from jax.experimental.pallas import tpu as pltpu
from jax.sharding import PartitionSpec as P

NODES = 64
ROWS = 3 * NODES
LAYER = 128
PIX_DEV = 128

TIME_STEP = 0.025
DAMPING = 0.5
KEEP = 1.0 - TIME_STEP * DAMPING

TANGENT = 32
E_START = 0
H_FIRST = 32
E_FIRST = 64
H_SECOND = 96
SECOND = 128
V_NEAR = 128
N_NEAR = V_NEAR + 32
FIRST = N_NEAR + 8

A1, L0, L1, B1 = range(4)

E_BASE = (NODES, 0, 2 * NODES)
H_BASE = (2 * NODES, 0, NODES)

BF16 = jnp.bfloat16
F32 = jnp.float32


def parity(c, face, other):
    d = face // 2
    sign = 1.0 if face % 2 else -1.0
    return 6.0 * sign * (c - d) * (d - other) * (other - c) / 2.0


def off_diagonal():
    points = np.array([-1.0, -1.0 / np.sqrt(5.0), 1.0 / np.sqrt(5.0), 1.0])
    barycentric = np.array(
        [1.0 / np.prod([points[j] - points[k] for k in range(4) if k != j]) for j in range(4)]
    )
    deriv = np.zeros((4, 4))
    for row in range(4):
        for column in range(4):
            if row != column:
                deriv[row, column] = (
                    barycentric[column] / barycentric[row] / (points[row] - points[column])
                )
    return (2.0 * deriv).tolist()


SLOPES = off_diagonal()


def slope(parts, row, scale):
    terms = [(scale * SLOPES[row][i]) * parts[i] for i in range(4) if i != row]
    return terms[0] + terms[1] + terms[2]


def halves(x):
    high = x.astype(BF16)
    return high, (x - high.astype(F32)).astype(BF16)


def dot_t(a, b):
    return lax.dot_general(a, b, (((1,), (1,)), ((), ())), preferred_element_type=F32)


def thrice(x):
    return jnp.concatenate([x, x, x], axis=0)


def folded(x):
    return x[0:NODES] + x[NODES : 2 * NODES] + x[2 * NODES : ROWS]


def stored(x, order=(1, 0, 2)):
    return jnp.concatenate([x[c * NODES : (c + 1) * NODES] for c in order], axis=0)


def one_hot(rows, targets):
    return (rows == targets).astype(F32).astype(BF16)


def picked(x, index):
    rows = x.shape[0]
    if rows < 8:
        index = index[0:rows]
    elif rows > 8:
        index = jnp.concatenate([index] * (rows // 8), axis=0)
    along = lax.GatherDimensionNumbers(
        offset_dims=(),
        collapsed_slice_dims=(1,),
        start_index_map=(1,),
        operand_batching_dims=(0,),
        start_indices_batching_dims=(0,),
    )
    mode = lax.GatherScatterMode.PROMISE_IN_BOUNDS
    return lax.gather(x, index[..., None], along, (1, 1), mode=mode)


def at_end(face):
    return 3 if face % 2 else 0


class Fields:
    def __init__(self, ref, base):
        self.ref, self.base = ref, base

    def rows(self, c, i, count=16):
        at = self.base[c] + 16 * i
        return slice(at, at + count)


def x_traces(field, layer, face):
    return [field.ref[layer, field.rows(c, at_end(face)), :] for c in (1, 2)]


def add_x(target, field, layer, scale, outer, base=None, ends=None):
    for c, other, sign in ((1, 2, 1.0), (2, 1, -1.0)):
        parts = [field.ref[layer, field.rows(other, i), :] for i in range(4)]
        for i in range(4):
            change = slope(parts, i, scale * sign)
            face = {0: 0, 3: 1}.get(i)
            traces = None if face is None else outer(face)
            if traces is not None:
                change += (-scale * parity(c, face, other)) * traces[other - 1]
            rows = target.rows(c, i)
            if ends is None:
                change += target.ref[layer, rows, :] if base is None else base[rows]
            elif ends[0] == i:
                change += ends[c]
            target.ref[layer, rows, :] = change
    if base is not None:
        rows = target.rows(0, 0, NODES)
        target.ref[layer, rows, :] = base[rows]


def add_yz(target, field, layer, index, scale, fresh=False):
    for c, other, sign in ((0, 1, 1.0), (1, 0, -1.0)):
        parts = [field.ref[layer, pl.ds(field.base[other] + k, 16, stride=4), :] for k in range(4)]
        for k in range(4):
            change = slope(parts, k, scale * sign)
            if k in (0, 3):
                face = 4 if k == 0 else 5
                got = picked(parts[3 - k], index(layer, face))
                change += (-scale * parity(c, face, other)) * got
            rows = pl.ds(target.base[c] + k, 16, stride=4)
            if fresh and c == 0:
                target.ref[layer, rows, :] = change
            else:
                target.ref[layer, rows, :] += change
    first = lax.broadcasted_iota(jnp.int32, (8, LAYER), 0) < 4
    sign = jnp.where(first, 1.0, -1.0) if field.base == E_BASE else jnp.where(first, -1.0, 1.0)
    for k in range(4):
        rows = [pl.ds(NODES + 4 * j + k, 8, stride=16) for j in range(4)]
        parts = [field.ref[layer, row, :] for row in rows]
        for j in range(4):
            change = slope(parts, j, scale)
            if j in (0, 3):
                face = 2 if j == 0 else 3
                got = picked(parts[3 - j], index(layer, face))
                change += (scale * parity(0, face, 2)) * got
            target.ref[layer, rows[j], :] += sign * change


def add_end(target, field, layer, i, index, scale, to_x):
    c, other, sign = (0, 1, 1.0) if to_x else (1, 0, -1.0)
    at = field.base[other] + 16 * i
    parts = [field.ref[layer, pl.ds(at + k, 4, stride=4), :] for k in range(4)]
    for k in range(4):
        change = slope(parts, k, scale * sign)
        if k in (0, 3):
            face = 4 if k == 0 else 5
            got = picked(parts[3 - k], index(layer, face))
            change += (-scale * parity(c, face, other)) * got
        target.ref[layer, pl.ds(target.base[c] + 16 * i + k, 4, stride=4), :] += change
    c, other, sign = (0, 2, -1.0) if to_x else (2, 0, 1.0)
    at = field.base[other] + 16 * i
    parts = [field.ref[layer, at + 4 * j : at + 4 * j + 4, :] for j in range(4)]
    for j in range(4):
        change = slope(parts, j, scale * sign)
        if j in (0, 3):
            face = 2 if j == 0 else 3
            got = picked(parts[3 - j], index(layer, face))
            change += (-scale * parity(c, face, other)) * got
        at = target.base[c] + 16 * i + 4 * j
        target.ref[layer, at : at + 4, :] += change


def add_into_end(target, field, layer, i, index, scale):
    for c, other, sign in ((1, 2, 1.0), (2, 1, -1.0)):
        parts = [field.ref[layer, field.rows(other, n), :] for n in range(4)]
        target.ref[layer, target.rows(c, i), :] += slope(parts, i, scale * sign)
    add_end(target, field, layer, i, index, scale, False)


def passed_back(v, i):
    terms = [
        (SLOPES[i][n] * SLOPES[n][i]) * v[16 * n : 16 * n + 16] for n in range(4) if n != i
    ]
    return terms[0] + terms[1] + terms[2]


def layers_of(x):
    return [x[:, at : at + LAYER] for at in range(0, x.shape[1], LAYER)]


def between(field, index, layer):
    def outer(face):
        if (layer, face) not in ((L0, 1), (L1, 0)):
            return None
        traces = x_traces(field, L0 + L1 - layer, face ^ 1)
        return [picked(t, index(layer, face)) for t in traces]

    return outer


def lone_h(index, fe, fh):
    for layer in (L0, L1):
        add_x(fh, fe, layer, TIME_STEP, between(fe, index, layer))
        add_yz(fh, fe, layer, index, TIME_STEP)


def lone_e(index, fe, fh, acc, drive, v):
    for i, layer in enumerate((L0, L1)):
        add_x(acc, fh, layer, 1.0, between(fh, index, layer), drive[i])
        add_yz(acc, fh, layer, index, 1.0)
        fe.ref[layer] -= TIME_STEP * thrice(v[i]) * acc.ref[layer]


def lonely(index, fe, fh, acc, drive, v, out_h, out_e):
    def ends_of(field):
        return x_traces(field, L1, 1), x_traces(field, L0, 0)

    found = [ends_of(fe)]
    lone_h(index, fe, fh)
    found.append(ends_of(fh))
    for i in range(2):
        out_h[i] = fh.ref[L0 + i]
    lone_e(index, fe, fh, acc, drive, v)
    found.append(ends_of(fe))
    for i in range(2):
        out_e[i] = fe.ref[L0 + i]
    for face, layer in enumerate((L0, L1)):
        add_into_end(fh, fe, layer, at_end(face), index, TIME_STEP)
    found.append(ends_of(fh))
    return [jnp.concatenate(sum(traces, []), axis=0) for traces in zip(*found)]


def respond(index, valid, fe, fh, acc, own_sent, v, w, near_v, sent_a, sent_b):
    own = (L0, L1)
    sides = ((A1, 1, L0, 0), (B1, 0, L1, 1))
    sent = (sent_a, sent_b)
    empty = jnp.zeros((16, LAYER), F32)

    def lifted(face, scale, y, z):
        return (-scale * parity(1, face, 2)) * z, (-scale * parity(2, face, 1)) * y

    def inward(side, start, scale, answers=None):
        near, _, layer, face = sides[side]
        traces = [sent[side][start + 16 * t : start + 16 * t + 16, :] for t in range(2)]
        if answers is not None:
            traces = [a + b for a, b in zip(traces, answers)]
        mask = jnp.concatenate([valid[side]] * 2, axis=0)
        return lifted(face, scale, *[picked(t, index(layer, face)) * mask for t in traces])

    def outward(side, start, scale, answers=None):
        near, face, layer, own_face = sides[side]
        traces = [own_sent[side, start + 16 * t : start + 16 * t + 16, :] for t in range(2)]
        if answers is not None:
            traces = [a + b for a, b in zip(traces, answers)]
        return lifted(face, scale, *[picked(t, index(near, face)) for t in traces])

    def put(target, layer, i, pair):
        target.ref[layer, target.rows(1, i), :] = pair[0]
        target.ref[layer, target.rows(2, i), :] = pair[1]

    def add(target, layer, i, pair):
        target.ref[layer, target.rows(1, i), :] += pair[0]
        target.ref[layer, target.rows(2, i), :] += pair[1]

    near_h, own_h = [], []
    for side, (near, face, layer, own_face) in enumerate(sides):
        near_h.append(outward(side, E_START, TIME_STEP))
        own_h.append(inward(side, E_START, TIME_STEP))
        put(fh, near, at_end(face), near_h[side])
        put(fh, layer, at_end(own_face), own_h[side])

    for side, (near, face, layer, own_face) in enumerate(sides):
        i = at_end(face)
        pair = outward(side, H_FIRST, 1.0, own_h[side])
        acc.ref[near, acc.rows(0, i), :] = empty
        add_end(acc, fh, near, i, index, 1.0, True)
        scale = -TIME_STEP * near_v[side, 0:16, :]
        put(fe, near, i, [scale * part for part in pair])
        fe.ref[near, fe.rows(0, i), :] = scale * acc.ref[near, acc.rows(0, i), :]

        i = at_end(own_face)
        pair = inward(side, H_FIRST, 1.0, near_h[side])
        acc.ref[layer, acc.rows(0, i), :] = empty
        add_end(acc, fh, layer, i, index, 1.0, True)
        for n in range(4):
            scale = -TIME_STEP * v[side][16 * n : 16 * n + 16]
            if n == i:
                put(fe, layer, n, [scale * part for part in pair])
                fe.ref[layer, fe.rows(0, n), :] = scale * acc.ref[layer, acc.rows(0, n), :]
            else:
                y, z = own_h[side]
                put(fe, layer, n, [scale * (SLOPES[n][i] * z), scale * (-SLOPES[n][i] * y)])
                fe.ref[layer, fe.rows(0, n), :] = empty

    for side, (near, face, layer, own_face) in enumerate(sides):
        i = at_end(face)
        pair = outward(side, E_FIRST, TIME_STEP, x_traces(fe, layer, own_face))
        back = 1.0 + TIME_STEP * TIME_STEP * near_v[side, 16:32, :]
        put(fh, near, i, [a + back * b for a, b in zip(pair, near_h[side])])
        add_end(fh, fe, near, i, index, TIME_STEP, False)
        ends = (at_end(own_face), *own_h[side])
        add_x(fh, fe, layer, TIME_STEP, between(fe, index, layer), None, ends)
        add_yz(fh, fe, layer, index, TIME_STEP, True)
        i = at_end(own_face)
        add(fh, layer, i, inward(side, E_FIRST, TIME_STEP, x_traces(fe, near, face)))

    current, second_e = [], []
    for i, layer in enumerate(own):
        current.append(TIME_STEP * thrice(w[i]) * fe.ref[layer])
        add_x(acc, fh, layer, 1.0, between(fh, index, layer), current[i])
        add_yz(acc, fh, layer, index, 1.0)
    for side, (near, face, layer, own_face) in enumerate(sides):
        i = at_end(own_face)
        add(acc, layer, i, inward(side, H_SECOND, 1.0, x_traces(fh, near, face)))
        second_e.append(fe.ref[layer] - TIME_STEP * thrice(v[side]) * acc.ref[layer])
    return second_e, current


def odd_rank():
    return lax.rem(lax.axis_index("space"), 2) == 1


def send(across, inside, at, up, down):
    odd = odd_rank()
    rows = slice(at, at + up.shape[0])
    across[rows, :] = jnp.where(odd, up, down)
    inside[rows, :] = jnp.where(odd, down, up)


def sides_of(across, inside, a, b, rows):
    odd = odd_rank()
    from_across, from_inside = across[0:rows, :], inside[0:rows, :]
    a[...] = jnp.where(odd, from_inside, from_across)
    b[...] = jnp.where(odd, from_across, from_inside)


def wrapped(fe, fh, acc):
    return Fields(fe, E_BASE), Fields(fh, H_BASE), Fields(acc, E_BASE)


def first_kernel(
    e_in, h_in, j_in, v_in, w_in, near_in, ports_in, profile_in, design_in, *rest
):
    design, v, w, lone_h1, lone_e1, first_j, source, places, valid, own_sent = rest[:10]
    across, inside, fe, fh, acc, neighbor, ports, profile, e, h, j, sems = rest[10:]
    fe, fh, acc = wrapped(fe, fh, acc)
    copies = []
    for origin, target in (
        (near_in, neighbor), (ports_in, ports), (profile_in, profile), (e_in, e), (h_in, h),
        (j_in, j), (w_in, w), (v_in, v), (design_in, design),
    ):
        copies.append(pltpu.make_async_copy(origin, target, sems.at[len(copies)]))
        copies[-1].start()
    for copy in copies:
        copy.wait()

    found = neighbor[...]
    place = jnp.where(found < 0, 0, jnp.bitwise_and(found, LAYER - 1))
    for i in range(2):
        columns = slice(i * LAYER, (i + 1) * LAYER)
        for face in range(6):
            places[6 * i + face] = jnp.broadcast_to(place[face : face + 1, columns], (8, LAYER))
        there = (found[i : i + 1, columns] >= 0).astype(F32)
        valid[i] = jnp.broadcast_to(there, (8, LAYER))
    electric = [stored(part) for part in layers_of(e[...])]
    magnetic = [stored(part, (1, 2, 0)) for part in layers_of(h[...])]
    current = [stored(part) for part in layers_of(j[...])]
    weight = layers_of(w[...])
    scale = layers_of(v[...])
    targets = lax.broadcasted_iota(jnp.int32, (2 * LAYER, ports.shape[1]), 0)
    spread_hot = one_hot(targets, jnp.bitwise_and(ports[...], 2 * LAYER - 1))
    high, low = halves(profile[...])
    spread = layers_of(dot_t(high, spread_hot) + dot_t(low, spread_hot))
    drive = []
    for i in range(2):
        fe.ref[L0 + i] = electric[i]
        fh.ref[L0 + i] = magnetic[i]
        source[i] = stored(spread[i])
        now = KEEP * current[i] + TIME_STEP * thrice(weight[i]) * electric[i]
        first_j[i] = now
        drive.append(now + source[i])

    up, down = lonely(own_index(places), fe, fh, acc, drive, scale, lone_h1, lone_e1)
    own_sent[0] = down
    own_sent[1] = up
    send(across, inside, 0, up, down)
    send(across, inside, V_NEAR, scale[1][48:NODES], scale[0][0:16])
    send(across, inside, V_NEAR + 16, passed_back(scale[1], 3), passed_back(scale[0], 0))
    blank = jnp.zeros((2, LAYER), F32)
    place = place.astype(F32)
    send(
        across,
        inside,
        N_NEAR,
        jnp.concatenate([place[:, LAYER : 2 * LAYER], blank], axis=0),
        jnp.concatenate([place[:, 0:LAYER], blank], axis=0),
    )


def own_index(places):
    def index(layer, face):
        return places[6 * (layer - L0) + face]

    return index


def index_of(places, near_places):
    def index(layer, face):
        if layer in (L0, L1):
            return places[6 * (layer - L0) + face]
        return near_places[6 * (layer == B1) + face]

    return index


def second_lone_step(lone_h1, lone_e1, first_j, v, w, source, places, work):
    fe, fh, acc = work
    index = own_index(places)
    current = []
    for i in range(2):
        electric = lone_e1[i]
        fe.ref[L0 + i] = electric
        fh.ref[L0 + i] = lone_h1[i]
        current.append(KEEP * first_j[i] + TIME_STEP * thrice(w[i]) * electric)
    lone_h(index, fe, fh)
    lone_e(index, fe, fh, acc, [current[i] + source[i] for i in range(2)], v)
    return current


def lone_kernel(lone_h1, lone_e1, first_j, v, w, source, places, design, *rest):
    lone_h2, lone_e2, lone_j2, pixels, *work = rest
    fe, fh, acc = wrapped(*work)
    pixel = jnp.bitwise_and(design[...], PIX_DEV - 1)
    pixels[...] = one_hot(lax.broadcasted_iota(jnp.int32, pixels.shape, 0), pixel)
    scale, weight = layers_of(v[...]), layers_of(w[...])
    current = second_lone_step(
        lone_h1, lone_e1, first_j, scale, weight, source, places, (fe, fh, acc)
    )
    for i in range(2):
        lone_h2[i] = fh.ref[L0 + i]
        lone_e2[i] = fe.ref[L0 + i]
        lone_j2[i] = current[i]


def middle_kernel(
    own_sent, lone_h2, lone_e2, lone_j2, v, w, source, places, valid, across_in, inside_in,
    *rest
):
    end_e, next_h, next_e, answer_e, own_next, near_v, near_places, across, inside = rest[:9]
    fe, fh, acc = wrapped(*rest[9:12])
    sent_a, sent_b = rest[12:]
    sides_of(across_in, inside_in, sent_a, sent_b, FIRST)
    for side, sent in enumerate((sent_a, sent_b)):
        near_v[side] = sent[V_NEAR : V_NEAR + 32, :]
        place = sent[N_NEAR : N_NEAR + 8, :].astype(jnp.int32)
        for face in range(6):
            near_places[6 * side + face] = jnp.broadcast_to(place[face : face + 1], (8, LAYER))
    index = index_of(places, near_places)
    scale, weight = layers_of(v[...]), layers_of(w[...])
    second_e, current = respond(
        index, valid, fe, fh, acc, own_sent, scale, weight, near_v, sent_a, sent_b
    )
    drive = []
    for i in range(2):
        answer_e[i] = fe.ref[L0 + i]
        electric = lone_e2[i] + second_e[i]
        end_e[i] = electric
        fe.ref[L0 + i] = electric
        fh.ref[L0 + i] += lone_h2[i]
        before = lone_j2[i] + current[i]
        now = KEEP * before + TIME_STEP * thrice(weight[i]) * electric
        drive.append(now + source[i])
    up, down = lonely(index, fe, fh, acc, drive, scale, next_h, next_e)
    own_next[0] = down
    own_next[1] = up
    send(across, inside, 0, up, down)


def early_kernel(
    lone_e1, answer_e, lone_j1, lone_j2, end_e, next_h, next_e, v, w, source, places, levels,
    *rest
):
    last_h, last_e, out, changes, *work = rest
    fe, fh, acc = wrapped(*work)
    scale, weight = layers_of(v[...]), layers_of(w[...])
    second_j, third_j = [], []
    for i in range(2):
        rise = TIME_STEP * thrice(weight[i])
        second_j.append(lone_j2[i] + rise * answer_e[i])
        third_j.append(KEEP * second_j[i] + rise * end_e[i])
    current = second_lone_step(
        next_h, next_e, third_j, scale, weight, source, places, (fe, fh, acc)
    )
    for i in range(2):
        electric = fe.ref[L0 + i]
        last_h[i] = fh.ref[L0 + i]
        last_e[i] = electric
        columns = slice(i * LAYER, (i + 1) * LAYER)
        level = [stored(levels[k, :, columns].astype(F32)) for k in range(5)]
        eps = (lone_e1[i] + answer_e[i]) * (level[1] - level[0])
        eps += end_e[i] * (level[2] - level[1]) + next_e[i] * (level[3] - level[2])
        eps += electric * (level[4] - level[3])
        drude = lone_j1[i] * level[0] + second_j[i] * level[1]
        drude += third_j[i] * level[2] + current[i] * level[3]
        out[0:NODES, columns] = folded(eps)
        out[NODES : 2 * NODES, columns] = folded(drude)
        changes[0, i] = level[3] - level[2]
        changes[1, i] = level[4] - level[3]
        changes[2, i] = level[3]


def last_kernel(
    own_sent, lone_h2, lone_e2, v, w, places, valid, near_v, near_places, inside_in, across_in,
    changes, early, pixels, *rest
):
    out_e, out_h, sums = rest[:3]
    fe, fh, acc = wrapped(*rest[3:6])
    sent_a, sent_b = rest[6:]
    sides_of(across_in, inside_in, sent_a, sent_b, SECOND)
    second_e, current = respond(
        index_of(places, near_places), valid, fe, fh, acc, own_sent,
        layers_of(v[...]), layers_of(w[...]), near_v, sent_a, sent_b,
    )
    parts = []
    for i in range(2):
        out_e[i] = lone_e2[i] + second_e[i]
        out_h[i] = lone_h2[i] + fh.ref[L0 + i]
        eps = folded(fe.ref[L0 + i] * changes[0, i] + second_e[i] * changes[1, i])
        drude = folded(current[i] * changes[2, i])
        columns = slice(i * LAYER, (i + 1) * LAYER)
        parts.append(jnp.concatenate([eps, drude], axis=0) + early[:, columns])
    both = jnp.concatenate(parts, axis=1)
    high, low = halves(both)
    sums[...] = dot_t(pixels[...], high) + dot_t(pixels[...], low)


def total_kernel(owners, parts, e, h, out_e, out_h, eps, drude, sums, sems):
    copies = []

    def write(origin, target):
        copies.append(pltpu.make_async_copy(origin, target, sems.at[len(copies)]))
        copies[-1].start()

    for field, base, target in ((e, E_BASE, out_e), (h, H_BASE, out_h)):
        for i in range(2):
            for c in range(3):
                there = target.at[pl.ds(c * NODES, NODES), pl.ds(i * LAYER, LAYER)]
                write(field.at[i, pl.ds(base[c], NODES), :], there)
    share = parts.shape[0] // owners
    total = parts[0:share]
    for owner in range(1, owners):
        total = total + parts[owner * share : (owner + 1) * share]
    total = total * (1.0 / owners)
    sums[0] = total[:, 0:NODES]
    sums[1] = total[:, NODES : 2 * NODES]
    write(sums.at[0], eps)
    write(sums.at[1], drude)
    for copy in copies:
        copy.wait()


def call(kernel, outs, args, scratch=(), spaces=None, out_spaces=None):
    moved = sum(4 * int(np.prod(o.shape)) for o in outs) + sum(
        a.dtype.itemsize * int(np.prod(a.shape)) for a in args
    )
    return pl.pallas_call(
        kernel,
        out_shape=outs,
        in_specs=[pl.BlockSpec(memory_space=s) for s in spaces or [pltpu.VMEM] * len(args)],
        out_specs=[pl.BlockSpec(memory_space=s) for s in out_spaces or [pltpu.VMEM] * len(outs)],
        scratch_shapes=list(scratch),
        compiler_params=pltpu.CompilerParams(vmem_limit_bytes=24 * 1024 * 1024),
        cost_estimate=pl.CostEstimate(flops=moved, bytes_accessed=moved, transcendentals=0),
    )(*args)


def f32(*shape):
    return jax.ShapeDtypeStruct(shape, F32)


def bf16(*shape):
    return jax.ShapeDtypeStruct(shape, BF16)


def exchange(across, inside, inside_first):
    size = lax.axis_size("space")

    def pairs(start):
        found = [(i, i + 1) for i in range(start, size - 1, 2)]
        return found + [(j, i) for i, j in found]

    if inside_first:
        inside = lax.ppermute(inside, "space", pairs(0))
    across = lax.ppermute(across, "space", pairs(1))
    if not inside_first:
        inside = lax.ppermute(inside, "space", pairs(0))
    return across, inside


def local(
    adj_e,
    adj_h,
    adj_j,
    fwd_e,
    inv_eps,
    drude_weight,
    neighbor,
    design_map,
    port_elems,
    port_profile,
):
    count = adj_e.shape[2]
    owners = lax.axis_size("exc")
    levels = fwd_e[0]
    field, nodal, sent = f32(2, ROWS, LAYER), f32(NODES, count), f32(2, SECOND, LAYER)
    indices = jax.ShapeDtypeStruct((12, 8, LAYER), jnp.int32)
    work = [pltpu.VMEM((4, ROWS, LAYER), F32)] * 3
    given = [adj_e[0], adj_h[0], adj_j[0], inv_eps, drude_weight]
    given += [neighbor, port_elems, port_profile[0], design_map.reshape(1, count)]
    design, v, w, h1, e1, j1, source, places, valid, own_sent, across, inside = call(
        first_kernel,
        [jax.ShapeDtypeStruct((1, count), jnp.int32), nodal, nodal]
        + [field] * 4
        + [indices, f32(2, 8, LAYER), sent]
        + [f32(FIRST, LAYER)] * 2,
        [pltpu.with_memory_space_constraint(a, pltpu.HBM) for a in given],
        work
        + [pltpu.VMEM(a.shape, a.dtype) for a in [neighbor, port_elems, port_profile[0]]]
        + [pltpu.VMEM((ROWS, count), F32)] * 3
        + [pltpu.SemaphoreType.DMA((9,))],
        spaces=[pltpu.HBM] * len(given),
    )
    across, inside = exchange(across, inside, False)
    h2, e2, j2, pixels = call(
        lone_kernel,
        [field] * 3 + [bf16(PIX_DEV, count)],
        [h1, e1, j1, v, w, source, places, design],
        work,
    )
    end_e, h3, e3, answer_e, own_sent, near_v, near_places, across, inside = call(
        middle_kernel,
        [field] * 4 + [sent, f32(2, 32, LAYER), indices] + [f32(SECOND, LAYER)] * 2,
        [own_sent, h2, e2, j2, v, w, source, places, valid, across, inside],
        work + [pltpu.VMEM((FIRST, LAYER), F32)] * 2,
    )
    across, inside = exchange(across, inside, True)
    h4, e4, early, changes = call(
        early_kernel,
        [field] * 2 + [f32(2 * NODES, count), f32(3, 2, ROWS, LAYER)],
        [e1, answer_e, j1, j2, end_e, h3, e3, v, w, source, places, levels],
        work,
    )
    e4, h4, sums = call(
        last_kernel,
        [field, field, f32(PIX_DEV, 2 * NODES)],
        [own_sent, h4, e4, v, w, places, valid, near_v, near_places]
        + [inside, across, changes, early, pixels],
        work + [pltpu.VMEM((SECOND, LAYER), F32)] * 2,
    )
    parts = lax.all_to_all(sums, "exc", split_axis=0, concat_axis=0, tiled=True)
    share = PIX_DEV // owners
    out_e, out_h, eps, drude = call(
        functools.partial(total_kernel, owners),
        [f32(ROWS, count)] * 2 + [f32(share, NODES)] * 2,
        [parts, e4, h4],
        [pltpu.VMEM((2, share, NODES), F32), pltpu.SemaphoreType.DMA((14,))],
        out_spaces=[pltpu.HBM] * 4,
    )
    return out_e[None], out_h[None], eps.T, drude.T


def solution(mesh):
    return jax.shard_map(
        local,
        mesh=mesh,
        in_specs=(
            P("exc", None, "space"),
            P("exc", None, "space"),
            P("exc", None, "space"),
            P("exc", None, None, "space"),
            P(None, "space"),
            P(None, "space"),
            P(None, "space"),
            P("space"),
            P("exc", "space"),
            P("exc", None, "space"),
        ),
        out_specs=(
            P("exc", None, "space"),
            P("exc", None, "space"),
            P(None, ("space", "exc")),
            P(None, ("space", "exc")),
        ),
        check_vma=False,
    )
```

```python
import functools

import jax
import jax.numpy as jnp
import numpy as np
from jax import lax
from jax.experimental import pallas as pl
from jax.experimental.pallas import tpu as pltpu
from jax.sharding import PartitionSpec as P

NODES = 64
ROWS = 3 * NODES
LAYER = 128
PIX_DEV = 128

TIME_STEP = 0.025
DAMPING = 0.5
KEEP = 1.0 - TIME_STEP * DAMPING

PER_STEP = 1.0 / TIME_STEP

TANGENT = 32
E_START = 0
H_FIRST = 32
E_FIRST = 64
H_SECOND = 96
SECOND = 128
V_NEAR = 128
N_NEAR = V_NEAR + 32
FIRST = N_NEAR + 8

A1, L0, L1, B1 = range(4)

BASE = (NODES, 0, 2 * NODES)

BF16 = jnp.bfloat16
F32 = jnp.float32


def parity(c, face, other):
    d = face // 2
    sign = 1.0 if face % 2 else -1.0
    return 6.0 * sign * (c - d) * (d - other) * (other - c) / 2.0


def off_diagonal():
    points = np.array([-1.0, -1.0 / np.sqrt(5.0), 1.0 / np.sqrt(5.0), 1.0])
    barycentric = np.array(
        [1.0 / np.prod([points[j] - points[k] for k in range(4) if k != j]) for j in range(4)]
    )
    deriv = np.zeros((4, 4))
    for row in range(4):
        for column in range(4):
            if row != column:
                deriv[row, column] = (
                    barycentric[column] / barycentric[row] / (points[row] - points[column])
                )
    return (2.0 * deriv).tolist()


SLOPES = off_diagonal()


def slope(parts, row, scale):
    total = None
    for i in (1, 2, 0, 3):
        factor = scale * SLOPES[row][i]
        if i == row:
            continue
        if abs(abs(factor) - 1.0) > 1e-9:
            term = factor * parts[i]
            total = term if total is None else total + term
        else:
            total = total + parts[i] if factor > 0 else total - parts[i]
    return total


def halves(x):
    high = x.astype(BF16)
    return high, (x - high.astype(F32)).astype(BF16)


def dot_t(a, b):
    return lax.dot_general(a, b, (((1,), (1,)), ((), ())), preferred_element_type=F32)


def thrice(x):
    return jnp.concatenate([x, x, x], axis=0)


def folded(x):
    return x[0:NODES] + x[NODES : 2 * NODES] + x[2 * NODES : ROWS]


def stored(x):
    return jnp.concatenate([x[NODES : 2 * NODES], x[0:NODES], x[2 * NODES : ROWS]], axis=0)


def one_hot(rows, targets):
    return (rows == targets).astype(F32).astype(BF16)


def picked(x, index):
    rows = x.shape[0]
    if rows < 8:
        index = index[0:rows]
    elif rows > 8:
        index = jnp.concatenate([index] * (rows // 8), axis=0)
    along = lax.GatherDimensionNumbers(
        offset_dims=(),
        collapsed_slice_dims=(1,),
        start_index_map=(1,),
        operand_batching_dims=(0,),
        start_indices_batching_dims=(0,),
    )
    mode = lax.GatherScatterMode.PROMISE_IN_BOUNDS
    return lax.gather(x, index[..., None], along, (1, 1), mode=mode)


def at_end(face):
    return 3 if face % 2 else 0


def x_traces(field, layer, face):
    at = 16 * at_end(face)
    return [field[layer, BASE[c] + at : BASE[c] + at + 16, :] for c in (1, 2)]


def lift_x(target, layer, face, scale, y, z):
    at = 16 * at_end(face)
    rows = slice(BASE[1] + at, BASE[1] + at + 16)
    target[layer, rows, :] += (-scale * parity(1, face, 2)) * z
    rows = slice(BASE[2] + at, BASE[2] + at + 16)
    target[layer, rows, :] += (-scale * parity(2, face, 1)) * y


def add_x(target, field, layer, scale, outer, base=None, ends=None):
    for c, other, sign in ((1, 2, 1.0), (2, 1, -1.0)):
        parts = [field[layer, BASE[other] + 16 * i : BASE[other] + 16 * i + 16, :] for i in range(4)]
        for i in range(4):
            change = slope(parts, i, scale * sign)
            face = {0: 0, 3: 1}.get(i)
            traces = None if face is None else outer(face)
            if traces is not None:
                change += (-scale * parity(c, face, other)) * traces[other - 1]
            rows = slice(BASE[c] + 16 * i, BASE[c] + 16 * i + 16)
            if ends is None:
                change += target[layer, rows, :] if base is None else base[rows]
            elif ends[0] == i:
                change += ends[c]
            target[layer, rows, :] = change
    if base is not None:
        rows = slice(BASE[0], BASE[0] + NODES)
        target[layer, rows, :] = base[rows]


def add_yz(target, field, layer, index, scale, fresh=False):
    for c, other, sign in ((0, 1, 1.0), (1, 0, -1.0)):
        parts = [field[layer, pl.ds(BASE[other] + k, 16, stride=4), :] for k in range(4)]
        for k in range(4):
            change = slope(parts, k, scale * sign)
            if k in (0, 3):
                face = 4 if k == 0 else 5
                got = picked(parts[3 - k], index(layer, face))
                change += (-scale * parity(c, face, other)) * got
            rows = pl.ds(BASE[c] + k, 16, stride=4)
            if fresh and c == 0:
                target[layer, rows, :] = change
            else:
                target[layer, rows, :] += change
    sign = jnp.where(lax.broadcasted_iota(jnp.int32, (8, LAYER), 0) < 4, -1.0, 1.0)
    for k in range(4):
        parts = [field[layer, pl.ds(BASE[0] + 4 * j + k, 8, stride=16), :] for j in range(4)]
        for j in range(4):
            change = slope(parts, j, scale)
            if j in (0, 3):
                face = 2 if j == 0 else 3
                got = picked(parts[3 - j], index(layer, face))
                change += (scale * parity(0, face, 2)) * got
            rows = pl.ds(BASE[0] + 4 * j + k, 8, stride=16)
            target[layer, rows, :] += sign * pltpu.roll(change, 4, 0)


def add_end(target, field, layer, i, index, scale, to_x):
    c, other, sign = (0, 1, 1.0) if to_x else (1, 0, -1.0)
    at = BASE[other] + 16 * i
    parts = [field[layer, pl.ds(at + k, 4, stride=4), :] for k in range(4)]
    for k in range(4):
        change = slope(parts, k, scale * sign)
        if k in (0, 3):
            face = 4 if k == 0 else 5
            got = picked(parts[3 - k], index(layer, face))
            change += (-scale * parity(c, face, other)) * got
        target[layer, pl.ds(BASE[c] + 16 * i + k, 4, stride=4), :] += change
    c, other, sign = (0, 2, -1.0) if to_x else (2, 0, 1.0)
    at = BASE[other] + 16 * i
    parts = [field[layer, at + 4 * j : at + 4 * j + 4, :] for j in range(4)]
    for j in range(4):
        change = slope(parts, j, scale * sign)
        if j in (0, 3):
            face = 2 if j == 0 else 3
            got = picked(parts[3 - j], index(layer, face))
            change += (-scale * parity(c, face, other)) * got
        at = BASE[c] + 16 * i + 4 * j
        target[layer, at : at + 4, :] += change


def add_into_end(target, field, layer, i, index, scale):
    for c, other, sign in ((1, 2, 1.0), (2, 1, -1.0)):
        parts = [field[layer, BASE[other] + 16 * n : BASE[other] + 16 * n + 16, :] for n in range(4)]
        rows = slice(BASE[c] + 16 * i, BASE[c] + 16 * i + 16)
        target[layer, rows, :] += slope(parts, i, scale * sign)
    add_end(target, field, layer, i, index, scale, False)


def passed_back(v, i):
    terms = [
        (SLOPES[i][n] * SLOPES[n][i]) * v[16 * n : 16 * n + 16] for n in range(4) if n != i
    ]
    return terms[0] + terms[1] + terms[2]


def layers_of(x):
    return [x[:, at : at + LAYER] for at in range(0, x.shape[1], LAYER)]


def between(field, index, layer):
    def outer(face):
        if (layer, face) not in ((L0, 1), (L1, 0)):
            return None
        traces = x_traces(field, L0 + L1 - layer, face ^ 1)
        return [picked(t, index(layer, face)) for t in traces]

    return outer


def lone_h(index, fe, fh):
    for layer in (L0, L1):
        add_x(fh, fe, layer, 1.0, between(fe, index, layer))
        add_yz(fh, fe, layer, index, 1.0)


def lone_e(index, fe, fh, acc, drive, v):
    for i, layer in enumerate((L0, L1)):
        add_x(acc, fh, layer, 1.0, between(fh, index, layer), drive[i])
        add_yz(acc, fh, layer, index, 1.0)
        fe[layer] -= thrice(v[i]) * acc[layer]


def lonely(index, fe, fh, acc, drive_of, v, out_h, out_e):
    def ends_of(field):
        return x_traces(field, L1, 1), x_traces(field, L0, 0)

    found = [ends_of(fe)]
    lone_h(index, fe, fh)
    found.append(ends_of(fh))
    for i in range(2):
        out_h[i] = fh[L0 + i]
    lone_e(index, fe, fh, acc, drive_of(), v)
    found.append(ends_of(fe))
    for i in range(2):
        out_e[i] = fe[L0 + i]
    for face, layer in enumerate((L0, L1)):
        add_into_end(fh, fe, layer, at_end(face), index, 1.0)
    found.append(ends_of(fh))
    return [jnp.concatenate(sum(traces, []), axis=0) for traces in zip(*found)]


def respond(index, valid, fe, fh, acc, lone, v, w, near_v, sent_a, sent_b):
    start_e, lone_h1, lone_e1 = lone
    own = (L0, L1)
    sides = ((A1, 1, L0, 0), (B1, 0, L1, 1))
    sent = (sent_a, sent_b)
    empty = jnp.zeros((16, LAYER), F32)

    def rows_at(c, i):
        return slice(BASE[c] + 16 * i, BASE[c] + 16 * i + 16)

    def lifted(face, scale, y, z):
        return (-scale * parity(1, face, 2)) * z, (-scale * parity(2, face, 1)) * y

    def inward(side, start, scale, answers=None):
        near, _, layer, face = sides[side]
        traces = [sent[side][start + 16 * t : start + 16 * t + 16, :] for t in range(2)]
        if answers is not None:
            traces = [a + b for a, b in zip(traces, answers)]
        mask = jnp.concatenate([valid[side]] * 2, axis=0)
        return lifted(face, scale, *[picked(t, index(layer, face)) * mask for t in traces])

    def outward(side, alone, scale, answers=None):
        near, face, layer, own_face = sides[side]
        traces = x_traces(alone, layer - L0, own_face)
        if answers is not None:
            traces = [a + b for a, b in zip(traces, answers)]
        return lifted(face, scale, *[picked(t, index(near, face)) for t in traces])

    def put(target, layer, i, pair):
        target[layer, rows_at(1, i), :] = pair[0]
        target[layer, rows_at(2, i), :] = pair[1]

    def add(target, layer, i, pair):
        target[layer, rows_at(1, i), :] += pair[0]
        target[layer, rows_at(2, i), :] += pair[1]

    near_h, own_h = [], []
    for side, (near, face, layer, own_face) in enumerate(sides):
        near_h.append(outward(side, start_e, 1.0))
        own_h.append(inward(side, E_START, 1.0))
        put(fh, near, at_end(face), near_h[side])
        put(fh, layer, at_end(own_face), own_h[side])

    for side, (near, face, layer, own_face) in enumerate(sides):
        i = at_end(face)
        pair = outward(side, lone_h1, 1.0, own_h[side])
        acc[near, rows_at(0, i), :] = empty
        add_end(acc, fh, near, i, index, 1.0, True)
        scale = -near_v[side, 0:16, :]
        put(fe, near, i, [scale * part for part in pair])
        fe[near, rows_at(0, i), :] = scale * acc[near, rows_at(0, i), :]

        i = at_end(own_face)
        pair = inward(side, H_FIRST, 1.0, near_h[side])
        acc[layer, rows_at(0, i), :] = empty
        add_end(acc, fh, layer, i, index, 1.0, True)
        for n in range(4):
            scale = -v[side, 16 * n : 16 * n + 16, :]
            if n == i:
                put(fe, layer, n, [scale * part for part in pair])
                fe[layer, rows_at(0, n), :] = scale * acc[layer, rows_at(0, n), :]
            else:
                y, z = own_h[side]
                put(fe, layer, n, [scale * (SLOPES[n][i] * z), scale * (-SLOPES[n][i] * y)])
                fe[layer, rows_at(0, n), :] = empty

    for side, (near, face, layer, own_face) in enumerate(sides):
        i = at_end(face)
        pair = outward(side, lone_e1, 1.0, x_traces(fe, layer, own_face))
        back = 1.0 + near_v[side, 16:32, :]
        put(fh, near, i, [a + back * b for a, b in zip(pair, near_h[side])])
        add_end(fh, fe, near, i, index, 1.0, False)
        ends = (at_end(own_face), *own_h[side])
        add_x(fh, fe, layer, 1.0, between(fe, index, layer), None, ends)
        add_yz(fh, fe, layer, index, 1.0, True)
        i = at_end(own_face)
        add(fh, layer, i, inward(side, E_FIRST, 1.0, x_traces(fe, near, face)))

    current, second_e = [], []
    for i, layer in enumerate(own):
        current.append(thrice(w[i]) * fe[layer])
        add_x(acc, fh, layer, 1.0, between(fh, index, layer), current[i])
        add_yz(acc, fh, layer, index, 1.0)
    for side, (near, face, layer, own_face) in enumerate(sides):
        i = at_end(own_face)
        add(acc, layer, i, inward(side, H_SECOND, 1.0, x_traces(fh, near, face)))
        second_e.append(fe[layer] - thrice(v[side]) * acc[layer])
    return second_e, current


def odd_rank():
    return lax.rem(lax.axis_index("space"), 2) == 1


def send(across, inside, at, up, down):
    odd = odd_rank()
    rows = slice(at, at + up.shape[0])
    across[rows, :] = jnp.where(odd, up, down)
    inside[rows, :] = jnp.where(odd, down, up)


def sides_of(across, inside, a, b, rows):
    odd = odd_rank()
    from_across, from_inside = across[0:rows, :], inside[0:rows, :]
    a[...] = jnp.where(odd, from_inside, from_across)
    b[...] = jnp.where(odd, from_across, from_inside)


def first_kernel(
    e_in, h_in, j_in, v_in, w_in, near_in, ports_in, profile_in, design_in, *rest
):
    design, start_e, lone_h1, lone_e1, first_j, v, w, source, places, valid = rest[:10]
    across, inside, fe, fh, acc, neighbor, ports, profile, e, h, j, v_all, w_all, sems = rest[10:]
    started = []

    def fetch(*pairs):
        copies = []
        for origin, target in pairs:
            copies.append(pltpu.make_async_copy(origin, target, sems.at[len(started)]))
            copies[-1].start()
            started.append(None)
        return copies

    def wait(copies):
        for copy in copies:
            copy.wait()

    scatter = fetch((near_in, neighbor), (ports_in, ports), (profile_in, profile))
    fields = fetch((e_in, e), (h_in, h))
    weights = fetch((j_in, j), (w_in, w_all), (v_in, v_all))
    later = fetch((design_in, design))

    wait(scatter)
    found = neighbor[...]
    place = jnp.where(found < 0, 0, jnp.bitwise_and(found, LAYER - 1))
    for i in range(2):
        columns = slice(i * LAYER, (i + 1) * LAYER)
        for face in range(6):
            places[6 * i + face] = jnp.broadcast_to(place[face : face + 1, columns], (8, LAYER))
        there = (found[i : i + 1, columns] >= 0).astype(F32)
        valid[i] = jnp.broadcast_to(there, (8, LAYER))
    targets = lax.broadcasted_iota(jnp.int32, (2 * LAYER, ports.shape[1]), 0)
    spread_hot = one_hot(targets, jnp.bitwise_and(ports[...], 2 * LAYER - 1))
    high, low = halves(PER_STEP * profile[...])
    spread = layers_of(dot_t(high, spread_hot) + dot_t(low, spread_hot))
    for i in range(2):
        source[i] = stored(spread[i])

    wait(fields)
    electric = [stored(part) for part in layers_of(e[...])]
    magnetic = [stored(part) for part in layers_of(h[...])]
    for i in range(2):
        start_e[i] = electric[i]
        fe[L0 + i] = electric[i]
        fh[L0 + i] = PER_STEP * magnetic[i]

    scale = []

    def drive_of():
        wait(weights)
        current = [stored(part) for part in layers_of(j[...])]
        weight = layers_of(w_all[...])
        drive = []
        for i, part in enumerate(layers_of(v_all[...])):
            scale.append((TIME_STEP * TIME_STEP) * part)
            v[i] = scale[i]
            w[i] = weight[i]
            now = (KEEP * PER_STEP) * current[i] + thrice(weight[i]) * start_e[i]
            first_j[i] = now
            drive.append(now + source[i])
        return drive

    up, down = lonely(own_index(places), fe, fh, acc, drive_of, v, lone_h1, lone_e1)
    wait(later)
    send(across, inside, 0, up, down)
    send(across, inside, V_NEAR, scale[1][48:NODES], scale[0][0:16])
    send(across, inside, V_NEAR + 16, passed_back(scale[1], 3), passed_back(scale[0], 0))
    blank = jnp.zeros((2, LAYER), F32)
    place = place.astype(F32)
    send(
        across,
        inside,
        N_NEAR,
        jnp.concatenate([place[:, LAYER : 2 * LAYER], blank], axis=0),
        jnp.concatenate([place[:, 0:LAYER], blank], axis=0),
    )


def own_index(places):
    def index(layer, face):
        return places[6 * (layer - L0) + face]

    return index


def second_lone_step(lone_h1, lone_e1, first_j, v, w, source, places, work):
    fe, fh, acc = work
    index = own_index(places)
    for i in range(2):
        fe[L0 + i] = lone_e1[i]
        fh[L0 + i] = lone_h1[i]
    current = [KEEP * first_j[i] + thrice(w[i]) * lone_e1[i] for i in range(2)]
    lone_h(index, fe, fh)
    lone_e(index, fe, fh, acc, [current[i] + source[i] for i in range(2)], v)
    return current


def lone_kernel(lone_h1, lone_e1, first_j, v, w, source, places, design, *rest):
    lone_h2, lone_e2, lone_j2, pixels, fe, fh, acc = rest
    pixel = jnp.bitwise_and(design[...], PIX_DEV - 1)
    pixels[...] = one_hot(lax.broadcasted_iota(jnp.int32, pixels.shape, 0), pixel)
    current = second_lone_step(
        lone_h1, lone_e1, first_j, v, w, source, places, (fe, fh, acc)
    )
    for i in range(2):
        lone_h2[i] = fh[L0 + i]
        lone_e2[i] = fe[L0 + i]
        lone_j2[i] = current[i]


def index_of(places, near_places):
    def index(layer, face):
        if layer in (L0, L1):
            return places[6 * (layer - L0) + face]
        return near_places[6 * (layer == B1) + face]

    return index


def middle_kernel(
    start_e, lone_h1, lone_e1, lone_h2, lone_e2, lone_j2, v, w, source, places,
    valid, across_in, inside_in, *rest
):
    end_e, next_h, next_e, next_j, answer_e, answer_j, near_v, near_places = rest[:8]
    inside, across = rest[8:10]
    fe, fh, acc, sent_a, sent_b = rest[10:]
    sides_of(across_in, inside_in, sent_a, sent_b, FIRST)
    for side, sent in enumerate((sent_a, sent_b)):
        near_v[side] = sent[V_NEAR : V_NEAR + 32, :]
        place = sent[N_NEAR : N_NEAR + 8, :].astype(jnp.int32)
        for face in range(6):
            near_places[6 * side + face] = jnp.broadcast_to(place[face : face + 1], (8, LAYER))
    index = index_of(places, near_places)
    second_e, current = respond(
        index, valid, fe, fh, acc, (start_e, lone_h1, lone_e1), v, w, near_v, sent_a, sent_b
    )
    drive = []
    for i in range(2):
        answer_e[i] = fe[L0 + i]
        answer_j[i] = current[i]
        electric = lone_e2[i] + second_e[i]
        end_e[i] = electric
        fe[L0 + i] = electric
        fh[L0 + i] += lone_h2[i]
        before = lone_j2[i] + current[i]
        now = KEEP * before + thrice(w[i]) * electric
        next_j[i] = now
        drive.append(now + source[i])
    up, down = lonely(index, fe, fh, acc, lambda: drive, v, next_h, next_e)
    send(across, inside, 0, up, down)


def early_kernel(
    lone_e1, answer_e, lone_j1, lone_j2, answer_j, end_e, next_h, next_e, next_j, v, w,
    source, places, levels, *rest
):
    last_h, last_e, out, changes, fe, fh, acc = rest
    current = second_lone_step(next_h, next_e, next_j, v, w, source, places, (fe, fh, acc))
    for i in range(2):
        electric = fe[L0 + i]
        last_h[i] = fh[L0 + i]
        last_e[i] = electric
        columns = slice(i * LAYER, (i + 1) * LAYER)
        level = [stored(levels[k, :, columns].astype(F32)) for k in range(5)]
        eps = (lone_e1[i] + answer_e[i]) * (level[1] - level[0])
        eps += end_e[i] * (level[2] - level[1]) + next_e[i] * (level[3] - level[2])
        eps += electric * (level[4] - level[3])
        drude = lone_j1[i] * level[0] + (lone_j2[i] + answer_j[i]) * level[1]
        drude += next_j[i] * level[2] + current[i] * level[3]
        out[0:NODES, columns] = folded(eps)
        out[NODES : 2 * NODES, columns] = TIME_STEP * folded(drude)
        changes[0, i] = level[3] - level[2]
        changes[1, i] = level[4] - level[3]
        changes[2, i] = level[3]


def last_kernel(
    start_e, lone_h1, lone_e1, lone_h2, lone_e2, v, w, places, valid, near_v, near_places,
    inside_in, across_in, changes, early, pixels, *rest
):
    out_e, out_h, sums = rest[:3]
    fe, fh, acc, sent_a, sent_b = rest[3:]
    sides_of(across_in, inside_in, sent_a, sent_b, SECOND)
    second_e, current = respond(
        index_of(places, near_places), valid, fe, fh, acc, (start_e, lone_h1, lone_e1),
        v, w, near_v, sent_a, sent_b,
    )
    parts = []
    for i in range(2):
        out_e[i] = lone_e2[i] + second_e[i]
        out_h[i] = TIME_STEP * (lone_h2[i] + fh[L0 + i])
        eps = folded(fe[L0 + i] * changes[0, i] + second_e[i] * changes[1, i])
        drude = TIME_STEP * folded(current[i] * changes[2, i])
        columns = slice(i * LAYER, (i + 1) * LAYER)
        parts.append(jnp.concatenate([eps, drude], axis=0) + early[:, columns])
    both = jnp.concatenate(parts, axis=1)
    high, low = halves(both)
    sums[...] = dot_t(pixels[...], high) + dot_t(pixels[...], low)


def total_kernel(owners, parts, e, h, out_e, out_h, eps, drude, sums, sems):
    copies = []

    def write(origin, target):
        copies.append(pltpu.make_async_copy(origin, target, sems.at[len(copies)]))
        copies[-1].start()

    for field, target in ((e, out_e), (h, out_h)):
        for i in range(2):
            for c in range(3):
                there = target.at[pl.ds(c * NODES, NODES), pl.ds(i * LAYER, LAYER)]
                write(field.at[i, pl.ds(BASE[c], NODES), :], there)
    share = parts.shape[0] // owners
    total = parts[0:share]
    for owner in range(1, owners):
        total = total + parts[owner * share : (owner + 1) * share]
    total = total * (1.0 / owners)
    sums[0] = total[:, 0:NODES]
    sums[1] = total[:, NODES : 2 * NODES]
    write(sums.at[0], eps)
    write(sums.at[1], drude)
    for copy in copies:
        copy.wait()


def call(kernel, outs, args, scratch=(), spaces=None, out_spaces=None):
    moved = sum(4 * int(np.prod(o.shape)) for o in outs) + sum(
        a.dtype.itemsize * int(np.prod(a.shape)) for a in args
    )
    return pl.pallas_call(
        kernel,
        out_shape=outs,
        in_specs=[pl.BlockSpec(memory_space=s) for s in spaces or [pltpu.VMEM] * len(args)],
        out_specs=[pl.BlockSpec(memory_space=s) for s in out_spaces or [pltpu.VMEM] * len(outs)],
        scratch_shapes=list(scratch),
        compiler_params=pltpu.CompilerParams(vmem_limit_bytes=24 * 1024 * 1024),
        cost_estimate=pl.CostEstimate(flops=moved, bytes_accessed=moved, transcendentals=0),
    )(*args)


def f32(*shape):
    return jax.ShapeDtypeStruct(shape, F32)


def bf16(*shape):
    return jax.ShapeDtypeStruct(shape, BF16)


def exchange(across, inside, inside_first):
    size = lax.axis_size("space")

    def pairs(start):
        found = [(i, i + 1) for i in range(start, size - 1, 2)]
        return found + [(j, i) for i, j in found]

    if inside_first:
        inside = lax.ppermute(inside, "space", pairs(0))
    across = lax.ppermute(across, "space", pairs(1))
    if not inside_first:
        inside = lax.ppermute(inside, "space", pairs(0))
    return across, inside


def local(
    adj_e,
    adj_h,
    adj_j,
    fwd_e,
    inv_eps,
    drude_weight,
    neighbor,
    design_map,
    port_elems,
    port_profile,
):
    count = adj_e.shape[2]
    owners = lax.axis_size("exc")
    levels = fwd_e[0]
    field, nodal = f32(2, ROWS, LAYER), f32(2, NODES, LAYER)
    indices = jax.ShapeDtypeStruct((12, 8, LAYER), jnp.int32)
    work = [pltpu.VMEM((4, ROWS, LAYER), F32)] * 3
    given = [adj_e[0], adj_h[0], adj_j[0], inv_eps, drude_weight]
    given += [neighbor, port_elems, port_profile[0], design_map.reshape(1, count)]
    received = [pltpu.VMEM((FIRST, LAYER), F32)] * 2
    design, start_e, h1, e1, j1, v, w, source, places, valid, *sent = call(
        first_kernel,
        [jax.ShapeDtypeStruct((1, count), jnp.int32)]
        + [field] * 4
        + [nodal, nodal, field, indices, f32(2, 8, LAYER)]
        + [f32(FIRST, LAYER)] * 2,
        [pltpu.with_memory_space_constraint(a, pltpu.HBM) for a in given],
        work
        + [pltpu.VMEM(a.shape, a.dtype) for a in [neighbor, port_elems, port_profile[0]]]
        + [pltpu.VMEM((ROWS, count), F32)] * 3
        + [pltpu.VMEM((NODES, count), F32)] * 2
        + [pltpu.SemaphoreType.DMA((9,))],
        spaces=[pltpu.HBM] * len(given),
    )
    across, inside = exchange(*sent, False)
    h2, e2, j2, pixels = call(
        lone_kernel,
        [field] * 3 + [bf16(PIX_DEV, count)],
        [h1, e1, j1, v, w, source, places, design],
        work,
    )
    end_e, h3, e3, j3, answer_e, answer_j, near_v, near_places, inside, across = call(
        middle_kernel,
        [field] * 6 + [f32(2, 32, LAYER), indices] + [f32(SECOND, LAYER)] * 2,
        [start_e, h1, e1, h2, e2, j2, v, w, source, places, valid, across, inside],
        work + received,
    )
    across, inside = exchange(across, inside, True)
    h4, e4, early, changes = call(
        early_kernel,
        [field] * 2 + [f32(2 * NODES, count), f32(3, 2, ROWS, LAYER)],
        [e1, answer_e, j1, j2, answer_j, end_e, h3, e3, j3, v, w, source, places, levels],
        work,
    )
    e4, h4, sums = call(
        last_kernel,
        [field, field, f32(PIX_DEV, 2 * NODES)],
        [end_e, h3, e3, h4, e4, v, w, places, valid, near_v, near_places]
        + [inside, across, changes, early, pixels],
        work + [pltpu.VMEM((SECOND, LAYER), F32)] * 2,
    )
    parts = lax.all_to_all(sums, "exc", split_axis=0, concat_axis=0, tiled=True)
    share = PIX_DEV // owners
    out_e, out_h, eps, drude = call(
        functools.partial(total_kernel, owners),
        [f32(ROWS, count)] * 2 + [f32(share, NODES)] * 2,
        [parts, e4, h4],
        [pltpu.VMEM((2, share, NODES), F32), pltpu.SemaphoreType.DMA((14,))],
        out_spaces=[pltpu.HBM] * 4,
    )
    return out_e[None], out_h[None], eps.T, drude.T


def solution(mesh):
    return jax.shard_map(
        local,
        mesh=mesh,
        in_specs=(
            P("exc", None, "space"),
            P("exc", None, "space"),
            P("exc", None, "space"),
            P("exc", None, None, "space"),
            P(None, "space"),
            P(None, "space"),
            P(None, "space"),
            P("space"),
            P("exc", "space"),
            P("exc", None, "space"),
        ),
        out_specs=(
            P("exc", None, "space"),
            P("exc", None, "space"),
            P(None, ("space", "exc")),
            P(None, ("space", "exc")),
        ),
        check_vma=False,
    )
```

```python
import functools

import jax
import jax.numpy as jnp
import numpy as np
from jax import lax
from jax.experimental import pallas as pl
from jax.experimental.pallas import tpu as pltpu
from jax.sharding import PartitionSpec as P

NODES = 64
ROWS = 3 * NODES
LAYER = 128
PIX_DEV = 128

TIME_STEP = 0.025
DAMPING = 0.5
KEEP = 1.0 - TIME_STEP * DAMPING

PER_STEP = 1.0 / TIME_STEP

TANGENT = 32
E_START = 0
H_FIRST = 32
E_FIRST = 64
H_SECOND = 96
SECOND = 128
V_NEAR = 128
N_NEAR = V_NEAR + 32
FIRST = N_NEAR + 8

A1, L0, L1, B1 = range(4)

BASE = (NODES, 0, 2 * NODES)

BF16 = jnp.bfloat16
F32 = jnp.float32


def parity(c, face, other):
    d = face // 2
    sign = 1.0 if face % 2 else -1.0
    return 6.0 * sign * (c - d) * (d - other) * (other - c) / 2.0


def off_diagonal():
    points = np.array([-1.0, -1.0 / np.sqrt(5.0), 1.0 / np.sqrt(5.0), 1.0])
    barycentric = np.array(
        [1.0 / np.prod([points[j] - points[k] for k in range(4) if k != j]) for j in range(4)]
    )
    deriv = np.zeros((4, 4))
    for row in range(4):
        for column in range(4):
            if row != column:
                deriv[row, column] = (
                    barycentric[column] / barycentric[row] / (points[row] - points[column])
                )
    return (2.0 * deriv).tolist()


SLOPES = off_diagonal()


def slope(parts, row, scale):
    total = None
    for i in (1, 2, 0, 3):
        factor = scale * SLOPES[row][i]
        if i == row:
            continue
        if abs(abs(factor) - 1.0) > 1e-9:
            term = factor * parts[i]
            total = term if total is None else total + term
        else:
            total = total + parts[i] if factor > 0 else total - parts[i]
    return total


def halves(x):
    high = x.astype(BF16)
    return high, (x - high.astype(F32)).astype(BF16)


def dot_t(a, b):
    return lax.dot_general(a, b, (((1,), (1,)), ((), ())), preferred_element_type=F32)


def thrice(x):
    return jnp.concatenate([x, x, x], axis=0)


def folded(x):
    return x[0:NODES] + x[NODES : 2 * NODES] + x[2 * NODES : ROWS]


def stored(x):
    return jnp.concatenate([x[NODES : 2 * NODES], x[0:NODES], x[2 * NODES : ROWS]], axis=0)


def one_hot(rows, targets):
    return (rows == targets).astype(F32).astype(BF16)


def picked(x, index):
    rows = x.shape[0]
    if rows < 8:
        index = index[0:rows]
    elif rows > 8:
        index = jnp.concatenate([index] * (rows // 8), axis=0)
    along = lax.GatherDimensionNumbers(
        offset_dims=(),
        collapsed_slice_dims=(1,),
        start_index_map=(1,),
        operand_batching_dims=(0,),
        start_indices_batching_dims=(0,),
    )
    mode = lax.GatherScatterMode.PROMISE_IN_BOUNDS
    return lax.gather(x, index[..., None], along, (1, 1), mode=mode)


def at_end(face):
    return 3 if face % 2 else 0


def x_traces(field, layer, face):
    at = 16 * at_end(face)
    return [field[layer, BASE[c] + at : BASE[c] + at + 16, :] for c in (1, 2)]


def lift_x(target, layer, face, scale, y, z):
    at = 16 * at_end(face)
    rows = slice(BASE[1] + at, BASE[1] + at + 16)
    target[layer, rows, :] += (-scale * parity(1, face, 2)) * z
    rows = slice(BASE[2] + at, BASE[2] + at + 16)
    target[layer, rows, :] += (-scale * parity(2, face, 1)) * y


def add_x(target, field, layer, scale, outer, base=None, ends=None):
    for c, other, sign in ((1, 2, 1.0), (2, 1, -1.0)):
        parts = [field[layer, BASE[other] + 16 * i : BASE[other] + 16 * i + 16, :] for i in range(4)]
        for i in range(4):
            change = slope(parts, i, scale * sign)
            face = {0: 0, 3: 1}.get(i)
            traces = None if face is None else outer(face)
            if traces is not None:
                change += (-scale * parity(c, face, other)) * traces[other - 1]
            rows = slice(BASE[c] + 16 * i, BASE[c] + 16 * i + 16)
            if ends is None:
                change += target[layer, rows, :] if base is None else base[rows]
            elif ends[0] == i:
                change += ends[c]
            target[layer, rows, :] = change
    if base is not None:
        rows = slice(BASE[0], BASE[0] + NODES)
        target[layer, rows, :] = base[rows]


def add_yz(target, field, layer, index, scale, fresh=False):
    for c, other, sign in ((0, 1, 1.0), (1, 0, -1.0)):
        parts = [field[layer, pl.ds(BASE[other] + k, 16, stride=4), :] for k in range(4)]
        for k in range(4):
            change = slope(parts, k, scale * sign)
            if k in (0, 3):
                face = 4 if k == 0 else 5
                got = picked(parts[3 - k], index(layer, face))
                change += (-scale * parity(c, face, other)) * got
            rows = pl.ds(BASE[c] + k, 16, stride=4)
            if fresh and c == 0:
                target[layer, rows, :] = change
            else:
                target[layer, rows, :] += change
    first = lax.broadcasted_iota(jnp.int32, (8, LAYER), 0) < 4
    mixed = jnp.where(first, index(layer, 2), index(layer, 3))
    for c, other, sign in ((0, 2, -scale), (2, 0, scale)):

        def pair(upper, lower):
            return jnp.where(first, sign * upper, sign * lower)

        d = SLOPES
        face_low = jnp.where(first, -scale * parity(c, 2, other), 0.0)
        face_high = jnp.where(first, 0.0, -scale * parity(c, 3, other))
        for i in range(4):
            at = BASE[other] + 16 * i
            low, high = field[layer, at : at + 8, :], field[layer, at + 8 : at + 16, :]
            low_turned, high_turned = pltpu.roll(low, 4, 0), pltpu.roll(high, 4, 0)
            got = picked(jnp.where(first, high_turned, low_turned), mixed)
            change_low = pair(d[0][1], d[1][0]) * low_turned + pair(d[0][2], d[1][3]) * high
            change_low += pair(d[0][3], d[1][2]) * high_turned + face_low * got
            change_high = pair(d[2][0], d[3][1]) * low + pair(d[2][1], d[3][0]) * low_turned
            change_high += pair(d[2][3], d[3][2]) * high_turned + face_high * got
            at = BASE[c] + 16 * i
            target[layer, at : at + 8, :] += change_low
            target[layer, at + 8 : at + 16, :] += change_high


def add_end(target, field, layer, i, index, scale, to_x):
    c, other, sign = (0, 1, 1.0) if to_x else (1, 0, -1.0)
    at = BASE[other] + 16 * i
    parts = [field[layer, pl.ds(at + k, 4, stride=4), :] for k in range(4)]
    for k in range(4):
        change = slope(parts, k, scale * sign)
        if k in (0, 3):
            face = 4 if k == 0 else 5
            got = picked(parts[3 - k], index(layer, face))
            change += (-scale * parity(c, face, other)) * got
        target[layer, pl.ds(BASE[c] + 16 * i + k, 4, stride=4), :] += change
    c, other, sign = (0, 2, -1.0) if to_x else (2, 0, 1.0)
    at = BASE[other] + 16 * i
    parts = [field[layer, at + 4 * j : at + 4 * j + 4, :] for j in range(4)]
    for j in range(4):
        change = slope(parts, j, scale * sign)
        if j in (0, 3):
            face = 2 if j == 0 else 3
            got = picked(parts[3 - j], index(layer, face))
            change += (-scale * parity(c, face, other)) * got
        at = BASE[c] + 16 * i + 4 * j
        target[layer, at : at + 4, :] += change


def add_into_end(target, field, layer, i, index, scale):
    for c, other, sign in ((1, 2, 1.0), (2, 1, -1.0)):
        parts = [field[layer, BASE[other] + 16 * n : BASE[other] + 16 * n + 16, :] for n in range(4)]
        rows = slice(BASE[c] + 16 * i, BASE[c] + 16 * i + 16)
        target[layer, rows, :] += slope(parts, i, scale * sign)
    add_end(target, field, layer, i, index, scale, False)


def passed_back(v, i):
    terms = [
        (SLOPES[i][n] * SLOPES[n][i]) * v[16 * n : 16 * n + 16] for n in range(4) if n != i
    ]
    return terms[0] + terms[1] + terms[2]


def layers_of(x):
    return [x[:, at : at + LAYER] for at in range(0, x.shape[1], LAYER)]


def between(field, index, layer):
    def outer(face):
        if (layer, face) not in ((L0, 1), (L1, 0)):
            return None
        traces = x_traces(field, L0 + L1 - layer, face ^ 1)
        return [picked(t, index(layer, face)) for t in traces]

    return outer


def lone_h(index, fe, fh):
    for layer in (L0, L1):
        add_x(fh, fe, layer, 1.0, between(fe, index, layer))
        add_yz(fh, fe, layer, index, 1.0)


def lone_e(index, fe, fh, acc, drive, v):
    for i, layer in enumerate((L0, L1)):
        add_x(acc, fh, layer, 1.0, between(fh, index, layer), drive[i])
        add_yz(acc, fh, layer, index, 1.0)
        fe[layer] -= thrice(v[i]) * acc[layer]


def lonely(index, fe, fh, acc, drive_of, v, out_h, out_e):
    def ends_of(field):
        return x_traces(field, L1, 1), x_traces(field, L0, 0)

    found = [ends_of(fe)]
    lone_h(index, fe, fh)
    found.append(ends_of(fh))
    for i in range(2):
        out_h[i] = fh[L0 + i]
    lone_e(index, fe, fh, acc, drive_of(), v)
    found.append(ends_of(fe))
    for i in range(2):
        out_e[i] = fe[L0 + i]
    for face, layer in enumerate((L0, L1)):
        add_into_end(fh, fe, layer, at_end(face), index, 1.0)
    found.append(ends_of(fh))
    return [jnp.concatenate(sum(traces, []), axis=0) for traces in zip(*found)]


def respond(index, valid, fe, fh, acc, lone, v, w, near_v, sent_a, sent_b):
    start_e, lone_h1, lone_e1 = lone
    own = (L0, L1)
    sides = ((A1, 1, L0, 0), (B1, 0, L1, 1))
    sent = (sent_a, sent_b)
    empty = jnp.zeros((16, LAYER), F32)

    def rows_at(c, i):
        return slice(BASE[c] + 16 * i, BASE[c] + 16 * i + 16)

    def lifted(face, scale, y, z):
        return (-scale * parity(1, face, 2)) * z, (-scale * parity(2, face, 1)) * y

    def inward(side, start, scale, answers=None):
        near, _, layer, face = sides[side]
        traces = [sent[side][start + 16 * t : start + 16 * t + 16, :] for t in range(2)]
        if answers is not None:
            traces = [a + b for a, b in zip(traces, answers)]
        mask = jnp.concatenate([valid[side]] * 2, axis=0)
        return lifted(face, scale, *[picked(t, index(layer, face)) * mask for t in traces])

    def outward(side, alone, scale, answers=None):
        near, face, layer, own_face = sides[side]
        traces = x_traces(alone, layer - L0, own_face)
        if answers is not None:
            traces = [a + b for a, b in zip(traces, answers)]
        return lifted(face, scale, *[picked(t, index(near, face)) for t in traces])

    def put(target, layer, i, pair):
        target[layer, rows_at(1, i), :] = pair[0]
        target[layer, rows_at(2, i), :] = pair[1]

    def add(target, layer, i, pair):
        target[layer, rows_at(1, i), :] += pair[0]
        target[layer, rows_at(2, i), :] += pair[1]

    near_h, own_h = [], []
    for side, (near, face, layer, own_face) in enumerate(sides):
        near_h.append(outward(side, start_e, 1.0))
        own_h.append(inward(side, E_START, 1.0))
        put(fh, near, at_end(face), near_h[side])
        put(fh, layer, at_end(own_face), own_h[side])

    for side, (near, face, layer, own_face) in enumerate(sides):
        i = at_end(face)
        pair = outward(side, lone_h1, 1.0, own_h[side])
        acc[near, rows_at(0, i), :] = empty
        add_end(acc, fh, near, i, index, 1.0, True)
        scale = -near_v[side, 0:16, :]
        put(fe, near, i, [scale * part for part in pair])
        fe[near, rows_at(0, i), :] = scale * acc[near, rows_at(0, i), :]

        i = at_end(own_face)
        pair = inward(side, H_FIRST, 1.0, near_h[side])
        acc[layer, rows_at(0, i), :] = empty
        add_end(acc, fh, layer, i, index, 1.0, True)
        for n in range(4):
            scale = -v[side, 16 * n : 16 * n + 16, :]
            if n == i:
                put(fe, layer, n, [scale * part for part in pair])
                fe[layer, rows_at(0, n), :] = scale * acc[layer, rows_at(0, n), :]
            else:
                y, z = own_h[side]
                put(fe, layer, n, [scale * (SLOPES[n][i] * z), scale * (-SLOPES[n][i] * y)])
                fe[layer, rows_at(0, n), :] = empty

    for side, (near, face, layer, own_face) in enumerate(sides):
        i = at_end(face)
        pair = outward(side, lone_e1, 1.0, x_traces(fe, layer, own_face))
        back = 1.0 + near_v[side, 16:32, :]
        put(fh, near, i, [a + back * b for a, b in zip(pair, near_h[side])])
        add_end(fh, fe, near, i, index, 1.0, False)
        ends = (at_end(own_face), *own_h[side])
        add_x(fh, fe, layer, 1.0, between(fe, index, layer), None, ends)
        add_yz(fh, fe, layer, index, 1.0, True)
        i = at_end(own_face)
        add(fh, layer, i, inward(side, E_FIRST, 1.0, x_traces(fe, near, face)))

    current, second_e = [], []
    for i, layer in enumerate(own):
        current.append(thrice(w[i]) * fe[layer])
        add_x(acc, fh, layer, 1.0, between(fh, index, layer), current[i])
        add_yz(acc, fh, layer, index, 1.0)
    for side, (near, face, layer, own_face) in enumerate(sides):
        i = at_end(own_face)
        add(acc, layer, i, inward(side, H_SECOND, 1.0, x_traces(fh, near, face)))
        second_e.append(fe[layer] - thrice(v[side]) * acc[layer])
    return second_e, current


def odd_rank():
    return lax.rem(lax.axis_index("space"), 2) == 1


def send(across, inside, at, up, down):
    odd = odd_rank()
    rows = slice(at, at + up.shape[0])
    across[rows, :] = jnp.where(odd, up, down)
    inside[rows, :] = jnp.where(odd, down, up)


def sides_of(across, inside, a, b, rows):
    odd = odd_rank()
    from_across, from_inside = across[0:rows, :], inside[0:rows, :]
    a[...] = jnp.where(odd, from_inside, from_across)
    b[...] = jnp.where(odd, from_across, from_inside)


def first_kernel(
    e_in, h_in, j_in, v_in, w_in, near_in, ports_in, profile_in, design_in, *rest
):
    design, start_e, lone_h1, lone_e1, first_j, v, w, source, places, valid = rest[:10]
    across, inside, fe, fh, acc, neighbor, ports, profile, e, h, j, v_all, w_all, sems = rest[10:]
    started = []

    def fetch(*pairs):
        copies = []
        for origin, target in pairs:
            copies.append(pltpu.make_async_copy(origin, target, sems.at[len(started)]))
            copies[-1].start()
            started.append(None)
        return copies

    def wait(copies):
        for copy in copies:
            copy.wait()

    scatter = fetch((near_in, neighbor), (ports_in, ports), (profile_in, profile))
    fields = fetch((e_in, e), (h_in, h))
    weights = fetch((j_in, j), (w_in, w_all), (v_in, v_all))
    later = fetch((design_in, design))

    wait(scatter)
    found = neighbor[...]
    place = jnp.where(found < 0, 0, jnp.bitwise_and(found, LAYER - 1))
    for i in range(2):
        columns = slice(i * LAYER, (i + 1) * LAYER)
        for face in range(6):
            places[6 * i + face] = jnp.broadcast_to(place[face : face + 1, columns], (8, LAYER))
        there = (found[i : i + 1, columns] >= 0).astype(F32)
        valid[i] = jnp.broadcast_to(there, (8, LAYER))
    targets = lax.broadcasted_iota(jnp.int32, (2 * LAYER, ports.shape[1]), 0)
    spread_hot = one_hot(targets, jnp.bitwise_and(ports[...], 2 * LAYER - 1))
    high, low = halves(PER_STEP * profile[...])
    spread = layers_of(dot_t(high, spread_hot) + dot_t(low, spread_hot))
    for i in range(2):
        source[i] = stored(spread[i])

    wait(fields)
    electric = [stored(part) for part in layers_of(e[...])]
    magnetic = [stored(part) for part in layers_of(h[...])]
    for i in range(2):
        start_e[i] = electric[i]
        fe[L0 + i] = electric[i]
        fh[L0 + i] = PER_STEP * magnetic[i]

    scale = []

    def drive_of():
        wait(weights)
        current = [stored(part) for part in layers_of(j[...])]
        weight = layers_of(w_all[...])
        drive = []
        for i, part in enumerate(layers_of(v_all[...])):
            scale.append((TIME_STEP * TIME_STEP) * part)
            v[i] = scale[i]
            w[i] = weight[i]
            now = (KEEP * PER_STEP) * current[i] + thrice(weight[i]) * start_e[i]
            first_j[i] = now
            drive.append(now + source[i])
        return drive

    up, down = lonely(own_index(places), fe, fh, acc, drive_of, v, lone_h1, lone_e1)
    wait(later)
    send(across, inside, 0, up, down)
    send(across, inside, V_NEAR, scale[1][48:NODES], scale[0][0:16])
    send(across, inside, V_NEAR + 16, passed_back(scale[1], 3), passed_back(scale[0], 0))
    blank = jnp.zeros((2, LAYER), F32)
    place = place.astype(F32)
    send(
        across,
        inside,
        N_NEAR,
        jnp.concatenate([place[:, LAYER : 2 * LAYER], blank], axis=0),
        jnp.concatenate([place[:, 0:LAYER], blank], axis=0),
    )


def own_index(places):
    def index(layer, face):
        return places[6 * (layer - L0) + face]

    return index


def second_lone_step(lone_h1, lone_e1, first_j, v, w, source, places, work):
    fe, fh, acc = work
    index = own_index(places)
    for i in range(2):
        fe[L0 + i] = lone_e1[i]
        fh[L0 + i] = lone_h1[i]
    current = [KEEP * first_j[i] + thrice(w[i]) * lone_e1[i] for i in range(2)]
    lone_h(index, fe, fh)
    lone_e(index, fe, fh, acc, [current[i] + source[i] for i in range(2)], v)
    return current


def lone_kernel(lone_h1, lone_e1, first_j, v, w, source, places, design, *rest):
    lone_h2, lone_e2, lone_j2, pixels, fe, fh, acc = rest
    pixel = jnp.bitwise_and(design[...], PIX_DEV - 1)
    pixels[...] = one_hot(lax.broadcasted_iota(jnp.int32, pixels.shape, 0), pixel)
    current = second_lone_step(
        lone_h1, lone_e1, first_j, v, w, source, places, (fe, fh, acc)
    )
    for i in range(2):
        lone_h2[i] = fh[L0 + i]
        lone_e2[i] = fe[L0 + i]
        lone_j2[i] = current[i]


def index_of(places, near_places):
    def index(layer, face):
        if layer in (L0, L1):
            return places[6 * (layer - L0) + face]
        return near_places[6 * (layer == B1) + face]

    return index


def middle_kernel(
    start_e, lone_h1, lone_e1, lone_h2, lone_e2, lone_j2, v, w, source, places,
    valid, across_in, inside_in, *rest
):
    end_e, next_h, next_e, next_j, answer_e, answer_j, near_v, near_places = rest[:8]
    inside, across = rest[8:10]
    fe, fh, acc, sent_a, sent_b = rest[10:]
    sides_of(across_in, inside_in, sent_a, sent_b, FIRST)
    for side, sent in enumerate((sent_a, sent_b)):
        near_v[side] = sent[V_NEAR : V_NEAR + 32, :]
        place = sent[N_NEAR : N_NEAR + 8, :].astype(jnp.int32)
        for face in range(6):
            near_places[6 * side + face] = jnp.broadcast_to(place[face : face + 1], (8, LAYER))
    index = index_of(places, near_places)
    second_e, current = respond(
        index, valid, fe, fh, acc, (start_e, lone_h1, lone_e1), v, w, near_v, sent_a, sent_b
    )
    drive = []
    for i in range(2):
        answer_e[i] = fe[L0 + i]
        answer_j[i] = current[i]
        electric = lone_e2[i] + second_e[i]
        end_e[i] = electric
        fe[L0 + i] = electric
        fh[L0 + i] += lone_h2[i]
        before = lone_j2[i] + current[i]
        now = KEEP * before + thrice(w[i]) * electric
        next_j[i] = now
        drive.append(now + source[i])
    up, down = lonely(index, fe, fh, acc, lambda: drive, v, next_h, next_e)
    send(across, inside, 0, up, down)


def early_kernel(
    lone_e1, answer_e, lone_j1, lone_j2, answer_j, end_e, next_h, next_e, next_j, v, w,
    source, places, levels, *rest
):
    last_h, last_e, out, changes, fe, fh, acc = rest
    current = second_lone_step(next_h, next_e, next_j, v, w, source, places, (fe, fh, acc))
    for i in range(2):
        electric = fe[L0 + i]
        last_h[i] = fh[L0 + i]
        last_e[i] = electric
        columns = slice(i * LAYER, (i + 1) * LAYER)
        level = [stored(levels[k, :, columns].astype(F32)) for k in range(5)]
        eps = (lone_e1[i] + answer_e[i]) * (level[1] - level[0])
        eps += end_e[i] * (level[2] - level[1]) + next_e[i] * (level[3] - level[2])
        eps += electric * (level[4] - level[3])
        drude = lone_j1[i] * level[0] + (lone_j2[i] + answer_j[i]) * level[1]
        drude += next_j[i] * level[2] + current[i] * level[3]
        out[0:NODES, columns] = folded(eps)
        out[NODES : 2 * NODES, columns] = TIME_STEP * folded(drude)
        changes[0, i] = level[3] - level[2]
        changes[1, i] = level[4] - level[3]
        changes[2, i] = level[3]


def last_kernel(
    start_e, lone_h1, lone_e1, lone_h2, lone_e2, v, w, places, valid, near_v, near_places,
    inside_in, across_in, changes, early, pixels, *rest
):
    out_e, out_h, sums = rest[:3]
    fe, fh, acc, sent_a, sent_b = rest[3:]
    sides_of(across_in, inside_in, sent_a, sent_b, SECOND)
    second_e, current = respond(
        index_of(places, near_places), valid, fe, fh, acc, (start_e, lone_h1, lone_e1),
        v, w, near_v, sent_a, sent_b,
    )
    parts = []
    for i in range(2):
        columns = slice(i * LAYER, (i + 1) * LAYER)
        electric = lone_e2[i] + second_e[i]
        magnetic = TIME_STEP * (lone_h2[i] + fh[L0 + i])
        for c in range(3):
            rows, there = slice(BASE[c], BASE[c] + NODES), slice(c * NODES, (c + 1) * NODES)
            out_e[there, columns] = electric[rows]
            out_h[there, columns] = magnetic[rows]
        eps = folded(fe[L0 + i] * changes[0, i] + second_e[i] * changes[1, i])
        drude = TIME_STEP * folded(current[i] * changes[2, i])
        parts.append(jnp.concatenate([eps, drude], axis=0) + early[:, columns])
    both = jnp.concatenate(parts, axis=1)
    high, low = halves(both)
    sums[...] = dot_t(pixels[...], high) + dot_t(pixels[...], low)


def total_kernel(owners, parts, e, h, out_e, out_h, eps, drude, sums, sems):
    copies = []

    def write(origin, target):
        copies.append(pltpu.make_async_copy(origin, target, sems.at[len(copies)]))
        copies[-1].start()

    write(e, out_e)
    write(h, out_h)
    share = parts.shape[0] // owners
    total = parts[0:share]
    for owner in range(1, owners):
        total = total + parts[owner * share : (owner + 1) * share]
    total = total * (1.0 / owners)
    sums[0] = total[:, 0:NODES]
    sums[1] = total[:, NODES : 2 * NODES]
    write(sums.at[0], eps)
    write(sums.at[1], drude)
    for copy in copies:
        copy.wait()


def call(kernel, outs, args, scratch=(), spaces=None, out_spaces=None):
    moved = sum(4 * int(np.prod(o.shape)) for o in outs) + sum(
        a.dtype.itemsize * int(np.prod(a.shape)) for a in args
    )
    return pl.pallas_call(
        kernel,
        out_shape=outs,
        in_specs=[pl.BlockSpec(memory_space=s) for s in spaces or [pltpu.VMEM] * len(args)],
        out_specs=[pl.BlockSpec(memory_space=s) for s in out_spaces or [pltpu.VMEM] * len(outs)],
        scratch_shapes=list(scratch),
        compiler_params=pltpu.CompilerParams(vmem_limit_bytes=24 * 1024 * 1024),
        cost_estimate=pl.CostEstimate(flops=moved, bytes_accessed=moved, transcendentals=0),
    )(*args)


def f32(*shape):
    return jax.ShapeDtypeStruct(shape, F32)


def bf16(*shape):
    return jax.ShapeDtypeStruct(shape, BF16)


def exchange(across, inside, inside_first):
    size = lax.axis_size("space")

    def pairs(start):
        found = [(i, i + 1) for i in range(start, size - 1, 2)]
        return found + [(j, i) for i, j in found]

    if inside_first:
        inside = lax.ppermute(inside, "space", pairs(0))
    across = lax.ppermute(across, "space", pairs(1))
    if not inside_first:
        inside = lax.ppermute(inside, "space", pairs(0))
    return across, inside


def local(
    adj_e,
    adj_h,
    adj_j,
    fwd_e,
    inv_eps,
    drude_weight,
    neighbor,
    design_map,
    port_elems,
    port_profile,
):
    count = adj_e.shape[2]
    owners = lax.axis_size("exc")
    levels = fwd_e[0]
    field, nodal = f32(2, ROWS, LAYER), f32(2, NODES, LAYER)
    indices = jax.ShapeDtypeStruct((12, 8, LAYER), jnp.int32)
    work = [pltpu.VMEM((4, ROWS, LAYER), F32)] * 3
    given = [adj_e[0], adj_h[0], adj_j[0], inv_eps, drude_weight]
    given += [neighbor, port_elems, port_profile[0], design_map.reshape(1, count)]
    received = [pltpu.VMEM((FIRST, LAYER), F32)] * 2
    design, start_e, h1, e1, j1, v, w, source, places, valid, *sent = call(
        first_kernel,
        [jax.ShapeDtypeStruct((1, count), jnp.int32)]
        + [field] * 4
        + [nodal, nodal, field, indices, f32(2, 8, LAYER)]
        + [f32(FIRST, LAYER)] * 2,
        [pltpu.with_memory_space_constraint(a, pltpu.HBM) for a in given],
        work
        + [pltpu.VMEM(a.shape, a.dtype) for a in [neighbor, port_elems, port_profile[0]]]
        + [pltpu.VMEM((ROWS, count), F32)] * 3
        + [pltpu.VMEM((NODES, count), F32)] * 2
        + [pltpu.SemaphoreType.DMA((9,))],
        spaces=[pltpu.HBM] * len(given),
    )
    across, inside = exchange(*sent, False)
    h2, e2, j2, pixels = call(
        lone_kernel,
        [field] * 3 + [bf16(PIX_DEV, count)],
        [h1, e1, j1, v, w, source, places, design],
        work,
    )
    end_e, h3, e3, j3, answer_e, answer_j, near_v, near_places, inside, across = call(
        middle_kernel,
        [field] * 6 + [f32(2, 32, LAYER), indices] + [f32(SECOND, LAYER)] * 2,
        [start_e, h1, e1, h2, e2, j2, v, w, source, places, valid, across, inside],
        work + received,
    )
    across, inside = exchange(across, inside, True)
    h4, e4, early, changes = call(
        early_kernel,
        [field] * 2 + [f32(2 * NODES, count), f32(3, 2, ROWS, LAYER)],
        [e1, answer_e, j1, j2, answer_j, end_e, h3, e3, j3, v, w, source, places, levels],
        work,
    )
    e4, h4, sums = call(
        last_kernel,
        [f32(ROWS, count)] * 2 + [f32(PIX_DEV, 2 * NODES)],
        [end_e, h3, e3, h4, e4, v, w, places, valid, near_v, near_places]
        + [inside, across, changes, early, pixels],
        work + [pltpu.VMEM((SECOND, LAYER), F32)] * 2,
    )
    parts = lax.all_to_all(sums, "exc", split_axis=0, concat_axis=0, tiled=True)
    share = PIX_DEV // owners
    out_e, out_h, eps, drude = call(
        functools.partial(total_kernel, owners),
        [f32(ROWS, count)] * 2 + [f32(share, NODES)] * 2,
        [parts, e4, h4],
        [pltpu.VMEM((2, share, NODES), F32), pltpu.SemaphoreType.DMA((4,))],
        out_spaces=[pltpu.HBM] * 4,
    )
    return out_e[None], out_h[None], eps.T, drude.T


def solution(mesh):
    return jax.shard_map(
        local,
        mesh=mesh,
        in_specs=(
            P("exc", None, "space"),
            P("exc", None, "space"),
            P("exc", None, "space"),
            P("exc", None, None, "space"),
            P(None, "space"),
            P(None, "space"),
            P(None, "space"),
            P("space"),
            P("exc", "space"),
            P("exc", None, "space"),
        ),
        out_specs=(
            P("exc", None, "space"),
            P("exc", None, "space"),
            P(None, ("space", "exc")),
            P(None, ("space", "exc")),
        ),
        check_vma=False,
    )
```

```python
import functools

import jax
import jax.numpy as jnp
import numpy as np
from jax import lax
from jax.experimental import pallas as pl
from jax.experimental.pallas import tpu as pltpu
from jax.sharding import PartitionSpec as P

NODES = 64
ROWS = 3 * NODES
LAYER = 128
PIX_DEV = 128

TIME_STEP = 0.025
DAMPING = 0.5
KEEP = 1.0 - TIME_STEP * DAMPING

PER_STEP = 1.0 / TIME_STEP

TANGENT = 32
E_START = 0
H_FIRST = 32
E_FIRST = 64
H_SECOND = 96
SECOND = 128
V_NEAR = 128
N_NEAR = V_NEAR + 32
FIRST = N_NEAR + 8

A1, L0, L1, B1 = range(4)

BASE = (NODES, 0, 2 * NODES)

BF16 = jnp.bfloat16
F32 = jnp.float32


def parity(c, face, other):
    d = face // 2
    sign = 1.0 if face % 2 else -1.0
    return 6.0 * sign * (c - d) * (d - other) * (other - c) / 2.0


def off_diagonal():
    points = np.array([-1.0, -1.0 / np.sqrt(5.0), 1.0 / np.sqrt(5.0), 1.0])
    barycentric = np.array(
        [1.0 / np.prod([points[j] - points[k] for k in range(4) if k != j]) for j in range(4)]
    )
    deriv = np.zeros((4, 4))
    for row in range(4):
        for column in range(4):
            if row != column:
                deriv[row, column] = (
                    barycentric[column] / barycentric[row] / (points[row] - points[column])
                )
    return (2.0 * deriv).tolist()


SLOPES = off_diagonal()


def slope(parts, row, scale):
    total = None
    for i in (1, 2, 0, 3):
        factor = scale * SLOPES[row][i]
        if i == row:
            continue
        if abs(abs(factor) - 1.0) > 1e-9:
            term = factor * parts[i]
            total = term if total is None else total + term
        else:
            total = total + parts[i] if factor > 0 else total - parts[i]
    return total


def halves(x):
    high = x.astype(BF16)
    return high, (x - high.astype(F32)).astype(BF16)


def dot_t(a, b):
    return lax.dot_general(a, b, (((1,), (1,)), ((), ())), preferred_element_type=F32)


def thrice(x):
    return jnp.concatenate([x, x, x], axis=0)


def folded(x):
    return x[0:NODES] + x[NODES : 2 * NODES] + x[2 * NODES : ROWS]


def stored(x):
    return jnp.concatenate([x[NODES : 2 * NODES], x[0:NODES], x[2 * NODES : ROWS]], axis=0)


def one_hot(rows, targets):
    return (rows == targets).astype(F32).astype(BF16)


def picked(x, index):
    rows = x.shape[0]
    if rows < 8:
        index = index[0:rows]
    elif rows > 8:
        index = jnp.concatenate([index] * (rows // 8), axis=0)
    along = lax.GatherDimensionNumbers(
        offset_dims=(),
        collapsed_slice_dims=(1,),
        start_index_map=(1,),
        operand_batching_dims=(0,),
        start_indices_batching_dims=(0,),
    )
    mode = lax.GatherScatterMode.PROMISE_IN_BOUNDS
    return lax.gather(x, index[..., None], along, (1, 1), mode=mode)


def at_end(face):
    return 3 if face % 2 else 0


def x_traces(field, layer, face):
    at = 16 * at_end(face)
    return [field[layer, BASE[c] + at : BASE[c] + at + 16, :] for c in (1, 2)]


def lift_x(target, layer, face, scale, y, z):
    at = 16 * at_end(face)
    rows = slice(BASE[1] + at, BASE[1] + at + 16)
    target[layer, rows, :] += (-scale * parity(1, face, 2)) * z
    rows = slice(BASE[2] + at, BASE[2] + at + 16)
    target[layer, rows, :] += (-scale * parity(2, face, 1)) * y


def rates(field, layer, index, outer, planes, use):
    for c, other, sign in ((0, 1, 1.0), (1, 0, -1.0)):
        parts = [field[layer, pl.ds(BASE[other] + k, 16, stride=4), :] for k in range(4)]
        for k in range(4):
            change = slope(parts, k, sign)
            if k in (0, 3):
                face = 4 if k == 0 else 5
                got = picked(parts[3 - k], index(layer, face))
                change += -parity(c, face, other) * got
            planes[layer, pl.ds(NODES * c + k, 16, stride=4), :] = change
    block = [
        [field[layer, BASE[c] + 8 * n : BASE[c] + 8 * n + 8, :] for n in range(8)] for c in range(3)
    ]

    first = lax.broadcasted_iota(jnp.int32, (8, LAYER), 0) < 4
    mixed = jnp.where(first, index(layer, 2), index(layer, 3))
    d = SLOPES

    def in_y(c, other, sign, i):
        def pair(upper, lower):
            return jnp.where(first, sign * upper, sign * lower)

        low, high = block[other][2 * i], block[other][2 * i + 1]
        low_turned, high_turned = pltpu.roll(low, 4, 0), pltpu.roll(high, 4, 0)
        got = picked(jnp.where(first, high_turned, low_turned), mixed)
        change_low = pair(d[0][1], d[1][0]) * low_turned + pair(d[0][2], d[1][3]) * high
        change_low += pair(d[0][3], d[1][2]) * high_turned
        change_low += jnp.where(first, -parity(c, 2, other), 0.0) * got
        change_high = pair(d[2][0], d[3][1]) * low + pair(d[2][1], d[3][0]) * low_turned
        change_high += pair(d[2][3], d[3][2]) * high_turned
        change_high += jnp.where(first, 0.0, -parity(c, 3, other)) * got
        return change_low, change_high

    def in_x(c, other, sign, i, half):
        change = slope([block[other][2 * m + half] for m in range(4)], i, sign)
        face = {0: 0, 3: 1}.get(i)
        if face is not None and traces[face] is not None:
            trace = traces[face][other - 1][8 * half : 8 * half + 8]
            change += -parity(c, face, other) * trace
        return change

    traces = [outer(0), outer(1)]
    for i in range(4):
        x_from_z = in_y(0, 2, -1.0, i)
        z_from_x = in_y(2, 0, 1.0, i)
        for half in range(2):
            n = 2 * i + half
            use(0, n, x_from_z[half] + planes[layer, 8 * n : 8 * n + 8, :])
            change = in_x(1, 2, 1.0, i, half)
            use(1, n, change + planes[layer, NODES + 8 * n : NODES + 8 * n + 8, :])
            use(2, n, z_from_x[half] + in_x(2, 1, -1.0, i, half))


def block_rows(c, n):
    return slice(BASE[c] + 8 * n, BASE[c] + 8 * n + 8)


def add_end(target, field, layer, i, index, scale, to_x):
    c, other, sign = (0, 1, 1.0) if to_x else (1, 0, -1.0)
    at = BASE[other] + 16 * i
    parts = [field[layer, pl.ds(at + k, 4, stride=4), :] for k in range(4)]
    for k in range(4):
        change = slope(parts, k, scale * sign)
        if k in (0, 3):
            face = 4 if k == 0 else 5
            got = picked(parts[3 - k], index(layer, face))
            change += (-scale * parity(c, face, other)) * got
        target[layer, pl.ds(BASE[c] + 16 * i + k, 4, stride=4), :] += change
    c, other, sign = (0, 2, -1.0) if to_x else (2, 0, 1.0)
    at = BASE[other] + 16 * i
    parts = [field[layer, at + 4 * j : at + 4 * j + 4, :] for j in range(4)]
    for j in range(4):
        change = slope(parts, j, scale * sign)
        if j in (0, 3):
            face = 2 if j == 0 else 3
            got = picked(parts[3 - j], index(layer, face))
            change += (-scale * parity(c, face, other)) * got
        at = BASE[c] + 16 * i + 4 * j
        target[layer, at : at + 4, :] += change


def add_into_end(target, field, layer, i, index, scale):
    for c, other, sign in ((1, 2, 1.0), (2, 1, -1.0)):
        parts = [field[layer, BASE[other] + 16 * n : BASE[other] + 16 * n + 16, :] for n in range(4)]
        rows = slice(BASE[c] + 16 * i, BASE[c] + 16 * i + 16)
        target[layer, rows, :] += slope(parts, i, scale * sign)
    add_end(target, field, layer, i, index, scale, False)


def passed_back(v, i):
    terms = [
        (SLOPES[i][n] * SLOPES[n][i]) * v[16 * n : 16 * n + 16] for n in range(4) if n != i
    ]
    return terms[0] + terms[1] + terms[2]


def layers_of(x):
    return [x[:, at : at + LAYER] for at in range(0, x.shape[1], LAYER)]


def between(field, index, layer):
    def outer(face):
        if (layer, face) not in ((L0, 1), (L1, 0)):
            return None
        traces = x_traces(field, L0 + L1 - layer, face ^ 1)
        return [picked(t, index(layer, face)) for t in traces]

    return outer


def lone_h(index, fe, fh, planes):
    for layer in (L0, L1):

        def use(c, n, change, layer=layer):
            fh[layer, block_rows(c, n), :] += change

        rates(fe, layer, index, between(fe, index, layer), planes, use)


def lone_e(index, fe, fh, planes, drive, v):
    for i, layer in enumerate((L0, L1)):

        def use(c, n, change, i=i, layer=layer):
            rows = block_rows(c, n)
            fe[layer, rows, :] -= v[i][8 * n : 8 * n + 8] * (drive[i][rows] + change)

        rates(fh, layer, index, between(fh, index, layer), planes, use)


def lonely(index, fe, fh, planes, drive_of, v_of, out_h, out_e):
    def ends_of(field):
        return x_traces(field, L1, 1), x_traces(field, L0, 0)

    found = [ends_of(fe)]
    lone_h(index, fe, fh, planes)
    found.append(ends_of(fh))
    for i in range(2):
        out_h[i] = fh[L0 + i]
    drive = drive_of()
    lone_e(index, fe, fh, planes, drive, v_of())
    found.append(ends_of(fe))
    for i in range(2):
        out_e[i] = fe[L0 + i]
    for face, layer in enumerate((L0, L1)):
        add_into_end(fh, fe, layer, at_end(face), index, 1.0)
    found.append(ends_of(fh))
    return [jnp.concatenate(sum(traces, []), axis=0) for traces in zip(*found)]


def respond(index, valid, fe, fh, acc, planes, lone, v, w, near_v, sent_a, sent_b):
    start_e, lone_h1, lone_e1 = lone
    own = (L0, L1)
    sides = ((A1, 1, L0, 0), (B1, 0, L1, 1))
    sent = (sent_a, sent_b)
    empty = jnp.zeros((16, LAYER), F32)

    def rows_at(c, i):
        return slice(BASE[c] + 16 * i, BASE[c] + 16 * i + 16)

    def lifted(face, scale, y, z):
        return (-scale * parity(1, face, 2)) * z, (-scale * parity(2, face, 1)) * y

    def arrived(side, start, answers=None):
        _, _, layer, face = sides[side]
        traces = [sent[side][start + 16 * t : start + 16 * t + 16, :] for t in range(2)]
        if answers is not None:
            traces = [a + b for a, b in zip(traces, answers)]
        mask = jnp.concatenate([valid[side]] * 2, axis=0)
        return [picked(t, index(layer, face)) * mask for t in traces]

    def inward(side, start, scale, answers=None):
        return lifted(sides[side][3], scale, *arrived(side, start, answers))

    def outer_of(side, field, start):
        near, near_face, layer, own_face = sides[side]
        inside = between(field, index, layer)

        def outer(face):
            if face != own_face:
                return inside(face)
            return arrived(side, start, x_traces(field, near, near_face))

        return outer

    def outward(side, alone, scale, answers=None):
        near, face, layer, own_face = sides[side]
        traces = x_traces(alone, layer - L0, own_face)
        if answers is not None:
            traces = [a + b for a, b in zip(traces, answers)]
        return lifted(face, scale, *[picked(t, index(near, face)) for t in traces])

    def put(target, layer, i, pair):
        target[layer, rows_at(1, i), :] = pair[0]
        target[layer, rows_at(2, i), :] = pair[1]

    near_h, own_h = [], []
    for side, (near, face, layer, own_face) in enumerate(sides):
        near_h.append(outward(side, start_e, 1.0))
        own_h.append(inward(side, E_START, 1.0))
        put(fh, near, at_end(face), near_h[side])
        put(fh, layer, at_end(own_face), own_h[side])

    for side, (near, face, layer, own_face) in enumerate(sides):
        i = at_end(face)
        pair = outward(side, lone_h1, 1.0, own_h[side])
        acc[near, rows_at(0, i), :] = empty
        add_end(acc, fh, near, i, index, 1.0, True)
        scale = -near_v[side, 0:16, :]
        put(fe, near, i, [scale * part for part in pair])
        fe[near, rows_at(0, i), :] = scale * acc[near, rows_at(0, i), :]

        i = at_end(own_face)
        pair = inward(side, H_FIRST, 1.0, near_h[side])
        acc[layer, rows_at(0, i), :] = empty
        add_end(acc, fh, layer, i, index, 1.0, True)
        for n in range(4):
            scale = -v[side, 16 * n : 16 * n + 16, :]
            if n == i:
                put(fe, layer, n, [scale * part for part in pair])
                fe[layer, rows_at(0, n), :] = scale * acc[layer, rows_at(0, n), :]
            else:
                y, z = own_h[side]
                put(fe, layer, n, [scale * (SLOPES[n][i] * z), scale * (-SLOPES[n][i] * y)])
                fe[layer, rows_at(0, n), :] = empty

    for side, (near, face, layer, own_face) in enumerate(sides):
        i = at_end(face)
        pair = outward(side, lone_e1, 1.0, x_traces(fe, layer, own_face))
        back = 1.0 + near_v[side, 16:32, :]
        put(fh, near, i, [a + back * b for a, b in zip(pair, near_h[side])])
        add_end(fh, fe, near, i, index, 1.0, False)

        def use_h(c, n, change, layer=layer, i=at_end(own_face), own=own_h[side]):
            if c > 0 and n // 2 == i:
                change += own[c - 1][8 * (n % 2) : 8 * (n % 2) + 8]
            fh[layer, block_rows(c, n), :] = change

        rates(fe, layer, index, outer_of(side, fe, E_FIRST), planes, use_h)

    current = []
    for side, layer in enumerate(own):
        current.append(thrice(w[side]) * fe[layer])

        def use_e(c, n, change, side=side, layer=layer):
            rows = block_rows(c, n)
            change = v[side][8 * n : 8 * n + 8] * (current[side][rows] + change)
            acc[layer, rows, :] = fe[layer, rows, :] - change

        rates(fh, layer, index, outer_of(side, fh, H_SECOND), planes, use_e)
    return current


def odd_rank():
    return lax.rem(lax.axis_index("space"), 2) == 1


def send(across, inside, at, up, down):
    odd = odd_rank()
    rows = slice(at, at + up.shape[0])
    across[rows, :] = jnp.where(odd, up, down)
    inside[rows, :] = jnp.where(odd, down, up)


def sides_of(across, inside, a, b, rows):
    odd = odd_rank()
    from_across, from_inside = across[0:rows, :], inside[0:rows, :]
    a[...] = jnp.where(odd, from_inside, from_across)
    b[...] = jnp.where(odd, from_across, from_inside)


def first_kernel(
    e_in, h_in, j_in, v_in, w_in, near_in, ports_in, profile_in, design_in, *rest
):
    design, start_e, lone_h1, lone_e1, first_j, v, w, source, places, valid = rest[:10]
    across, inside, fe, fh, _, planes, neighbor, ports, profile, e, h, j, v_all, w_all, sems = (
        rest[10:]
    )
    started = []

    def fetch(*pairs):
        copies = []
        for origin, target in pairs:
            copies.append(pltpu.make_async_copy(origin, target, sems.at[len(started)]))
            copies[-1].start()
            started.append(None)
        return copies

    def wait(copies):
        for copy in copies:
            copy.wait()

    scatter = fetch((near_in, neighbor), (ports_in, ports), (profile_in, profile))
    fields = fetch((e_in, e), (h_in, h))
    weights = fetch((j_in, j), (w_in, w_all), (v_in, v_all))
    later = fetch((design_in, design))

    wait(scatter)
    found = neighbor[...]
    place = jnp.where(found < 0, 0, jnp.bitwise_and(found, LAYER - 1))
    for i in range(2):
        columns = slice(i * LAYER, (i + 1) * LAYER)
        for face in range(6):
            places[6 * i + face] = jnp.broadcast_to(place[face : face + 1, columns], (8, LAYER))
        there = (found[i : i + 1, columns] >= 0).astype(F32)
        valid[i] = jnp.broadcast_to(there, (8, LAYER))
    targets = lax.broadcasted_iota(jnp.int32, (2 * LAYER, ports.shape[1]), 0)
    spread_hot = one_hot(targets, jnp.bitwise_and(ports[...], 2 * LAYER - 1))
    high, low = halves(PER_STEP * profile[...])
    spread = layers_of(dot_t(high, spread_hot) + dot_t(low, spread_hot))
    for i in range(2):
        source[i] = stored(spread[i])

    wait(fields)
    electric = [stored(part) for part in layers_of(e[...])]
    magnetic = [stored(part) for part in layers_of(h[...])]
    for i in range(2):
        start_e[i] = electric[i]
        fe[L0 + i] = electric[i]
        fh[L0 + i] = PER_STEP * magnetic[i]

    scale = []

    def drive_of():
        wait(weights)
        current = [stored(part) for part in layers_of(j[...])]
        weight = layers_of(w_all[...])
        drive = []
        for i, part in enumerate(layers_of(v_all[...])):
            scale.append((TIME_STEP * TIME_STEP) * part)
            v[i] = scale[i]
            w[i] = weight[i]
            now = (KEEP * PER_STEP) * current[i] + thrice(weight[i]) * start_e[i]
            first_j[i] = now
            drive.append(now + source[i])
        return drive

    up, down = lonely(
        own_index(places), fe, fh, planes, drive_of, lambda: scale, lone_h1, lone_e1
    )
    wait(later)
    send(across, inside, 0, up, down)
    send(across, inside, V_NEAR, scale[1][48:NODES], scale[0][0:16])
    send(across, inside, V_NEAR + 16, passed_back(scale[1], 3), passed_back(scale[0], 0))
    blank = jnp.zeros((2, LAYER), F32)
    place = place.astype(F32)
    send(
        across,
        inside,
        N_NEAR,
        jnp.concatenate([place[:, LAYER : 2 * LAYER], blank], axis=0),
        jnp.concatenate([place[:, 0:LAYER], blank], axis=0),
    )


def own_index(places):
    def index(layer, face):
        return places[6 * (layer - L0) + face]

    return index


def second_lone_step(lone_h1, lone_e1, first_j, v, w, source, places, work):
    fe, fh, _, planes = work
    index = own_index(places)
    for i in range(2):
        fe[L0 + i] = lone_e1[i]
        fh[L0 + i] = lone_h1[i]
    current = [KEEP * first_j[i] + thrice(w[i]) * lone_e1[i] for i in range(2)]
    lone_h(index, fe, fh, planes)
    lone_e(index, fe, fh, planes, [current[i] + source[i] for i in range(2)], v)
    return current


def lone_kernel(lone_h1, lone_e1, first_j, v, w, source, places, design, *rest):
    lone_h2, lone_e2, lone_j2, pixels, *work = rest
    fe, fh = work[:2]
    pixel = jnp.bitwise_and(design[...], PIX_DEV - 1)
    pixels[...] = one_hot(lax.broadcasted_iota(jnp.int32, pixels.shape, 0), pixel)
    current = second_lone_step(
        lone_h1, lone_e1, first_j, v, w, source, places, work
    )
    for i in range(2):
        lone_h2[i] = fh[L0 + i]
        lone_e2[i] = fe[L0 + i]
        lone_j2[i] = current[i]


def index_of(places, near_places):
    def index(layer, face):
        if layer in (L0, L1):
            return places[6 * (layer - L0) + face]
        return near_places[6 * (layer == B1) + face]

    return index


def middle_kernel(
    start_e, lone_h1, lone_e1, lone_h2, lone_e2, lone_j2, v, w, source, places,
    valid, across_in, inside_in, *rest
):
    end_e, next_h, next_e, next_j, answer_e, answer_j, near_v, near_places = rest[:8]
    inside, across = rest[8:10]
    fe, fh, acc, planes, sent_a, sent_b = rest[10:]
    sides_of(across_in, inside_in, sent_a, sent_b, FIRST)
    for side, sent in enumerate((sent_a, sent_b)):
        near_v[side] = sent[V_NEAR : V_NEAR + 32, :]
        place = sent[N_NEAR : N_NEAR + 8, :].astype(jnp.int32)
        for face in range(6):
            near_places[6 * side + face] = jnp.broadcast_to(place[face : face + 1], (8, LAYER))
    index = index_of(places, near_places)
    current = respond(
        index, valid, fe, fh, acc, planes, (start_e, lone_h1, lone_e1), v, w, near_v,
        sent_a, sent_b,
    )
    drive = []
    for i in range(2):
        answer_e[i] = fe[L0 + i]
        answer_j[i] = current[i]
        electric = lone_e2[i] + acc[L0 + i]
        end_e[i] = electric
        fe[L0 + i] = electric
        fh[L0 + i] += lone_h2[i]
        before = lone_j2[i] + current[i]
        now = KEEP * before + thrice(w[i]) * electric
        next_j[i] = now
        drive.append(now + source[i])
    up, down = lonely(index, fe, fh, planes, lambda: drive, lambda: v, next_h, next_e)
    send(across, inside, 0, up, down)


def early_kernel(
    lone_e1, answer_e, lone_j1, lone_j2, answer_j, end_e, next_h, next_e, next_j, v, w,
    source, places, levels, *rest
):
    last_h, last_e, out, changes, *work = rest
    fe, fh = work[:2]
    current = second_lone_step(next_h, next_e, next_j, v, w, source, places, work)
    for i in range(2):
        electric = fe[L0 + i]
        last_h[i] = fh[L0 + i]
        last_e[i] = electric
        columns = slice(i * LAYER, (i + 1) * LAYER)
        level = [stored(levels[k, :, columns].astype(F32)) for k in range(5)]
        eps = (lone_e1[i] + answer_e[i]) * (level[1] - level[0])
        eps += end_e[i] * (level[2] - level[1]) + next_e[i] * (level[3] - level[2])
        eps += electric * (level[4] - level[3])
        drude = lone_j1[i] * level[0] + (lone_j2[i] + answer_j[i]) * level[1]
        drude += next_j[i] * level[2] + current[i] * level[3]
        out[0:NODES, columns] = folded(eps)
        out[NODES : 2 * NODES, columns] = TIME_STEP * folded(drude)
        changes[0, i] = level[3] - level[2]
        changes[1, i] = level[4] - level[3]
        changes[2, i] = level[3]


def last_kernel(
    start_e, lone_h1, lone_e1, lone_h2, lone_e2, v, w, places, valid, near_v, near_places,
    inside_in, across_in, changes, early, pixels, *rest
):
    out_e, out_h, sums = rest[:3]
    fe, fh, acc, planes, sent_a, sent_b = rest[3:]
    sides_of(across_in, inside_in, sent_a, sent_b, SECOND)
    current = respond(
        index_of(places, near_places), valid, fe, fh, acc, planes, (start_e, lone_h1, lone_e1),
        v, w, near_v, sent_a, sent_b,
    )
    parts = []
    for i in range(2):
        columns = slice(i * LAYER, (i + 1) * LAYER)
        second_e = acc[L0 + i]
        electric = lone_e2[i] + second_e
        magnetic = TIME_STEP * (lone_h2[i] + fh[L0 + i])
        for c in range(3):
            rows, there = slice(BASE[c], BASE[c] + NODES), slice(c * NODES, (c + 1) * NODES)
            out_e[there, columns] = electric[rows]
            out_h[there, columns] = magnetic[rows]
        eps = folded(fe[L0 + i] * changes[0, i] + second_e * changes[1, i])
        drude = TIME_STEP * folded(current[i] * changes[2, i])
        parts.append(jnp.concatenate([eps, drude], axis=0) + early[:, columns])
    both = jnp.concatenate(parts, axis=1)
    high, low = halves(both)
    sums[...] = dot_t(pixels[...], high) + dot_t(pixels[...], low)


def total_kernel(owners, parts, e, h, out_e, out_h, eps, drude, sums, sems):
    copies = []

    def write(origin, target):
        copies.append(pltpu.make_async_copy(origin, target, sems.at[len(copies)]))
        copies[-1].start()

    write(e, out_e)
    write(h, out_h)
    share = parts.shape[0] // owners
    total = parts[0:share]
    for owner in range(1, owners):
        total = total + parts[owner * share : (owner + 1) * share]
    total = total * (1.0 / owners)
    sums[0] = total[:, 0:NODES]
    sums[1] = total[:, NODES : 2 * NODES]
    write(sums.at[0], eps)
    write(sums.at[1], drude)
    for copy in copies:
        copy.wait()


def call(kernel, outs, args, scratch=(), spaces=None, out_spaces=None):
    moved = sum(4 * int(np.prod(o.shape)) for o in outs) + sum(
        a.dtype.itemsize * int(np.prod(a.shape)) for a in args
    )
    return pl.pallas_call(
        kernel,
        out_shape=outs,
        in_specs=[pl.BlockSpec(memory_space=s) for s in spaces or [pltpu.VMEM] * len(args)],
        out_specs=[pl.BlockSpec(memory_space=s) for s in out_spaces or [pltpu.VMEM] * len(outs)],
        scratch_shapes=list(scratch),
        compiler_params=pltpu.CompilerParams(vmem_limit_bytes=24 * 1024 * 1024),
        cost_estimate=pl.CostEstimate(flops=moved, bytes_accessed=moved, transcendentals=0),
    )(*args)


def f32(*shape):
    return jax.ShapeDtypeStruct(shape, F32)


def bf16(*shape):
    return jax.ShapeDtypeStruct(shape, BF16)


def exchange(across, inside, inside_first):
    size = lax.axis_size("space")

    def pairs(start):
        found = [(i, i + 1) for i in range(start, size - 1, 2)]
        return found + [(j, i) for i, j in found]

    if inside_first:
        inside = lax.ppermute(inside, "space", pairs(0))
    across = lax.ppermute(across, "space", pairs(1))
    if not inside_first:
        inside = lax.ppermute(inside, "space", pairs(0))
    return across, inside


def local(
    adj_e,
    adj_h,
    adj_j,
    fwd_e,
    inv_eps,
    drude_weight,
    neighbor,
    design_map,
    port_elems,
    port_profile,
):
    count = adj_e.shape[2]
    owners = lax.axis_size("exc")
    levels = fwd_e[0]
    field, nodal = f32(2, ROWS, LAYER), f32(2, NODES, LAYER)
    indices = jax.ShapeDtypeStruct((12, 8, LAYER), jnp.int32)
    work = [pltpu.VMEM((4, ROWS, LAYER), F32)] * 3 + [pltpu.VMEM((4, 2 * NODES, LAYER), F32)]
    given = [adj_e[0], adj_h[0], adj_j[0], inv_eps, drude_weight]
    given += [neighbor, port_elems, port_profile[0], design_map.reshape(1, count)]
    received = [pltpu.VMEM((FIRST, LAYER), F32)] * 2
    design, start_e, h1, e1, j1, v, w, source, places, valid, *sent = call(
        first_kernel,
        [jax.ShapeDtypeStruct((1, count), jnp.int32)]
        + [field] * 4
        + [nodal, nodal, field, indices, f32(2, 8, LAYER)]
        + [f32(FIRST, LAYER)] * 2,
        [pltpu.with_memory_space_constraint(a, pltpu.HBM) for a in given],
        work
        + [pltpu.VMEM(a.shape, a.dtype) for a in [neighbor, port_elems, port_profile[0]]]
        + [pltpu.VMEM((ROWS, count), F32)] * 3
        + [pltpu.VMEM((NODES, count), F32)] * 2
        + [pltpu.SemaphoreType.DMA((9,))],
        spaces=[pltpu.HBM] * len(given),
    )
    across, inside = exchange(*sent, False)
    h2, e2, j2, pixels = call(
        lone_kernel,
        [field] * 3 + [bf16(PIX_DEV, count)],
        [h1, e1, j1, v, w, source, places, design],
        work,
    )
    end_e, h3, e3, j3, answer_e, answer_j, near_v, near_places, inside, across = call(
        middle_kernel,
        [field] * 6 + [f32(2, 32, LAYER), indices] + [f32(SECOND, LAYER)] * 2,
        [start_e, h1, e1, h2, e2, j2, v, w, source, places, valid, across, inside],
        work + received,
    )
    across, inside = exchange(across, inside, True)
    h4, e4, early, changes = call(
        early_kernel,
        [field] * 2 + [f32(2 * NODES, count), f32(3, 2, ROWS, LAYER)],
        [e1, answer_e, j1, j2, answer_j, end_e, h3, e3, j3, v, w, source, places, levels],
        work,
    )
    e4, h4, sums = call(
        last_kernel,
        [f32(ROWS, count)] * 2 + [f32(PIX_DEV, 2 * NODES)],
        [end_e, h3, e3, h4, e4, v, w, places, valid, near_v, near_places]
        + [inside, across, changes, early, pixels],
        work + [pltpu.VMEM((SECOND, LAYER), F32)] * 2,
    )
    parts = lax.all_to_all(sums, "exc", split_axis=0, concat_axis=0, tiled=True)
    share = PIX_DEV // owners
    out_e, out_h, eps, drude = call(
        functools.partial(total_kernel, owners),
        [f32(ROWS, count)] * 2 + [f32(share, NODES)] * 2,
        [parts, e4, h4],
        [pltpu.VMEM((2, share, NODES), F32), pltpu.SemaphoreType.DMA((4,))],
        out_spaces=[pltpu.HBM] * 4,
    )
    return out_e[None], out_h[None], eps.T, drude.T


def solution(mesh):
    return jax.shard_map(
        local,
        mesh=mesh,
        in_specs=(
            P("exc", None, "space"),
            P("exc", None, "space"),
            P("exc", None, "space"),
            P("exc", None, None, "space"),
            P(None, "space"),
            P(None, "space"),
            P(None, "space"),
            P("space"),
            P("exc", "space"),
            P("exc", None, "space"),
        ),
        out_specs=(
            P("exc", None, "space"),
            P("exc", None, "space"),
            P(None, ("space", "exc")),
            P(None, ("space", "exc")),
        ),
        check_vma=False,
    )
```

```python
import functools

import jax
import jax.numpy as jnp
import numpy as np
from jax import lax
from jax.experimental import pallas as pl
from jax.experimental.pallas import tpu as pltpu
from jax.sharding import PartitionSpec as P

NODES = 64
ROWS = 3 * NODES
LAYER = 128
PIX_DEV = 128

TIME_STEP = 0.025
DAMPING = 0.5
KEEP = 1.0 - TIME_STEP * DAMPING

PER_STEP = 1.0 / TIME_STEP

TANGENT = 32
E_START = 0
H_FIRST = 32
E_FIRST = 64
H_SECOND = 96
SECOND = 128
V_NEAR = 128
N_NEAR = V_NEAR + 32
FIRST = N_NEAR + 8

A1, L0, L1, B1 = range(4)

BASE = (NODES, 0, 2 * NODES)

BF16 = jnp.bfloat16
F32 = jnp.float32


def parity(c, face, other):
    d = face // 2
    sign = 1.0 if face % 2 else -1.0
    return 6.0 * sign * (c - d) * (d - other) * (other - c) / 2.0


def off_diagonal():
    points = np.array([-1.0, -1.0 / np.sqrt(5.0), 1.0 / np.sqrt(5.0), 1.0])
    barycentric = np.array(
        [1.0 / np.prod([points[j] - points[k] for k in range(4) if k != j]) for j in range(4)]
    )
    deriv = np.zeros((4, 4))
    for row in range(4):
        for column in range(4):
            if row != column:
                deriv[row, column] = (
                    barycentric[column] / barycentric[row] / (points[row] - points[column])
                )
    return (2.0 * deriv).tolist()


SLOPES = off_diagonal()


def slope(parts, row, scale):
    total = None
    for i in (1, 2, 0, 3):
        factor = scale * SLOPES[row][i]
        if i == row:
            continue
        if abs(abs(factor) - 1.0) > 1e-9:
            term = factor * parts[i]
            total = term if total is None else total + term
        else:
            total = total + parts[i] if factor > 0 else total - parts[i]
    return total


def halves(x):
    high = x.astype(BF16)
    return high, (x - high.astype(F32)).astype(BF16)


def dot_t(a, b):
    return lax.dot_general(a, b, (((1,), (1,)), ((), ())), preferred_element_type=F32)


def thrice(x):
    return jnp.concatenate([x, x, x], axis=0)


def folded(x):
    return x[0:NODES] + x[NODES : 2 * NODES] + x[2 * NODES : ROWS]


def stored(x):
    return jnp.concatenate([x[NODES : 2 * NODES], x[0:NODES], x[2 * NODES : ROWS]], axis=0)


def one_hot(rows, targets):
    return (rows == targets).astype(F32).astype(BF16)


def picked(x, index):
    rows = x.shape[0]
    if rows < 8:
        index = index[0:rows]
    elif rows > 8:
        index = jnp.concatenate([index] * (rows // 8), axis=0)
    along = lax.GatherDimensionNumbers(
        offset_dims=(),
        collapsed_slice_dims=(1,),
        start_index_map=(1,),
        operand_batching_dims=(0,),
        start_indices_batching_dims=(0,),
    )
    mode = lax.GatherScatterMode.PROMISE_IN_BOUNDS
    return lax.gather(x, index[..., None], along, (1, 1), mode=mode)


def at_end(face):
    return 3 if face % 2 else 0


def x_traces(field, layer, face):
    at = 16 * at_end(face)
    return [field[layer, BASE[c] + at : BASE[c] + at + 16, :] for c in (1, 2)]


def lift_x(target, layer, face, scale, y, z):
    at = 16 * at_end(face)
    rows = slice(BASE[1] + at, BASE[1] + at + 16)
    target[layer, rows, :] += (-scale * parity(1, face, 2)) * z
    rows = slice(BASE[2] + at, BASE[2] + at + 16)
    target[layer, rows, :] += (-scale * parity(2, face, 1)) * y


def rates(field, layer, index, outer, planes, use):
    for c, other, sign in ((0, 1, 1.0), (1, 0, -1.0)):
        parts = [field[layer, pl.ds(BASE[other] + k, 16, stride=4), :] for k in range(4)]
        for k in range(4):
            change = slope(parts, k, sign)
            if k in (0, 3):
                face = 4 if k == 0 else 5
                got = picked(parts[3 - k], index(layer, face))
                change += -parity(c, face, other) * got
            planes[layer, pl.ds(NODES * c + k, 16, stride=4), :] = change
    block = [
        [field[layer, BASE[c] + 8 * n : BASE[c] + 8 * n + 8, :] for n in range(8)] for c in range(3)
    ]

    first = lax.broadcasted_iota(jnp.int32, (8, LAYER), 0) < 4
    mixed = jnp.where(first, index(layer, 2), index(layer, 3))
    d = SLOPES

    def in_y(c, other, sign, i):
        def pair(upper, lower):
            return jnp.where(first, sign * upper, sign * lower)

        low, high = block[other][2 * i], block[other][2 * i + 1]
        low_turned, high_turned = pltpu.roll(low, 4, 0), pltpu.roll(high, 4, 0)
        got = picked(jnp.where(first, high_turned, low_turned), mixed)
        change_low = pair(d[0][1], d[1][0]) * low_turned + pair(d[0][2], d[1][3]) * high
        change_low += pair(d[0][3], d[1][2]) * high_turned
        change_low += jnp.where(first, -parity(c, 2, other), 0.0) * got
        change_high = pair(d[2][0], d[3][1]) * low + pair(d[2][1], d[3][0]) * low_turned
        change_high += pair(d[2][3], d[3][2]) * high_turned
        change_high += jnp.where(first, 0.0, -parity(c, 3, other)) * got
        return change_low, change_high

    def in_x(c, other, sign, i, half):
        change = slope([block[other][2 * m + half] for m in range(4)], i, sign)
        face = {0: 0, 3: 1}.get(i)
        if face is not None and traces[face] is not None:
            trace = traces[face][other - 1][8 * half : 8 * half + 8]
            change += -parity(c, face, other) * trace
        return change

    traces = [outer(0), outer(1)]
    for i in range(4):
        x_from_z = in_y(0, 2, -1.0, i)
        z_from_x = in_y(2, 0, 1.0, i)
        for half in range(2):
            n = 2 * i + half
            use(0, n, x_from_z[half] + planes[layer, 8 * n : 8 * n + 8, :])
            change = in_x(1, 2, 1.0, i, half)
            use(1, n, change + planes[layer, NODES + 8 * n : NODES + 8 * n + 8, :])
            use(2, n, z_from_x[half] + in_x(2, 1, -1.0, i, half))


def block_rows(c, n):
    return slice(BASE[c] + 8 * n, BASE[c] + 8 * n + 8)


def add_end(target, field, layer, i, index, scale, to_x):
    c, other, sign = (0, 1, 1.0) if to_x else (1, 0, -1.0)
    at = BASE[other] + 16 * i
    parts = [field[layer, pl.ds(at + k, 4, stride=4), :] for k in range(4)]
    for k in range(4):
        change = slope(parts, k, scale * sign)
        if k in (0, 3):
            face = 4 if k == 0 else 5
            got = picked(parts[3 - k], index(layer, face))
            change += (-scale * parity(c, face, other)) * got
        target[layer, pl.ds(BASE[c] + 16 * i + k, 4, stride=4), :] += change
    c, other, sign = (0, 2, -1.0) if to_x else (2, 0, 1.0)
    at = BASE[other] + 16 * i
    parts = [field[layer, at + 4 * j : at + 4 * j + 4, :] for j in range(4)]
    for j in range(4):
        change = slope(parts, j, scale * sign)
        if j in (0, 3):
            face = 2 if j == 0 else 3
            got = picked(parts[3 - j], index(layer, face))
            change += (-scale * parity(c, face, other)) * got
        at = BASE[c] + 16 * i + 4 * j
        target[layer, at : at + 4, :] += change


def add_into_end(target, field, layer, i, index, scale):
    for c, other, sign in ((1, 2, 1.0), (2, 1, -1.0)):
        parts = [field[layer, BASE[other] + 16 * n : BASE[other] + 16 * n + 16, :] for n in range(4)]
        rows = slice(BASE[c] + 16 * i, BASE[c] + 16 * i + 16)
        target[layer, rows, :] += slope(parts, i, scale * sign)
    add_end(target, field, layer, i, index, scale, False)


def passed_back(v, i):
    terms = [
        (SLOPES[i][n] * SLOPES[n][i]) * v[16 * n : 16 * n + 16] for n in range(4) if n != i
    ]
    return terms[0] + terms[1] + terms[2]


def layers_of(x):
    return [x[:, at : at + LAYER] for at in range(0, x.shape[1], LAYER)]


def between(field, index, layer):
    def outer(face):
        if (layer, face) not in ((L0, 1), (L1, 0)):
            return None
        traces = x_traces(field, L0 + L1 - layer, face ^ 1)
        return [picked(t, index(layer, face)) for t in traces]

    return outer


def lone_h(index, fe, fh, planes):
    for layer in (L0, L1):

        def use(c, n, change, layer=layer):
            fh[layer, block_rows(c, n), :] += change

        rates(fe, layer, index, between(fe, index, layer), planes, use)


def lone_e(index, fe, fh, planes, drive, v):
    for i, layer in enumerate((L0, L1)):

        def use(c, n, change, i=i, layer=layer):
            rows = block_rows(c, n)
            fe[layer, rows, :] -= v[i][8 * n : 8 * n + 8] * (drive[i][rows] + change)

        rates(fh, layer, index, between(fh, index, layer), planes, use)


def lonely(index, fe, fh, planes, drive_of, v_of, out_h, out_e):
    def ends_of(field):
        return x_traces(field, L1, 1), x_traces(field, L0, 0)

    found = [ends_of(fe)]
    lone_h(index, fe, fh, planes)
    found.append(ends_of(fh))
    for i in range(2):
        out_h[i] = fh[L0 + i]
    drive = drive_of()
    lone_e(index, fe, fh, planes, drive, v_of())
    found.append(ends_of(fe))
    for i in range(2):
        out_e[i] = fe[L0 + i]
    for face, layer in enumerate((L0, L1)):
        add_into_end(fh, fe, layer, at_end(face), index, 1.0)
    found.append(ends_of(fh))
    return [jnp.concatenate(sum(traces, []), axis=0) for traces in zip(*found)]


def respond(index, valid, fe, fh, acc, planes, lone, v, w, near_v, sent_a, sent_b):
    start_e, lone_h1, lone_e1 = lone
    own = (L0, L1)
    sides = ((A1, 1, L0, 0), (B1, 0, L1, 1))
    sent = (sent_a, sent_b)
    empty = jnp.zeros((16, LAYER), F32)

    def rows_at(c, i):
        return slice(BASE[c] + 16 * i, BASE[c] + 16 * i + 16)

    def lifted(face, scale, y, z):
        return (-scale * parity(1, face, 2)) * z, (-scale * parity(2, face, 1)) * y

    def arrived(side, start, answers=None):
        _, _, layer, face = sides[side]
        traces = [sent[side][start + 16 * t : start + 16 * t + 16, :] for t in range(2)]
        if answers is not None:
            traces = [a + b for a, b in zip(traces, answers)]
        there = jnp.concatenate([valid[side]] * 2, axis=0) > 0.0
        return [jnp.where(there, picked(t, index(layer, face)), 0.0) for t in traces]

    def inward(side, start, scale, answers=None):
        return lifted(sides[side][3], scale, *arrived(side, start, answers))

    def outer_of(side, field, start):
        near, near_face, layer, own_face = sides[side]
        inside = between(field, index, layer)

        def outer(face):
            if face != own_face:
                return inside(face)
            return arrived(side, start, x_traces(field, near, near_face))

        return outer

    def outward(side, alone, scale, answers=None):
        near, face, layer, own_face = sides[side]
        traces = x_traces(alone, layer - L0, own_face)
        if answers is not None:
            traces = [a + b for a, b in zip(traces, answers)]
        return lifted(face, scale, *[picked(t, index(near, face)) for t in traces])

    def put(target, layer, i, pair):
        target[layer, rows_at(1, i), :] = pair[0]
        target[layer, rows_at(2, i), :] = pair[1]

    near_h, own_h = [], []
    for side, (near, face, layer, own_face) in enumerate(sides):
        near_h.append(outward(side, start_e, 1.0))
        own_h.append(inward(side, E_START, 1.0))
        put(fh, near, at_end(face), near_h[side])
        put(fh, layer, at_end(own_face), own_h[side])

    for side, (near, face, layer, own_face) in enumerate(sides):
        i = at_end(face)
        pair = outward(side, lone_h1, 1.0, own_h[side])
        acc[near, rows_at(0, i), :] = empty
        add_end(acc, fh, near, i, index, 1.0, True)
        scale = -near_v[side, 0:16, :]
        put(fe, near, i, [scale * part for part in pair])
        fe[near, rows_at(0, i), :] = scale * acc[near, rows_at(0, i), :]

        i = at_end(own_face)
        pair = inward(side, H_FIRST, 1.0, near_h[side])
        acc[layer, rows_at(0, i), :] = empty
        add_end(acc, fh, layer, i, index, 1.0, True)
        for n in range(4):
            scale = -v[side, 16 * n : 16 * n + 16, :]
            if n == i:
                put(fe, layer, n, [scale * part for part in pair])
                fe[layer, rows_at(0, n), :] = scale * acc[layer, rows_at(0, n), :]
            else:
                y, z = own_h[side]
                put(fe, layer, n, [scale * (SLOPES[n][i] * z), scale * (-SLOPES[n][i] * y)])
                fe[layer, rows_at(0, n), :] = empty

    for side, (near, face, layer, own_face) in enumerate(sides):
        i = at_end(face)
        pair = outward(side, lone_e1, 1.0, x_traces(fe, layer, own_face))
        back = 1.0 + near_v[side, 16:32, :]
        put(fh, near, i, [a + back * b for a, b in zip(pair, near_h[side])])
        add_end(fh, fe, near, i, index, 1.0, False)

        def use_h(c, n, change, layer=layer, i=at_end(own_face), own=own_h[side]):
            if c > 0 and n // 2 == i:
                change += own[c - 1][8 * (n % 2) : 8 * (n % 2) + 8]
            fh[layer, block_rows(c, n), :] = change

        rates(fe, layer, index, outer_of(side, fe, E_FIRST), planes, use_h)

    current = []
    for side, layer in enumerate(own):
        current.append(thrice(w[side]) * fe[layer])

        def use_e(c, n, change, side=side, layer=layer):
            rows = block_rows(c, n)
            change = v[side][8 * n : 8 * n + 8] * (current[side][rows] + change)
            acc[layer, rows, :] = fe[layer, rows, :] - change

        rates(fh, layer, index, outer_of(side, fh, H_SECOND), planes, use_e)
    return current


def odd_rank():
    return lax.rem(lax.axis_index("space"), 2) == 1


def send(across, inside, at, up, down):
    odd = odd_rank()
    rows = slice(at, at + up.shape[0])
    across[rows, :] = jnp.where(odd, up, down)
    inside[rows, :] = jnp.where(odd, down, up)


def sides_of(across, inside, a, b, rows):
    odd = odd_rank()
    from_across, from_inside = across[0:rows, :], inside[0:rows, :]
    a[...] = jnp.where(odd, from_inside, from_across)
    b[...] = jnp.where(odd, from_across, from_inside)


def first_kernel(
    e_in, h_in, j_in, v_in, w_in, near_in, ports_in, profile_in, design_in, *rest
):
    design, start_e, lone_h1, lone_e1, first_j, v, w, source, places, valid = rest[:10]
    across, inside, fe, fh, _, planes, neighbor, ports, profile, e, h, j, v_all, w_all, sems = (
        rest[10:]
    )
    started = []

    def fetch(*pairs):
        copies = []
        for origin, target in pairs:
            copies.append(pltpu.make_async_copy(origin, target, sems.at[len(started)]))
            copies[-1].start()
            started.append(None)
        return copies

    def wait(copies):
        for copy in copies:
            copy.wait()

    scatter = fetch((near_in, neighbor), (ports_in, ports), (profile_in, profile))
    fields = fetch((e_in, e), (h_in, h))
    weights = fetch((j_in, j), (w_in, w_all), (v_in, v_all))
    later = fetch((design_in, design))

    wait(scatter)
    found = neighbor[...]
    place = jnp.where(found < 0, 0, jnp.bitwise_and(found, LAYER - 1))
    for i in range(2):
        columns = slice(i * LAYER, (i + 1) * LAYER)
        for face in range(6):
            places[6 * i + face] = jnp.broadcast_to(place[face : face + 1, columns], (8, LAYER))
        there = (found[i : i + 1, columns] >= 0).astype(F32)
        valid[i] = jnp.broadcast_to(there, (8, LAYER))
    targets = lax.broadcasted_iota(jnp.int32, (2 * LAYER, ports.shape[1]), 0)
    spread_hot = one_hot(targets, jnp.bitwise_and(ports[...], 2 * LAYER - 1))
    high, low = halves(PER_STEP * profile[...])
    spread = layers_of(dot_t(high, spread_hot) + dot_t(low, spread_hot))
    for i in range(2):
        source[i] = stored(spread[i])

    wait(fields)
    electric = [stored(part) for part in layers_of(e[...])]
    magnetic = [stored(part) for part in layers_of(h[...])]
    for i in range(2):
        start_e[i] = electric[i]
        fe[L0 + i] = electric[i]
        fh[L0 + i] = PER_STEP * magnetic[i]

    scale = []

    def drive_of():
        wait(weights)
        current = [stored(part) for part in layers_of(j[...])]
        weight = layers_of(w_all[...])
        drive = []
        for i, part in enumerate(layers_of(v_all[...])):
            scale.append((TIME_STEP * TIME_STEP) * part)
            v[i] = scale[i]
            w[i] = weight[i]
            now = (KEEP * PER_STEP) * current[i] + thrice(weight[i]) * start_e[i]
            first_j[i] = now
            drive.append(now + source[i])
        return drive

    up, down = lonely(
        own_index(places), fe, fh, planes, drive_of, lambda: scale, lone_h1, lone_e1
    )
    wait(later)
    send(across, inside, 0, up, down)
    send(across, inside, V_NEAR, scale[1][48:NODES], scale[0][0:16])
    send(across, inside, V_NEAR + 16, passed_back(scale[1], 3), passed_back(scale[0], 0))
    blank = jnp.zeros((2, LAYER), F32)
    place = place.astype(F32)
    send(
        across,
        inside,
        N_NEAR,
        jnp.concatenate([place[:, LAYER : 2 * LAYER], blank], axis=0),
        jnp.concatenate([place[:, 0:LAYER], blank], axis=0),
    )


def own_index(places):
    def index(layer, face):
        return places[6 * (layer - L0) + face]

    return index


def second_lone_step(lone_h1, lone_e1, first_j, v, w, source, places, work):
    fe, fh, _, planes = work
    index = own_index(places)
    for i in range(2):
        fe[L0 + i] = lone_e1[i]
        fh[L0 + i] = lone_h1[i]
    current = [KEEP * first_j[i] + thrice(w[i]) * lone_e1[i] for i in range(2)]
    lone_h(index, fe, fh, planes)
    lone_e(index, fe, fh, planes, [current[i] + source[i] for i in range(2)], v)
    return current


def lone_kernel(lone_h1, lone_e1, first_j, v, w, source, places, design, *rest):
    lone_h2, lone_e2, lone_j2, pixels, *work = rest
    fe, fh = work[:2]
    pixel = jnp.bitwise_and(design[...], PIX_DEV - 1)
    pixels[...] = one_hot(lax.broadcasted_iota(jnp.int32, pixels.shape, 0), pixel)
    current = second_lone_step(
        lone_h1, lone_e1, first_j, v, w, source, places, work
    )
    for i in range(2):
        lone_h2[i] = fh[L0 + i]
        lone_e2[i] = fe[L0 + i]
        lone_j2[i] = current[i]


def index_of(places, near_places):
    def index(layer, face):
        if layer in (L0, L1):
            return places[6 * (layer - L0) + face]
        return near_places[6 * (layer == B1) + face]

    return index


def middle_kernel(
    start_e, lone_h1, lone_e1, lone_h2, lone_e2, lone_j2, v, w, source, places,
    valid, across_in, inside_in, *rest
):
    end_e, next_h, next_e, next_j, answer_e, answer_j, near_v, near_places = rest[:8]
    inside, across = rest[8:10]
    fe, fh, acc, planes, sent_a, sent_b = rest[10:]
    sides_of(across_in, inside_in, sent_a, sent_b, FIRST)
    for side, sent in enumerate((sent_a, sent_b)):
        near_v[side] = sent[V_NEAR : V_NEAR + 32, :]
        place = sent[N_NEAR : N_NEAR + 8, :].astype(jnp.int32)
        place = jnp.bitwise_and(place, LAYER - 1)
        for face in range(6):
            near_places[6 * side + face] = jnp.broadcast_to(place[face : face + 1], (8, LAYER))
    index = index_of(places, near_places)
    current = respond(
        index, valid, fe, fh, acc, planes, (start_e, lone_h1, lone_e1), v, w, near_v,
        sent_a, sent_b,
    )
    drive = []
    for i in range(2):
        answer_e[i] = fe[L0 + i]
        answer_j[i] = current[i]
        electric = lone_e2[i] + acc[L0 + i]
        end_e[i] = electric
        fe[L0 + i] = electric
        fh[L0 + i] += lone_h2[i]
        before = lone_j2[i] + current[i]
        now = KEEP * before + thrice(w[i]) * electric
        next_j[i] = now
        drive.append(now + source[i])
    up, down = lonely(index, fe, fh, planes, lambda: drive, lambda: v, next_h, next_e)
    send(across, inside, 0, up, down)


def early_kernel(
    lone_e1, answer_e, lone_j1, lone_j2, answer_j, end_e, next_h, next_e, next_j, v, w,
    source, places, levels, *rest
):
    last_h, last_e, out, changes, *work = rest
    fe, fh = work[:2]
    current = second_lone_step(next_h, next_e, next_j, v, w, source, places, work)
    for i in range(2):
        electric = fe[L0 + i]
        last_h[i] = fh[L0 + i]
        last_e[i] = electric
        columns = slice(i * LAYER, (i + 1) * LAYER)
        level = [stored(levels[k, :, columns].astype(F32)) for k in range(5)]
        eps = (lone_e1[i] + answer_e[i]) * (level[1] - level[0])
        eps += end_e[i] * (level[2] - level[1]) + next_e[i] * (level[3] - level[2])
        eps += electric * (level[4] - level[3])
        drude = lone_j1[i] * level[0] + (lone_j2[i] + answer_j[i]) * level[1]
        drude += next_j[i] * level[2] + current[i] * level[3]
        out[0:NODES, columns] = folded(eps)
        out[NODES : 2 * NODES, columns] = TIME_STEP * folded(drude)
        changes[0, i] = level[3] - level[2]
        changes[1, i] = level[4] - level[3]
        changes[2, i] = level[3]


def last_kernel(
    start_e, lone_h1, lone_e1, lone_h2, lone_e2, v, w, places, valid, near_v, near_places,
    inside_in, across_in, changes, early, pixels, *rest
):
    out_e, out_h, sums = rest[:3]
    fe, fh, acc, planes, sent_a, sent_b = rest[3:]
    sides_of(across_in, inside_in, sent_a, sent_b, SECOND)
    current = respond(
        index_of(places, near_places), valid, fe, fh, acc, planes, (start_e, lone_h1, lone_e1),
        v, w, near_v, sent_a, sent_b,
    )
    parts = []
    for i in range(2):
        columns = slice(i * LAYER, (i + 1) * LAYER)
        second_e = acc[L0 + i]
        electric = lone_e2[i] + second_e
        magnetic = TIME_STEP * (lone_h2[i] + fh[L0 + i])
        for c in range(3):
            rows, there = slice(BASE[c], BASE[c] + NODES), slice(c * NODES, (c + 1) * NODES)
            out_e[there, columns] = electric[rows]
            out_h[there, columns] = magnetic[rows]
        eps = folded(fe[L0 + i] * changes[0, i] + second_e * changes[1, i])
        drude = TIME_STEP * folded(current[i] * changes[2, i])
        parts.append(jnp.concatenate([eps, drude], axis=0) + early[:, columns])
    both = jnp.concatenate(parts, axis=1)
    high, low = halves(both)
    sums[...] = dot_t(pixels[...], high) + dot_t(pixels[...], low)


def total_kernel(owners, parts, e, h, out_e, out_h, eps, drude, sums, sems):
    copies = []

    def write(origin, target):
        copies.append(pltpu.make_async_copy(origin, target, sems.at[len(copies)]))
        copies[-1].start()

    write(e, out_e)
    write(h, out_h)
    share = parts.shape[0] // owners
    total = parts[0:share]
    for owner in range(1, owners):
        total = total + parts[owner * share : (owner + 1) * share]
    total = total * (1.0 / owners)
    sums[0] = total[:, 0:NODES]
    sums[1] = total[:, NODES : 2 * NODES]
    write(sums.at[0], eps)
    write(sums.at[1], drude)
    for copy in copies:
        copy.wait()


def call(kernel, outs, args, scratch=(), spaces=None, out_spaces=None):
    moved = sum(4 * int(np.prod(o.shape)) for o in outs) + sum(
        a.dtype.itemsize * int(np.prod(a.shape)) for a in args
    )
    return pl.pallas_call(
        kernel,
        out_shape=outs,
        in_specs=[pl.BlockSpec(memory_space=s) for s in spaces or [pltpu.VMEM] * len(args)],
        out_specs=[pl.BlockSpec(memory_space=s) for s in out_spaces or [pltpu.VMEM] * len(outs)],
        scratch_shapes=list(scratch),
        compiler_params=pltpu.CompilerParams(vmem_limit_bytes=24 * 1024 * 1024),
        cost_estimate=pl.CostEstimate(flops=moved, bytes_accessed=moved, transcendentals=0),
    )(*args)


def f32(*shape):
    return jax.ShapeDtypeStruct(shape, F32)


def bf16(*shape):
    return jax.ShapeDtypeStruct(shape, BF16)


def exchange(across, inside, inside_first):
    size = lax.axis_size("space")

    def pairs(start):
        found = [(i, i + 1) for i in range(start, size - 1, 2)]
        return found + [(j, i) for i, j in found]

    if inside_first:
        inside = lax.ppermute(inside, "space", pairs(0))
    across = lax.ppermute(across, "space", pairs(1))
    if not inside_first:
        inside = lax.ppermute(inside, "space", pairs(0))
    return across, inside


def local(
    adj_e,
    adj_h,
    adj_j,
    fwd_e,
    inv_eps,
    drude_weight,
    neighbor,
    design_map,
    port_elems,
    port_profile,
):
    count = adj_e.shape[2]
    owners = lax.axis_size("exc")
    levels = fwd_e[0]
    field, nodal = f32(2, ROWS, LAYER), f32(2, NODES, LAYER)
    indices = jax.ShapeDtypeStruct((12, 8, LAYER), jnp.int32)
    work = [pltpu.VMEM((4, ROWS, LAYER), F32)] * 3 + [pltpu.VMEM((4, 2 * NODES, LAYER), F32)]
    given = [adj_e[0], adj_h[0], adj_j[0], inv_eps, drude_weight]
    given += [neighbor, port_elems, port_profile[0], design_map.reshape(1, count)]
    received = [pltpu.VMEM((FIRST, LAYER), F32)] * 2
    design, start_e, h1, e1, j1, v, w, source, places, valid, *sent = call(
        first_kernel,
        [jax.ShapeDtypeStruct((1, count), jnp.int32)]
        + [field] * 4
        + [nodal, nodal, field, indices, f32(2, 8, LAYER)]
        + [f32(FIRST, LAYER)] * 2,
        [pltpu.with_memory_space_constraint(a, pltpu.HBM) for a in given],
        work
        + [pltpu.VMEM(a.shape, a.dtype) for a in [neighbor, port_elems, port_profile[0]]]
        + [pltpu.VMEM((ROWS, count), F32)] * 3
        + [pltpu.VMEM((NODES, count), F32)] * 2
        + [pltpu.SemaphoreType.DMA((9,))],
        spaces=[pltpu.HBM] * len(given),
    )
    across, inside = exchange(*sent, False)
    h2, e2, j2, pixels = call(
        lone_kernel,
        [field] * 3 + [bf16(PIX_DEV, count)],
        [h1, e1, j1, v, w, source, places, design],
        work,
    )
    end_e, h3, e3, j3, answer_e, answer_j, near_v, near_places, inside, across = call(
        middle_kernel,
        [field] * 6 + [f32(2, 32, LAYER), indices] + [f32(SECOND, LAYER)] * 2,
        [start_e, h1, e1, h2, e2, j2, v, w, source, places, valid, across, inside],
        work + received,
    )
    across, inside = exchange(across, inside, True)
    h4, e4, early, changes = call(
        early_kernel,
        [field] * 2 + [f32(2 * NODES, count), f32(3, 2, ROWS, LAYER)],
        [e1, answer_e, j1, j2, answer_j, end_e, h3, e3, j3, v, w, source, places, levels],
        work,
    )
    e4, h4, sums = call(
        last_kernel,
        [f32(ROWS, count)] * 2 + [f32(PIX_DEV, 2 * NODES)],
        [end_e, h3, e3, h4, e4, v, w, places, valid, near_v, near_places]
        + [inside, across, changes, early, pixels],
        work + [pltpu.VMEM((SECOND, LAYER), F32)] * 2,
    )
    parts = lax.all_to_all(sums, "exc", split_axis=0, concat_axis=0, tiled=True)
    share = PIX_DEV // owners
    out_e, out_h, eps, drude = call(
        functools.partial(total_kernel, owners),
        [f32(ROWS, count)] * 2 + [f32(share, NODES)] * 2,
        [parts, e4, h4],
        [pltpu.VMEM((2, share, NODES), F32), pltpu.SemaphoreType.DMA((4,))],
        out_spaces=[pltpu.HBM] * 4,
    )
    return out_e[None], out_h[None], eps.T, drude.T


def solution(mesh):
    return jax.shard_map(
        local,
        mesh=mesh,
        in_specs=(
            P("exc", None, "space"),
            P("exc", None, "space"),
            P("exc", None, "space"),
            P("exc", None, None, "space"),
            P(None, "space"),
            P(None, "space"),
            P(None, "space"),
            P("space"),
            P("exc", "space"),
            P("exc", None, "space"),
        ),
        out_specs=(
            P("exc", None, "space"),
            P("exc", None, "space"),
            P(None, ("space", "exc")),
            P(None, ("space", "exc")),
        ),
        check_vma=False,
    )
```
